32 devices in a mesh: slab: 4 (over y, x), chan: 8 (over z, core).
Axes of the slice: x: 2, y: 2, z: 4, core: 2. Of those that a mesh axis runs over, the one named last changes fastest.
Arguments:
- x_in: bfloat16 [256, 8, 8, 128], P('chan', 'slab'), may hold values from -6 to 6
- weight: bfloat16 [256, 27, 256], P('chan'), may hold values from -0.109375 to 0.109375
- bias_vec: bfloat16 [256], P('chan'), may hold values from -3 to 3
- grad_out: bfloat16 [256, 8, 8, 128], P('chan', 'slab'), may hold values from -6 to 6
Outputs:
- activation: bfloat16 [256, 8, 8, 128], P('chan', 'slab')
- input_grad: bfloat16 [256, 8, 8, 128], P('chan', 'slab')
- weight_grad: float32 [256, 27, 256], P('chan')
- bias_grad: float32 [256], P('chan')
The draws below stay inside these ranges and needn't reach their ends.
All inputs are finite; a program needn't handle non-finite values.
Results may differ from the reference program's by a relative error of at most 0.008.
Values may be sent and summed in bfloat16 or wider, within the bound.
No kernel may reach another device: no remote copies, remote signals or barrier semaphores. Data moves between devices by JAX's collectives and lax.ppermute only.
A program may use at most 64 MiB of HBM per device.

```python
import math
import jax
import jax.numpy as jnp
from jax import lax

CIN = 256
COUT = 256
NY = 8
NZ = 128
NX = 8


def spiked(values, stream_key, source, target, parts, factor):
    owner, partner = [(jnp.arange(values.shape[position]) // (values.shape[position] // parts)).reshape([-1 if axis == position else 1 for axis in range(values.ndim)]) for position in (source, target)]
    chosen = jax.random.permutation(stream_key, parts)[partner]
    strong = (owner == chosen) | (owner == (partner + parts // 2) % parts)
    return jnp.where(strong, factor * values, values)


def steps_of(key, shape, split, least, top_value):
    def one(dim, shards_of):
        draws = jax.random.uniform(jax.random.fold_in(jax.random.fold_in(key, 6), dim), (shards_of,), jnp.float32, least / len(split), top_value / len(split))
        return jnp.repeat(jnp.exp(draws), shape[dim] // shards_of).reshape((-1,) + (1,) * (len(shape) - dim - 1))

    level = one(*split[0])
    for cut in split[1:]:
        level = level * one(*cut)
    return level


def bell_draw(own_key, shape, width, limit, pieces=(), held_as=jnp.bfloat16):
    array = width * jax.random.normal(own_key, shape, jnp.float32)
    if pieces:
        array = array * steps_of(own_key, shape, pieces, -0.22, 0.18)
    return jnp.clip(array, -limit, limit).astype(held_as)


def noise_with(own_key, extent, deviation, bound, pieces, heavy, kind=jnp.bfloat16):
    result = deviation * jax.random.normal(own_key, extent, jnp.float32)
    if pieces:
        result = result * steps_of(own_key, extent, pieces, -0.22, 0.18)
    return jnp.clip(spiked(result, jax.random.fold_in(own_key, 3), *heavy), -bound, bound).astype(kind)


def setup_inputs(seed: int = 0) -> dict:
    seeds = jax.random.split(jax.random.key(seed), 5)
    x_in = bell_draw(seeds[0], (CIN, NX, NY, NZ), 1.0, 6.0, ((0, 8), (1, 4)))
    weight = noise_with(seeds[1], (COUT, 27, CIN), (27 * CIN) ** -0.5, 0.109375, ((0, 8),), (0, 2, 8, 2.0))
    bias_vec = bell_draw(seeds[2], (COUT,), 0.5, 3.0, ((0, 8),))
    grad_out = bell_draw(seeds[3], (COUT, NX, NY, NZ), 1.0, 6.0, ((0, 8), (1, 4)))
    return dict(x_in=x_in, weight=weight, bias_vec=bias_vec, grad_out=grad_out)


def tap_list():
    return [(9 * i + 3 * j + l, i, j, l) for i in range(3) for j in range(3) for l in range(3)]

def reference(x_in, weight, bias_vec, grad_out):
    in_total = x_in.shape[0]
    out_total = weight.shape[0]
    n_cells = NX * NY * NZ
    pre_act = jnp.zeros((out_total, n_cells), jnp.float32) + bias_vec.astype(jnp.float32)[:, None]
    for k, i, j, l in tap_list():
        moved = jnp.roll(x_in, (1 - i, 1 - j, 1 - l), axis=(1, 2, 3)).reshape(in_total, n_cells)
        pre_act = pre_act + jnp.dot(weight[:, k, :], moved, preferred_element_type=jnp.float32)
    sigmoid_v = jax.nn.sigmoid(pre_act)
    activation = (pre_act * sigmoid_v).astype(jnp.bfloat16)
    slope = sigmoid_v * (1.0 + pre_act * (1.0 - sigmoid_v))
    grad_pre = (grad_out.reshape(out_total, n_cells).astype(jnp.float32) * slope).astype(jnp.bfloat16)
    grad_box = grad_pre.reshape(out_total, NX, NY, NZ)
    grad_scale = 1.0 / math.sqrt(n_cells)
    input_sum = jnp.zeros((in_total, n_cells), jnp.float32)
    filter_list = []
    for k, i, j, l in tap_list():
        back = jnp.roll(grad_box, (i - 1, j - 1, l - 1), axis=(1, 2, 3)).reshape(out_total, n_cells)
        input_sum = input_sum + jnp.dot(weight[:, k, :].T, back, preferred_element_type=jnp.float32)
        moved = jnp.roll(x_in, (1 - i, 1 - j, 1 - l), axis=(1, 2, 3)).reshape(in_total, n_cells)
        filter_list.append(lax.dot_general(grad_pre, moved, (((1,), (1,)), ((), ())), preferred_element_type=jnp.float32))
    weight_grad = jnp.stack(filter_list, axis=1) * grad_scale
    bias_grad = grad_scale * lax.optimization_barrier(jnp.sum(grad_pre.astype(jnp.float32), axis=1))
    return (activation.reshape(out_total, NX, NY, NZ), input_sum.astype(jnp.bfloat16).reshape(in_total, NX, NY, NZ), weight_grad, bias_grad)
```

```python
import functools
import math

import jax
import jax.numpy as jnp
from jax import lax
from jax.experimental import pallas as pl
from jax.experimental.pallas import tpu as pltpu
from jax.sharding import PartitionSpec as P

LANES = 128
VMEM = pl.BlockSpec(memory_space=pltpu.VMEM)
SMEM = pl.BlockSpec(memory_space=pltpu.SMEM)


def with_halo(block, sides, width):
    for axis, dim in sides:
        count = lax.axis_size(axis)
        forward = [(i, i + 1) for i in range(count - 1)]
        forward.append((count - 1, 0))
        backward = [(target, source) for source, target in forward]
        low = lax.ppermute(
            lax.slice_in_dim(block, block.shape[dim] - width, None, axis=dim), axis, forward
        )
        high = lax.ppermute(lax.slice_in_dim(block, 0, width, axis=dim), axis, backward)
        block = jnp.concatenate([low, block, high], axis=dim)
    return block


def tap_list():
    return [(9 * i + 3 * j + l, i, j, l) for i in range(3) for j in range(3) for l in range(3)]


def plain(x_in, weight, bias_vec, grad_out):
    out_local, n_taps, in_total = weight.shape
    n_planes, n_rows, n_depth = (x_in.shape[1], x_in.shape[2], x_in.shape[3])
    rimmed = with_halo(x_in, (("slab", 1),), 1)
    padded = lax.all_gather(rimmed, "chan", axis=0, tiled=True)
    own_planes = padded[:, 1 : n_planes + 1]
    pre_act = (
        jnp.zeros((out_local, n_planes, n_rows, n_depth), jnp.float32)
        + bias_vec.astype(jnp.float32)[:, None, None, None]
    )
    for i in range(3):
        w_plane = jnp.transpose(weight[:, 9 * i : 9 * i + 9], (1, 0, 2)).reshape(
            9 * out_local, in_total
        )
        plane_part = jnp.dot(
            w_plane,
            padded[:, i : i + n_planes].reshape(in_total, -1),
            preferred_element_type=jnp.float32,
        )
        plane_part = plane_part.reshape(9, out_local, n_planes, n_rows, n_depth)
        for j in range(3):
            for l in range(3):
                pre_act = pre_act + jnp.roll(plane_part[3 * j + l], (1 - j, 1 - l), axis=(2, 3))
    sigmoid_v = jax.nn.sigmoid(pre_act)
    activation = (pre_act * sigmoid_v).astype(jnp.bfloat16)
    slope = sigmoid_v * (1.0 + pre_act * (1.0 - sigmoid_v))
    grad_pre = (grad_out.astype(jnp.float32) * slope).astype(jnp.bfloat16)
    padded_grad = with_halo(grad_pre, (("slab", 1),), 1)
    shifted = jnp.stack(
        [
            jnp.roll(padded_grad[:, 2 - i : 2 - i + n_planes], (j - 1, l - 1), axis=(2, 3))
            for k, i, j, l in tap_list()
        ],
        0,
    )
    shifted = shifted.reshape(n_taps * out_local, -1)
    grad_scale = 1.0 / math.sqrt(lax.axis_size("slab") * n_planes * n_rows * n_depth)
    filter_local = lax.dot_general(
        shifted,
        own_planes.reshape(in_total, -1),
        (((1,), (1,)), ((), ())),
        preferred_element_type=jnp.float32,
    )
    filter_part = (
        jnp.transpose(filter_local.reshape(n_taps, out_local, in_total), (1, 0, 2)) * grad_scale
    )
    bias_part = grad_scale * jnp.sum(grad_pre.astype(jnp.float32), axis=(1, 2, 3))
    bias_row = jnp.concatenate(
        [bias_part[:, None, None], jnp.zeros((out_local, 1, in_total - 1), jnp.float32)], 2
    )
    summed_filters = lax.psum(jnp.concatenate([filter_part, bias_row], 1), "slab")
    weight_grad = summed_filters[:, :n_taps]
    bias_grad = summed_filters[:, n_taps, 0]
    flat_w = jnp.transpose(weight, (1, 0, 2)).reshape(n_taps * out_local, in_total)
    product = lax.dot_general(
        flat_w, shifted, (((0,), (0,)), ((), ())), preferred_element_type=jnp.float32
    )
    grad_in = lax.psum_scatter(
        product.reshape(
            in_total // lax.axis_size("chan") * lax.axis_size("chan"), n_planes, n_rows, n_depth
        ),
        "chan",
        scatter_dimension=0,
        tiled=True,
    )
    return (activation, grad_in.astype(jnp.bfloat16), weight_grad, bias_grad)


def call(body, out_shape, operands, specs=None, scratch=(), flops=0, name=None):
    read = sum(math.prod(a.shape) * a.dtype.itemsize for a in operands)
    written = sum(math.prod(a.shape) * a.dtype.itemsize for a in out_shape)
    return pl.pallas_call(
        body,
        out_shape=out_shape,
        in_specs=specs or [VMEM] * len(operands),
        out_specs=[VMEM] * len(out_shape),
        scratch_shapes=list(scratch),
        compiler_params=pltpu.CompilerParams(vmem_limit_bytes=24 * 2**20),
        cost_estimate=pl.CostEstimate(
            flops=flops, bytes_accessed=read + written, transcendentals=0
        ),
        name=name,
    )(*operands)


def shape_of(shape, dtype):
    return jax.ShapeDtypeStruct(shape, dtype)


def forward_body(n, rows, o, count, me_ref, w_ref, *refs):
    blocks = refs[:count]
    own_ref, low_ref, high_ref, x_ref, acc = refs[count:]
    me = me_ref[0]
    for r in range(count // 2):
        for side in range(2):
            mine = me if side == 0 else me + 1 - 2 * lax.rem(me, 2)
            source = lax.rem(mine - 2 * r + count, count)
            place = pl.ds(pl.multiple_of(source * o, o), o)
            for k in range(n * rows):
                x_ref[place, k * LANES : (k + 1) * LANES] = blocks[2 * r + side][k]
    w = w_ref[...].reshape(27 * o, w_ref.shape[2])
    seen = set()
    for p in range(n):
        for t in range(0, rows, 2):
            at = (p * rows + t) * LANES
            part = jnp.dot(
                w, x_ref[:, at : at + 2 * LANES], preferred_element_type=jnp.float32
            )
            for k, i, j, l in tap_list():
                for h in range(2):
                    slot = (l, p + 2 - i, (t + h + 1 - j) % rows)
                    value = part[k * o : (k + 1) * o, h * LANES : (h + 1) * LANES]
                    if slot in seen:
                        acc[slot] += value
                    else:
                        acc[slot] = value
                        seen.add(slot)
    for q in range(n + 2):
        for y in range(rows):
            total = (
                pltpu.roll(acc[0, q, y], 1, 1)
                + acc[1, q, y]
                + pltpu.roll(acc[2, q, y], LANES - 1, 1)
            )
            if q == 0:
                low_ref[y] = total.astype(low_ref.dtype)
            elif q == n + 1:
                high_ref[y] = total.astype(high_ref.dtype)
            else:
                own_ref[(q - 1) * rows + y] = total


def activation_body(n, rows, own_ref, below_ref, above_ref, bias_ref, go_ref, act_ref, gp_ref):
    for p in range(n):
        for y in range(rows):
            k = p * rows + y
            pre = own_ref[k] + bias_ref[...]
            if p == 0:
                pre = pre + below_ref[y].astype(jnp.float32)
            if p == n - 1:
                pre = pre + above_ref[y].astype(jnp.float32)
            s = jax.nn.sigmoid(pre)
            act_ref[k] = (pre * s).astype(act_ref.dtype)
            slope = s * (1.0 + pre * (1.0 - s))
            gp_ref[k] = (go_ref[k].astype(jnp.float32) * slope).astype(gp_ref.dtype)


def input_grad_body(
    n, rows, o, count, me_ref, gp_ref, below_ref, above_ref, wt_ref, mine_ref, other_ref, s_ref, w_ref
):
    me = me_ref[0]
    core = lax.rem(me, 2)
    for side in range(2):
        for r in range(count // 2):
            owner = lax.rem(me - core + 2 * r, count) + (core if side == 0 else 1 - core)
            rel = (side * (count // 2) + r) * o
            w_ref[rel : rel + o] = wt_ref[pl.ds(pl.multiple_of(owner * o, o), o)]
    for q in range(n + 2):
        for y in range(rows):
            if q == 0:
                value = below_ref[y]
            elif q == n + 1:
                value = above_ref[y]
            else:
                value = gp_ref[(q - 1) * rows + y]
            wide = value.astype(jnp.float32)
            turned = [
                pltpu.roll(wide, LANES - 1, 1).astype(value.dtype),
                value,
                pltpu.roll(wide, 1, 1).astype(value.dtype),
            ]
            for k, i, j, l in tap_list():
                p = q - 2 + i
                if 0 <= p < n:
                    at = (p * rows + (y + j - 1) % rows) * LANES
                    s_ref[k * o : (k + 1) * o, at : at + LANES] = turned[l]
    w = w_ref[...]
    half = count // 2 * o
    for t in range(0, n * rows, 2):
        part = jnp.dot(
            w, s_ref[:, t * LANES : (t + 2) * LANES], preferred_element_type=jnp.float32
        ).astype(mine_ref.dtype)
        for h in range(2):
            for r in range(count // 2):
                cut = part[r * o : (r + 1) * o, h * LANES : (h + 1) * LANES]
                mine_ref[r, t + h] = cut
                cut = part[half + r * o : half + (r + 1) * o, h * LANES : (h + 1) * LANES]
                other_ref[r, t + h] = cut


def filter_grad_body(scale, taps, s_ref, x_ref, gp_ref, first_ref, second_ref):
    o = gp_ref.shape[1]
    full = lax.dot_general(
        s_ref[...], x_ref[...], (((1,), (1,)), ((), ())), preferred_element_type=jnp.float32
    )
    full = (full * scale).astype(first_ref.dtype)
    first_ref[...] = full[: taps * o]
    second_ref[: (27 - taps) * o] = full[taps * o :]
    total = jnp.sum(gp_ref[...].astype(jnp.float32), axis=0)
    total = jnp.sum(total, axis=1, keepdims=True) * scale
    second_ref[(27 - taps) * o :] = jnp.broadcast_to(
        total, (o, second_ref.shape[1])
    ).astype(second_ref.dtype)


def pair_body(a_ref, b_ref, out_ref):
    out_ref[...] = (a_ref[...].astype(jnp.float32) + b_ref[...].astype(jnp.float32)).astype(
        out_ref.dtype
    )


def split_sum_body(a_ref, b_ref, *outs):
    for r, out in enumerate(outs):
        total = a_ref[r].astype(jnp.float32) + b_ref[r].astype(jnp.float32)
        out[...] = total.astype(out.dtype)


def sum_body(*refs):
    total = refs[0][...].astype(jnp.float32)
    for ref in refs[1:-1]:
        total = total + ref[...].astype(jnp.float32)
    refs[-1][...] = total.astype(refs[-1].dtype)


def last_body(taps, a_ref, b_ref, c_ref, d_ref, out_ref, bias_ref):
    o = out_ref.shape[1]
    f32 = jnp.float32
    for k in range(27):
        left, right, at = (a_ref, b_ref, k) if k < taps else (c_ref, d_ref, k - taps)
        cut = slice(at * o, (at + 1) * o)
        out_ref[k] = left[cut].astype(f32) + right[cut].astype(f32)
    cut = slice((27 - taps) * o, (28 - taps) * o)
    bias_ref[...] = (c_ref[cut].astype(f32) + d_ref[cut].astype(f32))[:, :LANES]


def rotate(value, axis, step):
    count = lax.axis_size(axis)
    return lax.ppermute(value, axis, [(i, (i + step) % count) for i in range(count)])


def swap(value, axis, bit):
    return lax.ppermute(value, axis, [(i, i ^ bit) for i in range(lax.axis_size(axis))])


def on_device(x_in, weight, bias_vec, grad_out):
    count = lax.axis_size("chan")
    o, _, c_all = weight.shape
    _, n, rows, depth = x_in.shape
    f32, bf16 = jnp.float32, jnp.bfloat16
    cells = n * rows
    scale = 1.0 / math.sqrt(lax.axis_size("slab") * cells * depth)
    me = lax.axis_index("chan").astype(jnp.int32).reshape(1)

    def by_row(a):
        return jnp.transpose(a, (1, 2, 0, 3)).reshape(cells, o, depth)

    def by_channel(a):
        return jnp.transpose(a.reshape(n, rows, o, depth), (2, 0, 1, 3))

    x_own = by_row(x_in)
    blocks = [x_own, swap(x_own, "chan", 1)]
    for r in range(1, count // 2):
        far = rotate(x_own, "chan", 2 * r)
        blocks += [far, swap(far, "chan", 1)]
    w_taps = jnp.transpose(weight, (1, 0, 2))
    w_back = jnp.transpose(w_taps.reshape(27 * o, c_all))
    go = by_row(grad_out)
    bias = jnp.broadcast_to(bias_vec.astype(f32)[:, None], (o, depth))

    own, low, high, x_all = call(
        functools.partial(forward_body, n, rows, o, count),
        [
            shape_of((cells, o, depth), f32),
            shape_of((rows, o, depth), bf16),
            shape_of((rows, o, depth), bf16),
            shape_of((c_all, cells * depth), bf16),
        ],
        [me, w_taps, *blocks],
        [SMEM] + [VMEM] * (1 + count),
        [pltpu.VMEM((3, n + 2, rows, o, depth), f32)],
        flops=2 * 27 * o * c_all * cells * depth,
        name="forward",
    )
    above = rotate(low, "slab", -1)
    below = rotate(high, "slab", 1)
    act, gp = call(
        functools.partial(activation_body, n, rows),
        [shape_of((cells, o, depth), bf16)] * 2,
        [own, below, above, bias, go],
        name="activation",
    )
    gp_above = rotate(gp[:rows], "slab", -1)
    gp_below = rotate(gp[cells - rows :], "slab", 1)
    half = (count // 2, cells, o, depth)
    mine, other, stacked = call(
        functools.partial(input_grad_body, n, rows, o, count),
        [
            shape_of(half, bf16),
            shape_of(half, bf16),
            shape_of((27 * o, cells * depth), bf16),
        ],
        [me, gp, gp_below, gp_above, w_back],
        [SMEM] + [VMEM] * 4,
        [pltpu.VMEM((c_all, 27 * o), bf16)],
        flops=2 * 27 * o * c_all * cells * depth,
        name="input_grad",
    )
    other = swap(other, "chan", 1)
    taps = 14
    first, second = call(
        functools.partial(filter_grad_body, scale, taps),
        [shape_of((taps * o, c_all), bf16), shape_of(((28 - taps) * o, c_all), bf16)],
        [stacked, x_all, gp],
        flops=2 * 27 * o * c_all * cells * depth,
        name="filter_grad",
    )
    first_far = swap(first, "slab", 1)
    second_far = swap(second, "slab", 2)
    sums = call(
        split_sum_body,
        [shape_of((cells, o, depth), f32)]
        + [shape_of((cells, o, depth), bf16)] * (count // 2 - 1),
        [mine, other],
        name="pair_sum",
    )
    far = [rotate(sums[r], "chan", 2 * r) for r in range(1, count // 2)]
    (first,) = call(pair_body, [shape_of(first.shape, bf16)], [first, first_far], name="first")
    (second,) = call(pair_body, [shape_of(second.shape, bf16)], [second, second_far], name="second")
    first_far = swap(first, "slab", 2)
    second_far = swap(second, "slab", 1)
    (grad_in,) = call(sum_body, [shape_of((cells, o, depth), bf16)], [sums[0], *far], name="sum")
    weight_grad, bias_grad = call(
        functools.partial(last_body, taps),
        [shape_of((27, o, c_all), f32), shape_of((o, LANES), f32)],
        [first, first_far, second, second_far],
        name="last",
    )
    return (
        by_channel(act),
        by_channel(grad_in),
        jnp.transpose(weight_grad, (1, 0, 2)),
        bias_grad[:, 0],
    )


def solution(mesh):
    placed = (
        P("chan", "slab", None, None),
        P("chan", None, None),
        P("chan"),
        P("chan", "slab", None, None),
    )

    def body(x_in, weight, bias_vec, grad_out):
        tiled = (
            weight.shape[0] % 32 == 0
            and x_in.shape[3] == LANES
            and lax.axis_size("slab") == 4
            and lax.axis_size("chan") % 2 == 0
        )
        return (on_device if tiled else plain)(x_in, weight, bias_vec, grad_out)

    return jax.shard_map(
        body,
        mesh=mesh,
        in_specs=placed,
        out_specs=(
            P("chan", "slab", None, None),
            P("chan", "slab", None, None),
            P("chan", None, None),
            P("chan"),
        ),
        check_vma=False,
    )
```

```python
import functools
import math

import jax
import jax.numpy as jnp
from jax import lax
from jax.experimental import pallas as pl
from jax.experimental.pallas import tpu as pltpu
from jax.sharding import PartitionSpec as P

LANES = 128
VMEM = pl.BlockSpec(memory_space=pltpu.VMEM)
SMEM = pl.BlockSpec(memory_space=pltpu.SMEM)


def with_halo(block, sides, width):
    for axis, dim in sides:
        count = lax.axis_size(axis)
        forward = [(i, i + 1) for i in range(count - 1)]
        forward.append((count - 1, 0))
        backward = [(target, source) for source, target in forward]
        low = lax.ppermute(
            lax.slice_in_dim(block, block.shape[dim] - width, None, axis=dim), axis, forward
        )
        high = lax.ppermute(lax.slice_in_dim(block, 0, width, axis=dim), axis, backward)
        block = jnp.concatenate([low, block, high], axis=dim)
    return block


def tap_list():
    return [(9 * i + 3 * j + l, i, j, l) for i in range(3) for j in range(3) for l in range(3)]


def plain(x_in, weight, bias_vec, grad_out):
    out_local, n_taps, in_total = weight.shape
    n_planes, n_rows, n_depth = (x_in.shape[1], x_in.shape[2], x_in.shape[3])
    rimmed = with_halo(x_in, (("slab", 1),), 1)
    padded = lax.all_gather(rimmed, "chan", axis=0, tiled=True)
    own_planes = padded[:, 1 : n_planes + 1]
    pre_act = (
        jnp.zeros((out_local, n_planes, n_rows, n_depth), jnp.float32)
        + bias_vec.astype(jnp.float32)[:, None, None, None]
    )
    for i in range(3):
        w_plane = jnp.transpose(weight[:, 9 * i : 9 * i + 9], (1, 0, 2)).reshape(
            9 * out_local, in_total
        )
        plane_part = jnp.dot(
            w_plane,
            padded[:, i : i + n_planes].reshape(in_total, -1),
            preferred_element_type=jnp.float32,
        )
        plane_part = plane_part.reshape(9, out_local, n_planes, n_rows, n_depth)
        for j in range(3):
            for l in range(3):
                pre_act = pre_act + jnp.roll(plane_part[3 * j + l], (1 - j, 1 - l), axis=(2, 3))
    sigmoid_v = jax.nn.sigmoid(pre_act)
    activation = (pre_act * sigmoid_v).astype(jnp.bfloat16)
    slope = sigmoid_v * (1.0 + pre_act * (1.0 - sigmoid_v))
    grad_pre = (grad_out.astype(jnp.float32) * slope).astype(jnp.bfloat16)
    padded_grad = with_halo(grad_pre, (("slab", 1),), 1)
    shifted = jnp.stack(
        [
            jnp.roll(padded_grad[:, 2 - i : 2 - i + n_planes], (j - 1, l - 1), axis=(2, 3))
            for k, i, j, l in tap_list()
        ],
        0,
    )
    shifted = shifted.reshape(n_taps * out_local, -1)
    grad_scale = 1.0 / math.sqrt(lax.axis_size("slab") * n_planes * n_rows * n_depth)
    filter_local = lax.dot_general(
        shifted,
        own_planes.reshape(in_total, -1),
        (((1,), (1,)), ((), ())),
        preferred_element_type=jnp.float32,
    )
    filter_part = (
        jnp.transpose(filter_local.reshape(n_taps, out_local, in_total), (1, 0, 2)) * grad_scale
    )
    bias_part = grad_scale * jnp.sum(grad_pre.astype(jnp.float32), axis=(1, 2, 3))
    bias_row = jnp.concatenate(
        [bias_part[:, None, None], jnp.zeros((out_local, 1, in_total - 1), jnp.float32)], 2
    )
    summed_filters = lax.psum(jnp.concatenate([filter_part, bias_row], 1), "slab")
    weight_grad = summed_filters[:, :n_taps]
    bias_grad = summed_filters[:, n_taps, 0]
    flat_w = jnp.transpose(weight, (1, 0, 2)).reshape(n_taps * out_local, in_total)
    product = lax.dot_general(
        flat_w, shifted, (((0,), (0,)), ((), ())), preferred_element_type=jnp.float32
    )
    grad_in = lax.psum_scatter(
        product.reshape(
            in_total // lax.axis_size("chan") * lax.axis_size("chan"), n_planes, n_rows, n_depth
        ),
        "chan",
        scatter_dimension=0,
        tiled=True,
    )
    return (activation, grad_in.astype(jnp.bfloat16), weight_grad, bias_grad)


def call(body, out_shape, operands, specs=None, scratch=(), flops=0, name=None):
    read = sum(math.prod(a.shape) * a.dtype.itemsize for a in operands)
    written = sum(math.prod(a.shape) * a.dtype.itemsize for a in out_shape)
    return pl.pallas_call(
        body,
        out_shape=out_shape,
        in_specs=specs or [VMEM] * len(operands),
        out_specs=[VMEM] * len(out_shape),
        scratch_shapes=list(scratch),
        compiler_params=pltpu.CompilerParams(vmem_limit_bytes=24 * 2**20),
        cost_estimate=pl.CostEstimate(
            flops=flops, bytes_accessed=read + written, transcendentals=0
        ),
        name=name,
    )(*operands)


def shape_of(shape, dtype):
    return jax.ShapeDtypeStruct(shape, dtype)


def prepare_body(w_ref, bias_ref, flat_ref, back_ref, wide_ref):
    flat = w_ref[...].reshape(flat_ref.shape)
    flat_ref[...] = flat
    back_ref[...] = jnp.transpose(flat)
    wide_ref[...] = jnp.broadcast_to(bias_ref[...].astype(jnp.float32), wide_ref.shape)


def forward_body(n, rows, o, owner_ref, w_ref, *refs):
    blocks = refs[:8]
    own_ref, low_ref, high_ref, x_ref, acc = refs[10:]
    for b in range(8):
        place = pl.ds(pl.multiple_of(owner_ref[b] * o, o), o)
        for k in range(n * rows):
            x_ref[place, k * LANES : (k + 1) * LANES] = blocks[b][k]
    w = w_ref[...]
    seen = set()
    for p in range(n):
        for t in range(0, rows, 2):
            at = (p * rows + t) * LANES
            part = jnp.dot(
                w, x_ref[:, at : at + 2 * LANES], preferred_element_type=jnp.float32
            )
            for k, i, j, l in tap_list():
                for h in range(2):
                    slot = (l, p + 2 - i, (t + h + 1 - j) % rows)
                    value = part[k * o : (k + 1) * o, h * LANES : (h + 1) * LANES]
                    if slot in seen:
                        acc[slot] += value
                    else:
                        acc[slot] = value
                        seen.add(slot)
    for q in range(n + 2):
        for y in range(rows):
            total = (
                pltpu.roll(acc[0, q, y], 1, 1)
                + acc[1, q, y]
                + pltpu.roll(acc[2, q, y], LANES - 1, 1)
            )
            if q == 0:
                low_ref[y] = total.astype(low_ref.dtype)
            elif q == n + 1:
                high_ref[y] = total.astype(high_ref.dtype)
            else:
                own_ref[(q - 1) * rows + y] = total
            if q == 1:
                low_ref[rows + y] = total.astype(low_ref.dtype)
            if q == n:
                high_ref[rows + y] = total.astype(high_ref.dtype)


def gradient_body(
    n,
    rows,
    o,
    scale,
    owner_ref,
    own_ref,
    low_ref,
    high_ref,
    below_ref,
    above_ref,
    bias_ref,
    go_ref,
    go_below_ref,
    go_above_ref,
    back_ref,
    act_ref,
    total_ref,
    s_ref,
    w_ref,
    other_ref,
):
    f32, bf16 = jnp.float32, jnp.bfloat16
    for b in range(8):
        place = pl.ds(pl.multiple_of(owner_ref[b] * o, o), o)
        w_ref[b * o : (b + 1) * o] = back_ref[place]
    total = jnp.zeros((o, LANES), f32)
    for q in range(n + 2):
        for y in range(rows):
            if q == 0:
                pre = below_ref[rows + y].astype(f32) + low_ref[y].astype(f32)
                go = go_below_ref[y]
            elif q == n + 1:
                pre = above_ref[rows + y].astype(f32) + high_ref[y].astype(f32)
                go = go_above_ref[y]
            else:
                pre = own_ref[(q - 1) * rows + y]
                go = go_ref[(q - 1) * rows + y]
                if q == 1:
                    pre = pre + below_ref[y].astype(f32)
                if q == n:
                    pre = pre + above_ref[y].astype(f32)
            pre = pre + bias_ref[...]
            s = jax.nn.sigmoid(pre)
            slope = s * (1.0 + pre * (1.0 - s))
            value = (go.astype(f32) * slope).astype(bf16)
            wide = value.astype(f32)
            if 1 <= q <= n:
                act_ref[(q - 1) * rows + y] = (pre * s).astype(bf16)
                total = total + wide
            turned = [
                pltpu.roll(wide, LANES - 1, 1).astype(bf16),
                value,
                pltpu.roll(wide, 1, 1).astype(bf16),
            ]
            for k, i, j, l in tap_list():
                p = q - 2 + i
                if 0 <= p < n:
                    at = (p * rows + (y + j - 1) % rows) * LANES
                    s_ref[k * o : (k + 1) * o, at : at + LANES] = turned[l]
    total_ref[...] = jnp.broadcast_to(
        jnp.sum(total, axis=1, keepdims=True) * scale, total_ref.shape
    )
    input_grad(n * rows, o, w_ref[4 * o :], s_ref, other_ref)


def input_grad(cells, o, w, s_ref, out_ref):
    for t in range(0, cells, 2):
        part = jnp.dot(
            w, s_ref[:, t * LANES : (t + 2) * LANES], preferred_element_type=jnp.float32
        ).astype(out_ref.dtype)
        for h in range(2):
            for r in range(4):
                cut = part[r * o : (r + 1) * o, h * LANES : (h + 1) * LANES]
                out_ref[r, t + h] = cut


def filter_grad_body(scale, taps, o, s_ref, x_ref, w_ref, total_ref, mine_ref, first_ref, second_ref):
    input_grad(mine_ref.shape[1], o, w_ref[: 4 * o], s_ref, mine_ref)
    full = lax.dot_general(
        s_ref[...], x_ref[...], (((1,), (1,)), ((), ())), preferred_element_type=jnp.float32
    )
    full = (full * scale).astype(first_ref.dtype)
    first_ref[...] = full[: taps * o]
    second_ref[: (27 - taps) * o] = full[taps * o :]
    row = jnp.concatenate([total_ref[...]] * (second_ref.shape[1] // LANES), axis=1)
    second_ref[(27 - taps) * o :] = row.astype(second_ref.dtype)


def middle_body(*refs):
    for p in range(3):
        total = refs[2 * p][...].astype(jnp.float32) + refs[2 * p + 1][...].astype(jnp.float32)
        refs[6 + p][...] = total.astype(refs[6 + p].dtype)


def split_sum_body(a_ref, b_ref, *outs):
    for r, out in enumerate(outs):
        total = a_ref[r].astype(jnp.float32) + b_ref[r].astype(jnp.float32)
        out[...] = total.astype(out.dtype)


def last_body(taps, a_ref, b_ref, c_ref, d_ref, g_ref, h_ref, k_ref, out_ref, bias_ref, grad_ref):
    o = out_ref.shape[1]
    f32 = jnp.float32
    for k in range(27):
        left, right, at = (a_ref, b_ref, k) if k < taps else (c_ref, d_ref, k - taps)
        cut = slice(at * o, (at + 1) * o)
        out_ref[k] = left[cut].astype(f32) + right[cut].astype(f32)
    cut = slice((27 - taps) * o, (28 - taps) * o)
    bias_ref[...] = (c_ref[cut].astype(f32) + d_ref[cut].astype(f32))[:, :LANES]
    total = g_ref[...] + h_ref[...].astype(f32) + k_ref[...].astype(f32)
    grad_ref[...] = total.astype(grad_ref.dtype)


def rotate(value, axis, step):
    count = lax.axis_size(axis)
    return lax.ppermute(value, axis, [(i, (i + step) % count) for i in range(count)])


def swap(value, axis, bit):
    return lax.ppermute(value, axis, [(i, i ^ bit) for i in range(lax.axis_size(axis))])


def on_device(x_in, weight, bias_vec, grad_out):
    o, _, c_all = weight.shape
    _, n, rows, depth = x_in.shape
    f32, bf16 = jnp.float32, jnp.bfloat16
    cells = n * rows
    flops = 2 * 27 * o * c_all * cells * depth
    scale = 1.0 / math.sqrt(lax.axis_size("slab") * cells * depth)
    me = lax.axis_index("chan").astype(jnp.int32)
    owners = jnp.bitwise_xor(me, jnp.array([0, 2, 4, 6, 1, 3, 5, 7], jnp.int32))

    def by_row(a):
        return jnp.transpose(a, (1, 2, 0, 3)).reshape(cells, o, depth)

    def by_channel(a):
        return jnp.transpose(a.reshape(n, rows, o, depth), (2, 0, 1, 3))

    x_own = by_row(x_in)
    x_a = swap(x_own, "chan", 2)
    x_b = swap(x_own, "chan", 4)
    x_side = swap(x_own, "chan", 1)
    w_taps = jnp.transpose(weight, (1, 0, 2))
    w_flat, w_back, bias = call(
        prepare_body,
        [
            shape_of((27 * o, c_all), bf16),
            shape_of((c_all, 27 * o), bf16),
            shape_of((o, LANES), f32),
        ],
        [w_taps, bias_vec[:, None]],
        name="prepare",
    )
    go = by_row(grad_out)
    x_a, w_flat, w_back, bias, go = lax.optimization_barrier((x_a, w_flat, w_back, bias, go))
    x_a_side = swap(x_a, "chan", 1)
    x_ab = swap(x_b, "chan", 2)
    x_b_side = swap(x_b, "chan", 1)
    go_above = rotate(go[:rows], "slab", -1)
    go_below = rotate(go[cells - rows :], "slab", 1)
    x_ab_side = swap(x_ab, "chan", 1)
    blocks = [x_own, x_a, x_b, x_ab, x_side, x_a_side, x_b_side, x_ab_side]

    own, low, high, x_all = call(
        functools.partial(forward_body, n, rows, o),
        [
            shape_of((cells, o, depth), f32),
            shape_of((2 * rows, o, depth), bf16),
            shape_of((2 * rows, o, depth), bf16),
            shape_of((c_all, cells * depth), bf16),
        ],
        [owners, w_flat, *blocks, go_below, go_above],
        [SMEM] + [VMEM] * 9 + [pl.BlockSpec(memory_space=pl.ANY)] * 2,
        [pltpu.VMEM((3, n + 2, rows, o, depth), f32)],
        flops=flops,
        name="forward",
    )
    above = rotate(low, "slab", -1)
    below = rotate(high, "slab", 1)
    half = (4, cells, o, depth)
    act, total, stacked, w_turned, other = call(
        functools.partial(gradient_body, n, rows, o, scale),
        [
            shape_of((cells, o, depth), bf16),
            shape_of((o, LANES), f32),
            shape_of((27 * o, cells * depth), bf16),
            shape_of((c_all, 27 * o), bf16),
            shape_of(half, bf16),
        ],
        [owners, own, low, high, below, above, bias, go, go_below, go_above, w_back],
        [SMEM] + [VMEM] * 10,
        flops=flops // 2,
        name="gradient",
    )
    other = swap(other, "chan", 1)
    taps = 14
    mine, first, second = call(
        functools.partial(filter_grad_body, scale, taps, o),
        [
            shape_of(half, bf16),
            shape_of((taps * o, c_all), bf16),
            shape_of(((28 - taps) * o, c_all), bf16),
        ],
        [stacked, x_all, w_turned, total],
        flops=flops + flops // 2,
        name="filter_grad",
    )
    g_own, g_a, g_b, g_ab = call(
        split_sum_body,
        [shape_of((cells, o, depth), f32)] + [shape_of((cells, o, depth), bf16)] * 3,
        [mine, other],
        name="pair_sum",
    )
    far = swap(g_ab, "chan", 2)
    near = swap(g_a, "chan", 2)
    first_far = swap(first, "slab", 1)
    second_far = swap(second, "slab", 2)
    g_b, first, second = call(
        middle_body,
        [shape_of(a.shape, bf16) for a in (g_b, first, second)],
        [g_b, far, first, first_far, second, second_far],
        name="middle",
    )
    across = swap(g_b, "chan", 4)
    first_far = swap(first, "slab", 2)
    second_far = swap(second, "slab", 1)
    weight_grad, bias_grad, grad_in = call(
        functools.partial(last_body, taps),
        [
            shape_of((27, o, c_all), f32),
            shape_of((o, LANES), f32),
            shape_of((cells, o, depth), bf16),
        ],
        [first, first_far, second, second_far, g_own, near, across],
        name="last",
    )
    return (
        by_channel(act),
        by_channel(grad_in),
        jnp.transpose(weight_grad, (1, 0, 2)),
        bias_grad[:, 0],
    )


def solution(mesh):
    placed = (
        P("chan", "slab", None, None),
        P("chan", None, None),
        P("chan"),
        P("chan", "slab", None, None),
    )

    def body(x_in, weight, bias_vec, grad_out):
        tiled = (
            weight.shape[0] % 32 == 0
            and x_in.shape[3] == LANES
            and lax.axis_size("slab") == 4
            and lax.axis_size("chan") == 8
            and x_in.shape[1] >= 2
        )
        return (on_device if tiled else plain)(x_in, weight, bias_vec, grad_out)

    return jax.shard_map(
        body,
        mesh=mesh,
        in_specs=placed,
        out_specs=(
            P("chan", "slab", None, None),
            P("chan", "slab", None, None),
            P("chan", None, None),
            P("chan"),
        ),
        check_vma=False,
    )
```

```python
import functools
import math

import jax
import jax.numpy as jnp
from jax import lax
from jax.experimental import pallas as pl
from jax.experimental.pallas import tpu as pltpu
from jax.sharding import PartitionSpec as P

LANES = 128
SUM_FLOPS = 20 * 10**8
VMEM = pl.BlockSpec(memory_space=pltpu.VMEM)
SMEM = pl.BlockSpec(memory_space=pltpu.SMEM)


def with_halo(block, sides, width):
    for axis, dim in sides:
        count = lax.axis_size(axis)
        forward = [(i, i + 1) for i in range(count - 1)]
        forward.append((count - 1, 0))
        backward = [(target, source) for source, target in forward]
        low = lax.ppermute(
            lax.slice_in_dim(block, block.shape[dim] - width, None, axis=dim), axis, forward
        )
        high = lax.ppermute(lax.slice_in_dim(block, 0, width, axis=dim), axis, backward)
        block = jnp.concatenate([low, block, high], axis=dim)
    return block


def tap_list():
    return [(9 * i + 3 * j + l, i, j, l) for i in range(3) for j in range(3) for l in range(3)]


def plain(x_in, weight, bias_vec, grad_out):
    out_local, n_taps, in_total = weight.shape
    n_planes, n_rows, n_depth = (x_in.shape[1], x_in.shape[2], x_in.shape[3])
    rimmed = with_halo(x_in, (("slab", 1),), 1)
    padded = lax.all_gather(rimmed, "chan", axis=0, tiled=True)
    own_planes = padded[:, 1 : n_planes + 1]
    pre_act = (
        jnp.zeros((out_local, n_planes, n_rows, n_depth), jnp.float32)
        + bias_vec.astype(jnp.float32)[:, None, None, None]
    )
    for i in range(3):
        w_plane = jnp.transpose(weight[:, 9 * i : 9 * i + 9], (1, 0, 2)).reshape(
            9 * out_local, in_total
        )
        plane_part = jnp.dot(
            w_plane,
            padded[:, i : i + n_planes].reshape(in_total, -1),
            preferred_element_type=jnp.float32,
        )
        plane_part = plane_part.reshape(9, out_local, n_planes, n_rows, n_depth)
        for j in range(3):
            for l in range(3):
                pre_act = pre_act + jnp.roll(plane_part[3 * j + l], (1 - j, 1 - l), axis=(2, 3))
    sigmoid_v = jax.nn.sigmoid(pre_act)
    activation = (pre_act * sigmoid_v).astype(jnp.bfloat16)
    slope = sigmoid_v * (1.0 + pre_act * (1.0 - sigmoid_v))
    grad_pre = (grad_out.astype(jnp.float32) * slope).astype(jnp.bfloat16)
    padded_grad = with_halo(grad_pre, (("slab", 1),), 1)
    shifted = jnp.stack(
        [
            jnp.roll(padded_grad[:, 2 - i : 2 - i + n_planes], (j - 1, l - 1), axis=(2, 3))
            for k, i, j, l in tap_list()
        ],
        0,
    )
    shifted = shifted.reshape(n_taps * out_local, -1)
    grad_scale = 1.0 / math.sqrt(lax.axis_size("slab") * n_planes * n_rows * n_depth)
    filter_local = lax.dot_general(
        shifted,
        own_planes.reshape(in_total, -1),
        (((1,), (1,)), ((), ())),
        preferred_element_type=jnp.float32,
    )
    filter_part = (
        jnp.transpose(filter_local.reshape(n_taps, out_local, in_total), (1, 0, 2)) * grad_scale
    )
    bias_part = grad_scale * jnp.sum(grad_pre.astype(jnp.float32), axis=(1, 2, 3))
    bias_row = jnp.concatenate(
        [bias_part[:, None, None], jnp.zeros((out_local, 1, in_total - 1), jnp.float32)], 2
    )
    summed_filters = lax.psum(jnp.concatenate([filter_part, bias_row], 1), "slab")
    weight_grad = summed_filters[:, :n_taps]
    bias_grad = summed_filters[:, n_taps, 0]
    flat_w = jnp.transpose(weight, (1, 0, 2)).reshape(n_taps * out_local, in_total)
    product = lax.dot_general(
        flat_w, shifted, (((0,), (0,)), ((), ())), preferred_element_type=jnp.float32
    )
    grad_in = lax.psum_scatter(
        product.reshape(
            in_total // lax.axis_size("chan") * lax.axis_size("chan"), n_planes, n_rows, n_depth
        ),
        "chan",
        scatter_dimension=0,
        tiled=True,
    )
    return (activation, grad_in.astype(jnp.bfloat16), weight_grad, bias_grad)


def call(body, out_shape, operands, specs=None, scratch=(), flops=0, name=None):
    read = sum(math.prod(a.shape) * a.dtype.itemsize for a in operands)
    written = sum(math.prod(a.shape) * a.dtype.itemsize for a in out_shape)
    return pl.pallas_call(
        body,
        out_shape=out_shape,
        in_specs=specs or [VMEM] * len(operands),
        out_specs=[VMEM] * len(out_shape),
        scratch_shapes=list(scratch),
        compiler_params=pltpu.CompilerParams(vmem_limit_bytes=24 * 2**20),
        cost_estimate=pl.CostEstimate(
            flops=flops, bytes_accessed=read + written, transcendentals=0
        ),
        name=name,
    )(*operands)


def shape_of(shape, dtype):
    return jax.ShapeDtypeStruct(shape, dtype)


def turn_body(in_ref, out_ref, wide_ref):
    cells, o, _ = out_ref.shape
    wide_ref[...] = in_ref[...].astype(jnp.float32).reshape(wide_ref.shape)
    for k in range(cells):
        out_ref[k] = wide_ref[pl.ds(k, o, stride=cells), :].astype(out_ref.dtype)


def prepare_body(w_ref, bias_ref, flat_ref, back_ref, wide_ref):
    flat = w_ref[...].reshape(flat_ref.shape)
    flat_ref[...] = flat
    back_ref[...] = jnp.transpose(flat)
    o = wide_ref.shape[0]
    row = jnp.broadcast_to(bias_ref[...].astype(jnp.float32), (o, o))
    same = lax.broadcasted_iota(jnp.int32, (o, o), 0) == lax.broadcasted_iota(jnp.int32, (o, o), 1)
    column = jnp.sum(jnp.where(same, row, 0.0), axis=1, keepdims=True)
    wide_ref[...] = jnp.broadcast_to(column, wide_ref.shape)


def owner(me_ref, b):
    return jnp.bitwise_xor(me_ref[0], 2 * (b % 4) + b // 4)


def forward_body(n, rows, o, me_ref, w_ref, *refs):
    blocks = refs[:8]
    own_ref, low_ref, high_ref, x_ref, acc = refs[8:]
    for b in range(8):
        place = pl.ds(pl.multiple_of(owner(me_ref, b) * o, o), o)
        for k in range(n * rows):
            x_ref[place, k * LANES : (k + 1) * LANES] = blocks[b][k]
    w = w_ref[...]
    seen = set()
    for p in range(n):
        for t in range(0, rows, 2):
            at = (p * rows + t) * LANES
            part = jnp.dot(
                w, x_ref[:, at : at + 2 * LANES], preferred_element_type=jnp.float32
            )
            for k, i, j, l in tap_list():
                for h in range(2):
                    slot = (l, p + 2 - i, (t + h + 1 - j) % rows)
                    value = part[k * o : (k + 1) * o, h * LANES : (h + 1) * LANES]
                    if slot in seen:
                        acc[slot] += value
                    else:
                        acc[slot] = value
                        seen.add(slot)
    for q in range(n + 2):
        for y in range(rows):
            total = (
                pltpu.roll(acc[0, q, y], 1, 1)
                + acc[1, q, y]
                + pltpu.roll(acc[2, q, y], LANES - 1, 1)
            )
            if q == 0:
                low_ref[y] = total.astype(low_ref.dtype)
            elif q == n + 1:
                high_ref[y] = total.astype(high_ref.dtype)
            else:
                own_ref[(q - 1) * rows + y] = total
            if q == 1:
                low_ref[rows + y] = total.astype(low_ref.dtype)
            if q == n:
                high_ref[rows + y] = total.astype(high_ref.dtype)


def gradient_body(
    n,
    rows,
    o,
    scale,
    me_ref,
    own_ref,
    low_ref,
    high_ref,
    below_ref,
    above_ref,
    bias_ref,
    go_ref,
    go_below_ref,
    go_above_ref,
    back_ref,
    act_ref,
    total_ref,
    s_ref,
    w_ref,
    other_ref,
    wide_ref,
):
    f32, bf16 = jnp.float32, jnp.bfloat16
    for b in range(8):
        place = pl.ds(pl.multiple_of(owner(me_ref, b) * o, o), o)
        w_ref[b * o : (b + 1) * o] = back_ref[place]
    total = jnp.zeros((o, LANES), f32)
    for q in range(n + 2):
        for y in range(rows):
            if q == 0:
                pre = below_ref[rows + y].astype(f32) + low_ref[y].astype(f32)
                go = go_below_ref[y]
            elif q == n + 1:
                pre = above_ref[rows + y].astype(f32) + high_ref[y].astype(f32)
                go = go_above_ref[y]
            else:
                pre = own_ref[(q - 1) * rows + y]
                go = go_ref[(q - 1) * rows + y]
                if q == 1:
                    pre = pre + below_ref[y].astype(f32)
                if q == n:
                    pre = pre + above_ref[y].astype(f32)
            pre = pre + bias_ref[...]
            s = jax.nn.sigmoid(pre)
            slope = s * (1.0 + pre * (1.0 - s))
            value = (go.astype(f32) * slope).astype(bf16)
            wide = value.astype(f32)
            if 1 <= q <= n:
                wide_ref[pl.ds((q - 1) * rows + y, o, stride=n * rows), :] = pre * s
                total = total + wide
            turned = [
                pltpu.roll(wide, LANES - 1, 1).astype(bf16),
                value,
                pltpu.roll(wide, 1, 1).astype(bf16),
            ]
            for k, i, j, l in tap_list():
                p = q - 2 + i
                if 0 <= p < n:
                    at = (p * rows + (y + j - 1) % rows) * LANES
                    s_ref[k * o : (k + 1) * o, at : at + LANES] = turned[l]
    act_ref[...] = wide_ref[...].reshape(act_ref.shape).astype(bf16)
    total_ref[...] = jnp.broadcast_to(
        jnp.sum(total, axis=1, keepdims=True) * scale, total_ref.shape
    )
    input_grad(n * rows, o, w_ref[4 * o :], s_ref, other_ref)


def input_grad(cells, o, w, s_ref, out_ref):
    for t in range(0, cells, 2):
        part = jnp.dot(
            w, s_ref[:, t * LANES : (t + 2) * LANES], preferred_element_type=jnp.float32
        ).astype(out_ref.dtype)
        for h in range(2):
            for r in range(4):
                cut = part[r * o : (r + 1) * o, h * LANES : (h + 1) * LANES]
                out_ref[r, t + h] = cut


def filter_grad_body(scale, taps, o, s_ref, x_ref, w_ref, total_ref, mine_ref, first_ref, second_ref):
    input_grad(mine_ref.shape[1], o, w_ref[: 4 * o], s_ref, mine_ref)
    full = lax.dot_general(
        s_ref[...], x_ref[...], (((1,), (1,)), ((), ())), preferred_element_type=jnp.float32
    )
    full = (full * scale).astype(first_ref.dtype)
    first_ref[...] = full[: taps * o]
    second_ref[: (27 - taps) * o] = full[taps * o :]
    row = jnp.concatenate([total_ref[...]] * (second_ref.shape[1] // LANES), axis=1)
    second_ref[(27 - taps) * o :] = row.astype(second_ref.dtype)


def pair_body(*refs):
    count = len(refs) // 3
    for p in range(count):
        total = refs[2 * p][...].astype(jnp.float32) + refs[2 * p + 1][...].astype(jnp.float32)
        refs[2 * count + p][...] = total.astype(refs[2 * count + p].dtype)


def split_sum_body(a_ref, b_ref, *outs):
    for r, out in enumerate(outs):
        total = a_ref[r].astype(jnp.float32) + b_ref[r].astype(jnp.float32)
        out[...] = total.astype(out.dtype)


def sum_body(a_ref, b_ref, c_ref, out_ref, token_ref, wide_ref):
    token_ref[...] = jnp.zeros_like(token_ref)
    cells, o, _ = a_ref.shape
    for k in range(cells):
        total = a_ref[k] + b_ref[k].astype(jnp.float32) + c_ref[k].astype(jnp.float32)
        wide_ref[pl.ds(k, o, stride=cells), :] = total
    out_ref[...] = wide_ref[...].reshape(out_ref.shape).astype(out_ref.dtype)


def last_body(taps, a_ref, b_ref, c_ref, d_ref, _, out_ref, bias_ref):
    o = out_ref.shape[1]
    f32 = jnp.float32
    for k in range(27):
        left, right, at = (a_ref, b_ref, k) if k < taps else (c_ref, d_ref, k - taps)
        cut = slice(at * o, (at + 1) * o)
        out_ref[k] = left[cut].astype(f32) + right[cut].astype(f32)
    cut = slice((27 - taps) * o, (28 - taps) * o)
    column = (c_ref[cut].astype(f32) + d_ref[cut].astype(f32))[:, :o]
    same = lax.broadcasted_iota(jnp.int32, (o, o), 0) == lax.broadcasted_iota(jnp.int32, (o, o), 1)
    bias_ref[...] = jnp.sum(jnp.where(same, column, 0.0), axis=0, keepdims=True)


def rotate(value, axis, step):
    count = lax.axis_size(axis)
    return lax.ppermute(value, axis, [(i, (i + step) % count) for i in range(count)])


def swap(value, axis, bit):
    return lax.ppermute(value, axis, [(i, i ^ bit) for i in range(lax.axis_size(axis))])


def on_device(x_in, weight, bias_vec, grad_out):
    o, _, c_all = weight.shape
    _, n, rows, depth = x_in.shape
    f32, bf16 = jnp.float32, jnp.bfloat16
    cells = n * rows
    flops = 2 * 27 * o * c_all * cells * depth
    scale = 1.0 / math.sqrt(lax.axis_size("slab") * cells * depth)
    me = lax.axis_index("chan").astype(jnp.int32).reshape(1)

    def by_row(a, name):
        shapes = [shape_of((cells, o, depth), bf16)]
        scratch = [pltpu.VMEM((o * cells, depth), f32)]
        return call(turn_body, shapes, [a], scratch=scratch, name=name)[0]

    x_own = by_row(x_in, "turn_x")
    x_a = swap(x_own, "chan", 2)
    x_b = swap(x_own, "chan", 4)
    x_side = swap(x_own, "chan", 1)
    w_taps = jnp.transpose(weight, (1, 0, 2))
    w_flat, w_back, bias = call(
        prepare_body,
        [
            shape_of((27 * o, c_all), bf16),
            shape_of((c_all, 27 * o), bf16),
            shape_of((o, LANES), f32),
        ],
        [w_taps, bias_vec[None, :]],
        name="prepare",
    )
    go = by_row(grad_out, "turn_go")
    go_above = rotate(go[:rows], "slab", -1)
    go_below = rotate(go[cells - rows :], "slab", 1)
    x_a_side = swap(x_a, "chan", 1)
    x_b, w_flat, w_back, bias, go, go_above, go_below = lax.optimization_barrier(
        (x_b, w_flat, w_back, bias, go, go_above, go_below)
    )
    x_ab = swap(x_b, "chan", 2)
    x_b_side = swap(x_b, "chan", 1)
    x_ab_side = swap(x_ab, "chan", 1)
    blocks = [x_own, x_a, x_b, x_ab, x_side, x_a_side, x_b_side, x_ab_side]

    own, low, high, x_all = call(
        functools.partial(forward_body, n, rows, o),
        [
            shape_of((cells, o, depth), f32),
            shape_of((2 * rows, o, depth), bf16),
            shape_of((2 * rows, o, depth), bf16),
            shape_of((c_all, cells * depth), bf16),
        ],
        [me, w_flat, *blocks],
        [SMEM] + [VMEM] * 9,
        [pltpu.VMEM((3, n + 2, rows, o, depth), f32)],
        flops=flops,
        name="forward",
    )
    above = rotate(low, "slab", -1)
    below = rotate(high, "slab", 1)
    half = (4, cells, o, depth)
    act, total, stacked, w_turned, other = call(
        functools.partial(gradient_body, n, rows, o, scale),
        [
            shape_of((o, n, rows, depth), bf16),
            shape_of((o, LANES), f32),
            shape_of((27 * o, cells * depth), bf16),
            shape_of((c_all, 27 * o), bf16),
            shape_of(half, bf16),
        ],
        [me, own, low, high, below, above, bias, go, go_below, go_above, w_back],
        [SMEM] + [VMEM] * 10,
        [pltpu.VMEM((o * cells, depth), f32)],
        flops=flops // 2,
        name="gradient",
    )
    other = swap(other, "chan", 1)
    taps = 14
    mine, first, second = call(
        functools.partial(filter_grad_body, scale, taps, o),
        [
            shape_of(half, bf16),
            shape_of((taps * o, c_all), bf16),
            shape_of(((28 - taps) * o, c_all), bf16),
        ],
        [stacked, x_all, w_turned, total],
        flops=flops + flops // 2,
        name="filter_grad",
    )
    g_own, g_a, g_b, g_ab = call(
        split_sum_body,
        [shape_of((cells, o, depth), f32)] + [shape_of((cells, o, depth), bf16)] * 3,
        [mine, other],
        name="pair_sum",
    )
    far = swap(g_ab, "chan", 2)
    near = swap(g_a, "chan", 2)
    first_far = swap(first, "slab", 1)
    second_far = swap(second, "slab", 2)
    (g_b,) = call(pair_body, [shape_of(g_b.shape, bf16)], [g_b, far], name="far_sum")
    across = swap(g_b, "chan", 4)
    first, second = call(
        pair_body,
        [shape_of(a.shape, bf16) for a in (first, second)],
        [first, first_far, second, second_far],
        name="filter_sum",
    )
    first_far = swap(first, "slab", 2)
    second_far = swap(second, "slab", 1)
    grad_in, token = call(
        sum_body,
        [shape_of((o, n, rows, depth), bf16), shape_of((8, LANES), f32)],
        [g_own, near, across],
        scratch=[pltpu.VMEM((o * cells, depth), f32)],
        flops=SUM_FLOPS,
        name="sum",
    )
    weight_grad, bias_grad = call(
        functools.partial(last_body, taps),
        [shape_of((27, o, c_all), f32), shape_of((1, o), f32)],
        [first, first_far, second, second_far, token],
        [VMEM] * 4 + [pl.BlockSpec(memory_space=pl.ANY)],
        name="last",
    )
    return act, grad_in, jnp.transpose(weight_grad, (1, 0, 2)), bias_grad[0]


def solution(mesh):
    placed = (
        P("chan", "slab", None, None),
        P("chan", None, None),
        P("chan"),
        P("chan", "slab", None, None),
    )

    def body(x_in, weight, bias_vec, grad_out):
        tiled = (
            weight.shape[0] % 32 == 0
            and x_in.shape[3] == LANES
            and lax.axis_size("slab") == 4
            and lax.axis_size("chan") == 8
            and x_in.shape[1] >= 2
        )
        return (on_device if tiled else plain)(x_in, weight, bias_vec, grad_out)

    return jax.shard_map(
        body,
        mesh=mesh,
        in_specs=placed,
        out_specs=(
            P("chan", "slab", None, None),
            P("chan", "slab", None, None),
            P("chan", None, None),
            P("chan"),
        ),
        check_vma=False,
    )
```

```python
import functools
import math

import jax
import jax.numpy as jnp
from jax import lax
from jax.experimental import pallas as pl
from jax.experimental.pallas import tpu as pltpu
from jax.sharding import PartitionSpec as P

LANES = 128
SUM_FLOPS = 20 * 10**8
ASSEMBLE_FLOPS = 0
VMEM = pl.BlockSpec(memory_space=pltpu.VMEM)
ANY = pl.BlockSpec(memory_space=pl.ANY)
HBM = pl.BlockSpec(memory_space=pltpu.HBM)
SMEM = pl.BlockSpec(memory_space=pltpu.SMEM)


def with_halo(block, sides, width):
    for axis, dim in sides:
        count = lax.axis_size(axis)
        forward = [(i, i + 1) for i in range(count - 1)]
        forward.append((count - 1, 0))
        backward = [(target, source) for source, target in forward]
        low = lax.ppermute(
            lax.slice_in_dim(block, block.shape[dim] - width, None, axis=dim), axis, forward
        )
        high = lax.ppermute(lax.slice_in_dim(block, 0, width, axis=dim), axis, backward)
        block = jnp.concatenate([low, block, high], axis=dim)
    return block


def tap_list():
    return [(9 * i + 3 * j + l, i, j, l) for i in range(3) for j in range(3) for l in range(3)]


def plain(x_in, weight, bias_vec, grad_out):
    out_local, n_taps, in_total = weight.shape
    n_planes, n_rows, n_depth = (x_in.shape[1], x_in.shape[2], x_in.shape[3])
    rimmed = with_halo(x_in, (("slab", 1),), 1)
    padded = lax.all_gather(rimmed, "chan", axis=0, tiled=True)
    own_planes = padded[:, 1 : n_planes + 1]
    pre_act = (
        jnp.zeros((out_local, n_planes, n_rows, n_depth), jnp.float32)
        + bias_vec.astype(jnp.float32)[:, None, None, None]
    )
    for i in range(3):
        w_plane = jnp.transpose(weight[:, 9 * i : 9 * i + 9], (1, 0, 2)).reshape(
            9 * out_local, in_total
        )
        plane_part = jnp.dot(
            w_plane,
            padded[:, i : i + n_planes].reshape(in_total, -1),
            preferred_element_type=jnp.float32,
        )
        plane_part = plane_part.reshape(9, out_local, n_planes, n_rows, n_depth)
        for j in range(3):
            for l in range(3):
                pre_act = pre_act + jnp.roll(plane_part[3 * j + l], (1 - j, 1 - l), axis=(2, 3))
    sigmoid_v = jax.nn.sigmoid(pre_act)
    activation = (pre_act * sigmoid_v).astype(jnp.bfloat16)
    slope = sigmoid_v * (1.0 + pre_act * (1.0 - sigmoid_v))
    grad_pre = (grad_out.astype(jnp.float32) * slope).astype(jnp.bfloat16)
    padded_grad = with_halo(grad_pre, (("slab", 1),), 1)
    shifted = jnp.stack(
        [
            jnp.roll(padded_grad[:, 2 - i : 2 - i + n_planes], (j - 1, l - 1), axis=(2, 3))
            for k, i, j, l in tap_list()
        ],
        0,
    )
    shifted = shifted.reshape(n_taps * out_local, -1)
    grad_scale = 1.0 / math.sqrt(lax.axis_size("slab") * n_planes * n_rows * n_depth)
    filter_local = lax.dot_general(
        shifted,
        own_planes.reshape(in_total, -1),
        (((1,), (1,)), ((), ())),
        preferred_element_type=jnp.float32,
    )
    filter_part = (
        jnp.transpose(filter_local.reshape(n_taps, out_local, in_total), (1, 0, 2)) * grad_scale
    )
    bias_part = grad_scale * jnp.sum(grad_pre.astype(jnp.float32), axis=(1, 2, 3))
    bias_row = jnp.concatenate(
        [bias_part[:, None, None], jnp.zeros((out_local, 1, in_total - 1), jnp.float32)], 2
    )
    summed_filters = lax.psum(jnp.concatenate([filter_part, bias_row], 1), "slab")
    weight_grad = summed_filters[:, :n_taps]
    bias_grad = summed_filters[:, n_taps, 0]
    flat_w = jnp.transpose(weight, (1, 0, 2)).reshape(n_taps * out_local, in_total)
    product = lax.dot_general(
        flat_w, shifted, (((0,), (0,)), ((), ())), preferred_element_type=jnp.float32
    )
    grad_in = lax.psum_scatter(
        product.reshape(
            in_total // lax.axis_size("chan") * lax.axis_size("chan"), n_planes, n_rows, n_depth
        ),
        "chan",
        scatter_dimension=0,
        tiled=True,
    )
    return (activation, grad_in.astype(jnp.bfloat16), weight_grad, bias_grad)


def call(body, out_shape, operands, specs=None, scratch=(), flops=0, name=None, aliases=None):
    read = sum(math.prod(a.shape) * a.dtype.itemsize for a in operands)
    written = sum(math.prod(a.shape) * a.dtype.itemsize for a in out_shape)
    return pl.pallas_call(
        body,
        out_shape=out_shape,
        in_specs=specs or [VMEM] * len(operands),
        out_specs=[VMEM] * len(out_shape),
        scratch_shapes=list(scratch),
        input_output_aliases=aliases or {},
        compiler_params=pltpu.CompilerParams(vmem_limit_bytes=24 * 2**20),
        cost_estimate=pl.CostEstimate(
            flops=flops, bytes_accessed=read + written, transcendentals=0
        ),
        name=name,
    )(*operands)


def shape_of(shape, dtype):
    return jax.ShapeDtypeStruct(shape, dtype)


def turned(value, wide_ref):
    o = value.shape[0]
    cells = wide_ref.shape[0] // o
    wide_ref[...] = value.astype(jnp.float32).reshape(wide_ref.shape)
    return [
        wide_ref[pl.ds(k, o, stride=cells), :].astype(value.dtype) for k in range(cells)
    ]


def prepare_body(
    x_hbm,
    go_hbm,
    w_hbm,
    bias_hbm,
    x_ref,
    go_ref,
    flat_ref,
    back_ref,
    bias_ref,
    go_in,
    w_in,
    bias_in,
    wide_ref,
    sems,
):
    copies = [
        pltpu.make_async_copy(source, target, sems.at[at])
        for at, (source, target) in enumerate(
            [(go_hbm, go_in), (w_hbm, w_in), (bias_hbm, bias_in), (x_hbm, x_ref)]
        )
    ]
    for copy in copies:
        copy.start()
    copies[0].wait()
    for k, value in enumerate(turned(go_in[...], wide_ref)):
        go_ref[k] = value
    copies[1].wait()
    copies[2].wait()
    copies[3].wait()
    flat = w_in[...].reshape(flat_ref.shape)
    flat_ref[...] = flat
    back_ref[...] = jnp.transpose(flat)
    o = bias_ref.shape[0]
    row = jnp.broadcast_to(bias_in[...].astype(jnp.float32), (o, o))
    same = lax.broadcasted_iota(jnp.int32, (o, o), 0) == lax.broadcasted_iota(jnp.int32, (o, o), 1)
    column = jnp.sum(jnp.where(same, row, 0.0), axis=1, keepdims=True)
    bias_ref[...] = jnp.broadcast_to(column, bias_ref.shape)


def place_block(me_ref, b, block_ref, x_ref, wide_ref):
    o = block_ref.shape[0]
    place = pl.ds(pl.multiple_of(owner(me_ref, b) * o, o), o)
    for k, value in enumerate(turned(block_ref[...], wide_ref)):
        x_ref[place, k * LANES : (k + 1) * LANES] = value


def assemble_body(places, me_ref, *refs):
    blocks, (x_ref, wide_ref) = refs[: len(places)], refs[-2:]
    for b, block in zip(places, blocks):
        place_block(me_ref, b, block, x_ref, wide_ref)


def owner(me_ref, b):
    return jnp.bitwise_xor(me_ref[0], 2 * (b % 4) + b // 4)


def forward_body(n, rows, o, places, me_ref, w_ref, *refs):
    blocks = refs[: len(places)]
    own_ref, low_ref, high_ref, x_ref, acc, wide_ref = refs[len(places) + 1 :]
    for b, block in zip(places, blocks):
        place_block(me_ref, b, block, x_ref, wide_ref)
    w = w_ref[...]
    seen = set()
    for p in range(n):
        for t in range(0, rows, 2):
            at = (p * rows + t) * LANES
            part = jnp.dot(
                w, x_ref[:, at : at + 2 * LANES], preferred_element_type=jnp.float32
            )
            for k, i, j, l in tap_list():
                for h in range(2):
                    slot = (l, p + 2 - i, (t + h + 1 - j) % rows)
                    value = part[k * o : (k + 1) * o, h * LANES : (h + 1) * LANES]
                    if slot in seen:
                        acc[slot] += value
                    else:
                        acc[slot] = value
                        seen.add(slot)
    for q in range(n + 2):
        for y in range(rows):
            total = (
                pltpu.roll(acc[0, q, y], 1, 1)
                + acc[1, q, y]
                + pltpu.roll(acc[2, q, y], LANES - 1, 1)
            )
            if q == 0:
                low_ref[y] = total.astype(low_ref.dtype)
            elif q == n + 1:
                high_ref[y] = total.astype(high_ref.dtype)
            else:
                own_ref[(q - 1) * rows + y] = total
            if q == 1:
                low_ref[rows + y] = total.astype(low_ref.dtype)
            if q == n:
                high_ref[rows + y] = total.astype(high_ref.dtype)


def gradient_body(
    n,
    rows,
    o,
    scale,
    me_ref,
    own_ref,
    low_ref,
    high_ref,
    below_ref,
    above_ref,
    bias_ref,
    go_ref,
    go_below_ref,
    go_above_ref,
    back_ref,
    act_ref,
    total_ref,
    s_ref,
    w_ref,
    other_ref,
    far_ref,
    wide_ref,
    rim_ref,
):
    f32, bf16 = jnp.float32, jnp.bfloat16
    for b in range(8):
        place = pl.ds(pl.multiple_of(owner(me_ref, b) * o, o), o)
        w_ref[b * o : (b + 1) * o] = back_ref[place]
    total = jnp.zeros((o, LANES), f32)
    go_below = turned(go_below_ref[:, n - 1 :], rim_ref)
    go_above = turned(go_above_ref[:, :1], rim_ref)
    for q in range(n + 2):
        for y in range(rows):
            if q == 0:
                pre = below_ref[rows + y].astype(f32) + low_ref[y].astype(f32)
                go = go_below[y]
            elif q == n + 1:
                pre = above_ref[rows + y].astype(f32) + high_ref[y].astype(f32)
                go = go_above[y]
            else:
                pre = own_ref[(q - 1) * rows + y]
                go = go_ref[(q - 1) * rows + y]
                if q == 1:
                    pre = pre + below_ref[y].astype(f32)
                if q == n:
                    pre = pre + above_ref[y].astype(f32)
            pre = pre + bias_ref[...]
            s = jax.nn.sigmoid(pre)
            slope = s * (1.0 + pre * (1.0 - s))
            value = (go.astype(f32) * slope).astype(bf16)
            wide = value.astype(f32)
            if 1 <= q <= n:
                wide_ref[pl.ds((q - 1) * rows + y, o, stride=n * rows), :] = pre * s
                total = total + wide
            shifts = [
                pltpu.roll(wide, LANES - 1, 1).astype(bf16),
                value,
                pltpu.roll(wide, 1, 1).astype(bf16),
            ]
            for k, i, j, l in tap_list():
                p = q - 2 + i
                if 0 <= p < n:
                    at = (p * rows + (y + j - 1) % rows) * LANES
                    s_ref[k * o : (k + 1) * o, at : at + LANES] = shifts[l]
    act_ref[...] = wide_ref[...].reshape(act_ref.shape).astype(bf16)
    total_ref[...] = jnp.broadcast_to(
        jnp.sum(total, axis=1, keepdims=True) * scale, total_ref.shape
    )
    input_grad(n * rows, o, w_ref[3 * o :], s_ref, [(far_ref, None)] + [(other_ref, r) for r in range(4)])


def input_grad(cells, o, w, s_ref, outs):
    for t in range(0, cells, 2):
        part = jnp.dot(
            w, s_ref[:, t * LANES : (t + 2) * LANES], preferred_element_type=jnp.float32
        ).astype(outs[0][0].dtype)
        for h in range(2):
            for r, (out_ref, at) in enumerate(outs):
                cut = part[r * o : (r + 1) * o, h * LANES : (h + 1) * LANES]
                if at is None:
                    out_ref[t + h] = cut
                else:
                    out_ref[at, t + h] = cut


def rest_body(o, s_ref, w_ref, out_ref):
    cells = out_ref.shape[1]
    input_grad(cells, o, w_ref[: 3 * o], s_ref, [(out_ref, r) for r in range(3)])


def filter_grad_body(scale, taps, o, s_ref, x_ref, total_ref, first_ref, second_ref):
    full = lax.dot_general(
        s_ref[...], x_ref[...], (((1,), (1,)), ((), ())), preferred_element_type=jnp.float32
    )
    full = (full * scale).astype(first_ref.dtype)
    first_ref[...] = full[: taps * o]
    second_ref[: (27 - taps) * o] = full[taps * o :]
    row = jnp.concatenate([total_ref[...]] * (second_ref.shape[1] // LANES), axis=1)
    second_ref[(27 - taps) * o :] = row.astype(second_ref.dtype)


def pair_body(*refs):
    count = len(refs) // 3
    for p in range(count):
        total = refs[2 * p][...].astype(jnp.float32) + refs[2 * p + 1][...].astype(jnp.float32)
        refs[2 * count + p][...] = total.astype(refs[2 * count + p].dtype)


def core_sum_body(mine_ref, other_ref, out_ref):
    total = mine_ref[...].astype(jnp.float32) + other_ref[3].astype(jnp.float32)
    out_ref[...] = total.astype(out_ref.dtype)


def chip_sum_body(rest_ref, other_ref, far_ref, own_ref, a_ref, b_ref):
    f32 = jnp.float32
    own_ref[...] = rest_ref[0].astype(f32) + other_ref[0].astype(f32)
    a_ref[...] = (rest_ref[1].astype(f32) + other_ref[1].astype(f32)).astype(a_ref.dtype)
    total = rest_ref[2].astype(f32) + other_ref[2].astype(f32) + far_ref[...].astype(f32)
    b_ref[...] = total.astype(b_ref.dtype)


def sum_body(a_ref, b_ref, c_ref, out_ref, token_ref, wide_ref):
    token_ref[...] = jnp.zeros_like(token_ref)
    cells, o, _ = a_ref.shape
    for k in range(cells):
        total = a_ref[k] + b_ref[k].astype(jnp.float32) + c_ref[k].astype(jnp.float32)
        wide_ref[pl.ds(k, o, stride=cells), :] = total
    out_ref[...] = wide_ref[...].reshape(out_ref.shape).astype(out_ref.dtype)


def last_body(taps, a_ref, b_ref, c_ref, d_ref, _, out_ref, bias_ref):
    o = out_ref.shape[1]
    f32 = jnp.float32
    for k in range(27):
        left, right, at = (a_ref, b_ref, k) if k < taps else (c_ref, d_ref, k - taps)
        cut = slice(at * o, (at + 1) * o)
        out_ref[k] = left[cut].astype(f32) + right[cut].astype(f32)
    cut = slice((27 - taps) * o, (28 - taps) * o)
    column = (c_ref[cut].astype(f32) + d_ref[cut].astype(f32))[:, :o]
    same = lax.broadcasted_iota(jnp.int32, (o, o), 0) == lax.broadcasted_iota(jnp.int32, (o, o), 1)
    bias_ref[...] = jnp.sum(jnp.where(same, column, 0.0), axis=0, keepdims=True)


def in_hbm(value):
    return pltpu.with_memory_space_constraint(value, pltpu.HBM)


def rotate(value, axis, step):
    count = lax.axis_size(axis)
    return lax.ppermute(value, axis, [(i, (i + step) % count) for i in range(count)])


def swap(value, axis, bit):
    return lax.ppermute(value, axis, [(i, i ^ bit) for i in range(lax.axis_size(axis))])


def on_device(x_in, weight, bias_vec, grad_out):
    o, _, c_all = weight.shape
    _, n, rows, depth = x_in.shape
    f32, bf16 = jnp.float32, jnp.bfloat16
    cells = n * rows
    flops = 2 * 27 * o * c_all * cells * depth
    scale = 1.0 / math.sqrt(lax.axis_size("slab") * cells * depth)
    me = lax.axis_index("chan").astype(jnp.int32).reshape(1)

    block_wide = [pltpu.VMEM((o * cells, depth), f32)]

    x_b = swap(x_in, "chan", 4)
    x_a = swap(x_in, "chan", 2)
    x_side = swap(x_in, "chan", 1)
    go_above = rotate(grad_out, "slab", -1)
    go_below = rotate(grad_out, "slab", 1)
    x_own, go, w_flat, w_back, bias = call(
        prepare_body,
        [
            shape_of((o, n, rows, depth), bf16),
            shape_of((cells, o, depth), bf16),
            shape_of((27 * o, c_all), bf16),
            shape_of((c_all, 27 * o), bf16),
            shape_of((o, LANES), f32),
        ],
        [in_hbm(a) for a in (x_in, grad_out, jnp.transpose(weight, (1, 0, 2)), bias_vec[None, :])],
        [HBM] * 4,
        [
            pltpu.VMEM((o, n, rows, depth), bf16),
            pltpu.VMEM((27, o, c_all), bf16),
            pltpu.VMEM((1, o), bf16),
            *block_wide,
            pltpu.SemaphoreType.DMA((4,)),
        ],
        name="prepare",
    )
    x_b, w_flat = lax.optimization_barrier((x_b, w_flat))
    x_ab = swap(x_b, "chan", 2)
    x_a_side = swap(x_a, "chan", 1)
    x_b_side = swap(x_b, "chan", 1)
    early, late = (0, 1, 2, 4, 5, 6), (3, 7)
    (x_all,) = call(
        functools.partial(assemble_body, early),
        [shape_of((c_all, cells * depth), bf16)],
        [me, x_own, x_a, x_b, x_side, x_a_side, x_b_side, go_above, go_below],
        [SMEM] + [VMEM] * 6 + [ANY] * 2,
        block_wide,
        flops=ASSEMBLE_FLOPS,
        name="assemble",
    )
    x_ab, x_all = lax.optimization_barrier((x_ab, x_all))
    x_ab_side = swap(x_ab, "chan", 1)
    own, low, high, x_all = call(
        functools.partial(forward_body, n, rows, o, late),
        [
            shape_of((cells, o, depth), f32),
            shape_of((2 * rows, o, depth), bf16),
            shape_of((2 * rows, o, depth), bf16),
            shape_of((c_all, cells * depth), bf16),
        ],
        [me, w_flat, x_ab, x_ab_side, x_all],
        [SMEM] + [VMEM] * 4,
        [pltpu.VMEM((3, n + 2, rows, o, depth), f32), *block_wide],
        flops=flops,
        name="forward",
        aliases={4: 3},
    )
    above = rotate(low, "slab", -1)
    below = rotate(high, "slab", 1)
    act, total, stacked, w_turned, other, far = call(
        functools.partial(gradient_body, n, rows, o, scale),
        [
            shape_of((o, n, rows, depth), bf16),
            shape_of((o, LANES), f32),
            shape_of((27 * o, cells * depth), bf16),
            shape_of((c_all, 27 * o), bf16),
            shape_of((4, cells, o, depth), bf16),
            shape_of((cells, o, depth), bf16),
        ],
        [me, own, low, high, below, above, bias, go, go_below, go_above, w_back],
        [SMEM] + [VMEM] * 10,
        [*block_wide, pltpu.VMEM((o * rows, depth), f32)],
        flops=flops // 2,
        name="gradient",
    )
    other = swap(other, "chan", 1)
    taps = 14
    first, second = call(
        functools.partial(filter_grad_body, scale, taps, o),
        [shape_of((taps * o, c_all), bf16), shape_of(((28 - taps) * o, c_all), bf16)],
        [stacked, x_all, total],
        flops=flops,
        name="filter_grad",
    )
    first_far = swap(first, "slab", 1)
    second_far = swap(second, "slab", 2)
    (far,) = call(core_sum_body, [shape_of(far.shape, bf16)], [far, other], name="core_sum")
    far = swap(far, "chan", 2)
    (rest,) = call(
        functools.partial(rest_body, o),
        [shape_of((3, cells, o, depth), bf16)],
        [stacked, w_turned],
        flops=flops // 2,
        name="rest",
    )
    g_own, g_a, g_b = call(
        chip_sum_body,
        [
            shape_of((cells, o, depth), f32),
            shape_of((cells, o, depth), bf16),
            shape_of((cells, o, depth), bf16),
        ],
        [rest, other, far],
        name="chip_sum",
    )
    near = swap(g_a, "chan", 2)
    across = swap(g_b, "chan", 4)
    first, second = call(
        pair_body,
        [shape_of(a.shape, bf16) for a in (first, second)],
        [first, first_far, second, second_far],
        name="filter_sum",
    )
    first_far = swap(first, "slab", 2)
    second_far = swap(second, "slab", 1)
    grad_in, token = call(
        sum_body,
        [shape_of((o, n, rows, depth), bf16), shape_of((8, LANES), f32)],
        [g_own, near, across],
        scratch=[pltpu.VMEM((o * cells, depth), f32)],
        flops=SUM_FLOPS,
        name="sum",
    )
    weight_grad, bias_grad = call(
        functools.partial(last_body, taps),
        [shape_of((27, o, c_all), f32), shape_of((1, o), f32)],
        [first, first_far, second, second_far, token],
        [VMEM] * 4 + [ANY],
        name="last",
    )
    return act, grad_in, jnp.transpose(weight_grad, (1, 0, 2)), bias_grad[0]


def solution(mesh):
    placed = (
        P("chan", "slab", None, None),
        P("chan", None, None),
        P("chan"),
        P("chan", "slab", None, None),
    )

    def body(x_in, weight, bias_vec, grad_out):
        tiled = (
            weight.shape[0] % 32 == 0
            and x_in.shape[3] == LANES
            and lax.axis_size("slab") == 4
            and lax.axis_size("chan") == 8
            and x_in.shape[1] >= 2
        )
        return (on_device if tiled else plain)(x_in, weight, bias_vec, grad_out)

    return jax.shard_map(
        body,
        mesh=mesh,
        in_specs=placed,
        out_specs=(
            P("chan", "slab", None, None),
            P("chan", "slab", None, None),
            P("chan", None, None),
            P("chan"),
        ),
        check_vma=False,
    )
```

```python
import functools
import math

import jax
import jax.numpy as jnp
from jax import lax
from jax.experimental import pallas as pl
from jax.experimental.pallas import tpu as pltpu
from jax.sharding import PartitionSpec as P

LANES = 128
SUM_FLOPS = 20 * 10**8
FORWARD_FLOPS = 0
VMEM = pl.BlockSpec(memory_space=pltpu.VMEM)
ANY = pl.BlockSpec(memory_space=pl.ANY)
HBM = pl.BlockSpec(memory_space=pltpu.HBM)
SMEM = pl.BlockSpec(memory_space=pltpu.SMEM)


def with_halo(block, sides, width):
    for axis, dim in sides:
        count = lax.axis_size(axis)
        forward = [(i, i + 1) for i in range(count - 1)]
        forward.append((count - 1, 0))
        backward = [(target, source) for source, target in forward]
        low = lax.ppermute(
            lax.slice_in_dim(block, block.shape[dim] - width, None, axis=dim), axis, forward
        )
        high = lax.ppermute(lax.slice_in_dim(block, 0, width, axis=dim), axis, backward)
        block = jnp.concatenate([low, block, high], axis=dim)
    return block


def tap_list():
    return [(9 * i + 3 * j + l, i, j, l) for i in range(3) for j in range(3) for l in range(3)]


def plain(x_in, weight, bias_vec, grad_out):
    out_local, n_taps, in_total = weight.shape
    n_planes, n_rows, n_depth = (x_in.shape[1], x_in.shape[2], x_in.shape[3])
    rimmed = with_halo(x_in, (("slab", 1),), 1)
    padded = lax.all_gather(rimmed, "chan", axis=0, tiled=True)
    own_planes = padded[:, 1 : n_planes + 1]
    pre_act = (
        jnp.zeros((out_local, n_planes, n_rows, n_depth), jnp.float32)
        + bias_vec.astype(jnp.float32)[:, None, None, None]
    )
    for i in range(3):
        w_plane = jnp.transpose(weight[:, 9 * i : 9 * i + 9], (1, 0, 2)).reshape(
            9 * out_local, in_total
        )
        plane_part = jnp.dot(
            w_plane,
            padded[:, i : i + n_planes].reshape(in_total, -1),
            preferred_element_type=jnp.float32,
        )
        plane_part = plane_part.reshape(9, out_local, n_planes, n_rows, n_depth)
        for j in range(3):
            for l in range(3):
                pre_act = pre_act + jnp.roll(plane_part[3 * j + l], (1 - j, 1 - l), axis=(2, 3))
    sigmoid_v = jax.nn.sigmoid(pre_act)
    activation = (pre_act * sigmoid_v).astype(jnp.bfloat16)
    slope = sigmoid_v * (1.0 + pre_act * (1.0 - sigmoid_v))
    grad_pre = (grad_out.astype(jnp.float32) * slope).astype(jnp.bfloat16)
    padded_grad = with_halo(grad_pre, (("slab", 1),), 1)
    shifted = jnp.stack(
        [
            jnp.roll(padded_grad[:, 2 - i : 2 - i + n_planes], (j - 1, l - 1), axis=(2, 3))
            for k, i, j, l in tap_list()
        ],
        0,
    )
    shifted = shifted.reshape(n_taps * out_local, -1)
    grad_scale = 1.0 / math.sqrt(lax.axis_size("slab") * n_planes * n_rows * n_depth)
    filter_local = lax.dot_general(
        shifted,
        own_planes.reshape(in_total, -1),
        (((1,), (1,)), ((), ())),
        preferred_element_type=jnp.float32,
    )
    filter_part = (
        jnp.transpose(filter_local.reshape(n_taps, out_local, in_total), (1, 0, 2)) * grad_scale
    )
    bias_part = grad_scale * jnp.sum(grad_pre.astype(jnp.float32), axis=(1, 2, 3))
    bias_row = jnp.concatenate(
        [bias_part[:, None, None], jnp.zeros((out_local, 1, in_total - 1), jnp.float32)], 2
    )
    summed_filters = lax.psum(jnp.concatenate([filter_part, bias_row], 1), "slab")
    weight_grad = summed_filters[:, :n_taps]
    bias_grad = summed_filters[:, n_taps, 0]
    flat_w = jnp.transpose(weight, (1, 0, 2)).reshape(n_taps * out_local, in_total)
    product = lax.dot_general(
        flat_w, shifted, (((0,), (0,)), ((), ())), preferred_element_type=jnp.float32
    )
    grad_in = lax.psum_scatter(
        product.reshape(
            in_total // lax.axis_size("chan") * lax.axis_size("chan"), n_planes, n_rows, n_depth
        ),
        "chan",
        scatter_dimension=0,
        tiled=True,
    )
    return (activation, grad_in.astype(jnp.bfloat16), weight_grad, bias_grad)


def call(body, out_shape, operands, specs=None, scratch=(), flops=0, name=None, aliases=None):
    read = sum(math.prod(a.shape) * a.dtype.itemsize for a in operands)
    written = sum(math.prod(a.shape) * a.dtype.itemsize for a in out_shape)
    return pl.pallas_call(
        body,
        out_shape=out_shape,
        in_specs=specs or [VMEM] * len(operands),
        out_specs=[VMEM] * len(out_shape),
        scratch_shapes=list(scratch),
        input_output_aliases=aliases or {},
        compiler_params=pltpu.CompilerParams(vmem_limit_bytes=24 * 2**20),
        cost_estimate=pl.CostEstimate(
            flops=flops, bytes_accessed=read + written, transcendentals=0
        ),
        name=name,
    )(*operands)


def shape_of(shape, dtype):
    return jax.ShapeDtypeStruct(shape, dtype)


def turned(value, wide_ref):
    o = value.shape[0]
    cells = wide_ref.shape[0] // o
    wide_ref[...] = value.astype(jnp.float32).reshape(wide_ref.shape)
    return [
        wide_ref[pl.ds(k, o, stride=cells), :].astype(value.dtype) for k in range(cells)
    ]


def prepare_body(
    n,
    rows,
    x_hbm,
    go_hbm,
    w_hbm,
    bias_hbm,
    x_ref,
    go_ref,
    go_low_ref,
    go_high_ref,
    flat_ref,
    back_ref,
    bias_ref,
    go_in,
    w_in,
    bias_in,
    wide_ref,
    sems,
):
    copies = [
        pltpu.make_async_copy(source, target, sems.at[at])
        for at, (source, target) in enumerate(
            [(go_hbm, go_in), (w_hbm, w_in), (bias_hbm, bias_in), (x_hbm, x_ref)]
        )
    ]
    for copy in copies:
        copy.start()
    copies[0].wait()
    for k, value in enumerate(turned(go_in[...], wide_ref)):
        go_ref[k] = value
        if k < rows:
            go_low_ref[k] = value
        if k >= (n - 1) * rows:
            go_high_ref[k - (n - 1) * rows] = value
    copies[1].wait()
    copies[2].wait()
    copies[3].wait()
    flat = w_in[...].reshape(flat_ref.shape)
    flat_ref[...] = flat
    back_ref[...] = jnp.transpose(flat)
    o = bias_ref.shape[0]
    row = jnp.broadcast_to(bias_in[...].astype(jnp.float32), (o, o))
    same = lax.broadcasted_iota(jnp.int32, (o, o), 0) == lax.broadcasted_iota(jnp.int32, (o, o), 1)
    column = jnp.sum(jnp.where(same, row, 0.0), axis=1, keepdims=True)
    bias_ref[...] = jnp.broadcast_to(column, bias_ref.shape)


def place_block(me_ref, b, block_ref, x_ref, wide_ref):
    o = block_ref.shape[0]
    place = pl.ds(pl.multiple_of(owner(me_ref, b) * o, o), o)
    for k, value in enumerate(turned(block_ref[...], wide_ref)):
        x_ref[place, k * LANES : (k + 1) * LANES] = value


def assemble_body(places, me_ref, *refs):
    blocks, (x_ref, wide_ref) = refs[: len(places)], refs[-2:]
    for b, block in zip(places, blocks):
        place_block(me_ref, b, block, x_ref, wide_ref)


def owner(me_ref, b):
    return jnp.bitwise_xor(me_ref[0], 2 * (b % 4) + b // 4)


def forward_body(n, rows, o, places, me_ref, w_ref, *refs):
    blocks = refs[: len(places)]
    own_ref, low_ref, high_ref, x_ref, acc, wide_ref = refs[len(places) + 1 :]
    for b, block in zip(places, blocks):
        place_block(me_ref, b, block, x_ref, wide_ref)
    w = w_ref[...]
    seen = set()
    for p in range(n):
        for t in range(0, rows, 2):
            at = (p * rows + t) * LANES
            part = jnp.dot(
                w, x_ref[:, at : at + 2 * LANES], preferred_element_type=jnp.float32
            )
            for k, i, j, l in tap_list():
                for h in range(2):
                    slot = (l, p + 2 - i, (t + h + 1 - j) % rows)
                    value = part[k * o : (k + 1) * o, h * LANES : (h + 1) * LANES]
                    if slot in seen:
                        acc[slot] += value
                    else:
                        acc[slot] = value
                        seen.add(slot)
    for q in range(n + 2):
        for y in range(rows):
            total = (
                pltpu.roll(acc[0, q, y], 1, 1)
                + acc[1, q, y]
                + pltpu.roll(acc[2, q, y], LANES - 1, 1)
            )
            if q == 0:
                low_ref[y] = total.astype(low_ref.dtype)
            elif q == n + 1:
                high_ref[y] = total.astype(high_ref.dtype)
            else:
                own_ref[(q - 1) * rows + y] = total
            if q == 1:
                low_ref[rows + y] = total.astype(low_ref.dtype)
            if q == n:
                high_ref[rows + y] = total.astype(high_ref.dtype)


def gradient_body(
    n,
    rows,
    o,
    scale,
    me_ref,
    own_ref,
    low_ref,
    high_ref,
    below_ref,
    above_ref,
    bias_ref,
    go_ref,
    go_below_ref,
    go_above_ref,
    back_ref,
    act_ref,
    total_ref,
    s_ref,
    w_ref,
    other_ref,
    far_ref,
    wide_ref,
):
    f32, bf16 = jnp.float32, jnp.bfloat16
    for b in range(8):
        place = pl.ds(pl.multiple_of(owner(me_ref, b) * o, o), o)
        w_ref[b * o : (b + 1) * o] = back_ref[place]
    total = jnp.zeros((o, LANES), f32)
    for q in range(n + 2):
        for y in range(rows):
            if q == 0:
                pre = below_ref[rows + y].astype(f32) + low_ref[y].astype(f32)
                go = go_below_ref[y]
            elif q == n + 1:
                pre = above_ref[rows + y].astype(f32) + high_ref[y].astype(f32)
                go = go_above_ref[y]
            else:
                pre = own_ref[(q - 1) * rows + y]
                go = go_ref[(q - 1) * rows + y]
                if q == 1:
                    pre = pre + below_ref[y].astype(f32)
                if q == n:
                    pre = pre + above_ref[y].astype(f32)
            pre = pre + bias_ref[...]
            s = jax.nn.sigmoid(pre)
            slope = s * (1.0 + pre * (1.0 - s))
            value = (go.astype(f32) * slope).astype(bf16)
            wide = value.astype(f32)
            if 1 <= q <= n:
                wide_ref[pl.ds((q - 1) * rows + y, o, stride=n * rows), :] = pre * s
                total = total + wide
            shifts = [
                pltpu.roll(wide, LANES - 1, 1).astype(bf16),
                value,
                pltpu.roll(wide, 1, 1).astype(bf16),
            ]
            for k, i, j, l in tap_list():
                p = q - 2 + i
                if 0 <= p < n:
                    at = (p * rows + (y + j - 1) % rows) * LANES
                    s_ref[k * o : (k + 1) * o, at : at + LANES] = shifts[l]
    act_ref[...] = wide_ref[...].reshape(act_ref.shape).astype(bf16)
    total_ref[...] = jnp.broadcast_to(
        jnp.sum(total, axis=1, keepdims=True) * scale, total_ref.shape
    )
    input_grad(n * rows, o, w_ref[3 * o :], s_ref, [(far_ref, None)] + [(other_ref, r) for r in range(4)])


def input_grad(cells, o, w, s_ref, outs):
    for t in range(0, cells, 2):
        part = jnp.dot(
            w, s_ref[:, t * LANES : (t + 2) * LANES], preferred_element_type=jnp.float32
        ).astype(outs[0][0].dtype)
        for h in range(2):
            for r, (out_ref, at) in enumerate(outs):
                cut = part[r * o : (r + 1) * o, h * LANES : (h + 1) * LANES]
                if at is None:
                    out_ref[t + h] = cut
                else:
                    out_ref[at, t + h] = cut


def rest_body(o, s_ref, w_ref, out_ref):
    cells = out_ref.shape[1]
    input_grad(cells, o, w_ref[: 3 * o], s_ref, [(out_ref, r) for r in range(3)])


def filter_grad_body(scale, taps, o, s_ref, x_ref, total_ref, first_ref, second_ref):
    full = lax.dot_general(
        s_ref[...], x_ref[...], (((1,), (1,)), ((), ())), preferred_element_type=jnp.float32
    )
    full = (full * scale).astype(first_ref.dtype)
    first_ref[...] = full[: taps * o]
    second_ref[: (27 - taps) * o] = full[taps * o :]
    row = jnp.concatenate([total_ref[...]] * (second_ref.shape[1] // LANES), axis=1)
    second_ref[(27 - taps) * o :] = row.astype(second_ref.dtype)


def second_body(rest_ref, other_ref, a_ref, b_ref, c_ref, d_ref, _, own_ref, near_ref, ab_ref, cd_ref):
    f32 = jnp.float32
    ab_ref[...] = (a_ref[...].astype(f32) + b_ref[...].astype(f32)).astype(ab_ref.dtype)
    cd_ref[...] = (c_ref[...].astype(f32) + d_ref[...].astype(f32)).astype(cd_ref.dtype)
    own_ref[...] = rest_ref[0].astype(f32) + other_ref[0].astype(f32)
    near_ref[...] = (rest_ref[1].astype(f32) + other_ref[1].astype(f32)).astype(near_ref.dtype)


def core_sum_body(mine_ref, other_ref, out_ref):
    total = mine_ref[...].astype(jnp.float32) + other_ref[3].astype(jnp.float32)
    out_ref[...] = total.astype(out_ref.dtype)


def chip_sum_body(rest_ref, other_ref, far_ref, b_ref):
    f32 = jnp.float32
    total = rest_ref[2].astype(f32) + other_ref[2].astype(f32) + far_ref[...].astype(f32)
    b_ref[...] = total.astype(b_ref.dtype)


def sum_body(a_ref, b_ref, out_ref):
    out_ref[...] = a_ref[...] + b_ref[...].astype(jnp.float32)


def last_body(taps, a_ref, b_ref, c_ref, d_ref, g_ref, h_ref, out_ref, bias_ref, grad_ref, wide_ref):
    o = out_ref.shape[1]
    f32 = jnp.float32
    cells = g_ref.shape[0]
    for k in range(cells):
        wide_ref[pl.ds(k, o, stride=cells), :] = g_ref[k] + h_ref[k].astype(f32)
    grad_ref[...] = wide_ref[...].reshape(grad_ref.shape).astype(grad_ref.dtype)
    for k in range(27):
        left, right, at = (a_ref, b_ref, k) if k < taps else (c_ref, d_ref, k - taps)
        cut = slice(at * o, (at + 1) * o)
        out_ref[k] = left[cut].astype(f32) + right[cut].astype(f32)
    cut = slice((27 - taps) * o, (28 - taps) * o)
    column = (c_ref[cut].astype(f32) + d_ref[cut].astype(f32))[:, :o]
    same = lax.broadcasted_iota(jnp.int32, (o, o), 0) == lax.broadcasted_iota(jnp.int32, (o, o), 1)
    bias_ref[...] = jnp.sum(jnp.where(same, column, 0.0), axis=0, keepdims=True)


def in_hbm(value):
    return pltpu.with_memory_space_constraint(value, pltpu.HBM)


def rotate(value, axis, step):
    count = lax.axis_size(axis)
    return lax.ppermute(value, axis, [(i, (i + step) % count) for i in range(count)])


def swap(value, axis, bit):
    return lax.ppermute(value, axis, [(i, i ^ bit) for i in range(lax.axis_size(axis))])


def on_device(x_in, weight, bias_vec, grad_out):
    o, _, c_all = weight.shape
    _, n, rows, depth = x_in.shape
    f32, bf16 = jnp.float32, jnp.bfloat16
    cells = n * rows
    flops = 2 * 27 * o * c_all * cells * depth
    scale = 1.0 / math.sqrt(lax.axis_size("slab") * cells * depth)
    me = lax.axis_index("chan").astype(jnp.int32).reshape(1)

    block_wide = [pltpu.VMEM((o * cells, depth), f32)]

    x_b = swap(x_in, "chan", 4)
    x_a = swap(x_in, "chan", 2)
    x_side = swap(x_in, "chan", 1)
    x_own, go, go_low, go_high, w_flat, w_back, bias = call(
        functools.partial(prepare_body, n, rows),
        [
            shape_of((o, n, rows, depth), bf16),
            shape_of((cells, o, depth), bf16),
            shape_of((rows, o, depth), bf16),
            shape_of((rows, o, depth), bf16),
            shape_of((27 * o, c_all), bf16),
            shape_of((c_all, 27 * o), bf16),
            shape_of((o, LANES), f32),
        ],
        [in_hbm(a) for a in (x_in, grad_out, jnp.transpose(weight, (1, 0, 2)), bias_vec[None, :])],
        [HBM] * 4,
        [
            pltpu.VMEM((o, n, rows, depth), bf16),
            pltpu.VMEM((27, o, c_all), bf16),
            pltpu.VMEM((1, o), bf16),
            *block_wide,
            pltpu.SemaphoreType.DMA((4,)),
        ],
        name="prepare",
    )
    go_above = rotate(go_low, "slab", -1)
    go_below = rotate(go_high, "slab", 1)
    x_b, w_flat = lax.optimization_barrier((x_b, w_flat))
    x_ab = swap(x_b, "chan", 2)
    x_a_side = swap(x_a, "chan", 1)
    x_b_side = swap(x_b, "chan", 1)
    early, late = (0, 1, 2, 4, 5, 6), (3, 7)
    (x_all,) = call(
        functools.partial(assemble_body, early),
        [shape_of((c_all, cells * depth), bf16)],
        [me, x_own, x_a, x_b, x_side, x_a_side, x_b_side, go_above],
        [SMEM] + [VMEM] * 6 + [ANY],
        block_wide,
        name="assemble",
    )
    x_ab, x_all = lax.optimization_barrier((x_ab, x_all))
    x_ab_side = swap(x_ab, "chan", 1)
    own, low, high, x_all = call(
        functools.partial(forward_body, n, rows, o, late),
        [
            shape_of((cells, o, depth), f32),
            shape_of((2 * rows, o, depth), bf16),
            shape_of((2 * rows, o, depth), bf16),
            shape_of((c_all, cells * depth), bf16),
        ],
        [me, w_flat, x_ab, x_ab_side, x_all],
        [SMEM] + [VMEM] * 4,
        [pltpu.VMEM((3, n + 2, rows, o, depth), f32), *block_wide],
        flops=FORWARD_FLOPS,
        name="forward",
        aliases={4: 3},
    )
    low, high, go_below = lax.optimization_barrier((low, high, go_below))
    above = rotate(low, "slab", -1)
    below = rotate(high, "slab", 1)
    act, total, stacked, w_turned, other, far = call(
        functools.partial(gradient_body, n, rows, o, scale),
        [
            shape_of((o, n, rows, depth), bf16),
            shape_of((o, LANES), f32),
            shape_of((27 * o, cells * depth), bf16),
            shape_of((c_all, 27 * o), bf16),
            shape_of((4, cells, o, depth), bf16),
            shape_of((cells, o, depth), bf16),
        ],
        [me, own, low, high, below, above, bias, go, go_below, go_above, w_back],
        [SMEM] + [VMEM] * 10,
        block_wide,
        flops=flops // 2,
        name="gradient",
    )
    other = swap(other, "chan", 1)
    taps = 14
    first, second = call(
        functools.partial(filter_grad_body, scale, taps, o),
        [shape_of((taps * o, c_all), bf16), shape_of(((28 - taps) * o, c_all), bf16)],
        [stacked, x_all, total],
        flops=flops,
        name="filter_grad",
    )
    first_far = swap(first, "slab", 1)
    second_far = swap(second, "slab", 2)
    (far,) = call(core_sum_body, [shape_of(far.shape, bf16)], [far, other], name="core_sum")
    far = swap(far, "chan", 2)
    (rest,) = call(
        functools.partial(rest_body, o),
        [shape_of((3, cells, o, depth), bf16)],
        [stacked, w_turned],
        flops=flops // 2,
        name="rest",
    )
    (far,) = call(
        chip_sum_body, [shape_of((cells, o, depth), bf16)], [rest, other, far], name="chip_sum"
    )
    across = swap(far, "chan", 4)
    own_sum, near, first, second = call(
        second_body,
        [
            shape_of((cells, o, depth), f32),
            shape_of((cells, o, depth), bf16),
            shape_of(first.shape, bf16),
            shape_of(second.shape, bf16),
        ],
        [rest, other, first, first_far, second, second_far, far],
        [VMEM] * 6 + [ANY],
        name="second_sum",
    )
    first_far = swap(first, "slab", 2)
    second_far = swap(second, "slab", 1)
    near = swap(near, "chan", 2)
    (own_sum,) = call(
        sum_body,
        [shape_of((cells, o, depth), f32)],
        [own_sum, across],
        flops=SUM_FLOPS,
        name="sum",
    )
    weight_grad, bias_grad, grad_in = call(
        functools.partial(last_body, taps),
        [
            shape_of((27, o, c_all), f32),
            shape_of((1, o), f32),
            shape_of((o, n, rows, depth), bf16),
        ],
        [first, first_far, second, second_far, own_sum, near],
        scratch=block_wide,
        name="last",
    )
    return act, grad_in, jnp.transpose(weight_grad, (1, 0, 2)), bias_grad[0]


def solution(mesh):
    placed = (
        P("chan", "slab", None, None),
        P("chan", None, None),
        P("chan"),
        P("chan", "slab", None, None),
    )

    def body(x_in, weight, bias_vec, grad_out):
        tiled = (
            weight.shape[0] % 32 == 0
            and x_in.shape[3] == LANES
            and lax.axis_size("slab") == 4
            and lax.axis_size("chan") == 8
            and x_in.shape[1] >= 2
        )
        return (on_device if tiled else plain)(x_in, weight, bias_vec, grad_out)

    return jax.shard_map(
        body,
        mesh=mesh,
        in_specs=placed,
        out_specs=(
            P("chan", "slab", None, None),
            P("chan", "slab", None, None),
            P("chan", None, None),
            P("chan"),
        ),
        check_vma=False,
    )
```

```python
import functools
import math

import jax
import jax.numpy as jnp
from jax import lax
from jax.experimental import pallas as pl
from jax.experimental.pallas import tpu as pltpu
from jax.sharding import PartitionSpec as P

LANES = 128
SUM_FLOPS = 20 * 10**8
FORWARD_FLOPS = 9 * 10**8
ASSEMBLE_FLOPS = 40 * 10**8
VMEM = pl.BlockSpec(memory_space=pltpu.VMEM)
ANY = pl.BlockSpec(memory_space=pl.ANY)
HBM = pl.BlockSpec(memory_space=pltpu.HBM)
SMEM = pl.BlockSpec(memory_space=pltpu.SMEM)


def with_halo(block, sides, width):
    for axis, dim in sides:
        count = lax.axis_size(axis)
        forward = [(i, i + 1) for i in range(count - 1)]
        forward.append((count - 1, 0))
        backward = [(target, source) for source, target in forward]
        low = lax.ppermute(
            lax.slice_in_dim(block, block.shape[dim] - width, None, axis=dim), axis, forward
        )
        high = lax.ppermute(lax.slice_in_dim(block, 0, width, axis=dim), axis, backward)
        block = jnp.concatenate([low, block, high], axis=dim)
    return block


def tap_list():
    return [(9 * i + 3 * j + l, i, j, l) for i in range(3) for j in range(3) for l in range(3)]


def plain(x_in, weight, bias_vec, grad_out):
    out_local, n_taps, in_total = weight.shape
    n_planes, n_rows, n_depth = (x_in.shape[1], x_in.shape[2], x_in.shape[3])
    rimmed = with_halo(x_in, (("slab", 1),), 1)
    padded = lax.all_gather(rimmed, "chan", axis=0, tiled=True)
    own_planes = padded[:, 1 : n_planes + 1]
    pre_act = (
        jnp.zeros((out_local, n_planes, n_rows, n_depth), jnp.float32)
        + bias_vec.astype(jnp.float32)[:, None, None, None]
    )
    for i in range(3):
        w_plane = jnp.transpose(weight[:, 9 * i : 9 * i + 9], (1, 0, 2)).reshape(
            9 * out_local, in_total
        )
        plane_part = jnp.dot(
            w_plane,
            padded[:, i : i + n_planes].reshape(in_total, -1),
            preferred_element_type=jnp.float32,
        )
        plane_part = plane_part.reshape(9, out_local, n_planes, n_rows, n_depth)
        for j in range(3):
            for l in range(3):
                pre_act = pre_act + jnp.roll(plane_part[3 * j + l], (1 - j, 1 - l), axis=(2, 3))
    sigmoid_v = jax.nn.sigmoid(pre_act)
    activation = (pre_act * sigmoid_v).astype(jnp.bfloat16)
    slope = sigmoid_v * (1.0 + pre_act * (1.0 - sigmoid_v))
    grad_pre = (grad_out.astype(jnp.float32) * slope).astype(jnp.bfloat16)
    padded_grad = with_halo(grad_pre, (("slab", 1),), 1)
    shifted = jnp.stack(
        [
            jnp.roll(padded_grad[:, 2 - i : 2 - i + n_planes], (j - 1, l - 1), axis=(2, 3))
            for k, i, j, l in tap_list()
        ],
        0,
    )
    shifted = shifted.reshape(n_taps * out_local, -1)
    grad_scale = 1.0 / math.sqrt(lax.axis_size("slab") * n_planes * n_rows * n_depth)
    filter_local = lax.dot_general(
        shifted,
        own_planes.reshape(in_total, -1),
        (((1,), (1,)), ((), ())),
        preferred_element_type=jnp.float32,
    )
    filter_part = (
        jnp.transpose(filter_local.reshape(n_taps, out_local, in_total), (1, 0, 2)) * grad_scale
    )
    bias_part = grad_scale * jnp.sum(grad_pre.astype(jnp.float32), axis=(1, 2, 3))
    bias_row = jnp.concatenate(
        [bias_part[:, None, None], jnp.zeros((out_local, 1, in_total - 1), jnp.float32)], 2
    )
    summed_filters = lax.psum(jnp.concatenate([filter_part, bias_row], 1), "slab")
    weight_grad = summed_filters[:, :n_taps]
    bias_grad = summed_filters[:, n_taps, 0]
    flat_w = jnp.transpose(weight, (1, 0, 2)).reshape(n_taps * out_local, in_total)
    product = lax.dot_general(
        flat_w, shifted, (((0,), (0,)), ((), ())), preferred_element_type=jnp.float32
    )
    grad_in = lax.psum_scatter(
        product.reshape(
            in_total // lax.axis_size("chan") * lax.axis_size("chan"), n_planes, n_rows, n_depth
        ),
        "chan",
        scatter_dimension=0,
        tiled=True,
    )
    return (activation, grad_in.astype(jnp.bfloat16), weight_grad, bias_grad)


def call(body, out_shape, operands, specs=None, scratch=(), flops=0, name=None, aliases=None):
    read = sum(math.prod(a.shape) * a.dtype.itemsize for a in operands)
    written = sum(math.prod(a.shape) * a.dtype.itemsize for a in out_shape)
    return pl.pallas_call(
        body,
        out_shape=out_shape,
        in_specs=specs or [VMEM] * len(operands),
        out_specs=[VMEM] * len(out_shape),
        scratch_shapes=list(scratch),
        input_output_aliases=aliases or {},
        compiler_params=pltpu.CompilerParams(vmem_limit_bytes=24 * 2**20),
        cost_estimate=pl.CostEstimate(
            flops=flops, bytes_accessed=read + written, transcendentals=0
        ),
        name=name,
    )(*operands)


def shape_of(shape, dtype):
    return jax.ShapeDtypeStruct(shape, dtype)


def turned(value, wide_ref):
    o = value.shape[0]
    cells = wide_ref.shape[0] // o
    wide_ref[...] = value.astype(jnp.float32).reshape(wide_ref.shape)
    return [
        wide_ref[pl.ds(k, o, stride=cells), :].astype(value.dtype) for k in range(cells)
    ]


def prepare_body(
    n,
    rows,
    x_hbm,
    go_hbm,
    w_hbm,
    bias_hbm,
    x_ref,
    go_ref,
    go_low_ref,
    go_high_ref,
    flat_ref,
    back_ref,
    bias_ref,
    go_in,
    w_in,
    bias_in,
    wide_ref,
    sems,
):
    copies = [
        pltpu.make_async_copy(source, target, sems.at[at])
        for at, (source, target) in enumerate(
            [(go_hbm, go_in), (w_hbm, w_in), (bias_hbm, bias_in), (x_hbm, x_ref)]
        )
    ]
    for copy in copies:
        copy.start()
    copies[0].wait()
    for k, value in enumerate(turned(go_in[...], wide_ref)):
        go_ref[k] = value
        if k < rows:
            go_low_ref[k] = value
        if k >= (n - 1) * rows:
            go_high_ref[k - (n - 1) * rows] = value
    copies[1].wait()
    copies[2].wait()
    copies[3].wait()
    flat = w_in[...].reshape(flat_ref.shape)
    flat_ref[...] = flat
    back_ref[...] = jnp.transpose(flat)
    o = bias_ref.shape[0]
    row = jnp.broadcast_to(bias_in[...].astype(jnp.float32), (o, o))
    same = lax.broadcasted_iota(jnp.int32, (o, o), 0) == lax.broadcasted_iota(jnp.int32, (o, o), 1)
    column = jnp.sum(jnp.where(same, row, 0.0), axis=1, keepdims=True)
    bias_ref[...] = jnp.broadcast_to(column, bias_ref.shape)


def place_block(me_ref, b, block_ref, x_ref, wide_ref):
    o = block_ref.shape[0]
    place = pl.ds(pl.multiple_of(owner(me_ref, b) * o, o), o)
    for k, value in enumerate(turned(block_ref[...], wide_ref)):
        x_ref[place, k * LANES : (k + 1) * LANES] = value


def assemble_body(places, me_ref, *refs):
    blocks, (x_ref, wide_ref) = refs[: len(places)], refs[-2:]
    for b, block in zip(places, blocks):
        place_block(me_ref, b, block, x_ref, wide_ref)


def owner(me_ref, b):
    return jnp.bitwise_xor(me_ref[0], 2 * (b % 4) + b // 4)


def forward_body(n, rows, o, places, me_ref, w_ref, *refs):
    blocks = refs[: len(places)]
    own_ref, low_ref, high_ref, x_ref, acc, wide_ref = refs[len(places) + 1 :]
    for b, block in zip(places, blocks):
        place_block(me_ref, b, block, x_ref, wide_ref)
    w = w_ref[...]
    seen = set()
    for p in range(n):
        for t in range(0, rows, 2):
            at = (p * rows + t) * LANES
            part = jnp.dot(
                w, x_ref[:, at : at + 2 * LANES], preferred_element_type=jnp.float32
            )
            for k, i, j, l in tap_list():
                for h in range(2):
                    slot = (l, p + 2 - i, (t + h + 1 - j) % rows)
                    value = part[k * o : (k + 1) * o, h * LANES : (h + 1) * LANES]
                    if slot in seen:
                        acc[slot] += value
                    else:
                        acc[slot] = value
                        seen.add(slot)
    for q in range(n + 2):
        for y in range(rows):
            total = (
                pltpu.roll(acc[0, q, y], 1, 1)
                + acc[1, q, y]
                + pltpu.roll(acc[2, q, y], LANES - 1, 1)
            )
            if q == 0:
                low_ref[y] = total.astype(low_ref.dtype)
            elif q == n + 1:
                high_ref[y] = total.astype(high_ref.dtype)
            else:
                own_ref[(q - 1) * rows + y] = total
            if q == 1:
                low_ref[rows + y] = total.astype(low_ref.dtype)
            if q == n:
                high_ref[rows + y] = total.astype(high_ref.dtype)


def gradient_body(
    n,
    rows,
    o,
    scale,
    me_ref,
    own_ref,
    low_ref,
    high_ref,
    below_ref,
    above_ref,
    bias_ref,
    go_ref,
    go_below_ref,
    go_above_ref,
    back_ref,
    act_ref,
    total_ref,
    s_ref,
    w_ref,
    other_ref,
    far_ref,
    wide_ref,
):
    f32, bf16 = jnp.float32, jnp.bfloat16
    for b in range(8):
        place = pl.ds(pl.multiple_of(owner(me_ref, b) * o, o), o)
        w_ref[b * o : (b + 1) * o] = back_ref[place]
    total = jnp.zeros((o, LANES), f32)
    for q in range(n + 2):
        for y in range(rows):
            if q == 0:
                pre = below_ref[rows + y].astype(f32) + low_ref[y].astype(f32)
                go = go_below_ref[y]
            elif q == n + 1:
                pre = above_ref[rows + y].astype(f32) + high_ref[y].astype(f32)
                go = go_above_ref[y]
            else:
                pre = own_ref[(q - 1) * rows + y]
                go = go_ref[(q - 1) * rows + y]
                if q == 1:
                    pre = pre + below_ref[y].astype(f32)
                if q == n:
                    pre = pre + above_ref[y].astype(f32)
            pre = pre + bias_ref[...]
            s = jax.nn.sigmoid(pre)
            slope = s * (1.0 + pre * (1.0 - s))
            value = (go.astype(f32) * slope).astype(bf16)
            wide = value.astype(f32)
            if 1 <= q <= n:
                wide_ref[pl.ds((q - 1) * rows + y, o, stride=n * rows), :] = pre * s
                total = total + wide
            shifts = [
                pltpu.roll(wide, LANES - 1, 1).astype(bf16),
                value,
                pltpu.roll(wide, 1, 1).astype(bf16),
            ]
            for k, i, j, l in tap_list():
                p = q - 2 + i
                if 0 <= p < n:
                    at = (p * rows + (y + j - 1) % rows) * LANES
                    s_ref[k * o : (k + 1) * o, at : at + LANES] = shifts[l]
    act_ref[...] = wide_ref[...].reshape(act_ref.shape).astype(bf16)
    total_ref[...] = jnp.broadcast_to(
        jnp.sum(total, axis=1, keepdims=True) * scale, total_ref.shape
    )
    input_grad(n * rows, o, w_ref[3 * o :], s_ref, [(far_ref, None)] + [(other_ref, r) for r in range(4)])


def input_grad(cells, o, w, s_ref, outs):
    for t in range(0, cells, 2):
        part = jnp.dot(
            w, s_ref[:, t * LANES : (t + 2) * LANES], preferred_element_type=jnp.float32
        ).astype(outs[0][0].dtype)
        for h in range(2):
            for r, (out_ref, at) in enumerate(outs):
                cut = part[r * o : (r + 1) * o, h * LANES : (h + 1) * LANES]
                if at is None:
                    out_ref[t + h] = cut
                else:
                    out_ref[at, t + h] = cut


def rest_body(o, s_ref, w_ref, out_ref):
    cells = out_ref.shape[1]
    input_grad(cells, o, w_ref[: 3 * o], s_ref, [(out_ref, r) for r in range(3)])


def filter_grad_body(scale, taps, o, s_ref, x_ref, total_ref, first_ref, second_ref):
    full = lax.dot_general(
        s_ref[...], x_ref[...], (((1,), (1,)), ((), ())), preferred_element_type=jnp.float32
    )
    full = (full * scale).astype(first_ref.dtype)
    first_ref[...] = full[: taps * o]
    second_ref[: (27 - taps) * o] = full[taps * o :]
    row = jnp.concatenate([total_ref[...]] * (second_ref.shape[1] // LANES), axis=1)
    second_ref[(27 - taps) * o :] = row.astype(second_ref.dtype)


def second_body(rest_ref, other_ref, a_ref, b_ref, c_ref, d_ref, _, own_ref, near_ref, ab_ref, cd_ref):
    f32 = jnp.float32
    ab_ref[...] = (a_ref[...].astype(f32) + b_ref[...].astype(f32)).astype(ab_ref.dtype)
    cd_ref[...] = (c_ref[...].astype(f32) + d_ref[...].astype(f32)).astype(cd_ref.dtype)
    own_ref[...] = rest_ref[0].astype(f32) + other_ref[0].astype(f32)
    near_ref[...] = (rest_ref[1].astype(f32) + other_ref[1].astype(f32)).astype(near_ref.dtype)


def core_sum_body(mine_ref, other_ref, out_ref):
    total = mine_ref[...].astype(jnp.float32) + other_ref[3].astype(jnp.float32)
    out_ref[...] = total.astype(out_ref.dtype)


def chip_sum_body(rest_ref, other_ref, far_ref, b_ref):
    f32 = jnp.float32
    total = rest_ref[2].astype(f32) + other_ref[2].astype(f32) + far_ref[...].astype(f32)
    b_ref[...] = total.astype(b_ref.dtype)


def sum_body(a_ref, b_ref, out_ref):
    out_ref[...] = a_ref[...] + b_ref[...].astype(jnp.float32)


def last_body(taps, a_ref, b_ref, c_ref, d_ref, g_ref, h_ref, out_ref, bias_ref, grad_ref, wide_ref):
    o = out_ref.shape[1]
    f32 = jnp.float32
    cells = g_ref.shape[0]
    for k in range(cells):
        wide_ref[pl.ds(k, o, stride=cells), :] = g_ref[k] + h_ref[k].astype(f32)
    grad_ref[...] = wide_ref[...].reshape(grad_ref.shape).astype(grad_ref.dtype)
    for k in range(27):
        left, right, at = (a_ref, b_ref, k) if k < taps else (c_ref, d_ref, k - taps)
        cut = slice(at * o, (at + 1) * o)
        out_ref[k] = left[cut].astype(f32) + right[cut].astype(f32)
    cut = slice((27 - taps) * o, (28 - taps) * o)
    column = (c_ref[cut].astype(f32) + d_ref[cut].astype(f32))[:, :o]
    same = lax.broadcasted_iota(jnp.int32, (o, o), 0) == lax.broadcasted_iota(jnp.int32, (o, o), 1)
    bias_ref[...] = jnp.sum(jnp.where(same, column, 0.0), axis=0, keepdims=True)


def in_hbm(value):
    return pltpu.with_memory_space_constraint(value, pltpu.HBM)


def rotate(value, axis, step):
    count = lax.axis_size(axis)
    return lax.ppermute(value, axis, [(i, (i + step) % count) for i in range(count)])


def swap(value, axis, bit):
    return lax.ppermute(value, axis, [(i, i ^ bit) for i in range(lax.axis_size(axis))])


def on_device(x_in, weight, bias_vec, grad_out):
    o, _, c_all = weight.shape
    _, n, rows, depth = x_in.shape
    f32, bf16 = jnp.float32, jnp.bfloat16
    cells = n * rows
    flops = 2 * 27 * o * c_all * cells * depth
    scale = 1.0 / math.sqrt(lax.axis_size("slab") * cells * depth)
    me = lax.axis_index("chan").astype(jnp.int32).reshape(1)

    block_wide = [pltpu.VMEM((o * cells, depth), f32)]

    x_b = swap(x_in, "chan", 4)
    x_a = swap(x_in, "chan", 2)
    x_side = swap(x_in, "chan", 1)
    x_own, go, go_low, go_high, w_flat, w_back, bias = call(
        functools.partial(prepare_body, n, rows),
        [
            shape_of((o, n, rows, depth), bf16),
            shape_of((cells, o, depth), bf16),
            shape_of((rows, o, depth), bf16),
            shape_of((rows, o, depth), bf16),
            shape_of((27 * o, c_all), bf16),
            shape_of((c_all, 27 * o), bf16),
            shape_of((o, LANES), f32),
        ],
        [in_hbm(a) for a in (x_in, grad_out, jnp.transpose(weight, (1, 0, 2)), bias_vec[None, :])],
        [HBM] * 4,
        [
            pltpu.VMEM((o, n, rows, depth), bf16),
            pltpu.VMEM((27, o, c_all), bf16),
            pltpu.VMEM((1, o), bf16),
            *block_wide,
            pltpu.SemaphoreType.DMA((4,)),
        ],
        name="prepare",
    )
    go_above = rotate(go_low, "slab", -1)
    go_below = rotate(go_high, "slab", 1)
    x_b, w_flat = lax.optimization_barrier((x_b, w_flat))
    x_ab = swap(x_b, "chan", 2)
    late_b, go_above, go_below = lax.optimization_barrier((x_b, go_above, go_below))
    x_a_side = swap(x_a, "chan", 1)
    x_b_side = swap(late_b, "chan", 1)
    early, late = (0, 1, 2, 3, 4, 5, 6), (7,)
    (x_all,) = call(
        functools.partial(assemble_body, early),
        [shape_of((c_all, cells * depth), bf16)],
        [me, x_own, x_a, x_b, x_ab, x_side, x_a_side, x_b_side],
        [SMEM] + [VMEM] * 7,
        block_wide,
        flops=ASSEMBLE_FLOPS,
        name="assemble",
    )
    x_ab_side = swap(x_ab, "chan", 1)
    own, low, high, x_all = call(
        functools.partial(forward_body, n, rows, o, late),
        [
            shape_of((cells, o, depth), f32),
            shape_of((2 * rows, o, depth), bf16),
            shape_of((2 * rows, o, depth), bf16),
            shape_of((c_all, cells * depth), bf16),
        ],
        [me, w_flat, x_ab_side, x_all],
        [SMEM] + [VMEM] * 3,
        [pltpu.VMEM((3, n + 2, rows, o, depth), f32), *block_wide],
        flops=FORWARD_FLOPS,
        name="forward",
        aliases={3: 3},
    )
    above = rotate(low, "slab", -1)
    below = rotate(high, "slab", 1)
    act, total, stacked, w_turned, other, far = call(
        functools.partial(gradient_body, n, rows, o, scale),
        [
            shape_of((o, n, rows, depth), bf16),
            shape_of((o, LANES), f32),
            shape_of((27 * o, cells * depth), bf16),
            shape_of((c_all, 27 * o), bf16),
            shape_of((4, cells, o, depth), bf16),
            shape_of((cells, o, depth), bf16),
        ],
        [me, own, low, high, below, above, bias, go, go_below, go_above, w_back],
        [SMEM] + [VMEM] * 10,
        block_wide,
        flops=flops // 2,
        name="gradient",
    )
    other = swap(other, "chan", 1)
    taps = 14
    first, second = call(
        functools.partial(filter_grad_body, scale, taps, o),
        [shape_of((taps * o, c_all), bf16), shape_of(((28 - taps) * o, c_all), bf16)],
        [stacked, x_all, total],
        flops=flops,
        name="filter_grad",
    )
    first_far = swap(first, "slab", 1)
    second_far = swap(second, "slab", 2)
    (far,) = call(core_sum_body, [shape_of(far.shape, bf16)], [far, other], name="core_sum")
    far = swap(far, "chan", 2)
    (rest,) = call(
        functools.partial(rest_body, o),
        [shape_of((3, cells, o, depth), bf16)],
        [stacked, w_turned],
        flops=flops // 2,
        name="rest",
    )
    (far,) = call(
        chip_sum_body, [shape_of((cells, o, depth), bf16)], [rest, other, far], name="chip_sum"
    )
    across = swap(far, "chan", 4)
    own_sum, near, first, second = call(
        second_body,
        [
            shape_of((cells, o, depth), f32),
            shape_of((cells, o, depth), bf16),
            shape_of(first.shape, bf16),
            shape_of(second.shape, bf16),
        ],
        [rest, other, first, first_far, second, second_far, far],
        [VMEM] * 6 + [ANY],
        name="second_sum",
    )
    first_far = swap(first, "slab", 2)
    second_far = swap(second, "slab", 1)
    near = swap(near, "chan", 2)
    (own_sum,) = call(
        sum_body,
        [shape_of((cells, o, depth), f32)],
        [own_sum, across],
        flops=SUM_FLOPS,
        name="sum",
    )
    weight_grad, bias_grad, grad_in = call(
        functools.partial(last_body, taps),
        [
            shape_of((27, o, c_all), f32),
            shape_of((1, o), f32),
            shape_of((o, n, rows, depth), bf16),
        ],
        [first, first_far, second, second_far, own_sum, near],
        scratch=block_wide,
        name="last",
    )
    return act, grad_in, jnp.transpose(weight_grad, (1, 0, 2)), bias_grad[0]


def solution(mesh):
    placed = (
        P("chan", "slab", None, None),
        P("chan", None, None),
        P("chan"),
        P("chan", "slab", None, None),
    )

    def body(x_in, weight, bias_vec, grad_out):
        tiled = (
            weight.shape[0] % 32 == 0
            and x_in.shape[3] == LANES
            and lax.axis_size("slab") == 4
            and lax.axis_size("chan") == 8
            and x_in.shape[1] >= 2
        )
        return (on_device if tiled else plain)(x_in, weight, bias_vec, grad_out)

    return jax.shard_map(
        body,
        mesh=mesh,
        in_specs=placed,
        out_specs=(
            P("chan", "slab", None, None),
            P("chan", "slab", None, None),
            P("chan", None, None),
            P("chan"),
        ),
        check_vma=False,
    )
```

```python
import functools
import math

import jax
import jax.numpy as jnp
from jax import lax
from jax.experimental import pallas as pl
from jax.experimental.pallas import tpu as pltpu
from jax.sharding import PartitionSpec as P

LANES = 128
FORWARD_FLOPS = 9 * 10**8
SUM_FLOPS = 20 * 10**8
ASSEMBLE_FLOPS = 40 * 10**8
VMEM = pl.BlockSpec(memory_space=pltpu.VMEM)
ANY = pl.BlockSpec(memory_space=pl.ANY)
HBM = pl.BlockSpec(memory_space=pltpu.HBM)
SMEM = pl.BlockSpec(memory_space=pltpu.SMEM)


def with_halo(block, sides, width):
    for axis, dim in sides:
        count = lax.axis_size(axis)
        forward = [(i, i + 1) for i in range(count - 1)]
        forward.append((count - 1, 0))
        backward = [(target, source) for source, target in forward]
        low = lax.ppermute(
            lax.slice_in_dim(block, block.shape[dim] - width, None, axis=dim), axis, forward
        )
        high = lax.ppermute(lax.slice_in_dim(block, 0, width, axis=dim), axis, backward)
        block = jnp.concatenate([low, block, high], axis=dim)
    return block


def tap_list():
    return [(9 * i + 3 * j + l, i, j, l) for i in range(3) for j in range(3) for l in range(3)]


def plain(x_in, weight, bias_vec, grad_out):
    out_local, n_taps, in_total = weight.shape
    n_planes, n_rows, n_depth = (x_in.shape[1], x_in.shape[2], x_in.shape[3])
    rimmed = with_halo(x_in, (("slab", 1),), 1)
    padded = lax.all_gather(rimmed, "chan", axis=0, tiled=True)
    own_planes = padded[:, 1 : n_planes + 1]
    pre_act = (
        jnp.zeros((out_local, n_planes, n_rows, n_depth), jnp.float32)
        + bias_vec.astype(jnp.float32)[:, None, None, None]
    )
    for i in range(3):
        w_plane = jnp.transpose(weight[:, 9 * i : 9 * i + 9], (1, 0, 2)).reshape(
            9 * out_local, in_total
        )
        plane_part = jnp.dot(
            w_plane,
            padded[:, i : i + n_planes].reshape(in_total, -1),
            preferred_element_type=jnp.float32,
        )
        plane_part = plane_part.reshape(9, out_local, n_planes, n_rows, n_depth)
        for j in range(3):
            for l in range(3):
                pre_act = pre_act + jnp.roll(plane_part[3 * j + l], (1 - j, 1 - l), axis=(2, 3))
    sigmoid_v = jax.nn.sigmoid(pre_act)
    activation = (pre_act * sigmoid_v).astype(jnp.bfloat16)
    slope = sigmoid_v * (1.0 + pre_act * (1.0 - sigmoid_v))
    grad_pre = (grad_out.astype(jnp.float32) * slope).astype(jnp.bfloat16)
    padded_grad = with_halo(grad_pre, (("slab", 1),), 1)
    shifted = jnp.stack(
        [
            jnp.roll(padded_grad[:, 2 - i : 2 - i + n_planes], (j - 1, l - 1), axis=(2, 3))
            for k, i, j, l in tap_list()
        ],
        0,
    )
    shifted = shifted.reshape(n_taps * out_local, -1)
    grad_scale = 1.0 / math.sqrt(lax.axis_size("slab") * n_planes * n_rows * n_depth)
    filter_local = lax.dot_general(
        shifted,
        own_planes.reshape(in_total, -1),
        (((1,), (1,)), ((), ())),
        preferred_element_type=jnp.float32,
    )
    filter_part = (
        jnp.transpose(filter_local.reshape(n_taps, out_local, in_total), (1, 0, 2)) * grad_scale
    )
    bias_part = grad_scale * jnp.sum(grad_pre.astype(jnp.float32), axis=(1, 2, 3))
    bias_row = jnp.concatenate(
        [bias_part[:, None, None], jnp.zeros((out_local, 1, in_total - 1), jnp.float32)], 2
    )
    summed_filters = lax.psum(jnp.concatenate([filter_part, bias_row], 1), "slab")
    weight_grad = summed_filters[:, :n_taps]
    bias_grad = summed_filters[:, n_taps, 0]
    flat_w = jnp.transpose(weight, (1, 0, 2)).reshape(n_taps * out_local, in_total)
    product = lax.dot_general(
        flat_w, shifted, (((0,), (0,)), ((), ())), preferred_element_type=jnp.float32
    )
    grad_in = lax.psum_scatter(
        product.reshape(
            in_total // lax.axis_size("chan") * lax.axis_size("chan"), n_planes, n_rows, n_depth
        ),
        "chan",
        scatter_dimension=0,
        tiled=True,
    )
    return (activation, grad_in.astype(jnp.bfloat16), weight_grad, bias_grad)


def call(body, out_shape, operands, specs=None, scratch=(), flops=0, name=None, aliases=None):
    read = sum(math.prod(a.shape) * a.dtype.itemsize for a in operands)
    written = sum(math.prod(a.shape) * a.dtype.itemsize for a in out_shape)
    return pl.pallas_call(
        body,
        out_shape=out_shape,
        in_specs=specs or [VMEM] * len(operands),
        out_specs=[VMEM] * len(out_shape),
        scratch_shapes=list(scratch),
        input_output_aliases=aliases or {},
        compiler_params=pltpu.CompilerParams(vmem_limit_bytes=24 * 2**20),
        cost_estimate=pl.CostEstimate(
            flops=flops, bytes_accessed=read + written, transcendentals=0
        ),
        name=name,
    )(*operands)


def shape_of(shape, dtype):
    return jax.ShapeDtypeStruct(shape, dtype)


def turned(value, wide_ref):
    o = value.shape[0]
    cells = wide_ref.shape[0] // o
    wide_ref[...] = value.astype(jnp.float32).reshape(wide_ref.shape)
    return [
        wide_ref[pl.ds(k, o, stride=cells), :].astype(value.dtype) for k in range(cells)
    ]


def prepare_body(
    n,
    rows,
    x_hbm,
    go_hbm,
    w_hbm,
    bias_hbm,
    x_ref,
    go_ref,
    go_low_ref,
    go_high_ref,
    flat_ref,
    back_ref,
    bias_ref,
    go_in,
    w_in,
    bias_in,
    wide_ref,
    sems,
):
    copies = [
        pltpu.make_async_copy(source, target, sems.at[at])
        for at, (source, target) in enumerate(
            [(go_hbm, go_in), (w_hbm, w_in), (bias_hbm, bias_in), (x_hbm, x_ref)]
        )
    ]
    for copy in copies:
        copy.start()
    copies[0].wait()
    for k, value in enumerate(turned(go_in[...], wide_ref)):
        go_ref[k] = value
        if k < rows:
            go_low_ref[k] = value
        if k >= (n - 1) * rows:
            go_high_ref[k - (n - 1) * rows] = value
    copies[1].wait()
    copies[2].wait()
    copies[3].wait()
    flat = w_in[...].reshape(flat_ref.shape)
    flat_ref[...] = flat
    back_ref[...] = jnp.transpose(flat)
    o = bias_ref.shape[0]
    row = jnp.broadcast_to(bias_in[...].astype(jnp.float32), (o, o))
    same = lax.broadcasted_iota(jnp.int32, (o, o), 0) == lax.broadcasted_iota(jnp.int32, (o, o), 1)
    column = jnp.sum(jnp.where(same, row, 0.0), axis=1, keepdims=True)
    bias_ref[...] = jnp.broadcast_to(column, bias_ref.shape)


def place_block(me_ref, b, block_ref, x_ref, wide_ref):
    o = block_ref.shape[0]
    place = pl.ds(pl.multiple_of(owner(me_ref, b) * o, o), o)
    for k, value in enumerate(turned(block_ref[...], wide_ref)):
        x_ref[place, k * LANES : (k + 1) * LANES] = value


def assemble_body(places, me_ref, *refs):
    blocks, (x_ref, wide_ref) = refs[: len(places)], refs[-2:]
    for b, block in zip(places, blocks):
        place_block(me_ref, b, block, x_ref, wide_ref)


def owner(me_ref, b):
    return jnp.bitwise_xor(me_ref[0], 2 * (b % 4) + b // 4)


def forward_body(n, rows, o, places, me_ref, w_ref, *refs):
    blocks = refs[: len(places)]
    own_ref, low_ref, high_ref, x_ref, acc, wide_ref = refs[len(places) + 1 :]
    for b, block in zip(places, blocks):
        place_block(me_ref, b, block, x_ref, wide_ref)
    w = w_ref[...]
    seen = set()
    for p in range(n):
        for t in range(0, rows, 2):
            at = (p * rows + t) * LANES
            part = jnp.dot(
                w, x_ref[:, at : at + 2 * LANES], preferred_element_type=jnp.float32
            )
            for k, i, j, l in tap_list():
                for h in range(2):
                    slot = (l, p + 2 - i, (t + h + 1 - j) % rows)
                    value = part[k * o : (k + 1) * o, h * LANES : (h + 1) * LANES]
                    if slot in seen:
                        acc[slot] += value
                    else:
                        acc[slot] = value
                        seen.add(slot)
    for q in range(n + 2):
        for y in range(rows):
            total = (
                pltpu.roll(acc[0, q, y], 1, 1)
                + acc[1, q, y]
                + pltpu.roll(acc[2, q, y], LANES - 1, 1)
            )
            if q == 0:
                low_ref[y] = total.astype(low_ref.dtype)
            elif q == n + 1:
                high_ref[y] = total.astype(high_ref.dtype)
            else:
                own_ref[(q - 1) * rows + y] = total
            if q == 1:
                low_ref[rows + y] = total.astype(low_ref.dtype)
            if q == n:
                high_ref[rows + y] = total.astype(high_ref.dtype)


def gradient_body(
    n,
    rows,
    o,
    scale,
    me_ref,
    own_ref,
    low_ref,
    high_ref,
    below_ref,
    above_ref,
    bias_ref,
    go_ref,
    go_below_ref,
    go_above_ref,
    back_ref,
    act_ref,
    total_ref,
    s_ref,
    other_ref,
    mine_ref,
    w_ref,
    wide_ref,
):
    f32, bf16 = jnp.float32, jnp.bfloat16
    for b in range(8):
        place = pl.ds(pl.multiple_of(owner(me_ref, b) * o, o), o)
        w_ref[b * o : (b + 1) * o] = back_ref[place]
    total = jnp.zeros((o, LANES), f32)
    for q in range(n + 2):
        for y in range(rows):
            if q == 0:
                pre = below_ref[rows + y].astype(f32) + low_ref[y].astype(f32)
                go = go_below_ref[y]
            elif q == n + 1:
                pre = above_ref[rows + y].astype(f32) + high_ref[y].astype(f32)
                go = go_above_ref[y]
            else:
                pre = own_ref[(q - 1) * rows + y]
                go = go_ref[(q - 1) * rows + y]
                if q == 1:
                    pre = pre + below_ref[y].astype(f32)
                if q == n:
                    pre = pre + above_ref[y].astype(f32)
            pre = pre + bias_ref[...]
            s = jax.nn.sigmoid(pre)
            slope = s * (1.0 + pre * (1.0 - s))
            value = (go.astype(f32) * slope).astype(bf16)
            wide = value.astype(f32)
            if 1 <= q <= n:
                wide_ref[pl.ds((q - 1) * rows + y, o, stride=n * rows), :] = pre * s
                total = total + wide
            shifts = [
                pltpu.roll(wide, LANES - 1, 1).astype(bf16),
                value,
                pltpu.roll(wide, 1, 1).astype(bf16),
            ]
            for k, i, j, l in tap_list():
                p = q - 2 + i
                if 0 <= p < n:
                    at = (p * rows + (y + j - 1) % rows) * LANES
                    s_ref[k * o : (k + 1) * o, at : at + LANES] = shifts[l]
    act_ref[...] = wide_ref[...].reshape(act_ref.shape).astype(bf16)
    total_ref[...] = jnp.broadcast_to(
        jnp.sum(total, axis=1, keepdims=True) * scale, total_ref.shape
    )
    input_grad(n * rows, o, w_ref[...], s_ref, [(ref, r) for ref in (mine_ref, other_ref) for r in range(4)])


def input_grad(cells, o, w, s_ref, outs):
    for t in range(0, cells, 2):
        part = jnp.dot(
            w, s_ref[:, t * LANES : (t + 2) * LANES], preferred_element_type=jnp.float32
        ).astype(outs[0][0].dtype)
        for h in range(2):
            for r, (out_ref, at) in enumerate(outs):
                cut = part[r * o : (r + 1) * o, h * LANES : (h + 1) * LANES]
                out_ref[at, t + h] = cut


def filter_grad_body(scale, taps, o, s_ref, x_ref, total_ref, first_ref, second_ref):
    full = lax.dot_general(
        s_ref[...], x_ref[...], (((1,), (1,)), ((), ())), preferred_element_type=jnp.float32
    )
    full = (full * scale).astype(first_ref.dtype)
    first_ref[...] = full[: taps * o]
    second_ref[: (27 - taps) * o] = full[taps * o :]
    row = jnp.concatenate([total_ref[...]] * (second_ref.shape[1] // LANES), axis=1)
    second_ref[(27 - taps) * o :] = row.astype(second_ref.dtype)


def pair_body(a_ref, b_ref, c_ref, d_ref, _, ab_ref, cd_ref):
    f32 = jnp.float32
    ab_ref[...] = (a_ref[...].astype(f32) + b_ref[...].astype(f32)).astype(ab_ref.dtype)
    cd_ref[...] = (c_ref[...].astype(f32) + d_ref[...].astype(f32)).astype(cd_ref.dtype)


def core_sum_body(mine_ref, other_ref, *outs):
    for r, out_ref in enumerate(outs):
        total = mine_ref[r].astype(jnp.float32) + other_ref[r].astype(jnp.float32)
        out_ref[...] = total.astype(out_ref.dtype)


def sum_body(a_ref, b_ref, c_ref, d_ref, out_ref):
    f32 = jnp.float32
    total = b_ref[...].astype(f32) + c_ref[...].astype(f32) + d_ref[...].astype(f32)
    out_ref[...] = a_ref[...] + total


def last_body(
    taps, a_ref, b_ref, c_ref, d_ref, g_ref, out_ref, bias_ref, grad_ref, wide_ref
):
    o = out_ref.shape[1]
    f32 = jnp.float32
    cells = g_ref.shape[0]
    for k in range(cells):
        wide_ref[pl.ds(k, o, stride=cells), :] = g_ref[k]
    grad_ref[...] = wide_ref[...].reshape(grad_ref.shape).astype(grad_ref.dtype)
    for k in range(27):
        left, right, at = (a_ref, b_ref, k) if k < taps else (c_ref, d_ref, k - taps)
        cut = slice(at * o, (at + 1) * o)
        out_ref[k] = left[cut].astype(f32) + right[cut].astype(f32)
    cut = slice((27 - taps) * o, (28 - taps) * o)
    column = (c_ref[cut].astype(f32) + d_ref[cut].astype(f32))[:, :o]
    same = lax.broadcasted_iota(jnp.int32, (o, o), 0) == lax.broadcasted_iota(jnp.int32, (o, o), 1)
    bias_ref[...] = jnp.sum(jnp.where(same, column, 0.0), axis=0, keepdims=True)


def in_hbm(value):
    return pltpu.with_memory_space_constraint(value, pltpu.HBM)


def rotate(value, axis, step):
    count = lax.axis_size(axis)
    return lax.ppermute(value, axis, [(i, (i + step) % count) for i in range(count)])


def swap(value, axis, bit):
    return lax.ppermute(value, axis, [(i, i ^ bit) for i in range(lax.axis_size(axis))])


def on_device(x_in, weight, bias_vec, grad_out):
    o, _, c_all = weight.shape
    _, n, rows, depth = x_in.shape
    f32, bf16 = jnp.float32, jnp.bfloat16
    cells = n * rows
    flops = 2 * 27 * o * c_all * cells * depth
    scale = 1.0 / math.sqrt(lax.axis_size("slab") * cells * depth)
    me = lax.axis_index("chan").astype(jnp.int32).reshape(1)

    block_wide = [pltpu.VMEM((o * cells, depth), f32)]

    x_ab = swap(x_in, "chan", 6)
    x_b = swap(x_in, "chan", 4)
    x_a = swap(x_in, "chan", 2)
    x_side = swap(x_in, "chan", 1)
    x_own, go, go_low, go_high, w_flat, w_back, bias = call(
        functools.partial(prepare_body, n, rows),
        [
            shape_of((o, n, rows, depth), bf16),
            shape_of((cells, o, depth), bf16),
            shape_of((rows, o, depth), bf16),
            shape_of((rows, o, depth), bf16),
            shape_of((27 * o, c_all), bf16),
            shape_of((c_all, 27 * o), bf16),
            shape_of((o, LANES), f32),
        ],
        [in_hbm(a) for a in (x_in, grad_out, jnp.transpose(weight, (1, 0, 2)), bias_vec[None, :])],
        [HBM] * 4,
        [
            pltpu.VMEM((o, n, rows, depth), bf16),
            pltpu.VMEM((27, o, c_all), bf16),
            pltpu.VMEM((1, o), bf16),
            *block_wide,
            pltpu.SemaphoreType.DMA((4,)),
        ],
        name="prepare",
    )
    go_above = rotate(go_low, "slab", -1)
    go_below = rotate(go_high, "slab", 1)
    x_b, w_flat = lax.optimization_barrier((x_b, w_flat))
    late_ab, go_above, go_below = lax.optimization_barrier((x_ab, go_above, go_below))
    x_a_side = swap(x_a, "chan", 1)
    x_b_side = swap(x_b, "chan", 1)
    early, late = (0, 1, 2, 3, 4, 5, 6), (7,)
    (x_all,) = call(
        functools.partial(assemble_body, early),
        [shape_of((c_all, cells * depth), bf16)],
        [me, x_own, x_a, x_b, x_ab, x_side, x_a_side, x_b_side],
        [SMEM] + [VMEM] * 7,
        block_wide,
        flops=ASSEMBLE_FLOPS,
        name="assemble",
    )
    x_ab_side = swap(late_ab, "chan", 1)
    own, low, high, x_all = call(
        functools.partial(forward_body, n, rows, o, late),
        [
            shape_of((cells, o, depth), f32),
            shape_of((2 * rows, o, depth), bf16),
            shape_of((2 * rows, o, depth), bf16),
            shape_of((c_all, cells * depth), bf16),
        ],
        [me, w_flat, x_ab_side, x_all],
        [SMEM] + [VMEM] * 3,
        [pltpu.VMEM((3, n + 2, rows, o, depth), f32), *block_wide],
        flops=FORWARD_FLOPS,
        name="forward",
        aliases={3: 3},
    )
    above = rotate(low, "slab", -1)
    below = rotate(high, "slab", 1)
    act, total, stacked, other, mine = call(
        functools.partial(gradient_body, n, rows, o, scale),
        [
            shape_of((o, n, rows, depth), bf16),
            shape_of((o, LANES), f32),
            shape_of((27 * o, cells * depth), bf16),
            shape_of((4, cells, o, depth), bf16),
            shape_of((4, cells, o, depth), bf16),
        ],
        [me, own, low, high, below, above, bias, go, go_below, go_above, w_back],
        [SMEM] + [VMEM] * 10,
        [pltpu.VMEM((c_all, 27 * o), bf16), *block_wide],
        flops=flops,
        name="gradient",
    )
    other = swap(other, "chan", 1)
    taps = 14
    first, second = call(
        functools.partial(filter_grad_body, scale, taps, o),
        [shape_of((taps * o, c_all), bf16), shape_of(((28 - taps) * o, c_all), bf16)],
        [stacked, x_all, total],
        flops=flops,
        name="filter_grad",
    )
    first_far = swap(first, "slab", 1)
    second_far = swap(second, "slab", 2)
    g_own, g_a, g_b, g_ab = call(
        core_sum_body,
        [shape_of((cells, o, depth), f32)] + [shape_of((cells, o, depth), bf16)] * 3,
        [mine, other],
        name="core_sum",
    )
    g_ab = swap(g_ab, "chan", 6)
    g_b = swap(g_b, "chan", 4)
    g_a = swap(g_a, "chan", 2)
    first, second = call(
        pair_body,
        [shape_of(first.shape, bf16), shape_of(second.shape, bf16)],
        [first, first_far, second, second_far, g_own],
        [VMEM] * 4 + [ANY],
        name="pair_sum",
    )
    first_far = swap(first, "slab", 2)
    second_far = swap(second, "slab", 1)
    (g_own,) = call(
        sum_body,
        [shape_of((cells, o, depth), f32)],
        [g_own, g_ab, g_b, g_a],
        flops=SUM_FLOPS,
        name="sum",
    )
    weight_grad, bias_grad, grad_in = call(
        functools.partial(last_body, taps),
        [
            shape_of((27, o, c_all), f32),
            shape_of((1, o), f32),
            shape_of((o, n, rows, depth), bf16),
        ],
        [first, first_far, second, second_far, g_own],
        scratch=block_wide,
        name="last",
    )
    return act, grad_in, jnp.transpose(weight_grad, (1, 0, 2)), bias_grad[0]


def solution(mesh):
    placed = (
        P("chan", "slab", None, None),
        P("chan", None, None),
        P("chan"),
        P("chan", "slab", None, None),
    )

    def body(x_in, weight, bias_vec, grad_out):
        tiled = (
            weight.shape[0] % 32 == 0
            and x_in.shape[3] == LANES
            and lax.axis_size("slab") == 4
            and lax.axis_size("chan") == 8
            and x_in.shape[1] >= 2
        )
        return (on_device if tiled else plain)(x_in, weight, bias_vec, grad_out)

    return jax.shard_map(
        body,
        mesh=mesh,
        in_specs=placed,
        out_specs=(
            P("chan", "slab", None, None),
            P("chan", "slab", None, None),
            P("chan", None, None),
            P("chan"),
        ),
        check_vma=False,
    )
```

```python
import functools
import math

import jax
import jax.numpy as jnp
from jax import lax
from jax.experimental import pallas as pl
from jax.experimental.pallas import tpu as pltpu
from jax.sharding import PartitionSpec as P

LANES = 128
FORWARD_FLOPS = 9 * 10**8
SUM_FLOPS = 50 * 10**8
ASSEMBLE_FLOPS = 40 * 10**8
VMEM = pl.BlockSpec(memory_space=pltpu.VMEM)
ANY = pl.BlockSpec(memory_space=pl.ANY)
HBM = pl.BlockSpec(memory_space=pltpu.HBM)
SMEM = pl.BlockSpec(memory_space=pltpu.SMEM)


def with_halo(block, sides, width):
    for axis, dim in sides:
        count = lax.axis_size(axis)
        forward = [(i, i + 1) for i in range(count - 1)]
        forward.append((count - 1, 0))
        backward = [(target, source) for source, target in forward]
        low = lax.ppermute(
            lax.slice_in_dim(block, block.shape[dim] - width, None, axis=dim), axis, forward
        )
        high = lax.ppermute(lax.slice_in_dim(block, 0, width, axis=dim), axis, backward)
        block = jnp.concatenate([low, block, high], axis=dim)
    return block


def tap_list():
    return [(9 * i + 3 * j + l, i, j, l) for i in range(3) for j in range(3) for l in range(3)]


def plain(x_in, weight, bias_vec, grad_out):
    out_local, n_taps, in_total = weight.shape
    n_planes, n_rows, n_depth = (x_in.shape[1], x_in.shape[2], x_in.shape[3])
    rimmed = with_halo(x_in, (("slab", 1),), 1)
    padded = lax.all_gather(rimmed, "chan", axis=0, tiled=True)
    own_planes = padded[:, 1 : n_planes + 1]
    pre_act = (
        jnp.zeros((out_local, n_planes, n_rows, n_depth), jnp.float32)
        + bias_vec.astype(jnp.float32)[:, None, None, None]
    )
    for i in range(3):
        w_plane = jnp.transpose(weight[:, 9 * i : 9 * i + 9], (1, 0, 2)).reshape(
            9 * out_local, in_total
        )
        plane_part = jnp.dot(
            w_plane,
            padded[:, i : i + n_planes].reshape(in_total, -1),
            preferred_element_type=jnp.float32,
        )
        plane_part = plane_part.reshape(9, out_local, n_planes, n_rows, n_depth)
        for j in range(3):
            for l in range(3):
                pre_act = pre_act + jnp.roll(plane_part[3 * j + l], (1 - j, 1 - l), axis=(2, 3))
    sigmoid_v = jax.nn.sigmoid(pre_act)
    activation = (pre_act * sigmoid_v).astype(jnp.bfloat16)
    slope = sigmoid_v * (1.0 + pre_act * (1.0 - sigmoid_v))
    grad_pre = (grad_out.astype(jnp.float32) * slope).astype(jnp.bfloat16)
    padded_grad = with_halo(grad_pre, (("slab", 1),), 1)
    shifted = jnp.stack(
        [
            jnp.roll(padded_grad[:, 2 - i : 2 - i + n_planes], (j - 1, l - 1), axis=(2, 3))
            for k, i, j, l in tap_list()
        ],
        0,
    )
    shifted = shifted.reshape(n_taps * out_local, -1)
    grad_scale = 1.0 / math.sqrt(lax.axis_size("slab") * n_planes * n_rows * n_depth)
    filter_local = lax.dot_general(
        shifted,
        own_planes.reshape(in_total, -1),
        (((1,), (1,)), ((), ())),
        preferred_element_type=jnp.float32,
    )
    filter_part = (
        jnp.transpose(filter_local.reshape(n_taps, out_local, in_total), (1, 0, 2)) * grad_scale
    )
    bias_part = grad_scale * jnp.sum(grad_pre.astype(jnp.float32), axis=(1, 2, 3))
    bias_row = jnp.concatenate(
        [bias_part[:, None, None], jnp.zeros((out_local, 1, in_total - 1), jnp.float32)], 2
    )
    summed_filters = lax.psum(jnp.concatenate([filter_part, bias_row], 1), "slab")
    weight_grad = summed_filters[:, :n_taps]
    bias_grad = summed_filters[:, n_taps, 0]
    flat_w = jnp.transpose(weight, (1, 0, 2)).reshape(n_taps * out_local, in_total)
    product = lax.dot_general(
        flat_w, shifted, (((0,), (0,)), ((), ())), preferred_element_type=jnp.float32
    )
    grad_in = lax.psum_scatter(
        product.reshape(
            in_total // lax.axis_size("chan") * lax.axis_size("chan"), n_planes, n_rows, n_depth
        ),
        "chan",
        scatter_dimension=0,
        tiled=True,
    )
    return (activation, grad_in.astype(jnp.bfloat16), weight_grad, bias_grad)


def call(body, out_shape, operands, specs=None, scratch=(), flops=0, name=None, aliases=None):
    read = sum(math.prod(a.shape) * a.dtype.itemsize for a in operands)
    written = sum(math.prod(a.shape) * a.dtype.itemsize for a in out_shape)
    return pl.pallas_call(
        body,
        out_shape=out_shape,
        in_specs=specs or [VMEM] * len(operands),
        out_specs=[VMEM] * len(out_shape),
        scratch_shapes=list(scratch),
        input_output_aliases=aliases or {},
        compiler_params=pltpu.CompilerParams(vmem_limit_bytes=24 * 2**20),
        cost_estimate=pl.CostEstimate(
            flops=flops, bytes_accessed=read + written, transcendentals=0
        ),
        name=name,
    )(*operands)


def shape_of(shape, dtype):
    return jax.ShapeDtypeStruct(shape, dtype)


def turned(value, wide_ref):
    o = value.shape[0]
    cells = wide_ref.shape[0] // o
    wide_ref[...] = value.astype(jnp.float32).reshape(wide_ref.shape)
    return [
        wide_ref[pl.ds(k, o, stride=cells), :].astype(value.dtype) for k in range(cells)
    ]


def prepare_body(
    n,
    rows,
    x_hbm,
    go_hbm,
    w_hbm,
    bias_hbm,
    x_ref,
    go_ref,
    go_low_ref,
    go_high_ref,
    flat_ref,
    back_ref,
    bias_ref,
    go_in,
    w_in,
    bias_in,
    wide_ref,
    sems,
):
    copies = [
        pltpu.make_async_copy(source, target, sems.at[at])
        for at, (source, target) in enumerate(
            [(go_hbm, go_in), (w_hbm, w_in), (bias_hbm, bias_in), (x_hbm, x_ref)]
        )
    ]
    for copy in copies:
        copy.start()
    copies[0].wait()
    for k, value in enumerate(turned(go_in[...], wide_ref)):
        go_ref[k] = value
        if k < rows:
            go_low_ref[k] = value
        if k >= (n - 1) * rows:
            go_high_ref[k - (n - 1) * rows] = value
    copies[1].wait()
    copies[2].wait()
    copies[3].wait()
    flat = w_in[...].reshape(flat_ref.shape)
    flat_ref[...] = flat
    back_ref[...] = jnp.transpose(flat)
    o = bias_ref.shape[0]
    row = jnp.broadcast_to(bias_in[...].astype(jnp.float32), (o, o))
    same = lax.broadcasted_iota(jnp.int32, (o, o), 0) == lax.broadcasted_iota(jnp.int32, (o, o), 1)
    column = jnp.sum(jnp.where(same, row, 0.0), axis=1, keepdims=True)
    bias_ref[...] = jnp.broadcast_to(column, bias_ref.shape)


def place_block(me_ref, b, block_ref, x_ref, wide_ref):
    o = block_ref.shape[0]
    place = pl.ds(pl.multiple_of(owner(me_ref, b) * o, o), o)
    for k, value in enumerate(turned(block_ref[...], wide_ref)):
        x_ref[place, k * LANES : (k + 1) * LANES] = value


def assemble_body(places, me_ref, *refs):
    blocks, (x_ref, wide_ref) = refs[: len(places)], refs[-2:]
    for b, block in zip(places, blocks):
        place_block(me_ref, b, block, x_ref, wide_ref)


def owner(me_ref, b):
    return jnp.bitwise_xor(me_ref[0], 2 * (b % 4) + b // 4)


def forward_body(n, rows, o, places, me_ref, w_ref, *refs):
    blocks = refs[: len(places)]
    own_ref, low_ref, high_ref, x_ref, acc, wide_ref = refs[len(places) + 1 :]
    for b, block in zip(places, blocks):
        place_block(me_ref, b, block, x_ref, wide_ref)
    w = w_ref[...]
    seen = set()
    for p in range(n):
        for t in range(0, rows, 2):
            at = (p * rows + t) * LANES
            part = jnp.dot(
                w, x_ref[:, at : at + 2 * LANES], preferred_element_type=jnp.float32
            )
            for k, i, j, l in tap_list():
                for h in range(2):
                    slot = (l, p + 2 - i, (t + h + 1 - j) % rows)
                    value = part[k * o : (k + 1) * o, h * LANES : (h + 1) * LANES]
                    if slot in seen:
                        acc[slot] += value
                    else:
                        acc[slot] = value
                        seen.add(slot)
    for q in range(n + 2):
        for y in range(rows):
            total = (
                pltpu.roll(acc[0, q, y], 1, 1)
                + acc[1, q, y]
                + pltpu.roll(acc[2, q, y], LANES - 1, 1)
            )
            if q == 0:
                low_ref[y] = total.astype(low_ref.dtype)
            elif q == n + 1:
                high_ref[y] = total.astype(high_ref.dtype)
            else:
                own_ref[(q - 1) * rows + y] = total
            if q == 1:
                low_ref[rows + y] = total.astype(low_ref.dtype)
            if q == n:
                high_ref[rows + y] = total.astype(high_ref.dtype)


def gradient_body(
    n,
    rows,
    o,
    scale,
    me_ref,
    own_ref,
    low_ref,
    high_ref,
    below_ref,
    above_ref,
    bias_ref,
    go_ref,
    go_below_ref,
    go_above_ref,
    back_ref,
    act_ref,
    total_ref,
    s_ref,
    other_ref,
    mine_ref,
    w_ref,
    wide_ref,
):
    f32, bf16 = jnp.float32, jnp.bfloat16
    for b in range(8):
        place = pl.ds(pl.multiple_of(owner(me_ref, b) * o, o), o)
        w_ref[b * o : (b + 1) * o] = back_ref[place]
    total = jnp.zeros((o, LANES), f32)
    for q in range(n + 2):
        for y in range(rows):
            if q == 0:
                pre = below_ref[rows + y].astype(f32) + low_ref[y].astype(f32)
                go = go_below_ref[y]
            elif q == n + 1:
                pre = above_ref[rows + y].astype(f32) + high_ref[y].astype(f32)
                go = go_above_ref[y]
            else:
                pre = own_ref[(q - 1) * rows + y]
                go = go_ref[(q - 1) * rows + y]
                if q == 1:
                    pre = pre + below_ref[y].astype(f32)
                if q == n:
                    pre = pre + above_ref[y].astype(f32)
            pre = pre + bias_ref[...]
            s = jax.nn.sigmoid(pre)
            slope = s * (1.0 + pre * (1.0 - s))
            value = (go.astype(f32) * slope).astype(bf16)
            wide = value.astype(f32)
            if 1 <= q <= n:
                wide_ref[pl.ds((q - 1) * rows + y, o, stride=n * rows), :] = pre * s
                total = total + wide
            shifts = [
                pltpu.roll(wide, LANES - 1, 1).astype(bf16),
                value,
                pltpu.roll(wide, 1, 1).astype(bf16),
            ]
            for k, i, j, l in tap_list():
                p = q - 2 + i
                if 0 <= p < n:
                    at = (p * rows + (y + j - 1) % rows) * LANES
                    s_ref[k * o : (k + 1) * o, at : at + LANES] = shifts[l]
    act_ref[...] = wide_ref[...].reshape(act_ref.shape).astype(bf16)
    total_ref[...] = jnp.broadcast_to(
        jnp.sum(total, axis=1, keepdims=True) * scale, total_ref.shape
    )
    input_grad(n * rows, o, w_ref[...], s_ref, [(ref, r) for ref in (mine_ref, other_ref) for r in range(4)])


def input_grad(cells, o, w, s_ref, outs):
    for t in range(0, cells, 2):
        part = jnp.dot(
            w, s_ref[:, t * LANES : (t + 2) * LANES], preferred_element_type=jnp.float32
        ).astype(outs[0][0].dtype)
        for h in range(2):
            for r, (out_ref, at) in enumerate(outs):
                cut = part[r * o : (r + 1) * o, h * LANES : (h + 1) * LANES]
                out_ref[at, t + h] = cut


def filter_grad_body(scale, o, s_ref, x_ref, total_ref, out_ref):
    full = lax.dot_general(
        s_ref[...], x_ref[...], (((1,), (1,)), ((), ())), preferred_element_type=jnp.float32
    )
    out_ref[: 27 * o] = (full * scale).astype(out_ref.dtype)
    row = jnp.concatenate([total_ref[...]] * (out_ref.shape[1] // LANES), axis=1)
    out_ref[27 * o :] = row.astype(out_ref.dtype)


def pair_body(a_ref, b_ref, _, out_ref):
    f32 = jnp.float32
    out_ref[...] = (a_ref[...].astype(f32) + b_ref[...].astype(f32)).astype(out_ref.dtype)


def core_sum_body(mine_ref, other_ref, *outs):
    for r, out_ref in enumerate(outs):
        total = mine_ref[r].astype(jnp.float32) + other_ref[r].astype(jnp.float32)
        out_ref[...] = total.astype(out_ref.dtype)


def sum_body(a_ref, b_ref, c_ref, d_ref, out_ref):
    f32 = jnp.float32
    total = b_ref[...].astype(f32) + c_ref[...].astype(f32) + d_ref[...].astype(f32)
    out_ref[...] = a_ref[...] + total


def last_body(a_ref, b_ref, g_ref, out_ref, bias_ref, grad_ref, wide_ref):
    o = out_ref.shape[1]
    f32 = jnp.float32
    cells = g_ref.shape[0]
    for k in range(cells):
        wide_ref[pl.ds(k, o, stride=cells), :] = g_ref[k]
    grad_ref[...] = wide_ref[...].reshape(grad_ref.shape).astype(grad_ref.dtype)
    for k in range(27):
        cut = slice(k * o, (k + 1) * o)
        out_ref[k] = a_ref[cut].astype(f32) + b_ref[cut].astype(f32)
    cut = slice(27 * o, 28 * o)
    column = (a_ref[cut].astype(f32) + b_ref[cut].astype(f32))[:, :o]
    same = lax.broadcasted_iota(jnp.int32, (o, o), 0) == lax.broadcasted_iota(jnp.int32, (o, o), 1)
    bias_ref[...] = jnp.sum(jnp.where(same, column, 0.0), axis=0, keepdims=True)


def in_hbm(value):
    return pltpu.with_memory_space_constraint(value, pltpu.HBM)


def rotate(value, axis, step):
    count = lax.axis_size(axis)
    return lax.ppermute(value, axis, [(i, (i + step) % count) for i in range(count)])


def swap(value, axis, bit):
    return lax.ppermute(value, axis, [(i, i ^ bit) for i in range(lax.axis_size(axis))])


def cross(value, phase):
    slabs, chans = lax.axis_size("slab"), lax.axis_size("chan")
    pairs = [
        (s * chans + c, (s ^ (1 + (c + phase) % 2)) * chans + c)
        for s in range(slabs)
        for c in range(chans)
    ]
    return lax.ppermute(value, ("slab", "chan"), pairs)


def on_device(x_in, weight, bias_vec, grad_out):
    o, _, c_all = weight.shape
    _, n, rows, depth = x_in.shape
    f32, bf16 = jnp.float32, jnp.bfloat16
    cells = n * rows
    flops = 2 * 27 * o * c_all * cells * depth
    scale = 1.0 / math.sqrt(lax.axis_size("slab") * cells * depth)
    me = lax.axis_index("chan").astype(jnp.int32).reshape(1)

    block_wide = [pltpu.VMEM((o * cells, depth), f32)]

    x_b = swap(x_in, "chan", 4)
    x_a = swap(x_in, "chan", 2)
    x_side = swap(x_in, "chan", 1)
    x_own, go, go_low, go_high, w_flat, w_back, bias = call(
        functools.partial(prepare_body, n, rows),
        [
            shape_of((o, n, rows, depth), bf16),
            shape_of((cells, o, depth), bf16),
            shape_of((rows, o, depth), bf16),
            shape_of((rows, o, depth), bf16),
            shape_of((27 * o, c_all), bf16),
            shape_of((c_all, 27 * o), bf16),
            shape_of((o, LANES), f32),
        ],
        [in_hbm(a) for a in (x_in, grad_out, jnp.transpose(weight, (1, 0, 2)), bias_vec[None, :])],
        [HBM] * 4,
        [
            pltpu.VMEM((o, n, rows, depth), bf16),
            pltpu.VMEM((27, o, c_all), bf16),
            pltpu.VMEM((1, o), bf16),
            *block_wide,
            pltpu.SemaphoreType.DMA((4,)),
        ],
        name="prepare",
    )
    go_above = rotate(go_low, "slab", -1)
    go_below = rotate(go_high, "slab", 1)
    x_b, w_flat = lax.optimization_barrier((x_b, w_flat))
    x_ab = swap(x_b, "chan", 2)
    late_b, go_above, go_below = lax.optimization_barrier((x_b, go_above, go_below))
    x_a_side = swap(x_a, "chan", 1)
    x_b_side = swap(late_b, "chan", 1)
    early, late = (0, 1, 2, 3, 4, 5, 6), (7,)
    (x_all,) = call(
        functools.partial(assemble_body, early),
        [shape_of((c_all, cells * depth), bf16)],
        [me, x_own, x_a, x_b, x_ab, x_side, x_a_side, x_b_side],
        [SMEM] + [VMEM] * 7,
        block_wide,
        flops=ASSEMBLE_FLOPS,
        name="assemble",
    )
    x_ab_side = swap(x_ab, "chan", 1)
    own, low, high, x_all = call(
        functools.partial(forward_body, n, rows, o, late),
        [
            shape_of((cells, o, depth), f32),
            shape_of((2 * rows, o, depth), bf16),
            shape_of((2 * rows, o, depth), bf16),
            shape_of((c_all, cells * depth), bf16),
        ],
        [me, w_flat, x_ab_side, x_all],
        [SMEM] + [VMEM] * 3,
        [pltpu.VMEM((3, n + 2, rows, o, depth), f32), *block_wide],
        flops=FORWARD_FLOPS,
        name="forward",
        aliases={3: 3},
    )
    above = rotate(low, "slab", -1)
    below = rotate(high, "slab", 1)
    act, total, stacked, other, mine = call(
        functools.partial(gradient_body, n, rows, o, scale),
        [
            shape_of((o, n, rows, depth), bf16),
            shape_of((o, LANES), f32),
            shape_of((27 * o, cells * depth), bf16),
            shape_of((4, cells, o, depth), bf16),
            shape_of((4, cells, o, depth), bf16),
        ],
        [me, own, low, high, below, above, bias, go, go_below, go_above, w_back],
        [SMEM] + [VMEM] * 10,
        [pltpu.VMEM((c_all, 27 * o), bf16), *block_wide],
        flops=flops,
        name="gradient",
    )
    other = swap(other, "chan", 1)
    (filters,) = call(
        functools.partial(filter_grad_body, scale, o),
        [shape_of((28 * o, c_all), bf16)],
        [stacked, x_all, total],
        flops=flops,
        name="filter_grad",
    )
    filters_far = cross(filters, 0)
    g_own, g_a, g_b, g_ab = call(
        core_sum_body,
        [shape_of((cells, o, depth), f32)] + [shape_of((cells, o, depth), bf16)] * 3,
        [mine, other],
        name="core_sum",
    )
    g_ab = swap(g_ab, "chan", 6)
    g_b = swap(g_b, "chan", 4)
    g_a = swap(g_a, "chan", 2)
    (filters,) = call(
        pair_body,
        [shape_of(filters.shape, bf16)],
        [filters, filters_far, g_own],
        [VMEM] * 2 + [ANY],
        name="pair_sum",
    )
    filters_far = cross(filters, 1)
    (g_own,) = call(
        sum_body,
        [shape_of((cells, o, depth), f32)],
        [g_own, g_ab, g_b, g_a],
        flops=SUM_FLOPS,
        name="sum",
    )
    weight_grad, bias_grad, grad_in = call(
        last_body,
        [
            shape_of((27, o, c_all), f32),
            shape_of((1, o), f32),
            shape_of((o, n, rows, depth), bf16),
        ],
        [filters, filters_far, g_own],
        scratch=block_wide,
        name="last",
    )
    return act, grad_in, jnp.transpose(weight_grad, (1, 0, 2)), bias_grad[0]


def solution(mesh):
    placed = (
        P("chan", "slab", None, None),
        P("chan", None, None),
        P("chan"),
        P("chan", "slab", None, None),
    )

    def body(x_in, weight, bias_vec, grad_out):
        tiled = (
            weight.shape[0] % 32 == 0
            and x_in.shape[3] == LANES
            and lax.axis_size("slab") == 4
            and lax.axis_size("chan") == 8
            and x_in.shape[1] >= 2
        )
        return (on_device if tiled else plain)(x_in, weight, bias_vec, grad_out)

    return jax.shard_map(
        body,
        mesh=mesh,
        in_specs=placed,
        out_specs=(
            P("chan", "slab", None, None),
            P("chan", "slab", None, None),
            P("chan", None, None),
            P("chan"),
        ),
        check_vma=False,
    )
```

```python
import functools
import math

import jax
import jax.numpy as jnp
from jax import lax
from jax.experimental import pallas as pl
from jax.experimental.pallas import tpu as pltpu
from jax.sharding import PartitionSpec as P

LANES = 128
FORWARD_FLOPS = 9 * 10**8
SUM_FLOPS = 24 * 10**8
ASSEMBLE_FLOPS = 40 * 10**8
VMEM = pl.BlockSpec(memory_space=pltpu.VMEM)
ANY = pl.BlockSpec(memory_space=pl.ANY)
HBM = pl.BlockSpec(memory_space=pltpu.HBM)
SMEM = pl.BlockSpec(memory_space=pltpu.SMEM)


def with_halo(block, sides, width):
    for axis, dim in sides:
        count = lax.axis_size(axis)
        forward = [(i, i + 1) for i in range(count - 1)]
        forward.append((count - 1, 0))
        backward = [(target, source) for source, target in forward]
        low = lax.ppermute(
            lax.slice_in_dim(block, block.shape[dim] - width, None, axis=dim), axis, forward
        )
        high = lax.ppermute(lax.slice_in_dim(block, 0, width, axis=dim), axis, backward)
        block = jnp.concatenate([low, block, high], axis=dim)
    return block


def tap_list():
    return [(9 * i + 3 * j + l, i, j, l) for i in range(3) for j in range(3) for l in range(3)]


def plain(x_in, weight, bias_vec, grad_out):
    out_local, n_taps, in_total = weight.shape
    n_planes, n_rows, n_depth = (x_in.shape[1], x_in.shape[2], x_in.shape[3])
    rimmed = with_halo(x_in, (("slab", 1),), 1)
    padded = lax.all_gather(rimmed, "chan", axis=0, tiled=True)
    own_planes = padded[:, 1 : n_planes + 1]
    pre_act = (
        jnp.zeros((out_local, n_planes, n_rows, n_depth), jnp.float32)
        + bias_vec.astype(jnp.float32)[:, None, None, None]
    )
    for i in range(3):
        w_plane = jnp.transpose(weight[:, 9 * i : 9 * i + 9], (1, 0, 2)).reshape(
            9 * out_local, in_total
        )
        plane_part = jnp.dot(
            w_plane,
            padded[:, i : i + n_planes].reshape(in_total, -1),
            preferred_element_type=jnp.float32,
        )
        plane_part = plane_part.reshape(9, out_local, n_planes, n_rows, n_depth)
        for j in range(3):
            for l in range(3):
                pre_act = pre_act + jnp.roll(plane_part[3 * j + l], (1 - j, 1 - l), axis=(2, 3))
    sigmoid_v = jax.nn.sigmoid(pre_act)
    activation = (pre_act * sigmoid_v).astype(jnp.bfloat16)
    slope = sigmoid_v * (1.0 + pre_act * (1.0 - sigmoid_v))
    grad_pre = (grad_out.astype(jnp.float32) * slope).astype(jnp.bfloat16)
    padded_grad = with_halo(grad_pre, (("slab", 1),), 1)
    shifted = jnp.stack(
        [
            jnp.roll(padded_grad[:, 2 - i : 2 - i + n_planes], (j - 1, l - 1), axis=(2, 3))
            for k, i, j, l in tap_list()
        ],
        0,
    )
    shifted = shifted.reshape(n_taps * out_local, -1)
    grad_scale = 1.0 / math.sqrt(lax.axis_size("slab") * n_planes * n_rows * n_depth)
    filter_local = lax.dot_general(
        shifted,
        own_planes.reshape(in_total, -1),
        (((1,), (1,)), ((), ())),
        preferred_element_type=jnp.float32,
    )
    filter_part = (
        jnp.transpose(filter_local.reshape(n_taps, out_local, in_total), (1, 0, 2)) * grad_scale
    )
    bias_part = grad_scale * jnp.sum(grad_pre.astype(jnp.float32), axis=(1, 2, 3))
    bias_row = jnp.concatenate(
        [bias_part[:, None, None], jnp.zeros((out_local, 1, in_total - 1), jnp.float32)], 2
    )
    summed_filters = lax.psum(jnp.concatenate([filter_part, bias_row], 1), "slab")
    weight_grad = summed_filters[:, :n_taps]
    bias_grad = summed_filters[:, n_taps, 0]
    flat_w = jnp.transpose(weight, (1, 0, 2)).reshape(n_taps * out_local, in_total)
    product = lax.dot_general(
        flat_w, shifted, (((0,), (0,)), ((), ())), preferred_element_type=jnp.float32
    )
    grad_in = lax.psum_scatter(
        product.reshape(
            in_total // lax.axis_size("chan") * lax.axis_size("chan"), n_planes, n_rows, n_depth
        ),
        "chan",
        scatter_dimension=0,
        tiled=True,
    )
    return (activation, grad_in.astype(jnp.bfloat16), weight_grad, bias_grad)


def call(body, out_shape, operands, specs=None, scratch=(), flops=0, name=None, aliases=None):
    read = sum(math.prod(a.shape) * a.dtype.itemsize for a in operands)
    written = sum(math.prod(a.shape) * a.dtype.itemsize for a in out_shape)
    return pl.pallas_call(
        body,
        out_shape=out_shape,
        in_specs=specs or [VMEM] * len(operands),
        out_specs=[VMEM] * len(out_shape),
        scratch_shapes=list(scratch),
        input_output_aliases=aliases or {},
        compiler_params=pltpu.CompilerParams(vmem_limit_bytes=24 * 2**20),
        cost_estimate=pl.CostEstimate(
            flops=flops, bytes_accessed=read + written, transcendentals=0
        ),
        name=name,
    )(*operands)


def shape_of(shape, dtype):
    return jax.ShapeDtypeStruct(shape, dtype)


def turned(value, wide_ref):
    o = value.shape[0]
    cells = wide_ref.shape[0] // o
    wide_ref[...] = value.astype(jnp.float32).reshape(wide_ref.shape)
    return [
        wide_ref[pl.ds(k, o, stride=cells), :].astype(value.dtype) for k in range(cells)
    ]


def prepare_body(
    n,
    rows,
    me_ref,
    x_hbm,
    go_hbm,
    w_hbm,
    bias_hbm,
    x_ref,
    go_ref,
    go_low_ref,
    go_high_ref,
    flat_ref,
    back_ref,
    bias_ref,
    go_in,
    w_in,
    bias_in,
    back_in,
    wide_ref,
    sems,
):
    copies = [
        pltpu.make_async_copy(source, target, sems.at[at])
        for at, (source, target) in enumerate(
            [(go_hbm, go_in), (w_hbm, w_in), (bias_hbm, bias_in), (x_hbm, x_ref)]
        )
    ]
    for copy in copies:
        copy.start()
    copies[0].wait()
    for k, value in enumerate(turned(go_in[...], wide_ref)):
        go_ref[k] = value
        if k < rows:
            go_low_ref[k] = value
        if k >= (n - 1) * rows:
            go_high_ref[k - (n - 1) * rows] = value
    copies[1].wait()
    copies[2].wait()
    copies[3].wait()
    flat = w_in[...].reshape(flat_ref.shape)
    flat_ref[...] = flat
    o = bias_ref.shape[0]
    back_in[...] = jnp.transpose(flat)
    for b in range(8):
        place = pl.ds(pl.multiple_of(owner(me_ref, b) * o, o), o)
        back_ref[b * o : (b + 1) * o] = back_in[place]
    row = jnp.broadcast_to(bias_in[...].astype(jnp.float32), (o, o))
    same = lax.broadcasted_iota(jnp.int32, (o, o), 0) == lax.broadcasted_iota(jnp.int32, (o, o), 1)
    column = jnp.sum(jnp.where(same, row, 0.0), axis=1, keepdims=True)
    bias_ref[...] = jnp.broadcast_to(column, bias_ref.shape)


def place_block(me_ref, b, block_ref, x_ref, wide_ref):
    o = block_ref.shape[0]
    place = pl.ds(pl.multiple_of(owner(me_ref, b) * o, o), o)
    for k, value in enumerate(turned(block_ref[...], wide_ref)):
        x_ref[place, k * LANES : (k + 1) * LANES] = value


def assemble_body(places, me_ref, *refs):
    blocks, (x_ref, wide_ref) = refs[: len(places)], refs[-2:]
    for b, block in zip(places, blocks):
        place_block(me_ref, b, block, x_ref, wide_ref)


def owner(me_ref, b):
    return jnp.bitwise_xor(me_ref[0], 2 * (b % 4) + b // 4)


def forward_body(n, rows, o, places, me_ref, w_ref, *refs):
    blocks = refs[: len(places)]
    own_ref, low_ref, high_ref, x_ref, acc, wide_ref = refs[len(places) + 1 :]
    for b, block in zip(places, blocks):
        place_block(me_ref, b, block, x_ref, wide_ref)
    w = w_ref[...]
    seen = set()
    for p in range(n):
        for t in range(0, rows, 2):
            at = (p * rows + t) * LANES
            part = jnp.dot(
                w, x_ref[:, at : at + 2 * LANES], preferred_element_type=jnp.float32
            )
            for k, i, j, l in tap_list():
                for h in range(2):
                    slot = (l, p + 2 - i, (t + h + 1 - j) % rows)
                    value = part[k * o : (k + 1) * o, h * LANES : (h + 1) * LANES]
                    if slot in seen:
                        acc[slot] += value
                    else:
                        acc[slot] = value
                        seen.add(slot)
    for q in range(n + 2):
        for y in range(rows):
            total = (
                pltpu.roll(acc[0, q, y], 1, 1)
                + acc[1, q, y]
                + pltpu.roll(acc[2, q, y], LANES - 1, 1)
            )
            if q == 0:
                low_ref[y] = total.astype(low_ref.dtype)
            elif q == n + 1:
                high_ref[y] = total.astype(high_ref.dtype)
            else:
                own_ref[(q - 1) * rows + y] = total
            if q == 1:
                low_ref[rows + y] = total.astype(low_ref.dtype)
            if q == n:
                high_ref[rows + y] = total.astype(high_ref.dtype)


def gradient_body(
    n,
    rows,
    o,
    scale,
    own_ref,
    low_ref,
    high_ref,
    below_ref,
    above_ref,
    bias_ref,
    go_ref,
    go_below_ref,
    go_above_ref,
    w_ref,
    act_ref,
    total_ref,
    s_ref,
    other_ref,
    mine_ref,
    wide_ref,
):
    f32, bf16 = jnp.float32, jnp.bfloat16
    total = jnp.zeros((o, LANES), f32)

    def shift_row(y, total):
        for q in range(n + 2):
            if q == 0:
                pre = below_ref[rows + y].astype(f32) + low_ref[y].astype(f32)
                go = go_below_ref[y]
            elif q == n + 1:
                pre = above_ref[rows + y].astype(f32) + high_ref[y].astype(f32)
                go = go_above_ref[y]
            else:
                pre = own_ref[(q - 1) * rows + y]
                go = go_ref[(q - 1) * rows + y]
                if q == 1:
                    pre = pre + below_ref[y].astype(f32)
                if q == n:
                    pre = pre + above_ref[y].astype(f32)
            pre = pre + bias_ref[...]
            s = jax.nn.sigmoid(pre)
            slope = s * (1.0 + pre * (1.0 - s))
            value = (go.astype(f32) * slope).astype(bf16)
            wide = value.astype(f32)
            if 1 <= q <= n:
                wide_ref[pl.ds((q - 1) * rows + y, o, stride=n * rows), :] = pre * s
                total = total + wide
            shifts = [
                pltpu.roll(wide, LANES - 1, 1).astype(bf16),
                value,
                pltpu.roll(wide, 1, 1).astype(bf16),
            ]
            for k, i, j, l in tap_list():
                p = q - 2 + i
                if 0 <= p < n:
                    at = (p * rows + (y + j - 1) % rows) * LANES
                    s_ref[k * o : (k + 1) * o, at : at + LANES] = shifts[l]
        return total

    def multiply(t):
        at = t * LANES
        part = jnp.dot(
            w_ref[...], s_ref[:, at : at + 2 * LANES], preferred_element_type=f32
        ).astype(bf16)
        for h in range(2):
            for b in range(8):
                cut = part[b * o : (b + 1) * o, h * LANES : (h + 1) * LANES]
                (mine_ref if b < 4 else other_ref)[b % 4, t + h] = cut

    total = shift_row(rows - 1, total)
    total = shift_row(0, total)
    for t in range(0, rows, 2):
        for y in (t + 1, t + 2):
            if y < rows - 1:
                total = shift_row(y, total)
        for p in range(n):
            multiply(p * rows + t)
    act_ref[...] = wide_ref[...].reshape(act_ref.shape).astype(bf16)
    total_ref[...] = jnp.broadcast_to(
        jnp.sum(total, axis=1, keepdims=True) * scale, total_ref.shape
    )


def filter_grad_body(scale, taps, o, s_ref, x_ref, total_ref, first_ref, second_ref):
    full = lax.dot_general(
        s_ref[...], x_ref[...], (((1,), (1,)), ((), ())), preferred_element_type=jnp.float32
    )
    full = (full * scale).astype(first_ref.dtype)
    first_ref[...] = full[: taps * o]
    second_ref[: (27 - taps) * o] = full[taps * o :]
    row = jnp.concatenate([total_ref[...]] * (second_ref.shape[1] // LANES), axis=1)
    second_ref[(27 - taps) * o :] = row.astype(second_ref.dtype)


def pair_body(a_ref, b_ref, _, out_ref):
    f32 = jnp.float32
    out_ref[...] = (a_ref[...].astype(f32) + b_ref[...].astype(f32)).astype(out_ref.dtype)


def core_sum_body(mine_ref, other_ref, *outs):
    for r, out_ref in enumerate(outs):
        total = mine_ref[r].astype(jnp.float32) + other_ref[r].astype(jnp.float32)
        out_ref[...] = total.astype(out_ref.dtype)


def sum_body(a_ref, b_ref, c_ref, d_ref, out_ref, token_ref, wide_ref):
    f32 = jnp.float32
    cells, o, _ = a_ref.shape
    for k in range(cells):
        total = a_ref[k] + b_ref[k].astype(f32) + c_ref[k].astype(f32) + d_ref[k].astype(f32)
        wide_ref[pl.ds(k, o, stride=cells), :] = total
    out_ref[...] = wide_ref[...].reshape(out_ref.shape).astype(out_ref.dtype)
    token_ref[...] = jnp.zeros_like(token_ref)


def last_body(taps, a_ref, b_ref, c_ref, d_ref, _, out_ref, bias_ref):
    o = out_ref.shape[1]
    f32 = jnp.float32
    for k in range(27):
        left, right, at = (a_ref, b_ref, k) if k < taps else (c_ref, d_ref, k - taps)
        cut = slice(at * o, (at + 1) * o)
        out_ref[k] = left[cut].astype(f32) + right[cut].astype(f32)
    cut = slice((27 - taps) * o, (28 - taps) * o)
    column = (c_ref[cut].astype(f32) + d_ref[cut].astype(f32))[:, :o]
    same = lax.broadcasted_iota(jnp.int32, (o, o), 0) == lax.broadcasted_iota(jnp.int32, (o, o), 1)
    bias_ref[...] = jnp.sum(jnp.where(same, column, 0.0), axis=0, keepdims=True)


def in_hbm(value):
    return pltpu.with_memory_space_constraint(value, pltpu.HBM)


def rotate(value, axis, step):
    count = lax.axis_size(axis)
    return lax.ppermute(value, axis, [(i, (i + step) % count) for i in range(count)])


def swap(value, axis, bit):
    return lax.ppermute(value, axis, [(i, i ^ bit) for i in range(lax.axis_size(axis))])


def cross(value, phase):
    slabs, chans = lax.axis_size("slab"), lax.axis_size("chan")
    pairs = [
        (s * chans + c, (s ^ (1 + (c + phase) % 2)) * chans + c)
        for s in range(slabs)
        for c in range(chans)
    ]
    return lax.ppermute(value, ("slab", "chan"), pairs)


def on_device(x_in, weight, bias_vec, grad_out):
    o, _, c_all = weight.shape
    _, n, rows, depth = x_in.shape
    f32, bf16 = jnp.float32, jnp.bfloat16
    cells = n * rows
    flops = 2 * 27 * o * c_all * cells * depth
    scale = 1.0 / math.sqrt(lax.axis_size("slab") * cells * depth)
    me = lax.axis_index("chan").astype(jnp.int32).reshape(1)

    block_wide = [pltpu.VMEM((o * cells, depth), f32)]

    x_b = swap(x_in, "chan", 4)
    x_a = swap(x_in, "chan", 2)
    x_side = swap(x_in, "chan", 1)
    x_own, go, go_low, go_high, w_flat, w_back, bias = call(
        functools.partial(prepare_body, n, rows),
        [
            shape_of((o, n, rows, depth), bf16),
            shape_of((cells, o, depth), bf16),
            shape_of((rows, o, depth), bf16),
            shape_of((rows, o, depth), bf16),
            shape_of((27 * o, c_all), bf16),
            shape_of((c_all, 27 * o), bf16),
            shape_of((o, LANES), f32),
        ],
        [me] + [in_hbm(a) for a in (x_in, grad_out, jnp.transpose(weight, (1, 0, 2)), bias_vec[None, :])],
        [SMEM] + [HBM] * 4,
        [
            pltpu.VMEM((o, n, rows, depth), bf16),
            pltpu.VMEM((27, o, c_all), bf16),
            pltpu.VMEM((1, o), bf16),
            pltpu.VMEM((c_all, 27 * o), bf16),
            *block_wide,
            pltpu.SemaphoreType.DMA((4,)),
        ],
        name="prepare",
    )
    go_above = rotate(go_low, "slab", -1)
    go_below = rotate(go_high, "slab", 1)
    x_b, w_flat = lax.optimization_barrier((x_b, w_flat))
    x_ab = swap(x_b, "chan", 2)
    late_b, go_above, go_below = lax.optimization_barrier((x_b, go_above, go_below))
    x_a_side = swap(x_a, "chan", 1)
    x_b_side = swap(late_b, "chan", 1)
    early, late = (0, 1, 2, 3, 4, 5, 6), (7,)
    (x_all,) = call(
        functools.partial(assemble_body, early),
        [shape_of((c_all, cells * depth), bf16)],
        [me, x_own, x_a, x_b, x_ab, x_side, x_a_side, x_b_side],
        [SMEM] + [VMEM] * 7,
        block_wide,
        flops=ASSEMBLE_FLOPS,
        name="assemble",
    )
    x_ab_side = swap(x_ab, "chan", 1)
    own, low, high, x_all = call(
        functools.partial(forward_body, n, rows, o, late),
        [
            shape_of((cells, o, depth), f32),
            shape_of((2 * rows, o, depth), bf16),
            shape_of((2 * rows, o, depth), bf16),
            shape_of((c_all, cells * depth), bf16),
        ],
        [me, w_flat, x_ab_side, x_all],
        [SMEM] + [VMEM] * 3,
        [pltpu.VMEM((3, n + 2, rows, o, depth), f32), *block_wide],
        flops=FORWARD_FLOPS,
        name="forward",
        aliases={3: 3},
    )
    above = rotate(low, "slab", -1)
    below = rotate(high, "slab", 1)
    act, total, stacked, other, mine = call(
        functools.partial(gradient_body, n, rows, o, scale),
        [
            shape_of((o, n, rows, depth), bf16),
            shape_of((o, LANES), f32),
            shape_of((27 * o, cells * depth), bf16),
            shape_of((4, cells, o, depth), bf16),
            shape_of((4, cells, o, depth), bf16),
        ],
        [own, low, high, below, above, bias, go, go_below, go_above, w_back],
        [VMEM] * 10,
        block_wide,
        flops=flops,
        name="gradient",
    )
    other = swap(other, "chan", 1)
    taps = 14
    first, second = call(
        functools.partial(filter_grad_body, scale, taps, o),
        [shape_of((taps * o, c_all), bf16), shape_of(((28 - taps) * o, c_all), bf16)],
        [stacked, x_all, total],
        flops=flops,
        name="filter_grad",
    )
    first_far = cross(first, 0)
    second_far = cross(second, 0)
    g_own, g_a, g_b, g_ab = call(
        core_sum_body,
        [shape_of((cells, o, depth), f32)] + [shape_of((cells, o, depth), bf16)] * 3,
        [mine, other],
        name="core_sum",
    )
    g_ab = swap(g_ab, "chan", 6)
    g_b = swap(g_b, "chan", 4)
    g_a = swap(g_a, "chan", 2)
    first, second = (
        call(
            pair_body,
            [shape_of(a.shape, bf16)],
            [a, b, g_own],
            [VMEM] * 2 + [ANY],
            name="pair_sum",
        )[0]
        for a, b in ((first, first_far), (second, second_far))
    )
    first_far = cross(first, 1)
    second_far = cross(second, 1)
    grad_in, token = call(
        sum_body,
        [shape_of((o, n, rows, depth), bf16), shape_of((8, LANES), f32)],
        [g_own, g_ab, g_b, g_a],
        scratch=block_wide,
        flops=SUM_FLOPS,
        name="sum",
    )
    weight_grad, bias_grad = call(
        functools.partial(last_body, taps),
        [shape_of((27, o, c_all), f32), shape_of((1, o), f32)],
        [first, first_far, second, second_far, token],
        [VMEM] * 4 + [ANY],
        name="last",
    )
    return act, grad_in, jnp.transpose(weight_grad, (1, 0, 2)), bias_grad[0]


def solution(mesh):
    placed = (
        P("chan", "slab", None, None),
        P("chan", None, None),
        P("chan"),
        P("chan", "slab", None, None),
    )

    def body(x_in, weight, bias_vec, grad_out):
        tiled = (
            weight.shape[0] % 32 == 0
            and x_in.shape[3] == LANES
            and lax.axis_size("slab") == 4
            and lax.axis_size("chan") == 8
            and x_in.shape[1] >= 2
        )
        return (on_device if tiled else plain)(x_in, weight, bias_vec, grad_out)

    return jax.shard_map(
        body,
        mesh=mesh,
        in_specs=placed,
        out_specs=(
            P("chan", "slab", None, None),
            P("chan", "slab", None, None),
            P("chan", None, None),
            P("chan"),
        ),
        check_vma=False,
    )
```

```python
import functools
import math

import jax
import jax.numpy as jnp
from jax import lax
from jax.experimental import pallas as pl
from jax.experimental.pallas import tpu as pltpu
from jax.sharding import PartitionSpec as P

LANES = 128
FORWARD_FLOPS = 9 * 10**8
SUM_FLOPS = 24 * 10**8
ASSEMBLE_FLOPS = 40 * 10**8
VMEM = pl.BlockSpec(memory_space=pltpu.VMEM)
ANY = pl.BlockSpec(memory_space=pl.ANY)
HBM = pl.BlockSpec(memory_space=pltpu.HBM)
SMEM = pl.BlockSpec(memory_space=pltpu.SMEM)


def with_halo(block, sides, width):
    for axis, dim in sides:
        count = lax.axis_size(axis)
        forward = [(i, i + 1) for i in range(count - 1)]
        forward.append((count - 1, 0))
        backward = [(target, source) for source, target in forward]
        low = lax.ppermute(
            lax.slice_in_dim(block, block.shape[dim] - width, None, axis=dim), axis, forward
        )
        high = lax.ppermute(lax.slice_in_dim(block, 0, width, axis=dim), axis, backward)
        block = jnp.concatenate([low, block, high], axis=dim)
    return block


def tap_list():
    return [(9 * i + 3 * j + l, i, j, l) for i in range(3) for j in range(3) for l in range(3)]


def plain(x_in, weight, bias_vec, grad_out):
    out_local, n_taps, in_total = weight.shape
    n_planes, n_rows, n_depth = (x_in.shape[1], x_in.shape[2], x_in.shape[3])
    rimmed = with_halo(x_in, (("slab", 1),), 1)
    padded = lax.all_gather(rimmed, "chan", axis=0, tiled=True)
    own_planes = padded[:, 1 : n_planes + 1]
    pre_act = (
        jnp.zeros((out_local, n_planes, n_rows, n_depth), jnp.float32)
        + bias_vec.astype(jnp.float32)[:, None, None, None]
    )
    for i in range(3):
        w_plane = jnp.transpose(weight[:, 9 * i : 9 * i + 9], (1, 0, 2)).reshape(
            9 * out_local, in_total
        )
        plane_part = jnp.dot(
            w_plane,
            padded[:, i : i + n_planes].reshape(in_total, -1),
            preferred_element_type=jnp.float32,
        )
        plane_part = plane_part.reshape(9, out_local, n_planes, n_rows, n_depth)
        for j in range(3):
            for l in range(3):
                pre_act = pre_act + jnp.roll(plane_part[3 * j + l], (1 - j, 1 - l), axis=(2, 3))
    sigmoid_v = jax.nn.sigmoid(pre_act)
    activation = (pre_act * sigmoid_v).astype(jnp.bfloat16)
    slope = sigmoid_v * (1.0 + pre_act * (1.0 - sigmoid_v))
    grad_pre = (grad_out.astype(jnp.float32) * slope).astype(jnp.bfloat16)
    padded_grad = with_halo(grad_pre, (("slab", 1),), 1)
    shifted = jnp.stack(
        [
            jnp.roll(padded_grad[:, 2 - i : 2 - i + n_planes], (j - 1, l - 1), axis=(2, 3))
            for k, i, j, l in tap_list()
        ],
        0,
    )
    shifted = shifted.reshape(n_taps * out_local, -1)
    grad_scale = 1.0 / math.sqrt(lax.axis_size("slab") * n_planes * n_rows * n_depth)
    filter_local = lax.dot_general(
        shifted,
        own_planes.reshape(in_total, -1),
        (((1,), (1,)), ((), ())),
        preferred_element_type=jnp.float32,
    )
    filter_part = (
        jnp.transpose(filter_local.reshape(n_taps, out_local, in_total), (1, 0, 2)) * grad_scale
    )
    bias_part = grad_scale * jnp.sum(grad_pre.astype(jnp.float32), axis=(1, 2, 3))
    bias_row = jnp.concatenate(
        [bias_part[:, None, None], jnp.zeros((out_local, 1, in_total - 1), jnp.float32)], 2
    )
    summed_filters = lax.psum(jnp.concatenate([filter_part, bias_row], 1), "slab")
    weight_grad = summed_filters[:, :n_taps]
    bias_grad = summed_filters[:, n_taps, 0]
    flat_w = jnp.transpose(weight, (1, 0, 2)).reshape(n_taps * out_local, in_total)
    product = lax.dot_general(
        flat_w, shifted, (((0,), (0,)), ((), ())), preferred_element_type=jnp.float32
    )
    grad_in = lax.psum_scatter(
        product.reshape(
            in_total // lax.axis_size("chan") * lax.axis_size("chan"), n_planes, n_rows, n_depth
        ),
        "chan",
        scatter_dimension=0,
        tiled=True,
    )
    return (activation, grad_in.astype(jnp.bfloat16), weight_grad, bias_grad)


def call(body, out_shape, operands, specs=None, scratch=(), flops=0, name=None, aliases=None):
    read = sum(math.prod(a.shape) * a.dtype.itemsize for a in operands)
    written = sum(math.prod(a.shape) * a.dtype.itemsize for a in out_shape)
    return pl.pallas_call(
        body,
        out_shape=out_shape,
        in_specs=specs or [VMEM] * len(operands),
        out_specs=[VMEM] * len(out_shape),
        scratch_shapes=list(scratch),
        input_output_aliases=aliases or {},
        compiler_params=pltpu.CompilerParams(vmem_limit_bytes=24 * 2**20),
        cost_estimate=pl.CostEstimate(
            flops=flops, bytes_accessed=read + written, transcendentals=0
        ),
        name=name,
    )(*operands)


def shape_of(shape, dtype):
    return jax.ShapeDtypeStruct(shape, dtype)


def turned(value, wide_ref):
    o = value.shape[0]
    cells = wide_ref.shape[0] // o
    wide_ref[...] = value.astype(jnp.float32).reshape(wide_ref.shape)
    return [
        wide_ref[pl.ds(k, o, stride=cells), :].astype(value.dtype) for k in range(cells)
    ]


def prepare_body(
    n,
    rows,
    me_ref,
    x_hbm,
    go_hbm,
    w_hbm,
    bias_hbm,
    x_ref,
    go_ref,
    go_low_ref,
    go_high_ref,
    flat_ref,
    back_ref,
    bias_ref,
    go_in,
    w_in,
    bias_in,
    back_in,
    wide_ref,
    sems,
):
    copies = [
        pltpu.make_async_copy(source, target, sems.at[at])
        for at, (source, target) in enumerate(
            [(go_hbm, go_in), (w_hbm, w_in), (bias_hbm, bias_in), (x_hbm, x_ref)]
        )
    ]
    for copy in copies:
        copy.start()
    copies[0].wait()
    for k, value in enumerate(turned(go_in[...], wide_ref)):
        go_ref[k] = value
        if k < rows:
            go_low_ref[k] = value
        if k >= (n - 1) * rows:
            go_high_ref[k - (n - 1) * rows] = value
    copies[1].wait()
    copies[2].wait()
    copies[3].wait()
    flat = w_in[...].reshape(flat_ref.shape)
    flat_ref[...] = flat
    o = bias_ref.shape[0]
    back_in[...] = jnp.transpose(flat)
    for b in range(8):
        place = pl.ds(pl.multiple_of(owner(me_ref, b) * o, o), o)
        back_ref[b * o : (b + 1) * o] = back_in[place]
    row = jnp.broadcast_to(bias_in[...].astype(jnp.float32), (o, o))
    same = lax.broadcasted_iota(jnp.int32, (o, o), 0) == lax.broadcasted_iota(jnp.int32, (o, o), 1)
    column = jnp.sum(jnp.where(same, row, 0.0), axis=1, keepdims=True)
    bias_ref[...] = jnp.broadcast_to(column, bias_ref.shape)


def place_block(me_ref, b, block_ref, x_ref, wide_ref):
    o = block_ref.shape[0]
    place = pl.ds(pl.multiple_of(owner(me_ref, b) * o, o), o)
    for k, value in enumerate(turned(block_ref[...], wide_ref)):
        x_ref[place, k * LANES : (k + 1) * LANES] = value


def assemble_body(places, me_ref, *refs):
    blocks, (x_ref, wide_ref) = refs[: len(places)], refs[-2:]
    for b, block in zip(places, blocks):
        place_block(me_ref, b, block, x_ref, wide_ref)


def owner(me_ref, b):
    return jnp.bitwise_xor(me_ref[0], 2 * (b % 4) + b // 4)


def forward_body(n, rows, o, places, me_ref, w_ref, *refs):
    blocks = refs[: len(places)]
    own_ref, low_ref, high_ref, x_ref, acc, wide_ref = refs[len(places) + 1 :]
    for b, block in zip(places, blocks):
        place_block(me_ref, b, block, x_ref, wide_ref)
    w = w_ref[...]
    seen = set()
    for p in range(n):
        for t in range(0, rows, 2):
            at = (p * rows + t) * LANES
            part = jnp.dot(
                w, x_ref[:, at : at + 2 * LANES], preferred_element_type=jnp.float32
            )
            for k, i, j, l in tap_list():
                for h in range(2):
                    slot = (l, p + 2 - i, (t + h + 1 - j) % rows)
                    value = part[k * o : (k + 1) * o, h * LANES : (h + 1) * LANES]
                    if slot in seen:
                        acc[slot] += value
                    else:
                        acc[slot] = value
                        seen.add(slot)
    for q in range(n + 2):
        for y in range(rows):
            total = (
                pltpu.roll(acc[0, q, y], 1, 1)
                + acc[1, q, y]
                + pltpu.roll(acc[2, q, y], LANES - 1, 1)
            )
            if q == 0:
                low_ref[y] = total.astype(low_ref.dtype)
            elif q == n + 1:
                high_ref[y] = total.astype(high_ref.dtype)
            else:
                own_ref[(q - 1) * rows + y] = total
            if q == 1:
                low_ref[rows + y] = total.astype(low_ref.dtype)
            if q == n:
                high_ref[rows + y] = total.astype(high_ref.dtype)


def gradient_body(
    n,
    rows,
    o,
    scale,
    own_ref,
    low_ref,
    high_ref,
    below_ref,
    above_ref,
    bias_ref,
    go_ref,
    go_below_ref,
    go_above_ref,
    w_ref,
    act_ref,
    total_ref,
    s_ref,
    other_ref,
    mine_ref,
    wide_ref,
):
    f32, bf16 = jnp.float32, jnp.bfloat16
    total = jnp.zeros((o, LANES), f32)

    def shift_row(y, total):
        for q in range(n + 2):
            if q == 0:
                pre = below_ref[rows + y].astype(f32) + low_ref[y].astype(f32)
                go = go_below_ref[y]
            elif q == n + 1:
                pre = above_ref[rows + y].astype(f32) + high_ref[y].astype(f32)
                go = go_above_ref[y]
            else:
                pre = own_ref[(q - 1) * rows + y]
                go = go_ref[(q - 1) * rows + y]
                if q == 1:
                    pre = pre + below_ref[y].astype(f32)
                if q == n:
                    pre = pre + above_ref[y].astype(f32)
            pre = pre + bias_ref[...]
            s = jax.nn.sigmoid(pre)
            slope = s * (1.0 + pre * (1.0 - s))
            value = (go.astype(f32) * slope).astype(bf16)
            wide = value.astype(f32)
            if 1 <= q <= n:
                wide_ref[pl.ds((q - 1) * rows + y, o, stride=n * rows), :] = pre * s
                total = total + wide
            shifts = [
                pltpu.roll(wide, LANES - 1, 1).astype(bf16),
                value,
                pltpu.roll(wide, 1, 1).astype(bf16),
            ]
            for k, i, j, l in tap_list():
                p = q - 2 + i
                if 0 <= p < n:
                    at = (p * rows + (y + j - 1) % rows) * LANES
                    s_ref[k * o : (k + 1) * o, at : at + LANES] = shifts[l]
        return total

    def multiply(t):
        at = t * LANES
        part = jnp.dot(
            w_ref[...], s_ref[:, at : at + 2 * LANES], preferred_element_type=f32
        ).astype(bf16)
        for h in range(2):
            for b in range(8):
                cut = part[b * o : (b + 1) * o, h * LANES : (h + 1) * LANES]
                (mine_ref if b < 4 else other_ref)[b % 4, t + h] = cut

    for y in range(rows):
        total = shift_row(y, total)
    for t in range(0, n * rows, 2):
        multiply(t)
    act_ref[...] = wide_ref[...].reshape(act_ref.shape).astype(bf16)
    total_ref[...] = jnp.broadcast_to(
        jnp.sum(total, axis=1, keepdims=True) * scale, total_ref.shape
    )


def filter_grad_body(scale, start, o, s_ref, x_ref, total_ref, _, out_ref):
    taps = min(27 - start, out_ref.shape[0] // o)
    part = lax.dot_general(
        s_ref[start * o : (start + taps) * o],
        x_ref[...],
        (((1,), (1,)), ((), ())),
        preferred_element_type=jnp.float32,
    )
    out_ref[: taps * o] = (part * scale).astype(out_ref.dtype)
    if out_ref.shape[0] > taps * o:
        row = jnp.concatenate([total_ref[...]] * (out_ref.shape[1] // LANES), axis=1)
        out_ref[taps * o :] = row.astype(out_ref.dtype)


def pair_body(a_ref, b_ref, _, out_ref):
    f32 = jnp.float32
    out_ref[...] = (a_ref[...].astype(f32) + b_ref[...].astype(f32)).astype(out_ref.dtype)


def core_sum_body(mine_ref, other_ref, *outs):
    for r, out_ref in enumerate(outs):
        total = mine_ref[r].astype(jnp.float32) + other_ref[r].astype(jnp.float32)
        out_ref[...] = total.astype(out_ref.dtype)


def sum_body(a_ref, b_ref, c_ref, d_ref, out_ref):
    f32 = jnp.float32
    total = b_ref[...].astype(f32) + c_ref[...].astype(f32) + d_ref[...].astype(f32)
    out_ref[...] = a_ref[...] + total


def last_body(
    taps, a_ref, b_ref, c_ref, d_ref, g_ref, out_ref, bias_ref, grad_ref, wide_ref
):
    o = out_ref.shape[1]
    f32 = jnp.float32
    cells = g_ref.shape[0]
    for k in range(cells):
        wide_ref[pl.ds(k, o, stride=cells), :] = g_ref[k]
    grad_ref[...] = wide_ref[...].reshape(grad_ref.shape).astype(grad_ref.dtype)
    for k in range(27):
        left, right, at = (a_ref, b_ref, k) if k < taps else (c_ref, d_ref, k - taps)
        cut = slice(at * o, (at + 1) * o)
        out_ref[k] = left[cut].astype(f32) + right[cut].astype(f32)
    cut = slice((27 - taps) * o, (28 - taps) * o)
    column = (c_ref[cut].astype(f32) + d_ref[cut].astype(f32))[:, :o]
    same = lax.broadcasted_iota(jnp.int32, (o, o), 0) == lax.broadcasted_iota(jnp.int32, (o, o), 1)
    bias_ref[...] = jnp.sum(jnp.where(same, column, 0.0), axis=0, keepdims=True)


def in_hbm(value):
    return pltpu.with_memory_space_constraint(value, pltpu.HBM)


def rotate(value, axis, step):
    count = lax.axis_size(axis)
    return lax.ppermute(value, axis, [(i, (i + step) % count) for i in range(count)])


def swap(value, axis, bit):
    return lax.ppermute(value, axis, [(i, i ^ bit) for i in range(lax.axis_size(axis))])


def cross(value, phase):
    slabs, chans = lax.axis_size("slab"), lax.axis_size("chan")
    pairs = [
        (s * chans + c, (s ^ (1 + (c + phase) % 2)) * chans + c)
        for s in range(slabs)
        for c in range(chans)
    ]
    return lax.ppermute(value, ("slab", "chan"), pairs)


def on_device(x_in, weight, bias_vec, grad_out):
    o, _, c_all = weight.shape
    _, n, rows, depth = x_in.shape
    f32, bf16 = jnp.float32, jnp.bfloat16
    cells = n * rows
    flops = 2 * 27 * o * c_all * cells * depth
    scale = 1.0 / math.sqrt(lax.axis_size("slab") * cells * depth)
    me = lax.axis_index("chan").astype(jnp.int32).reshape(1)

    block_wide = [pltpu.VMEM((o * cells, depth), f32)]

    x_b = swap(x_in, "chan", 4)
    x_a = swap(x_in, "chan", 2)
    x_side = swap(x_in, "chan", 1)
    x_own, go, go_low, go_high, w_flat, w_back, bias = call(
        functools.partial(prepare_body, n, rows),
        [
            shape_of((o, n, rows, depth), bf16),
            shape_of((cells, o, depth), bf16),
            shape_of((rows, o, depth), bf16),
            shape_of((rows, o, depth), bf16),
            shape_of((27 * o, c_all), bf16),
            shape_of((c_all, 27 * o), bf16),
            shape_of((o, LANES), f32),
        ],
        [me] + [in_hbm(a) for a in (x_in, grad_out, jnp.transpose(weight, (1, 0, 2)), bias_vec[None, :])],
        [SMEM] + [HBM] * 4,
        [
            pltpu.VMEM((o, n, rows, depth), bf16),
            pltpu.VMEM((27, o, c_all), bf16),
            pltpu.VMEM((1, o), bf16),
            pltpu.VMEM((c_all, 27 * o), bf16),
            *block_wide,
            pltpu.SemaphoreType.DMA((4,)),
        ],
        name="prepare",
    )
    go_above = rotate(go_low, "slab", -1)
    go_below = rotate(go_high, "slab", 1)
    x_b, w_flat = lax.optimization_barrier((x_b, w_flat))
    x_ab = swap(x_b, "chan", 2)
    late_b, go_above, go_below = lax.optimization_barrier((x_b, go_above, go_below))
    x_a_side = swap(x_a, "chan", 1)
    x_b_side = swap(late_b, "chan", 1)
    early, late = (0, 1, 2, 3, 4, 5, 6), (7,)
    (x_all,) = call(
        functools.partial(assemble_body, early),
        [shape_of((c_all, cells * depth), bf16)],
        [me, x_own, x_a, x_b, x_ab, x_side, x_a_side, x_b_side],
        [SMEM] + [VMEM] * 7,
        block_wide,
        flops=ASSEMBLE_FLOPS,
        name="assemble",
    )
    x_ab_side = swap(x_ab, "chan", 1)
    own, low, high, x_all = call(
        functools.partial(forward_body, n, rows, o, late),
        [
            shape_of((cells, o, depth), f32),
            shape_of((2 * rows, o, depth), bf16),
            shape_of((2 * rows, o, depth), bf16),
            shape_of((c_all, cells * depth), bf16),
        ],
        [me, w_flat, x_ab_side, x_all],
        [SMEM] + [VMEM] * 3,
        [pltpu.VMEM((3, n + 2, rows, o, depth), f32), *block_wide],
        flops=FORWARD_FLOPS,
        name="forward",
        aliases={3: 3},
    )
    above = rotate(low, "slab", -1)
    below = rotate(high, "slab", 1)
    act, total, stacked, other, mine = call(
        functools.partial(gradient_body, n, rows, o, scale),
        [
            shape_of((o, n, rows, depth), bf16),
            shape_of((o, LANES), f32),
            shape_of((27 * o, cells * depth), bf16),
            shape_of((4, cells, o, depth), bf16),
            shape_of((4, cells, o, depth), bf16),
        ],
        [own, low, high, below, above, bias, go, go_below, go_above, w_back],
        [VMEM] * 10,
        block_wide,
        flops=flops,
        name="gradient",
    )
    other = swap(other, "chan", 1)
    taps = 14
    def filter_grad(start, taps, after, name):
        return call(
            functools.partial(filter_grad_body, scale, start, o),
            [shape_of((taps * o, c_all), bf16)],
            [stacked, x_all, total, after],
            [VMEM] * 3 + [ANY],
            flops=flops // 2,
            name=name,
        )[0]

    first = filter_grad(0, taps, total, "filter_first")
    first_far = cross(first, 0)
    g_own, g_a, g_b, g_ab = call(
        core_sum_body,
        [shape_of((cells, o, depth), f32)] + [shape_of((cells, o, depth), bf16)] * 3,
        [mine, other],
        name="core_sum",
    )
    second = filter_grad(taps, 28 - taps, g_own, "filter_second")
    second_far = cross(second, 0)
    g_ab = swap(g_ab, "chan", 6)
    g_b = swap(g_b, "chan", 4)
    g_a = swap(g_a, "chan", 2)
    first, second = (
        call(
            pair_body,
            [shape_of(a.shape, bf16)],
            [a, b, g_own],
            [VMEM] * 2 + [ANY],
            name="pair_sum",
        )[0]
        for a, b in ((first, first_far), (second, second_far))
    )
    first_far = cross(first, 1)
    second_far = cross(second, 1)
    (g_own,) = call(
        sum_body,
        [shape_of((cells, o, depth), f32)],
        [g_own, g_ab, g_b, g_a],
        flops=SUM_FLOPS,
        name="sum",
    )
    weight_grad, bias_grad, grad_in = call(
        functools.partial(last_body, taps),
        [
            shape_of((27, o, c_all), f32),
            shape_of((1, o), f32),
            shape_of((o, n, rows, depth), bf16),
        ],
        [first, first_far, second, second_far, g_own],
        scratch=block_wide,
        name="last",
    )
    return act, grad_in, jnp.transpose(weight_grad, (1, 0, 2)), bias_grad[0]


def solution(mesh):
    placed = (
        P("chan", "slab", None, None),
        P("chan", None, None),
        P("chan"),
        P("chan", "slab", None, None),
    )

    def body(x_in, weight, bias_vec, grad_out):
        tiled = (
            weight.shape[0] % 32 == 0
            and x_in.shape[3] == LANES
            and lax.axis_size("slab") == 4
            and lax.axis_size("chan") == 8
            and x_in.shape[1] >= 2
        )
        return (on_device if tiled else plain)(x_in, weight, bias_vec, grad_out)

    return jax.shard_map(
        body,
        mesh=mesh,
        in_specs=placed,
        out_specs=(
            P("chan", "slab", None, None),
            P("chan", "slab", None, None),
            P("chan", None, None),
            P("chan"),
        ),
        check_vma=False,
    )
```

```python
import functools
import math

import jax
import jax.numpy as jnp
from jax import lax
from jax.experimental import pallas as pl
from jax.experimental.pallas import tpu as pltpu
from jax.sharding import PartitionSpec as P

LANES = 128
FORWARD_FLOPS = 9 * 10**8
SUM_FLOPS = 24 * 10**8
ASSEMBLE_FLOPS = 40 * 10**8
VMEM = pl.BlockSpec(memory_space=pltpu.VMEM)
ANY = pl.BlockSpec(memory_space=pl.ANY)
HBM = pl.BlockSpec(memory_space=pltpu.HBM)
SMEM = pl.BlockSpec(memory_space=pltpu.SMEM)


def with_halo(block, sides, width):
    for axis, dim in sides:
        count = lax.axis_size(axis)
        forward = [(i, i + 1) for i in range(count - 1)]
        forward.append((count - 1, 0))
        backward = [(target, source) for source, target in forward]
        low = lax.ppermute(
            lax.slice_in_dim(block, block.shape[dim] - width, None, axis=dim), axis, forward
        )
        high = lax.ppermute(lax.slice_in_dim(block, 0, width, axis=dim), axis, backward)
        block = jnp.concatenate([low, block, high], axis=dim)
    return block


def tap_list():
    return [(9 * i + 3 * j + l, i, j, l) for i in range(3) for j in range(3) for l in range(3)]


def plain(x_in, weight, bias_vec, grad_out):
    out_local, n_taps, in_total = weight.shape
    n_planes, n_rows, n_depth = (x_in.shape[1], x_in.shape[2], x_in.shape[3])
    rimmed = with_halo(x_in, (("slab", 1),), 1)
    padded = lax.all_gather(rimmed, "chan", axis=0, tiled=True)
    own_planes = padded[:, 1 : n_planes + 1]
    pre_act = (
        jnp.zeros((out_local, n_planes, n_rows, n_depth), jnp.float32)
        + bias_vec.astype(jnp.float32)[:, None, None, None]
    )
    for i in range(3):
        w_plane = jnp.transpose(weight[:, 9 * i : 9 * i + 9], (1, 0, 2)).reshape(
            9 * out_local, in_total
        )
        plane_part = jnp.dot(
            w_plane,
            padded[:, i : i + n_planes].reshape(in_total, -1),
            preferred_element_type=jnp.float32,
        )
        plane_part = plane_part.reshape(9, out_local, n_planes, n_rows, n_depth)
        for j in range(3):
            for l in range(3):
                pre_act = pre_act + jnp.roll(plane_part[3 * j + l], (1 - j, 1 - l), axis=(2, 3))
    sigmoid_v = jax.nn.sigmoid(pre_act)
    activation = (pre_act * sigmoid_v).astype(jnp.bfloat16)
    slope = sigmoid_v * (1.0 + pre_act * (1.0 - sigmoid_v))
    grad_pre = (grad_out.astype(jnp.float32) * slope).astype(jnp.bfloat16)
    padded_grad = with_halo(grad_pre, (("slab", 1),), 1)
    shifted = jnp.stack(
        [
            jnp.roll(padded_grad[:, 2 - i : 2 - i + n_planes], (j - 1, l - 1), axis=(2, 3))
            for k, i, j, l in tap_list()
        ],
        0,
    )
    shifted = shifted.reshape(n_taps * out_local, -1)
    grad_scale = 1.0 / math.sqrt(lax.axis_size("slab") * n_planes * n_rows * n_depth)
    filter_local = lax.dot_general(
        shifted,
        own_planes.reshape(in_total, -1),
        (((1,), (1,)), ((), ())),
        preferred_element_type=jnp.float32,
    )
    filter_part = (
        jnp.transpose(filter_local.reshape(n_taps, out_local, in_total), (1, 0, 2)) * grad_scale
    )
    bias_part = grad_scale * jnp.sum(grad_pre.astype(jnp.float32), axis=(1, 2, 3))
    bias_row = jnp.concatenate(
        [bias_part[:, None, None], jnp.zeros((out_local, 1, in_total - 1), jnp.float32)], 2
    )
    summed_filters = lax.psum(jnp.concatenate([filter_part, bias_row], 1), "slab")
    weight_grad = summed_filters[:, :n_taps]
    bias_grad = summed_filters[:, n_taps, 0]
    flat_w = jnp.transpose(weight, (1, 0, 2)).reshape(n_taps * out_local, in_total)
    product = lax.dot_general(
        flat_w, shifted, (((0,), (0,)), ((), ())), preferred_element_type=jnp.float32
    )
    grad_in = lax.psum_scatter(
        product.reshape(
            in_total // lax.axis_size("chan") * lax.axis_size("chan"), n_planes, n_rows, n_depth
        ),
        "chan",
        scatter_dimension=0,
        tiled=True,
    )
    return (activation, grad_in.astype(jnp.bfloat16), weight_grad, bias_grad)


def call(body, out_shape, operands, specs=None, scratch=(), flops=0, name=None, aliases=None):
    read = sum(math.prod(a.shape) * a.dtype.itemsize for a in operands)
    written = sum(math.prod(a.shape) * a.dtype.itemsize for a in out_shape)
    return pl.pallas_call(
        body,
        out_shape=out_shape,
        in_specs=specs or [VMEM] * len(operands),
        out_specs=[VMEM] * len(out_shape),
        scratch_shapes=list(scratch),
        input_output_aliases=aliases or {},
        compiler_params=pltpu.CompilerParams(vmem_limit_bytes=24 * 2**20),
        cost_estimate=pl.CostEstimate(
            flops=flops, bytes_accessed=read + written, transcendentals=0
        ),
        name=name,
    )(*operands)


def shape_of(shape, dtype):
    return jax.ShapeDtypeStruct(shape, dtype)


def turned(value, wide_ref):
    o = value.shape[0]
    cells = wide_ref.shape[0] // o
    wide_ref[...] = value.astype(jnp.float32).reshape(wide_ref.shape)
    return [
        wide_ref[pl.ds(k, o, stride=cells), :].astype(value.dtype) for k in range(cells)
    ]


def prepare_body(
    n,
    rows,
    x_hbm,
    go_hbm,
    w_hbm,
    bias_hbm,
    x_ref,
    go_ref,
    go_low_ref,
    go_high_ref,
    flat_ref,
    back_ref,
    bias_ref,
    go_in,
    w_in,
    bias_in,
    wide_ref,
    sems,
):
    copies = [
        pltpu.make_async_copy(source, target, sems.at[at])
        for at, (source, target) in enumerate(
            [(go_hbm, go_in), (w_hbm, w_in), (bias_hbm, bias_in), (x_hbm, x_ref)]
        )
    ]
    for copy in copies:
        copy.start()
    copies[0].wait()
    for k, value in enumerate(turned(go_in[...], wide_ref)):
        go_ref[k] = value
        if k < rows:
            go_low_ref[k] = value
        if k >= (n - 1) * rows:
            go_high_ref[k - (n - 1) * rows] = value
    copies[1].wait()
    copies[2].wait()
    copies[3].wait()
    flat = w_in[...].reshape(flat_ref.shape)
    flat_ref[...] = flat
    back_ref[...] = jnp.transpose(flat)
    o = bias_ref.shape[0]
    row = jnp.broadcast_to(bias_in[...].astype(jnp.float32), (o, o))
    same = lax.broadcasted_iota(jnp.int32, (o, o), 0) == lax.broadcasted_iota(jnp.int32, (o, o), 1)
    column = jnp.sum(jnp.where(same, row, 0.0), axis=1, keepdims=True)
    bias_ref[...] = jnp.broadcast_to(column, bias_ref.shape)


def by_core(even, odd, me_ref):
    core = lax.rem(me_ref[0], 2)
    return (1 - core) * owner(me_ref, even) + core * owner(me_ref, odd)


def place_block(me_ref, b, block_ref, x_ref, wide_ref):
    o = block_ref.shape[0]
    at = b(me_ref) if callable(b) else owner(me_ref, b)
    place = pl.ds(pl.multiple_of(at * o, o), o)
    for k, value in enumerate(turned(block_ref[...], wide_ref)):
        x_ref[place, k * LANES : (k + 1) * LANES] = value


def assemble_body(places, me_ref, *refs):
    blocks, (x_ref, wide_ref) = refs[: len(places)], refs[-2:]
    for b, block in zip(places, blocks):
        place_block(me_ref, b, block, x_ref, wide_ref)


def owner(me_ref, b):
    return jnp.bitwise_xor(me_ref[0], 2 * (b % 4) + b // 4)


def forward_body(n, rows, o, me_ref, w_ref, *refs):
    blocks = refs[:4]
    own_ref, low_ref, high_ref, x_ref, acc, w_copy, wide_ref = refs[5:]
    w_copy[...] = w_ref[...]
    for core, pair in enumerate((blocks[:2], blocks[2:])):

        @pl.when(lax.rem(me_ref[0], 2) == core)
        def _():
            for b, block in zip((3, 7), pair):
                place_block(me_ref, b, block, x_ref, wide_ref)

    w = w_copy[...]
    seen = set()
    for p in range(n):
        for t in range(0, rows, 2):
            at = (p * rows + t) * LANES
            part = jnp.dot(
                w, x_ref[:, at : at + 2 * LANES], preferred_element_type=jnp.float32
            )
            for k, i, j, l in tap_list():
                for h in range(2):
                    slot = (l, p + 2 - i, (t + h + 1 - j) % rows)
                    value = part[k * o : (k + 1) * o, h * LANES : (h + 1) * LANES]
                    if slot in seen:
                        acc[slot] += value
                    else:
                        acc[slot] = value
                        seen.add(slot)
    for q in range(n + 2):
        for y in range(rows):
            total = (
                pltpu.roll(acc[0, q, y], 1, 1)
                + acc[1, q, y]
                + pltpu.roll(acc[2, q, y], LANES - 1, 1)
            )
            if q == 0:
                low_ref[y] = total.astype(low_ref.dtype)
            elif q == n + 1:
                high_ref[y] = total.astype(high_ref.dtype)
            else:
                own_ref[(q - 1) * rows + y] = total
            if q == 1:
                low_ref[rows + y] = total.astype(low_ref.dtype)
            if q == n:
                high_ref[rows + y] = total.astype(high_ref.dtype)


def gradient_body(
    n,
    rows,
    o,
    scale,
    me_ref,
    own_ref,
    low_ref,
    high_ref,
    below_ref,
    above_ref,
    bias_ref,
    go_ref,
    go_below_ref,
    go_above_ref,
    back_ref,
    act_ref,
    total_ref,
    s_ref,
    other_ref,
    mine_ref,
    w_ref,
    wide_ref,
):
    f32, bf16 = jnp.float32, jnp.bfloat16
    for b in range(8):
        place = pl.ds(pl.multiple_of(owner(me_ref, b) * o, o), o)
        w_ref[b * o : (b + 1) * o] = back_ref[place]
    total = jnp.zeros((o, LANES), f32)
    for q in range(n + 2):
        for y in range(rows):
            if q == 0:
                pre = below_ref[rows + y].astype(f32) + low_ref[y].astype(f32)
                go = go_below_ref[y]
            elif q == n + 1:
                pre = above_ref[rows + y].astype(f32) + high_ref[y].astype(f32)
                go = go_above_ref[y]
            else:
                pre = own_ref[(q - 1) * rows + y]
                go = go_ref[(q - 1) * rows + y]
                if q == 1:
                    pre = pre + below_ref[y].astype(f32)
                if q == n:
                    pre = pre + above_ref[y].astype(f32)
            pre = pre + bias_ref[...]
            s = jax.nn.sigmoid(pre)
            slope = s * (1.0 + pre * (1.0 - s))
            value = (go.astype(f32) * slope).astype(bf16)
            wide = value.astype(f32)
            if 1 <= q <= n:
                wide_ref[pl.ds((q - 1) * rows + y, o, stride=n * rows), :] = pre * s
                total = total + wide
            shifts = [
                pltpu.roll(wide, LANES - 1, 1).astype(bf16),
                value,
                pltpu.roll(wide, 1, 1).astype(bf16),
            ]
            for k, i, j, l in tap_list():
                p = q - 2 + i
                if 0 <= p < n:
                    at = (p * rows + (y + j - 1) % rows) * LANES
                    s_ref[k * o : (k + 1) * o, at : at + LANES] = shifts[l]
    act_ref[...] = wide_ref[...].reshape(act_ref.shape).astype(bf16)
    total_ref[...] = jnp.broadcast_to(
        jnp.sum(total, axis=1, keepdims=True) * scale, total_ref.shape
    )
    input_grad(n * rows, o, w_ref[...], s_ref, [(ref, r) for ref in (mine_ref, other_ref) for r in range(4)])


def input_grad(cells, o, w, s_ref, outs):
    for t in range(0, cells, 2):
        part = jnp.dot(
            w, s_ref[:, t * LANES : (t + 2) * LANES], preferred_element_type=jnp.float32
        ).astype(outs[0][0].dtype)
        for h in range(2):
            for r, (out_ref, at) in enumerate(outs):
                cut = part[r * o : (r + 1) * o, h * LANES : (h + 1) * LANES]
                out_ref[at, t + h] = cut


def filter_grad_body(scale, start, o, s_ref, x_ref, total_ref, _, out_ref):
    taps = min(27 - start, out_ref.shape[0] // o)
    part = lax.dot_general(
        s_ref[start * o : (start + taps) * o],
        x_ref[...],
        (((1,), (1,)), ((), ())),
        preferred_element_type=jnp.float32,
    )
    out_ref[: taps * o] = (part * scale).astype(out_ref.dtype)
    if out_ref.shape[0] > taps * o:
        row = jnp.concatenate([total_ref[...]] * (out_ref.shape[1] // LANES), axis=1)
        out_ref[taps * o :] = row.astype(out_ref.dtype)


def pair_body(a_ref, b_ref, _, out_ref):
    f32 = jnp.float32
    out_ref[...] = (a_ref[...].astype(f32) + b_ref[...].astype(f32)).astype(out_ref.dtype)


def core_sum_body(mine_ref, other_ref, *outs):
    for r, out_ref in enumerate(outs):
        total = mine_ref[r].astype(jnp.float32) + other_ref[r].astype(jnp.float32)
        out_ref[...] = total.astype(out_ref.dtype)


def sum_body(a_ref, b_ref, c_ref, d_ref, out_ref):
    f32 = jnp.float32
    total = b_ref[...].astype(f32) + c_ref[...].astype(f32) + d_ref[...].astype(f32)
    out_ref[...] = a_ref[...] + total


def last_body(
    taps, a_ref, b_ref, c_ref, d_ref, g_ref, out_ref, bias_ref, grad_ref, wide_ref
):
    o = out_ref.shape[1]
    f32 = jnp.float32
    cells = g_ref.shape[0]
    for k in range(cells):
        wide_ref[pl.ds(k, o, stride=cells), :] = g_ref[k]
    grad_ref[...] = wide_ref[...].reshape(grad_ref.shape).astype(grad_ref.dtype)
    for k in range(27):
        left, right, at = (a_ref, b_ref, k) if k < taps else (c_ref, d_ref, k - taps)
        cut = slice(at * o, (at + 1) * o)
        out_ref[k] = left[cut].astype(f32) + right[cut].astype(f32)
    cut = slice((27 - taps) * o, (28 - taps) * o)
    column = (c_ref[cut].astype(f32) + d_ref[cut].astype(f32))[:, :o]
    same = lax.broadcasted_iota(jnp.int32, (o, o), 0) == lax.broadcasted_iota(jnp.int32, (o, o), 1)
    bias_ref[...] = jnp.sum(jnp.where(same, column, 0.0), axis=0, keepdims=True)


def in_hbm(value):
    return pltpu.with_memory_space_constraint(value, pltpu.HBM)


def rotate(value, axis, step):
    count = lax.axis_size(axis)
    return lax.ppermute(value, axis, [(i, (i + step) % count) for i in range(count)])


def swap(value, axis, bit):
    return lax.ppermute(value, axis, [(i, i ^ bit) for i in range(lax.axis_size(axis))])


def core_swap(value, even, odd):
    steps = (even, odd)
    pairs = [(c, c ^ steps[c % 2]) for c in range(lax.axis_size("chan")) if steps[c % 2]]
    return lax.ppermute(value, "chan", pairs)


def cross(value, phase):
    slabs, chans = lax.axis_size("slab"), lax.axis_size("chan")
    pairs = [
        (s * chans + c, (s ^ (1 + (c + phase) % 2)) * chans + c)
        for s in range(slabs)
        for c in range(chans)
    ]
    return lax.ppermute(value, ("slab", "chan"), pairs)


def on_device(x_in, weight, bias_vec, grad_out):
    o, _, c_all = weight.shape
    _, n, rows, depth = x_in.shape
    f32, bf16 = jnp.float32, jnp.bfloat16
    cells = n * rows
    flops = 2 * 27 * o * c_all * cells * depth
    scale = 1.0 / math.sqrt(lax.axis_size("slab") * cells * depth)
    me = lax.axis_index("chan").astype(jnp.int32).reshape(1)

    block_wide = [pltpu.VMEM((o * cells, depth), f32)]

    x_1 = core_swap(x_in, 4, 2)
    x_2 = core_swap(x_in, 2, 4)
    x_side = swap(x_in, "chan", 1)
    x_own, go, go_low, go_high, w_flat, w_back, bias = call(
        functools.partial(prepare_body, n, rows),
        [
            shape_of((o, n, rows, depth), bf16),
            shape_of((cells, o, depth), bf16),
            shape_of((rows, o, depth), bf16),
            shape_of((rows, o, depth), bf16),
            shape_of((27 * o, c_all), bf16),
            shape_of((c_all, 27 * o), bf16),
            shape_of((o, LANES), f32),
        ],
        [in_hbm(a) for a in (x_in, grad_out, jnp.transpose(weight, (1, 0, 2)), bias_vec[None, :])],
        [HBM] * 4,
        [
            pltpu.VMEM((o, n, rows, depth), bf16),
            pltpu.VMEM((27, o, c_all), bf16),
            pltpu.VMEM((1, o), bf16),
            *block_wide,
            pltpu.SemaphoreType.DMA((4,)),
        ],
        name="prepare",
    )
    go_above = rotate(go_low, "slab", -1)
    go_below = rotate(go_high, "slab", 1)
    x_1, w_flat = lax.optimization_barrier((x_1, w_flat))
    ab_0 = core_swap(x_1, 2, None)
    ab_1 = core_swap(x_2, None, 2)
    late_2, go_above, go_below = lax.optimization_barrier((x_2, go_above, go_below))
    x_1_side = swap(x_1, "chan", 1)
    x_2_side = swap(late_2, "chan", 1)
    ab_0_side = core_swap(ab_0, 1, None)
    ab_1_side = core_swap(ab_1, None, 1)
    early = [
        0,
        functools.partial(by_core, 2, 1),
        functools.partial(by_core, 1, 2),
        4,
        functools.partial(by_core, 5, 6),
        functools.partial(by_core, 6, 5),
    ]
    (x_all,) = call(
        functools.partial(assemble_body, early),
        [shape_of((c_all, cells * depth), bf16)],
        [me, x_own, x_1, x_2, x_side, x_1_side, x_2_side],
        [SMEM] + [VMEM] * 6,
        block_wide,
        flops=ASSEMBLE_FLOPS,
        name="assemble",
    )
    own, low, high, x_all = call(
        functools.partial(forward_body, n, rows, o),
        [
            shape_of((cells, o, depth), f32),
            shape_of((2 * rows, o, depth), bf16),
            shape_of((2 * rows, o, depth), bf16),
            shape_of((c_all, cells * depth), bf16),
        ],
        [me, w_flat, ab_0, ab_1_side, ab_1, ab_0_side, x_all],
        [SMEM] + [VMEM] * 6,
        [
            pltpu.VMEM((3, n + 2, rows, o, depth), f32),
            pltpu.VMEM((27 * o, c_all), bf16),
            *block_wide,
        ],
        flops=FORWARD_FLOPS,
        name="forward",
        aliases={6: 3},
    )
    above = rotate(low, "slab", -1)
    below = rotate(high, "slab", 1)
    act, total, stacked, other, mine = call(
        functools.partial(gradient_body, n, rows, o, scale),
        [
            shape_of((o, n, rows, depth), bf16),
            shape_of((o, LANES), f32),
            shape_of((27 * o, cells * depth), bf16),
            shape_of((4, cells, o, depth), bf16),
            shape_of((4, cells, o, depth), bf16),
        ],
        [me, own, low, high, below, above, bias, go, go_below, go_above, w_back],
        [SMEM] + [VMEM] * 10,
        [pltpu.VMEM((c_all, 27 * o), bf16), *block_wide],
        flops=flops,
        name="gradient",
    )
    other = swap(other, "chan", 1)
    taps = 14
    def filter_grad(start, taps, after, name):
        return call(
            functools.partial(filter_grad_body, scale, start, o),
            [shape_of((taps * o, c_all), bf16)],
            [stacked, x_all, total, after],
            [VMEM] * 3 + [ANY],
            flops=flops // 2,
            name=name,
        )[0]

    first = filter_grad(0, taps, total, "filter_first")
    first_far = cross(first, 0)
    g_own, g_a, g_b, g_ab = call(
        core_sum_body,
        [shape_of((cells, o, depth), f32)] + [shape_of((cells, o, depth), bf16)] * 3,
        [mine, other],
        name="core_sum",
    )
    second = filter_grad(taps, 28 - taps, g_own, "filter_second")
    second_far = cross(second, 0)
    g_ab = swap(g_ab, "chan", 6)
    g_b = swap(g_b, "chan", 4)
    g_a = swap(g_a, "chan", 2)
    first, second = (
        call(
            pair_body,
            [shape_of(a.shape, bf16)],
            [a, b, g_own],
            [VMEM] * 2 + [ANY],
            name="pair_sum",
        )[0]
        for a, b in ((first, first_far), (second, second_far))
    )
    first_far = cross(first, 1)
    second_far = cross(second, 1)
    (g_own,) = call(
        sum_body,
        [shape_of((cells, o, depth), f32)],
        [g_own, g_ab, g_b, g_a],
        flops=SUM_FLOPS,
        name="sum",
    )
    weight_grad, bias_grad, grad_in = call(
        functools.partial(last_body, taps),
        [
            shape_of((27, o, c_all), f32),
            shape_of((1, o), f32),
            shape_of((o, n, rows, depth), bf16),
        ],
        [first, first_far, second, second_far, g_own],
        scratch=block_wide,
        name="last",
    )
    return act, grad_in, jnp.transpose(weight_grad, (1, 0, 2)), bias_grad[0]


def solution(mesh):
    placed = (
        P("chan", "slab", None, None),
        P("chan", None, None),
        P("chan"),
        P("chan", "slab", None, None),
    )

    def body(x_in, weight, bias_vec, grad_out):
        tiled = (
            weight.shape[0] % 32 == 0
            and x_in.shape[3] == LANES
            and lax.axis_size("slab") == 4
            and lax.axis_size("chan") == 8
            and x_in.shape[1] >= 2
        )
        return (on_device if tiled else plain)(x_in, weight, bias_vec, grad_out)

    return jax.shard_map(
        body,
        mesh=mesh,
        in_specs=placed,
        out_specs=(
            P("chan", "slab", None, None),
            P("chan", "slab", None, None),
            P("chan", None, None),
            P("chan"),
        ),
        check_vma=False,
    )
```

```python
import functools
import math

import jax
import jax.numpy as jnp
from jax import lax
from jax.experimental import pallas as pl
from jax.experimental.pallas import tpu as pltpu
from jax.sharding import PartitionSpec as P

LANES = 128
FORWARD_FLOPS = 9 * 10**8
SUM_FLOPS = 24 * 10**8
ASSEMBLE_FLOPS = 40 * 10**8
VMEM = pl.BlockSpec(memory_space=pltpu.VMEM)
ANY = pl.BlockSpec(memory_space=pl.ANY)
HBM = pl.BlockSpec(memory_space=pltpu.HBM)
SMEM = pl.BlockSpec(memory_space=pltpu.SMEM)


def with_halo(block, sides, width):
    for axis, dim in sides:
        count = lax.axis_size(axis)
        forward = [(i, i + 1) for i in range(count - 1)]
        forward.append((count - 1, 0))
        backward = [(target, source) for source, target in forward]
        low = lax.ppermute(
            lax.slice_in_dim(block, block.shape[dim] - width, None, axis=dim), axis, forward
        )
        high = lax.ppermute(lax.slice_in_dim(block, 0, width, axis=dim), axis, backward)
        block = jnp.concatenate([low, block, high], axis=dim)
    return block


def tap_list():
    return [(9 * i + 3 * j + l, i, j, l) for i in range(3) for j in range(3) for l in range(3)]


def plain(x_in, weight, bias_vec, grad_out):
    out_local, n_taps, in_total = weight.shape
    n_planes, n_rows, n_depth = (x_in.shape[1], x_in.shape[2], x_in.shape[3])
    rimmed = with_halo(x_in, (("slab", 1),), 1)
    padded = lax.all_gather(rimmed, "chan", axis=0, tiled=True)
    own_planes = padded[:, 1 : n_planes + 1]
    pre_act = (
        jnp.zeros((out_local, n_planes, n_rows, n_depth), jnp.float32)
        + bias_vec.astype(jnp.float32)[:, None, None, None]
    )
    for i in range(3):
        w_plane = jnp.transpose(weight[:, 9 * i : 9 * i + 9], (1, 0, 2)).reshape(
            9 * out_local, in_total
        )
        plane_part = jnp.dot(
            w_plane,
            padded[:, i : i + n_planes].reshape(in_total, -1),
            preferred_element_type=jnp.float32,
        )
        plane_part = plane_part.reshape(9, out_local, n_planes, n_rows, n_depth)
        for j in range(3):
            for l in range(3):
                pre_act = pre_act + jnp.roll(plane_part[3 * j + l], (1 - j, 1 - l), axis=(2, 3))
    sigmoid_v = jax.nn.sigmoid(pre_act)
    activation = (pre_act * sigmoid_v).astype(jnp.bfloat16)
    slope = sigmoid_v * (1.0 + pre_act * (1.0 - sigmoid_v))
    grad_pre = (grad_out.astype(jnp.float32) * slope).astype(jnp.bfloat16)
    padded_grad = with_halo(grad_pre, (("slab", 1),), 1)
    shifted = jnp.stack(
        [
            jnp.roll(padded_grad[:, 2 - i : 2 - i + n_planes], (j - 1, l - 1), axis=(2, 3))
            for k, i, j, l in tap_list()
        ],
        0,
    )
    shifted = shifted.reshape(n_taps * out_local, -1)
    grad_scale = 1.0 / math.sqrt(lax.axis_size("slab") * n_planes * n_rows * n_depth)
    filter_local = lax.dot_general(
        shifted,
        own_planes.reshape(in_total, -1),
        (((1,), (1,)), ((), ())),
        preferred_element_type=jnp.float32,
    )
    filter_part = (
        jnp.transpose(filter_local.reshape(n_taps, out_local, in_total), (1, 0, 2)) * grad_scale
    )
    bias_part = grad_scale * jnp.sum(grad_pre.astype(jnp.float32), axis=(1, 2, 3))
    bias_row = jnp.concatenate(
        [bias_part[:, None, None], jnp.zeros((out_local, 1, in_total - 1), jnp.float32)], 2
    )
    summed_filters = lax.psum(jnp.concatenate([filter_part, bias_row], 1), "slab")
    weight_grad = summed_filters[:, :n_taps]
    bias_grad = summed_filters[:, n_taps, 0]
    flat_w = jnp.transpose(weight, (1, 0, 2)).reshape(n_taps * out_local, in_total)
    product = lax.dot_general(
        flat_w, shifted, (((0,), (0,)), ((), ())), preferred_element_type=jnp.float32
    )
    grad_in = lax.psum_scatter(
        product.reshape(
            in_total // lax.axis_size("chan") * lax.axis_size("chan"), n_planes, n_rows, n_depth
        ),
        "chan",
        scatter_dimension=0,
        tiled=True,
    )
    return (activation, grad_in.astype(jnp.bfloat16), weight_grad, bias_grad)


def call(body, out_shape, operands, specs=None, scratch=(), flops=0, name=None, aliases=None):
    read = sum(math.prod(a.shape) * a.dtype.itemsize for a in operands)
    written = sum(math.prod(a.shape) * a.dtype.itemsize for a in out_shape)
    return pl.pallas_call(
        body,
        out_shape=out_shape,
        in_specs=specs or [VMEM] * len(operands),
        out_specs=[VMEM] * len(out_shape),
        scratch_shapes=list(scratch),
        input_output_aliases=aliases or {},
        compiler_params=pltpu.CompilerParams(vmem_limit_bytes=24 * 2**20),
        cost_estimate=pl.CostEstimate(
            flops=flops, bytes_accessed=read + written, transcendentals=0
        ),
        name=name,
    )(*operands)


def shape_of(shape, dtype):
    return jax.ShapeDtypeStruct(shape, dtype)


def turned(value, wide_ref):
    o = value.shape[0]
    cells = wide_ref.shape[0] // o
    wide_ref[...] = value.astype(jnp.float32).reshape(wide_ref.shape)
    return [
        wide_ref[pl.ds(k, o, stride=cells), :].astype(value.dtype) for k in range(cells)
    ]


def prepare_body(
    n,
    rows,
    x_hbm,
    go_hbm,
    w_hbm,
    bias_hbm,
    x_ref,
    go_ref,
    go_low_ref,
    go_high_ref,
    flat_ref,
    back_ref,
    bias_ref,
    go_in,
    w_in,
    bias_in,
    wide_ref,
    sems,
):
    copies = [
        pltpu.make_async_copy(source, target, sems.at[at])
        for at, (source, target) in enumerate(
            [(go_hbm, go_in), (w_hbm, w_in), (bias_hbm, bias_in), (x_hbm, x_ref)]
        )
    ]
    for copy in copies:
        copy.start()
    copies[0].wait()
    for k, value in enumerate(turned(go_in[...], wide_ref)):
        go_ref[k] = value
        if k < rows:
            go_low_ref[k] = value
        if k >= (n - 1) * rows:
            go_high_ref[k - (n - 1) * rows] = value
    copies[1].wait()
    copies[2].wait()
    copies[3].wait()
    flat = w_in[...].reshape(flat_ref.shape)
    flat_ref[...] = flat
    back_ref[...] = jnp.transpose(flat)
    o = bias_ref.shape[0]
    row = jnp.broadcast_to(bias_in[...].astype(jnp.float32), (o, o))
    same = lax.broadcasted_iota(jnp.int32, (o, o), 0) == lax.broadcasted_iota(jnp.int32, (o, o), 1)
    column = jnp.sum(jnp.where(same, row, 0.0), axis=1, keepdims=True)
    bias_ref[...] = jnp.broadcast_to(column, bias_ref.shape)


def place_block(me_ref, b, block_ref, x_ref, wide_ref):
    o = block_ref.shape[0]
    place = pl.ds(pl.multiple_of(owner(me_ref, b) * o, o), o)
    for k, value in enumerate(turned(block_ref[...], wide_ref)):
        x_ref[place, k * LANES : (k + 1) * LANES] = value


def assemble_body(places, me_ref, *refs):
    blocks, (x_ref, wide_ref) = refs[: len(places)], refs[-2:]
    for b, block in zip(places, blocks):
        place_block(me_ref, b, block, x_ref, wide_ref)


def owner(me_ref, b):
    return jnp.bitwise_xor(me_ref[0], 2 * (b % 4) + b // 4)


def forward_body(n, rows, o, places, me_ref, w_ref, *refs):
    blocks = refs[: len(places)]
    own_ref, low_ref, high_ref, x_ref, acc, wide_ref = refs[len(places) + 1 :]
    for b, block in zip(places, blocks):
        place_block(me_ref, b, block, x_ref, wide_ref)
    w = w_ref[...]
    seen = set()
    for p in range(n):
        for t in range(0, rows, 2):
            at = (p * rows + t) * LANES
            part = jnp.dot(
                w, x_ref[:, at : at + 2 * LANES], preferred_element_type=jnp.float32
            )
            for k, i, j, l in tap_list():
                for h in range(2):
                    slot = (l, p + 2 - i, (t + h + 1 - j) % rows)
                    value = part[k * o : (k + 1) * o, h * LANES : (h + 1) * LANES]
                    if slot in seen:
                        acc[slot] += value
                    else:
                        acc[slot] = value
                        seen.add(slot)
    for q in range(n + 2):
        for y in range(rows):
            total = (
                pltpu.roll(acc[0, q, y], 1, 1)
                + acc[1, q, y]
                + pltpu.roll(acc[2, q, y], LANES - 1, 1)
            )
            if q == 0:
                low_ref[y] = total.astype(low_ref.dtype)
            elif q == n + 1:
                high_ref[y] = total.astype(high_ref.dtype)
            else:
                own_ref[(q - 1) * rows + y] = total
            if q == 1:
                low_ref[rows + y] = total.astype(low_ref.dtype)
            if q == n:
                high_ref[rows + y] = total.astype(high_ref.dtype)


def gradient_body(
    n,
    rows,
    o,
    scale,
    me_ref,
    own_ref,
    low_ref,
    high_ref,
    below_ref,
    above_ref,
    bias_ref,
    go_ref,
    go_below_ref,
    go_above_ref,
    back_ref,
    act_ref,
    total_ref,
    s_ref,
    other_ref,
    mine_ref,
    w_ref,
    wide_ref,
):
    f32, bf16 = jnp.float32, jnp.bfloat16
    for b in range(8):
        place = pl.ds(pl.multiple_of(owner(me_ref, b) * o, o), o)
        w_ref[b * o : (b + 1) * o] = back_ref[place]
    total = jnp.zeros((o, LANES), f32)
    for q in range(n + 2):
        for y in range(rows):
            if q == 0:
                pre = below_ref[rows + y].astype(f32) + low_ref[y].astype(f32)
                go = go_below_ref[y]
            elif q == n + 1:
                pre = above_ref[rows + y].astype(f32) + high_ref[y].astype(f32)
                go = go_above_ref[y]
            else:
                pre = own_ref[(q - 1) * rows + y]
                go = go_ref[(q - 1) * rows + y]
                if q == 1:
                    pre = pre + below_ref[y].astype(f32)
                if q == n:
                    pre = pre + above_ref[y].astype(f32)
            pre = pre + bias_ref[...]
            s = jax.nn.sigmoid(pre)
            slope = s * (1.0 + pre * (1.0 - s))
            value = (go.astype(f32) * slope).astype(bf16)
            wide = value.astype(f32)
            if 1 <= q <= n:
                wide_ref[pl.ds((q - 1) * rows + y, o, stride=n * rows), :] = pre * s
                total = total + wide
            shifts = [
                pltpu.roll(wide, LANES - 1, 1).astype(bf16),
                value,
                pltpu.roll(wide, 1, 1).astype(bf16),
            ]
            for k, i, j, l in tap_list():
                p = q - 2 + i
                if 0 <= p < n:
                    at = (p * rows + (y + j - 1) % rows) * LANES
                    s_ref[k * o : (k + 1) * o, at : at + LANES] = shifts[l]
    act_ref[...] = wide_ref[...].reshape(act_ref.shape).astype(bf16)
    total_ref[...] = jnp.broadcast_to(
        jnp.sum(total, axis=1, keepdims=True) * scale, total_ref.shape
    )
    input_grad(n * rows, o, w_ref[...], s_ref, [(ref, r) for ref in (mine_ref, other_ref) for r in range(4)])


def input_grad(cells, o, w, s_ref, outs):
    for t in range(0, cells, 2):
        part = jnp.dot(
            w, s_ref[:, t * LANES : (t + 2) * LANES], preferred_element_type=jnp.float32
        ).astype(outs[0][0].dtype)
        for h in range(2):
            for r, (out_ref, at) in enumerate(outs):
                cut = part[r * o : (r + 1) * o, h * LANES : (h + 1) * LANES]
                out_ref[at, t + h] = cut


def filter_grad_body(scale, taps, o, s_ref, x_ref, total_ref, first_ref, second_ref):
    full = lax.dot_general(
        s_ref[...], x_ref[...], (((1,), (1,)), ((), ())), preferred_element_type=jnp.float32
    )
    full = (full * scale).astype(first_ref.dtype)
    first_ref[...] = full[: taps * o]
    second_ref[: (27 - taps) * o] = full[taps * o :]
    row = jnp.concatenate([total_ref[...]] * (second_ref.shape[1] // LANES), axis=1)
    second_ref[(27 - taps) * o :] = row.astype(second_ref.dtype)


def pair_body(a_ref, b_ref, _, out_ref):
    f32 = jnp.float32
    out_ref[...] = (a_ref[...].astype(f32) + b_ref[...].astype(f32)).astype(out_ref.dtype)


def core_sum_body(mine_ref, other_ref, *outs):
    for r, out_ref in enumerate(outs):
        total = mine_ref[r].astype(jnp.float32) + other_ref[r].astype(jnp.float32)
        out_ref[...] = total.astype(out_ref.dtype)


def sum_body(a_ref, b_ref, c_ref, d_ref, out_ref):
    f32 = jnp.float32
    total = b_ref[...].astype(f32) + c_ref[...].astype(f32) + d_ref[...].astype(f32)
    out_ref[...] = a_ref[...] + total


def last_body(
    taps, a_ref, b_ref, c_ref, d_ref, g_ref, out_ref, bias_ref, grad_ref, wide_ref
):
    o = out_ref.shape[1]
    f32 = jnp.float32
    cells = g_ref.shape[0]
    for k in range(cells):
        wide_ref[pl.ds(k, o, stride=cells), :] = g_ref[k]
    grad_ref[...] = wide_ref[...].reshape(grad_ref.shape).astype(grad_ref.dtype)
    for k in range(27):
        left, right, at = (a_ref, b_ref, k) if k < taps else (c_ref, d_ref, k - taps)
        cut = slice(at * o, (at + 1) * o)
        out_ref[k] = left[cut].astype(f32) + right[cut].astype(f32)
    cut = slice((27 - taps) * o, (28 - taps) * o)
    column = (c_ref[cut].astype(f32) + d_ref[cut].astype(f32))[:, :o]
    same = lax.broadcasted_iota(jnp.int32, (o, o), 0) == lax.broadcasted_iota(jnp.int32, (o, o), 1)
    bias_ref[...] = jnp.sum(jnp.where(same, column, 0.0), axis=0, keepdims=True)


def in_hbm(value):
    return pltpu.with_memory_space_constraint(value, pltpu.HBM)


def rotate(value, axis, step):
    count = lax.axis_size(axis)
    return lax.ppermute(value, axis, [(i, (i + step) % count) for i in range(count)])


def swap(value, axis, bit):
    return lax.ppermute(value, axis, [(i, i ^ bit) for i in range(lax.axis_size(axis))])


def cross(value, phase):
    slabs, chans = lax.axis_size("slab"), lax.axis_size("chan")
    pairs = [
        (s * chans + c, (s ^ (1 + (c + phase) % 2)) * chans + c)
        for s in range(slabs)
        for c in range(chans)
    ]
    return lax.ppermute(value, ("slab", "chan"), pairs)


def on_device(x_in, weight, bias_vec, grad_out):
    o, _, c_all = weight.shape
    _, n, rows, depth = x_in.shape
    f32, bf16 = jnp.float32, jnp.bfloat16
    cells = n * rows
    flops = 2 * 27 * o * c_all * cells * depth
    scale = 1.0 / math.sqrt(lax.axis_size("slab") * cells * depth)
    me = lax.axis_index("chan").astype(jnp.int32).reshape(1)

    block_wide = [pltpu.VMEM((o * cells, depth), f32)]

    x_b = swap(x_in, "chan", 4)
    x_a = swap(x_in, "chan", 2)
    x_side = swap(x_in, "chan", 1)
    x_own, go, go_low, go_high, w_flat, w_back, bias = call(
        functools.partial(prepare_body, n, rows),
        [
            shape_of((o, n, rows, depth), bf16),
            shape_of((cells, o, depth), bf16),
            shape_of((rows, o, depth), bf16),
            shape_of((rows, o, depth), bf16),
            shape_of((27 * o, c_all), bf16),
            shape_of((c_all, 27 * o), bf16),
            shape_of((o, LANES), f32),
        ],
        [in_hbm(a) for a in (x_in, grad_out, jnp.transpose(weight, (1, 0, 2)), bias_vec[None, :])],
        [HBM] * 4,
        [
            pltpu.VMEM((o, n, rows, depth), bf16),
            pltpu.VMEM((27, o, c_all), bf16),
            pltpu.VMEM((1, o), bf16),
            *block_wide,
            pltpu.SemaphoreType.DMA((4,)),
        ],
        name="prepare",
    )
    go_above = rotate(go_low, "slab", -1)
    go_below = rotate(go_high, "slab", 1)
    x_b, w_flat = lax.optimization_barrier((x_b, w_flat))
    x_ab = swap(x_b, "chan", 2)
    late_b, go_above, go_below = lax.optimization_barrier((x_b, go_above, go_below))
    x_a_side = swap(x_a, "chan", 1)
    x_b_side = swap(late_b, "chan", 1)
    early, late = (0, 1, 2, 3, 4, 5, 6), (7,)
    (x_all,) = call(
        functools.partial(assemble_body, early),
        [shape_of((c_all, cells * depth), bf16)],
        [me, x_own, x_a, x_b, x_ab, x_side, x_a_side, x_b_side],
        [SMEM] + [VMEM] * 7,
        block_wide,
        flops=ASSEMBLE_FLOPS,
        name="assemble",
    )
    x_ab_side = swap(x_ab, "chan", 1)
    own, low, high, x_all = call(
        functools.partial(forward_body, n, rows, o, late),
        [
            shape_of((cells, o, depth), f32),
            shape_of((2 * rows, o, depth), bf16),
            shape_of((2 * rows, o, depth), bf16),
            shape_of((c_all, cells * depth), bf16),
        ],
        [me, w_flat, x_ab_side, x_all],
        [SMEM] + [VMEM] * 3,
        [pltpu.VMEM((3, n + 2, rows, o, depth), f32), *block_wide],
        flops=FORWARD_FLOPS,
        name="forward",
        aliases={3: 3},
    )
    above = rotate(low, "slab", -1)
    below = rotate(high, "slab", 1)
    act, total, stacked, other, mine = call(
        functools.partial(gradient_body, n, rows, o, scale),
        [
            shape_of((o, n, rows, depth), bf16),
            shape_of((o, LANES), f32),
            shape_of((27 * o, cells * depth), bf16),
            shape_of((4, cells, o, depth), bf16),
            shape_of((4, cells, o, depth), bf16),
        ],
        [me, own, low, high, below, above, bias, go, go_below, go_above, w_back],
        [SMEM] + [VMEM] * 10,
        [pltpu.VMEM((c_all, 27 * o), bf16), *block_wide],
        flops=flops,
        name="gradient",
    )
    other = swap(other, "chan", 1)
    taps = 14
    first, second = call(
        functools.partial(filter_grad_body, scale, taps, o),
        [shape_of((taps * o, c_all), bf16), shape_of(((28 - taps) * o, c_all), bf16)],
        [stacked, x_all, total],
        flops=flops,
        name="filter_grad",
    )
    first_far = cross(first, 0)
    second_far = cross(second, 0)
    g_own, g_a, g_b, g_ab = call(
        core_sum_body,
        [shape_of((cells, o, depth), f32)] + [shape_of((cells, o, depth), bf16)] * 3,
        [mine, other],
        name="core_sum",
    )
    g_ab = swap(g_ab, "chan", 6)
    g_b = swap(g_b, "chan", 4)
    g_a = swap(g_a, "chan", 2)
    first, second = (
        call(
            pair_body,
            [shape_of(a.shape, bf16)],
            [a, b, g_own],
            [VMEM] * 2 + [ANY],
            name="pair_sum",
        )[0]
        for a, b in ((first, first_far), (second, second_far))
    )
    first_far = cross(first, 1)
    second_far = cross(second, 1)
    (g_own,) = call(
        sum_body,
        [shape_of((cells, o, depth), f32)],
        [g_own, g_a, g_b, g_ab],
        flops=SUM_FLOPS,
        name="sum",
    )
    weight_grad, bias_grad, grad_in = call(
        functools.partial(last_body, taps),
        [
            shape_of((27, o, c_all), f32),
            shape_of((1, o), f32),
            shape_of((o, n, rows, depth), bf16),
        ],
        [first, first_far, second, second_far, g_own],
        scratch=block_wide,
        name="last",
    )
    return act, grad_in, jnp.transpose(weight_grad, (1, 0, 2)), bias_grad[0]


def solution(mesh):
    placed = (
        P("chan", "slab", None, None),
        P("chan", None, None),
        P("chan"),
        P("chan", "slab", None, None),
    )

    def body(x_in, weight, bias_vec, grad_out):
        tiled = (
            weight.shape[0] % 32 == 0
            and x_in.shape[3] == LANES
            and lax.axis_size("slab") == 4
            and lax.axis_size("chan") == 8
            and x_in.shape[1] >= 2
        )
        return (on_device if tiled else plain)(x_in, weight, bias_vec, grad_out)

    return jax.shard_map(
        body,
        mesh=mesh,
        in_specs=placed,
        out_specs=(
            P("chan", "slab", None, None),
            P("chan", "slab", None, None),
            P("chan", None, None),
            P("chan"),
        ),
        check_vma=False,
    )
```

```python
import functools
import math

import jax
import jax.numpy as jnp
from jax import lax
from jax.experimental import pallas as pl
from jax.experimental.pallas import tpu as pltpu
from jax.sharding import PartitionSpec as P

LANES = 128
FORWARD_FLOPS = 9 * 10**8
SUM_FLOPS = 24 * 10**8
ASSEMBLE_FLOPS = 40 * 10**8
VMEM = pl.BlockSpec(memory_space=pltpu.VMEM)
ANY = pl.BlockSpec(memory_space=pl.ANY)
HBM = pl.BlockSpec(memory_space=pltpu.HBM)
SMEM = pl.BlockSpec(memory_space=pltpu.SMEM)


def with_halo(block, sides, width):
    for axis, dim in sides:
        count = lax.axis_size(axis)
        forward = [(i, i + 1) for i in range(count - 1)]
        forward.append((count - 1, 0))
        backward = [(target, source) for source, target in forward]
        low = lax.ppermute(
            lax.slice_in_dim(block, block.shape[dim] - width, None, axis=dim), axis, forward
        )
        high = lax.ppermute(lax.slice_in_dim(block, 0, width, axis=dim), axis, backward)
        block = jnp.concatenate([low, block, high], axis=dim)
    return block


def tap_list():
    return [(9 * i + 3 * j + l, i, j, l) for i in range(3) for j in range(3) for l in range(3)]


def plain(x_in, weight, bias_vec, grad_out):
    out_local, n_taps, in_total = weight.shape
    n_planes, n_rows, n_depth = (x_in.shape[1], x_in.shape[2], x_in.shape[3])
    rimmed = with_halo(x_in, (("slab", 1),), 1)
    padded = lax.all_gather(rimmed, "chan", axis=0, tiled=True)
    own_planes = padded[:, 1 : n_planes + 1]
    pre_act = (
        jnp.zeros((out_local, n_planes, n_rows, n_depth), jnp.float32)
        + bias_vec.astype(jnp.float32)[:, None, None, None]
    )
    for i in range(3):
        w_plane = jnp.transpose(weight[:, 9 * i : 9 * i + 9], (1, 0, 2)).reshape(
            9 * out_local, in_total
        )
        plane_part = jnp.dot(
            w_plane,
            padded[:, i : i + n_planes].reshape(in_total, -1),
            preferred_element_type=jnp.float32,
        )
        plane_part = plane_part.reshape(9, out_local, n_planes, n_rows, n_depth)
        for j in range(3):
            for l in range(3):
                pre_act = pre_act + jnp.roll(plane_part[3 * j + l], (1 - j, 1 - l), axis=(2, 3))
    sigmoid_v = jax.nn.sigmoid(pre_act)
    activation = (pre_act * sigmoid_v).astype(jnp.bfloat16)
    slope = sigmoid_v * (1.0 + pre_act * (1.0 - sigmoid_v))
    grad_pre = (grad_out.astype(jnp.float32) * slope).astype(jnp.bfloat16)
    padded_grad = with_halo(grad_pre, (("slab", 1),), 1)
    shifted = jnp.stack(
        [
            jnp.roll(padded_grad[:, 2 - i : 2 - i + n_planes], (j - 1, l - 1), axis=(2, 3))
            for k, i, j, l in tap_list()
        ],
        0,
    )
    shifted = shifted.reshape(n_taps * out_local, -1)
    grad_scale = 1.0 / math.sqrt(lax.axis_size("slab") * n_planes * n_rows * n_depth)
    filter_local = lax.dot_general(
        shifted,
        own_planes.reshape(in_total, -1),
        (((1,), (1,)), ((), ())),
        preferred_element_type=jnp.float32,
    )
    filter_part = (
        jnp.transpose(filter_local.reshape(n_taps, out_local, in_total), (1, 0, 2)) * grad_scale
    )
    bias_part = grad_scale * jnp.sum(grad_pre.astype(jnp.float32), axis=(1, 2, 3))
    bias_row = jnp.concatenate(
        [bias_part[:, None, None], jnp.zeros((out_local, 1, in_total - 1), jnp.float32)], 2
    )
    summed_filters = lax.psum(jnp.concatenate([filter_part, bias_row], 1), "slab")
    weight_grad = summed_filters[:, :n_taps]
    bias_grad = summed_filters[:, n_taps, 0]
    flat_w = jnp.transpose(weight, (1, 0, 2)).reshape(n_taps * out_local, in_total)
    product = lax.dot_general(
        flat_w, shifted, (((0,), (0,)), ((), ())), preferred_element_type=jnp.float32
    )
    grad_in = lax.psum_scatter(
        product.reshape(
            in_total // lax.axis_size("chan") * lax.axis_size("chan"), n_planes, n_rows, n_depth
        ),
        "chan",
        scatter_dimension=0,
        tiled=True,
    )
    return (activation, grad_in.astype(jnp.bfloat16), weight_grad, bias_grad)


def call(body, out_shape, operands, specs=None, scratch=(), flops=0, name=None, aliases=None):
    read = sum(math.prod(a.shape) * a.dtype.itemsize for a in operands)
    written = sum(math.prod(a.shape) * a.dtype.itemsize for a in out_shape)
    return pl.pallas_call(
        body,
        out_shape=out_shape,
        in_specs=specs or [VMEM] * len(operands),
        out_specs=[VMEM] * len(out_shape),
        scratch_shapes=list(scratch),
        input_output_aliases=aliases or {},
        compiler_params=pltpu.CompilerParams(vmem_limit_bytes=24 * 2**20),
        cost_estimate=pl.CostEstimate(
            flops=flops, bytes_accessed=read + written, transcendentals=0
        ),
        name=name,
    )(*operands)


def shape_of(shape, dtype):
    return jax.ShapeDtypeStruct(shape, dtype)


def turned(value, wide_ref):
    o = value.shape[0]
    cells = wide_ref.shape[0] // o
    wide_ref[...] = value.astype(jnp.float32).reshape(wide_ref.shape)
    return [
        wide_ref[pl.ds(k, o, stride=cells), :].astype(value.dtype) for k in range(cells)
    ]


def prepare_body(
    n,
    rows,
    x_hbm,
    go_hbm,
    w_hbm,
    bias_hbm,
    x_ref,
    go_ref,
    go_low_ref,
    go_high_ref,
    flat_ref,
    back_ref,
    bias_ref,
    go_in,
    w_in,
    bias_in,
    wide_ref,
    sems,
):
    copies = [
        pltpu.make_async_copy(source, target, sems.at[at])
        for at, (source, target) in enumerate(
            [(go_hbm, go_in), (w_hbm, w_in), (bias_hbm, bias_in), (x_hbm, x_ref)]
        )
    ]
    for copy in copies:
        copy.start()
    copies[0].wait()
    for k, value in enumerate(turned(go_in[...], wide_ref)):
        go_ref[k] = value
        if k < rows:
            go_low_ref[k] = value
        if k >= (n - 1) * rows:
            go_high_ref[k - (n - 1) * rows] = value
    copies[1].wait()
    copies[2].wait()
    copies[3].wait()
    flat = w_in[...].reshape(flat_ref.shape)
    flat_ref[...] = flat
    back_ref[...] = jnp.transpose(flat)
    o = bias_ref.shape[0]
    row = jnp.broadcast_to(bias_in[...].astype(jnp.float32), (o, o))
    same = lax.broadcasted_iota(jnp.int32, (o, o), 0) == lax.broadcasted_iota(jnp.int32, (o, o), 1)
    column = jnp.sum(jnp.where(same, row, 0.0), axis=1, keepdims=True)
    bias_ref[...] = jnp.broadcast_to(column, bias_ref.shape)


def place_block(me_ref, b, block_ref, x_ref, wide_ref):
    o = block_ref.shape[0]
    place = pl.ds(pl.multiple_of(owner(me_ref, b) * o, o), o)
    for k, value in enumerate(turned(block_ref[...], wide_ref)):
        x_ref[place, k * LANES : (k + 1) * LANES] = value


def assemble_body(places, me_ref, *refs):
    blocks, (x_ref, wide_ref) = refs[: len(places)], refs[-2:]
    for b, block in zip(places, blocks):
        place_block(me_ref, b, block, x_ref, wide_ref)


def owner(me_ref, b):
    return jnp.bitwise_xor(me_ref[0], 2 * (b % 4) + b // 4)


def forward_body(n, rows, o, places, me_ref, w_ref, *refs):
    blocks = refs[: len(places)]
    own_ref, low_ref, high_ref, x_ref, acc, wide_ref = refs[len(places) + 1 :]
    for b, block in zip(places, blocks):
        place_block(me_ref, b, block, x_ref, wide_ref)
    w = w_ref[...]
    seen = set()
    for p in range(n):
        for t in range(0, rows, 2):
            at = (p * rows + t) * LANES
            part = jnp.dot(
                w, x_ref[:, at : at + 2 * LANES], preferred_element_type=jnp.float32
            )
            for k, i, j, l in tap_list():
                for h in range(2):
                    slot = (l, p + 2 - i, (t + h + 1 - j) % rows)
                    value = part[k * o : (k + 1) * o, h * LANES : (h + 1) * LANES]
                    if slot in seen:
                        acc[slot] += value
                    else:
                        acc[slot] = value
                        seen.add(slot)
    for q in range(n + 2):
        for y in range(rows):
            total = (
                pltpu.roll(acc[0, q, y], 1, 1)
                + acc[1, q, y]
                + pltpu.roll(acc[2, q, y], LANES - 1, 1)
            )
            if q == 0:
                low_ref[y] = total.astype(low_ref.dtype)
            elif q == n + 1:
                high_ref[y] = total.astype(high_ref.dtype)
            else:
                own_ref[(q - 1) * rows + y] = total
            if q == 1:
                low_ref[rows + y] = total.astype(low_ref.dtype)
            if q == n:
                high_ref[rows + y] = total.astype(high_ref.dtype)


def gradient_body(
    n,
    rows,
    o,
    scale,
    me_ref,
    own_ref,
    low_ref,
    high_ref,
    below_ref,
    above_ref,
    bias_ref,
    go_ref,
    go_below_ref,
    go_above_ref,
    back_ref,
    act_ref,
    total_ref,
    s_ref,
    other_ref,
    mine_ref,
    w_ref,
    wide_ref,
):
    f32, bf16 = jnp.float32, jnp.bfloat16
    for b in range(8):
        place = pl.ds(pl.multiple_of(owner(me_ref, b) * o, o), o)
        w_ref[b * o : (b + 1) * o] = back_ref[place]
    total = jnp.zeros((o, LANES), f32)
    for q in range(n + 2):
        for y in range(rows):
            if q == 0:
                pre = below_ref[rows + y].astype(f32) + low_ref[y].astype(f32)
                go = go_below_ref[y]
            elif q == n + 1:
                pre = above_ref[rows + y].astype(f32) + high_ref[y].astype(f32)
                go = go_above_ref[y]
            else:
                pre = own_ref[(q - 1) * rows + y]
                go = go_ref[(q - 1) * rows + y]
                if q == 1:
                    pre = pre + below_ref[y].astype(f32)
                if q == n:
                    pre = pre + above_ref[y].astype(f32)
            pre = pre + bias_ref[...]
            s = jax.nn.sigmoid(pre)
            slope = s * (1.0 + pre * (1.0 - s))
            value = (go.astype(f32) * slope).astype(bf16)
            wide = value.astype(f32)
            if 1 <= q <= n:
                wide_ref[pl.ds((q - 1) * rows + y, o, stride=n * rows), :] = pre * s
                total = total + wide
            shifts = [
                pltpu.roll(wide, LANES - 1, 1).astype(bf16),
                value,
                pltpu.roll(wide, 1, 1).astype(bf16),
            ]
            for k, i, j, l in tap_list():
                p = q - 2 + i
                if 0 <= p < n:
                    at = (p * rows + (y + j - 1) % rows) * LANES
                    s_ref[k * o : (k + 1) * o, at : at + LANES] = shifts[l]
    act_ref[...] = wide_ref[...].reshape(act_ref.shape).astype(bf16)
    total_ref[...] = jnp.broadcast_to(
        jnp.sum(total, axis=1, keepdims=True) * scale, total_ref.shape
    )
    input_grad(n * rows, o, w_ref[...], s_ref, [(ref, r) for ref in (mine_ref, other_ref) for r in range(4)])


def input_grad(cells, o, w, s_ref, outs):
    for t in range(0, cells, 2):
        part = jnp.dot(
            w, s_ref[:, t * LANES : (t + 2) * LANES], preferred_element_type=jnp.float32
        ).astype(outs[0][0].dtype)
        for h in range(2):
            for r, (out_ref, at) in enumerate(outs):
                cut = part[r * o : (r + 1) * o, h * LANES : (h + 1) * LANES]
                out_ref[at, t + h] = cut


def filter_grad_body(scale, taps, o, s_ref, x_ref, total_ref, first_ref, second_ref):
    full = lax.dot_general(
        s_ref[...], x_ref[...], (((1,), (1,)), ((), ())), preferred_element_type=jnp.float32
    )
    full = (full * scale).astype(first_ref.dtype)
    first_ref[...] = full[: taps * o]
    second_ref[: (27 - taps) * o] = full[taps * o :]
    row = jnp.concatenate([total_ref[...]] * (second_ref.shape[1] // LANES), axis=1)
    second_ref[(27 - taps) * o :] = row.astype(second_ref.dtype)


def pair_body(a_ref, b_ref, _, out_ref):
    f32 = jnp.float32
    out_ref[...] = (a_ref[...].astype(f32) + b_ref[...].astype(f32)).astype(out_ref.dtype)


def core_sum_body(mine_ref, other_ref, *outs):
    for r, out_ref in enumerate(outs):
        total = mine_ref[r].astype(jnp.float32) + other_ref[r].astype(jnp.float32)
        out_ref[...] = total.astype(out_ref.dtype)


def sum_body(a_ref, b_ref, c_ref, d_ref, out_ref):
    f32 = jnp.float32
    total = b_ref[...].astype(f32) + c_ref[...].astype(f32) + d_ref[...].astype(f32)
    out_ref[...] = a_ref[...] + total


def last_body(
    taps, a_ref, b_ref, c_ref, d_ref, g_ref, out_ref, bias_ref, grad_ref, wide_ref
):
    o = out_ref.shape[1]
    f32 = jnp.float32
    cells = g_ref.shape[0]
    for k in range(cells):
        wide_ref[pl.ds(k, o, stride=cells), :] = g_ref[k]
    grad_ref[...] = wide_ref[...].reshape(grad_ref.shape).astype(grad_ref.dtype)
    for k in range(27):
        left, right, at = (a_ref, b_ref, k) if k < taps else (c_ref, d_ref, k - taps)
        cut = slice(at * o, (at + 1) * o)
        out_ref[k] = left[cut].astype(f32) + right[cut].astype(f32)
    cut = slice((27 - taps) * o, (28 - taps) * o)
    column = (c_ref[cut].astype(f32) + d_ref[cut].astype(f32))[:, :o]
    same = lax.broadcasted_iota(jnp.int32, (o, o), 0) == lax.broadcasted_iota(jnp.int32, (o, o), 1)
    bias_ref[...] = jnp.sum(jnp.where(same, column, 0.0), axis=0, keepdims=True)


def in_hbm(value):
    return pltpu.with_memory_space_constraint(value, pltpu.HBM)


def rotate(value, axis, step):
    count = lax.axis_size(axis)
    return lax.ppermute(value, axis, [(i, (i + step) % count) for i in range(count)])


def swap(value, axis, bit):
    return lax.ppermute(value, axis, [(i, i ^ bit) for i in range(lax.axis_size(axis))])


def cross(value, phase):
    slabs, chans = lax.axis_size("slab"), lax.axis_size("chan")
    pairs = [
        (s * chans + c, (s ^ (1 + (c + phase) % 2)) * chans + c)
        for s in range(slabs)
        for c in range(chans)
    ]
    return lax.ppermute(value, ("slab", "chan"), pairs)


def on_device(x_in, weight, bias_vec, grad_out):
    o, _, c_all = weight.shape
    _, n, rows, depth = x_in.shape
    f32, bf16 = jnp.float32, jnp.bfloat16
    cells = n * rows
    flops = 2 * 27 * o * c_all * cells * depth
    scale = 1.0 / math.sqrt(lax.axis_size("slab") * cells * depth)
    me = lax.axis_index("chan").astype(jnp.int32).reshape(1)

    block_wide = [pltpu.VMEM((o * cells, depth), f32)]

    x_b = swap(x_in, "chan", 4)
    x_a = swap(x_in, "chan", 2)
    x_side = swap(x_in, "chan", 1)
    x_own, go, go_low, go_high, w_flat, w_back, bias = call(
        functools.partial(prepare_body, n, rows),
        [
            shape_of((o, n, rows, depth), bf16),
            shape_of((cells, o, depth), bf16),
            shape_of((rows, o, depth), bf16),
            shape_of((rows, o, depth), bf16),
            shape_of((27 * o, c_all), bf16),
            shape_of((c_all, 27 * o), bf16),
            shape_of((o, LANES), f32),
        ],
        [in_hbm(a) for a in (x_in, grad_out, jnp.transpose(weight, (1, 0, 2)), bias_vec[None, :])],
        [HBM] * 4,
        [
            pltpu.VMEM((o, n, rows, depth), bf16),
            pltpu.VMEM((27, o, c_all), bf16),
            pltpu.VMEM((1, o), bf16),
            *block_wide,
            pltpu.SemaphoreType.DMA((4,)),
        ],
        name="prepare",
    )
    go_above = rotate(go_low, "slab", -1)
    go_below = rotate(go_high, "slab", 1)
    x_b, w_flat = lax.optimization_barrier((x_b, w_flat))
    x_ab = swap(x_b, "chan", 2)
    late_b, go_above, go_below = lax.optimization_barrier((x_b, go_above, go_below))
    x_a_side = swap(x_a, "chan", 1)
    x_b_side = swap(late_b, "chan", 1)
    early, late = (0, 1, 2, 3, 4, 5, 6), (7,)
    (x_all,) = call(
        functools.partial(assemble_body, early),
        [shape_of((c_all, cells * depth), bf16)],
        [me, x_own, x_a, x_b, x_ab, x_side, x_a_side, x_b_side],
        [SMEM] + [VMEM] * 7,
        block_wide,
        flops=ASSEMBLE_FLOPS,
        name="assemble",
    )
    x_ab_side = swap(x_ab, "chan", 1)
    own, low, high, x_all = call(
        functools.partial(forward_body, n, rows, o, late),
        [
            shape_of((cells, o, depth), f32),
            shape_of((2 * rows, o, depth), bf16),
            shape_of((2 * rows, o, depth), bf16),
            shape_of((c_all, cells * depth), bf16),
        ],
        [me, w_flat, x_ab_side, x_all],
        [SMEM] + [VMEM] * 3,
        [pltpu.VMEM((3, n + 2, rows, o, depth), f32), *block_wide],
        flops=FORWARD_FLOPS,
        name="forward",
        aliases={3: 3},
    )
    above = rotate(low, "slab", -1)
    below = rotate(high, "slab", 1)
    act, total, stacked, other, mine = call(
        functools.partial(gradient_body, n, rows, o, scale),
        [
            shape_of((o, n, rows, depth), bf16),
            shape_of((o, LANES), f32),
            shape_of((27 * o, cells * depth), bf16),
            shape_of((4, cells, o, depth), bf16),
            shape_of((4, cells, o, depth), bf16),
        ],
        [me, own, low, high, below, above, bias, go, go_below, go_above, w_back],
        [SMEM] + [VMEM] * 10,
        [pltpu.VMEM((c_all, 27 * o), bf16), *block_wide],
        flops=flops,
        name="gradient",
    )
    other = swap(other, "chan", 1)
    taps = 14
    first, second = call(
        functools.partial(filter_grad_body, scale, taps, o),
        [shape_of((taps * o, c_all), bf16), shape_of(((28 - taps) * o, c_all), bf16)],
        [stacked, x_all, total],
        flops=flops,
        name="filter_grad",
    )
    first_far = cross(first, 0)
    second_far = cross(second, 0)
    g_own, g_a, g_b, g_ab = call(
        core_sum_body,
        [shape_of((cells, o, depth), f32)] + [shape_of((cells, o, depth), bf16)] * 3,
        [mine, other],
        name="core_sum",
    )
    g_ab = swap(g_ab, "chan", 6)
    g_b = swap(g_b, "chan", 4)
    g_a = swap(g_a, "chan", 2)
    first, second = (
        call(
            pair_body,
            [shape_of(a.shape, bf16)],
            [a, b, g_own],
            [VMEM] * 2 + [ANY],
            name="pair_sum",
        )[0]
        for a, b in ((first, first_far), (second, second_far))
    )
    first_far = cross(first, 1)
    second_far = cross(second, 1)
    (g_own,) = call(
        sum_body,
        [shape_of((cells, o, depth), f32)],
        [g_own, g_b, g_ab, g_a],
        flops=SUM_FLOPS,
        name="sum",
    )
    weight_grad, bias_grad, grad_in = call(
        functools.partial(last_body, taps),
        [
            shape_of((27, o, c_all), f32),
            shape_of((1, o), f32),
            shape_of((o, n, rows, depth), bf16),
        ],
        [first, first_far, second, second_far, g_own],
        scratch=block_wide,
        name="last",
    )
    return act, grad_in, jnp.transpose(weight_grad, (1, 0, 2)), bias_grad[0]


def solution(mesh):
    placed = (
        P("chan", "slab", None, None),
        P("chan", None, None),
        P("chan"),
        P("chan", "slab", None, None),
    )

    def body(x_in, weight, bias_vec, grad_out):
        tiled = (
            weight.shape[0] % 32 == 0
            and x_in.shape[3] == LANES
            and lax.axis_size("slab") == 4
            and lax.axis_size("chan") == 8
            and x_in.shape[1] >= 2
        )
        return (on_device if tiled else plain)(x_in, weight, bias_vec, grad_out)

    return jax.shard_map(
        body,
        mesh=mesh,
        in_specs=placed,
        out_specs=(
            P("chan", "slab", None, None),
            P("chan", "slab", None, None),
            P("chan", None, None),
            P("chan"),
        ),
        check_vma=False,
    )
```

```python
import functools
import math

import jax
import jax.numpy as jnp
from jax import lax
from jax.experimental import pallas as pl
from jax.experimental.pallas import tpu as pltpu
from jax.sharding import PartitionSpec as P

LANES = 128
FORWARD_FLOPS = 9 * 10**8
SUM_FLOPS = 24 * 10**8
ASSEMBLE_FLOPS = 40 * 10**8
VMEM = pl.BlockSpec(memory_space=pltpu.VMEM)
ANY = pl.BlockSpec(memory_space=pl.ANY)
HBM = pl.BlockSpec(memory_space=pltpu.HBM)
SMEM = pl.BlockSpec(memory_space=pltpu.SMEM)


def with_halo(block, sides, width):
    for axis, dim in sides:
        count = lax.axis_size(axis)
        forward = [(i, i + 1) for i in range(count - 1)]
        forward.append((count - 1, 0))
        backward = [(target, source) for source, target in forward]
        low = lax.ppermute(
            lax.slice_in_dim(block, block.shape[dim] - width, None, axis=dim), axis, forward
        )
        high = lax.ppermute(lax.slice_in_dim(block, 0, width, axis=dim), axis, backward)
        block = jnp.concatenate([low, block, high], axis=dim)
    return block


def tap_list():
    return [(9 * i + 3 * j + l, i, j, l) for i in range(3) for j in range(3) for l in range(3)]


def plain(x_in, weight, bias_vec, grad_out):
    out_local, n_taps, in_total = weight.shape
    n_planes, n_rows, n_depth = (x_in.shape[1], x_in.shape[2], x_in.shape[3])
    rimmed = with_halo(x_in, (("slab", 1),), 1)
    padded = lax.all_gather(rimmed, "chan", axis=0, tiled=True)
    own_planes = padded[:, 1 : n_planes + 1]
    pre_act = (
        jnp.zeros((out_local, n_planes, n_rows, n_depth), jnp.float32)
        + bias_vec.astype(jnp.float32)[:, None, None, None]
    )
    for i in range(3):
        w_plane = jnp.transpose(weight[:, 9 * i : 9 * i + 9], (1, 0, 2)).reshape(
            9 * out_local, in_total
        )
        plane_part = jnp.dot(
            w_plane,
            padded[:, i : i + n_planes].reshape(in_total, -1),
            preferred_element_type=jnp.float32,
        )
        plane_part = plane_part.reshape(9, out_local, n_planes, n_rows, n_depth)
        for j in range(3):
            for l in range(3):
                pre_act = pre_act + jnp.roll(plane_part[3 * j + l], (1 - j, 1 - l), axis=(2, 3))
    sigmoid_v = jax.nn.sigmoid(pre_act)
    activation = (pre_act * sigmoid_v).astype(jnp.bfloat16)
    slope = sigmoid_v * (1.0 + pre_act * (1.0 - sigmoid_v))
    grad_pre = (grad_out.astype(jnp.float32) * slope).astype(jnp.bfloat16)
    padded_grad = with_halo(grad_pre, (("slab", 1),), 1)
    shifted = jnp.stack(
        [
            jnp.roll(padded_grad[:, 2 - i : 2 - i + n_planes], (j - 1, l - 1), axis=(2, 3))
            for k, i, j, l in tap_list()
        ],
        0,
    )
    shifted = shifted.reshape(n_taps * out_local, -1)
    grad_scale = 1.0 / math.sqrt(lax.axis_size("slab") * n_planes * n_rows * n_depth)
    filter_local = lax.dot_general(
        shifted,
        own_planes.reshape(in_total, -1),
        (((1,), (1,)), ((), ())),
        preferred_element_type=jnp.float32,
    )
    filter_part = (
        jnp.transpose(filter_local.reshape(n_taps, out_local, in_total), (1, 0, 2)) * grad_scale
    )
    bias_part = grad_scale * jnp.sum(grad_pre.astype(jnp.float32), axis=(1, 2, 3))
    bias_row = jnp.concatenate(
        [bias_part[:, None, None], jnp.zeros((out_local, 1, in_total - 1), jnp.float32)], 2
    )
    summed_filters = lax.psum(jnp.concatenate([filter_part, bias_row], 1), "slab")
    weight_grad = summed_filters[:, :n_taps]
    bias_grad = summed_filters[:, n_taps, 0]
    flat_w = jnp.transpose(weight, (1, 0, 2)).reshape(n_taps * out_local, in_total)
    product = lax.dot_general(
        flat_w, shifted, (((0,), (0,)), ((), ())), preferred_element_type=jnp.float32
    )
    grad_in = lax.psum_scatter(
        product.reshape(
            in_total // lax.axis_size("chan") * lax.axis_size("chan"), n_planes, n_rows, n_depth
        ),
        "chan",
        scatter_dimension=0,
        tiled=True,
    )
    return (activation, grad_in.astype(jnp.bfloat16), weight_grad, bias_grad)


def call(body, out_shape, operands, specs=None, scratch=(), flops=0, name=None, aliases=None, out_specs=None):
    read = sum(math.prod(a.shape) * a.dtype.itemsize for a in operands)
    written = sum(math.prod(a.shape) * a.dtype.itemsize for a in out_shape)
    return pl.pallas_call(
        body,
        out_shape=out_shape,
        in_specs=specs or [VMEM] * len(operands),
        out_specs=out_specs or [VMEM] * len(out_shape),
        scratch_shapes=list(scratch),
        input_output_aliases=aliases or {},
        compiler_params=pltpu.CompilerParams(vmem_limit_bytes=24 * 2**20),
        cost_estimate=pl.CostEstimate(
            flops=flops, bytes_accessed=read + written, transcendentals=0
        ),
        name=name,
    )(*operands)


def shape_of(shape, dtype):
    return jax.ShapeDtypeStruct(shape, dtype)


def by_parity(slab_ref, a, b):
    even = lax.rem(slab_ref[0], 2) == 0
    f32 = jnp.float32
    wide = a.astype(f32), b.astype(f32)
    return (
        jnp.where(even, wide[0], wide[1]).astype(a.dtype),
        jnp.where(even, wide[1], wide[0]).astype(a.dtype),
    )


def turned(value, wide_ref):
    o = value.shape[0]
    cells = wide_ref.shape[0] // o
    wide_ref[...] = value.astype(jnp.float32).reshape(wide_ref.shape)
    return [
        wide_ref[pl.ds(k, o, stride=cells), :].astype(value.dtype) for k in range(cells)
    ]


def prepare_body(
    n,
    rows,
    slab_ref,
    x_hbm,
    go_hbm,
    w_hbm,
    bias_hbm,
    x_ref,
    go_ref,
    go_first_ref,
    go_second_ref,
    flat_ref,
    back_ref,
    bias_ref,
    go_in,
    w_in,
    bias_in,
    wide_ref,
    sems,
):
    copies = [
        pltpu.make_async_copy(source, target, sems.at[at])
        for at, (source, target) in enumerate(
            [(go_hbm, go_in), (w_hbm, w_in), (bias_hbm, bias_in), (x_hbm, x_ref)]
        )
    ]
    for copy in copies:
        copy.start()
    copies[0].wait()
    values = turned(go_in[...], wide_ref)
    for k, value in enumerate(values):
        go_ref[k] = value
    for y in range(rows):
        low, high = values[y], values[(n - 1) * rows + y]
        go_first_ref[y], go_second_ref[y] = by_parity(slab_ref, high, low)
    copies[1].wait()
    copies[2].wait()
    copies[3].wait()
    flat = w_in[...].reshape(flat_ref.shape)
    flat_ref[...] = flat
    back_ref[...] = jnp.transpose(flat)
    o = bias_ref.shape[0]
    row = jnp.broadcast_to(bias_in[...].astype(jnp.float32), (o, o))
    same = lax.broadcasted_iota(jnp.int32, (o, o), 0) == lax.broadcasted_iota(jnp.int32, (o, o), 1)
    column = jnp.sum(jnp.where(same, row, 0.0), axis=1, keepdims=True)
    bias_ref[...] = jnp.broadcast_to(column, bias_ref.shape)


def place_block(me_ref, b, block_ref, x_ref, wide_ref):
    o = block_ref.shape[0]
    place = pl.ds(pl.multiple_of(owner(me_ref, b) * o, o), o)
    for k, value in enumerate(turned(block_ref[...], wide_ref)):
        x_ref[place, k * LANES : (k + 1) * LANES] = value


def assemble_body(places, me_ref, *refs):
    blocks, (x_ref, wide_ref) = refs[: len(places)], refs[-2:]
    for b, block in zip(places, blocks):
        place_block(me_ref, b, block, x_ref, wide_ref)


def owner(me_ref, b):
    return jnp.bitwise_xor(me_ref[0], 2 * (b % 4) + b // 4)


def forward_body(n, rows, o, places, me_ref, slab_ref, w_ref, *refs):
    blocks = refs[: len(places)]
    own_ref, first_ref, second_ref, x_ref, acc, wide_ref = refs[len(places) + 1 :]
    for b, block in zip(places, blocks):
        place_block(me_ref, b, block, x_ref, wide_ref)
    w = w_ref[...]
    seen = set()
    for p in range(n):
        for t in range(0, rows, 2):
            at = (p * rows + t) * LANES
            part = jnp.dot(
                w, x_ref[:, at : at + 2 * LANES], preferred_element_type=jnp.float32
            )
            for k, i, j, l in tap_list():
                for h in range(2):
                    slot = (l, p + 2 - i, (t + h + 1 - j) % rows)
                    value = part[k * o : (k + 1) * o, h * LANES : (h + 1) * LANES]
                    if slot in seen:
                        acc[slot] += value
                    else:
                        acc[slot] = value
                        seen.add(slot)
    for y in range(rows):
        totals = [
            pltpu.roll(acc[0, q, y], 1, 1) + acc[1, q, y] + pltpu.roll(acc[2, q, y], LANES - 1, 1)
            for q in range(n + 2)
        ]
        for p in range(n):
            own_ref[p * rows + y] = totals[p + 1]
        for at, low, high in ((y, 0, n + 1), (rows + y, 1, n)):
            first, second = by_parity(slab_ref, totals[high], totals[low])
            first_ref[at] = first.astype(first_ref.dtype)
            second_ref[at] = second.astype(second_ref.dtype)


def gradient_body(
    n,
    rows,
    o,
    scale,
    me_ref,
    slab_ref,
    own_ref,
    first_ref,
    second_ref,
    first_in_ref,
    second_in_ref,
    bias_ref,
    go_ref,
    go_first_ref,
    go_second_ref,
    back_ref,
    act_ref,
    total_ref,
    s_ref,
    other_ref,
    mine_ref,
    w_ref,
    wide_ref,
):
    f32, bf16 = jnp.float32, jnp.bfloat16
    for b in range(8):
        place = pl.ds(pl.multiple_of(owner(me_ref, b) * o, o), o)
        w_ref[b * o : (b + 1) * o] = back_ref[place]
    total = jnp.zeros((o, LANES), f32)
    even = lax.rem(slab_ref[0], 2) == 0

    def above(first, second, at):
        return jnp.where(even, first[at].astype(f32), second[at].astype(f32))

    def below(first, second, at):
        return above(second, first, at)

    for q in range(n + 2):
        for y in range(rows):
            if q == 0:
                pre = below(first_in_ref, second_in_ref, rows + y) + below(first_ref, second_ref, y)
                go = below(go_first_ref, go_second_ref, y)
            elif q == n + 1:
                pre = above(first_in_ref, second_in_ref, rows + y) + above(first_ref, second_ref, y)
                go = above(go_first_ref, go_second_ref, y)
            else:
                pre = own_ref[(q - 1) * rows + y]
                go = go_ref[(q - 1) * rows + y]
                if q == 1:
                    pre = pre + below(first_in_ref, second_in_ref, y)
                if q == n:
                    pre = pre + above(first_in_ref, second_in_ref, y)
            pre = pre + bias_ref[...]
            s = jax.nn.sigmoid(pre)
            slope = s * (1.0 + pre * (1.0 - s))
            value = (go.astype(f32) * slope).astype(bf16)
            wide = value.astype(f32)
            if 1 <= q <= n:
                wide_ref[pl.ds((q - 1) * rows + y, o, stride=n * rows), :] = pre * s
                total = total + wide
            shifts = [
                pltpu.roll(wide, LANES - 1, 1).astype(bf16),
                value,
                pltpu.roll(wide, 1, 1).astype(bf16),
            ]
            for k, i, j, l in tap_list():
                p = q - 2 + i
                if 0 <= p < n:
                    at = (p * rows + (y + j - 1) % rows) * LANES
                    s_ref[k * o : (k + 1) * o, at : at + LANES] = shifts[l]
    act_ref[...] = wide_ref[...].reshape(act_ref.shape).astype(bf16)
    total_ref[...] = jnp.broadcast_to(
        jnp.sum(total, axis=1, keepdims=True) * scale, total_ref.shape
    )
    input_grad(n * rows, o, w_ref[...], s_ref, [(ref, r) for ref in (mine_ref, other_ref) for r in range(4)])


def input_grad(cells, o, w, s_ref, outs):
    for t in range(0, cells, 2):
        part = jnp.dot(
            w, s_ref[:, t * LANES : (t + 2) * LANES], preferred_element_type=jnp.float32
        ).astype(outs[0][0].dtype)
        for h in range(2):
            for r, (out_ref, at) in enumerate(outs):
                cut = part[r * o : (r + 1) * o, h * LANES : (h + 1) * LANES]
                out_ref[at, t + h] = cut


def filter_grad_body(scale, taps, o, s_ref, x_ref, total_ref, first_ref, second_ref):
    full = lax.dot_general(
        s_ref[...], x_ref[...], (((1,), (1,)), ((), ())), preferred_element_type=jnp.float32
    )
    full = (full * scale).astype(first_ref.dtype)
    first_ref[...] = full[: taps * o]
    second_ref[: (27 - taps) * o] = full[taps * o :]
    row = jnp.concatenate([total_ref[...]] * (second_ref.shape[1] // LANES), axis=1)
    second_ref[(27 - taps) * o :] = row.astype(second_ref.dtype)


def pair_body(a_ref, b_ref, _, out_ref):
    f32 = jnp.float32
    out_ref[...] = (a_ref[...].astype(f32) + b_ref[...].astype(f32)).astype(out_ref.dtype)


def core_sum_body(mine_ref, other_ref, *outs):
    for r, out_ref in enumerate(outs):
        total = mine_ref[r].astype(jnp.float32) + other_ref[r].astype(jnp.float32)
        out_ref[...] = total.astype(out_ref.dtype)


def sum_body(a_ref, b_ref, c_ref, d_ref, out_ref):
    f32 = jnp.float32
    total = b_ref[...].astype(f32) + c_ref[...].astype(f32) + d_ref[...].astype(f32)
    out_ref[...] = a_ref[...] + total


def last_body(
    taps, a_ref, b_ref, c_ref, d_ref, g_ref, out_hbm, bias_ref, grad_hbm, wide_ref, grad_ref, out_ref, sems
):
    o = out_ref.shape[1]
    f32 = jnp.float32
    cells = g_ref.shape[0]
    copies = []

    def send(source, target):
        copies.append(pltpu.make_async_copy(source, target, sems.at[len(copies)]))
        copies[-1].start()

    for k in range(cells):
        wide_ref[pl.ds(k, o, stride=cells), :] = g_ref[k]
    grad_ref[...] = wide_ref[...].reshape(grad_ref.shape).astype(grad_ref.dtype)
    send(grad_ref, grad_hbm)
    for k in range(27):
        left, right, at = (a_ref, b_ref, k) if k < taps else (c_ref, d_ref, k - taps)
        cut = slice(at * o, (at + 1) * o)
        out_ref[k] = left[cut].astype(f32) + right[cut].astype(f32)
        if k % 9 == 8:
            send(out_ref.at[pl.ds(k - 8, 9)], out_hbm.at[pl.ds(k - 8, 9)])
    cut = slice((27 - taps) * o, (28 - taps) * o)
    column = (c_ref[cut].astype(f32) + d_ref[cut].astype(f32))[:, :o]
    same = lax.broadcasted_iota(jnp.int32, (o, o), 0) == lax.broadcasted_iota(jnp.int32, (o, o), 1)
    bias_ref[...] = jnp.sum(jnp.where(same, column, 0.0), axis=0, keepdims=True)
    for copy in copies:
        copy.wait()


def in_hbm(value):
    return pltpu.with_memory_space_constraint(value, pltpu.HBM)


def swap(value, axis, bit):
    return lax.ppermute(value, axis, [(i, i ^ bit) for i in range(lax.axis_size(axis))])


def cross(value, phase):
    slabs, chans = lax.axis_size("slab"), lax.axis_size("chan")
    pairs = [
        (s * chans + c, (s ^ (1 + (c + phase) % 2)) * chans + c)
        for s in range(slabs)
        for c in range(chans)
    ]
    return lax.ppermute(value, ("slab", "chan"), pairs)


def on_device(x_in, weight, bias_vec, grad_out):
    o, _, c_all = weight.shape
    _, n, rows, depth = x_in.shape
    f32, bf16 = jnp.float32, jnp.bfloat16
    cells = n * rows
    flops = 2 * 27 * o * c_all * cells * depth
    scale = 1.0 / math.sqrt(lax.axis_size("slab") * cells * depth)
    me = lax.axis_index("chan").astype(jnp.int32).reshape(1)
    slab = lax.axis_index("slab").astype(jnp.int32).reshape(1)

    block_wide = [pltpu.VMEM((o * cells, depth), f32)]

    x_b = swap(x_in, "chan", 4)
    x_a = swap(x_in, "chan", 2)
    x_side = swap(x_in, "chan", 1)
    x_own, go, go_first, go_second, w_flat, w_back, bias = call(
        functools.partial(prepare_body, n, rows),
        [
            shape_of((o, n, rows, depth), bf16),
            shape_of((cells, o, depth), bf16),
            shape_of((rows, o, depth), bf16),
            shape_of((rows, o, depth), bf16),
            shape_of((27 * o, c_all), bf16),
            shape_of((c_all, 27 * o), bf16),
            shape_of((o, LANES), f32),
        ],
        [slab] + [in_hbm(a) for a in (x_in, grad_out, jnp.transpose(weight, (1, 0, 2)), bias_vec[None, :])],
        [SMEM] + [HBM] * 4,
        [
            pltpu.VMEM((o, n, rows, depth), bf16),
            pltpu.VMEM((27, o, c_all), bf16),
            pltpu.VMEM((1, o), bf16),
            *block_wide,
            pltpu.SemaphoreType.DMA((4,)),
        ],
        name="prepare",
    )
    go_first = swap(go_first, "slab", 1)
    go_second = swap(go_second, "slab", 3)
    x_b, w_flat = lax.optimization_barrier((x_b, w_flat))
    x_ab = swap(x_b, "chan", 2)
    late_b, go_first, go_second = lax.optimization_barrier((x_b, go_first, go_second))
    x_a_side = swap(x_a, "chan", 1)
    x_b_side = swap(late_b, "chan", 1)
    early, late = (0, 1, 2, 3, 4, 5, 6), (7,)
    (x_all,) = call(
        functools.partial(assemble_body, early),
        [shape_of((c_all, cells * depth), bf16)],
        [me, x_own, x_a, x_b, x_ab, x_side, x_a_side, x_b_side],
        [SMEM] + [VMEM] * 7,
        block_wide,
        flops=ASSEMBLE_FLOPS,
        name="assemble",
    )
    x_ab_side = swap(x_ab, "chan", 1)
    own, first, second, x_all = call(
        functools.partial(forward_body, n, rows, o, late),
        [
            shape_of((cells, o, depth), f32),
            shape_of((2 * rows, o, depth), bf16),
            shape_of((2 * rows, o, depth), bf16),
            shape_of((c_all, cells * depth), bf16),
        ],
        [me, slab, w_flat, x_ab_side, x_all],
        [SMEM] * 2 + [VMEM] * 3,
        [pltpu.VMEM((3, n + 2, rows, o, depth), f32), *block_wide],
        flops=FORWARD_FLOPS,
        name="forward",
        aliases={4: 3},
    )
    first_in = swap(first, "slab", 1)
    second_in = swap(second, "slab", 3)
    act, total, stacked, other, mine = call(
        functools.partial(gradient_body, n, rows, o, scale),
        [
            shape_of((o, n, rows, depth), bf16),
            shape_of((o, LANES), f32),
            shape_of((27 * o, cells * depth), bf16),
            shape_of((4, cells, o, depth), bf16),
            shape_of((4, cells, o, depth), bf16),
        ],
        [me, slab, own, first, second, first_in, second_in, bias, go, go_first, go_second, w_back],
        [SMEM] * 2 + [VMEM] * 10,
        [pltpu.VMEM((c_all, 27 * o), bf16), *block_wide],
        flops=flops,
        name="gradient",
    )
    other = swap(other, "chan", 1)
    taps = 14
    first, second = call(
        functools.partial(filter_grad_body, scale, taps, o),
        [shape_of((taps * o, c_all), bf16), shape_of(((28 - taps) * o, c_all), bf16)],
        [stacked, x_all, total],
        flops=flops,
        name="filter_grad",
    )
    first_far = cross(first, 0)
    second_far = cross(second, 0)
    g_own, g_a, g_b, g_ab = call(
        core_sum_body,
        [shape_of((cells, o, depth), f32)] + [shape_of((cells, o, depth), bf16)] * 3,
        [mine, other],
        name="core_sum",
    )
    g_ab = swap(g_ab, "chan", 6)
    g_b = swap(g_b, "chan", 4)
    g_a = swap(g_a, "chan", 2)
    first, second = (
        call(
            pair_body,
            [shape_of(a.shape, bf16)],
            [a, b, g_own],
            [VMEM] * 2 + [ANY],
            name="pair_sum",
        )[0]
        for a, b in ((first, first_far), (second, second_far))
    )
    first_far = cross(first, 1)
    second_far = cross(second, 1)
    (g_own,) = call(
        sum_body,
        [shape_of((cells, o, depth), f32)],
        [g_own, g_b, g_ab, g_a],
        flops=SUM_FLOPS,
        name="sum",
    )
    weight_grad, bias_grad, grad_in = call(
        functools.partial(last_body, taps),
        [
            shape_of((27, o, c_all), f32),
            shape_of((1, o), f32),
            shape_of((o, n, rows, depth), bf16),
        ],
        [first, first_far, second, second_far, g_own],
        scratch=[
            *block_wide,
            pltpu.VMEM((o, n, rows, depth), bf16),
            pltpu.VMEM((27, o, c_all), f32),
            pltpu.SemaphoreType.DMA((4,)),
        ],
        name="last",
        out_specs=[HBM, VMEM, HBM],
    )
    return act, grad_in, jnp.transpose(weight_grad, (1, 0, 2)), bias_grad[0]


def solution(mesh):
    placed = (
        P("chan", "slab", None, None),
        P("chan", None, None),
        P("chan"),
        P("chan", "slab", None, None),
    )

    def body(x_in, weight, bias_vec, grad_out):
        tiled = (
            weight.shape[0] % 32 == 0
            and x_in.shape[3] == LANES
            and lax.axis_size("slab") == 4
            and lax.axis_size("chan") == 8
            and x_in.shape[1] >= 2
        )
        return (on_device if tiled else plain)(x_in, weight, bias_vec, grad_out)

    return jax.shard_map(
        body,
        mesh=mesh,
        in_specs=placed,
        out_specs=(
            P("chan", "slab", None, None),
            P("chan", "slab", None, None),
            P("chan", None, None),
            P("chan"),
        ),
        check_vma=False,
    )
```

```python
import functools
import math

import jax
import jax.numpy as jnp
from jax import lax
from jax.experimental import pallas as pl
from jax.experimental.pallas import tpu as pltpu
from jax.sharding import PartitionSpec as P

LANES = 128
FORWARD_FLOPS = 9 * 10**8
SUM_FLOPS = 24 * 10**8
ASSEMBLE_FLOPS = 40 * 10**8
VMEM = pl.BlockSpec(memory_space=pltpu.VMEM)
ANY = pl.BlockSpec(memory_space=pl.ANY)
HBM = pl.BlockSpec(memory_space=pltpu.HBM)
SMEM = pl.BlockSpec(memory_space=pltpu.SMEM)


def with_halo(block, sides, width):
    for axis, dim in sides:
        count = lax.axis_size(axis)
        forward = [(i, i + 1) for i in range(count - 1)]
        forward.append((count - 1, 0))
        backward = [(target, source) for source, target in forward]
        low = lax.ppermute(
            lax.slice_in_dim(block, block.shape[dim] - width, None, axis=dim), axis, forward
        )
        high = lax.ppermute(lax.slice_in_dim(block, 0, width, axis=dim), axis, backward)
        block = jnp.concatenate([low, block, high], axis=dim)
    return block


def tap_list():
    return [(9 * i + 3 * j + l, i, j, l) for i in range(3) for j in range(3) for l in range(3)]


def plain(x_in, weight, bias_vec, grad_out):
    out_local, n_taps, in_total = weight.shape
    n_planes, n_rows, n_depth = (x_in.shape[1], x_in.shape[2], x_in.shape[3])
    rimmed = with_halo(x_in, (("slab", 1),), 1)
    padded = lax.all_gather(rimmed, "chan", axis=0, tiled=True)
    own_planes = padded[:, 1 : n_planes + 1]
    pre_act = (
        jnp.zeros((out_local, n_planes, n_rows, n_depth), jnp.float32)
        + bias_vec.astype(jnp.float32)[:, None, None, None]
    )
    for i in range(3):
        w_plane = jnp.transpose(weight[:, 9 * i : 9 * i + 9], (1, 0, 2)).reshape(
            9 * out_local, in_total
        )
        plane_part = jnp.dot(
            w_plane,
            padded[:, i : i + n_planes].reshape(in_total, -1),
            preferred_element_type=jnp.float32,
        )
        plane_part = plane_part.reshape(9, out_local, n_planes, n_rows, n_depth)
        for j in range(3):
            for l in range(3):
                pre_act = pre_act + jnp.roll(plane_part[3 * j + l], (1 - j, 1 - l), axis=(2, 3))
    sigmoid_v = jax.nn.sigmoid(pre_act)
    activation = (pre_act * sigmoid_v).astype(jnp.bfloat16)
    slope = sigmoid_v * (1.0 + pre_act * (1.0 - sigmoid_v))
    grad_pre = (grad_out.astype(jnp.float32) * slope).astype(jnp.bfloat16)
    padded_grad = with_halo(grad_pre, (("slab", 1),), 1)
    shifted = jnp.stack(
        [
            jnp.roll(padded_grad[:, 2 - i : 2 - i + n_planes], (j - 1, l - 1), axis=(2, 3))
            for k, i, j, l in tap_list()
        ],
        0,
    )
    shifted = shifted.reshape(n_taps * out_local, -1)
    grad_scale = 1.0 / math.sqrt(lax.axis_size("slab") * n_planes * n_rows * n_depth)
    filter_local = lax.dot_general(
        shifted,
        own_planes.reshape(in_total, -1),
        (((1,), (1,)), ((), ())),
        preferred_element_type=jnp.float32,
    )
    filter_part = (
        jnp.transpose(filter_local.reshape(n_taps, out_local, in_total), (1, 0, 2)) * grad_scale
    )
    bias_part = grad_scale * jnp.sum(grad_pre.astype(jnp.float32), axis=(1, 2, 3))
    bias_row = jnp.concatenate(
        [bias_part[:, None, None], jnp.zeros((out_local, 1, in_total - 1), jnp.float32)], 2
    )
    summed_filters = lax.psum(jnp.concatenate([filter_part, bias_row], 1), "slab")
    weight_grad = summed_filters[:, :n_taps]
    bias_grad = summed_filters[:, n_taps, 0]
    flat_w = jnp.transpose(weight, (1, 0, 2)).reshape(n_taps * out_local, in_total)
    product = lax.dot_general(
        flat_w, shifted, (((0,), (0,)), ((), ())), preferred_element_type=jnp.float32
    )
    grad_in = lax.psum_scatter(
        product.reshape(
            in_total // lax.axis_size("chan") * lax.axis_size("chan"), n_planes, n_rows, n_depth
        ),
        "chan",
        scatter_dimension=0,
        tiled=True,
    )
    return (activation, grad_in.astype(jnp.bfloat16), weight_grad, bias_grad)


def call(body, out_shape, operands, specs=None, scratch=(), flops=0, name=None, aliases=None):
    read = sum(math.prod(a.shape) * a.dtype.itemsize for a in operands)
    written = sum(math.prod(a.shape) * a.dtype.itemsize for a in out_shape)
    return pl.pallas_call(
        body,
        out_shape=out_shape,
        in_specs=specs or [VMEM] * len(operands),
        out_specs=[VMEM] * len(out_shape),
        scratch_shapes=list(scratch),
        input_output_aliases=aliases or {},
        compiler_params=pltpu.CompilerParams(vmem_limit_bytes=24 * 2**20),
        cost_estimate=pl.CostEstimate(
            flops=flops, bytes_accessed=read + written, transcendentals=0
        ),
        name=name,
    )(*operands)


def shape_of(shape, dtype):
    return jax.ShapeDtypeStruct(shape, dtype)


def turned(value, wide_ref):
    o = value.shape[0]
    cells = wide_ref.shape[0] // o
    wide_ref[...] = value.astype(jnp.float32).reshape(wide_ref.shape)
    return [
        wide_ref[pl.ds(k, o, stride=cells), :].astype(value.dtype) for k in range(cells)
    ]


def prepare_body(
    n,
    rows,
    x_hbm,
    go_hbm,
    w_hbm,
    bias_hbm,
    x_ref,
    go_ref,
    go_low_ref,
    go_high_ref,
    flat_ref,
    own_0_ref,
    own_1_ref,
    rim_0_ref,
    rim_1_ref,
    bias_ref,
    go_in,
    w_in,
    bias_in,
    wide_ref,
    sems,
):
    copies = [
        pltpu.make_async_copy(source, target, sems.at[at])
        for at, (source, target) in enumerate(
            [(go_hbm, go_in), (w_hbm, w_in), (bias_hbm, bias_in), (x_hbm, x_ref)]
        )
    ]
    for copy in copies:
        copy.start()
    copies[0].wait()
    for k, value in enumerate(turned(go_in[...], wide_ref)):
        go_ref[k] = value
        if k < rows:
            go_low_ref[k] = value
        if k >= (n - 1) * rows:
            go_high_ref[k - (n - 1) * rows] = value
    copies[1].wait()
    copies[2].wait()
    copies[3].wait()
    flat = w_in[...].reshape(flat_ref.shape)
    flat_ref[...] = flat
    third = flat.shape[0] // 3
    own_0_ref[...] = jnp.transpose(flat[: 2 * third])
    own_1_ref[...] = jnp.transpose(flat[third:])
    rim_0_ref[...] = jnp.transpose(flat[2 * third :])
    rim_1_ref[...] = jnp.transpose(flat[:third])
    o = bias_ref.shape[0]
    row = jnp.broadcast_to(bias_in[...].astype(jnp.float32), (o, o))
    same = lax.broadcasted_iota(jnp.int32, (o, o), 0) == lax.broadcasted_iota(jnp.int32, (o, o), 1)
    column = jnp.sum(jnp.where(same, row, 0.0), axis=1, keepdims=True)
    bias_ref[...] = jnp.broadcast_to(column, bias_ref.shape)


def place_block(me_ref, b, block_ref, x_ref, wide_ref):
    o = block_ref.shape[0]
    place = pl.ds(pl.multiple_of(owner(me_ref, b) * o, o), o)
    for k, value in enumerate(turned(block_ref[...], wide_ref)):
        x_ref[place, k * LANES : (k + 1) * LANES] = value


def assemble_body(places, me_ref, *refs):
    blocks, (x_ref, wide_ref) = refs[: len(places)], refs[-2:]
    for b, block in zip(places, blocks):
        place_block(me_ref, b, block, x_ref, wide_ref)


def owner(me_ref, b):
    return jnp.bitwise_xor(me_ref[0], 2 * (b % 4) + b // 4)


def forward_body(n, rows, o, places, me_ref, w_ref, *refs):
    blocks = refs[: len(places)]
    own_ref, low_ref, high_ref, first_ref, last_ref, x_ref, acc, wide_ref = refs[len(places) + 1 :]
    for b, block in zip(places, blocks):
        place_block(me_ref, b, block, x_ref, wide_ref)
    w = w_ref[...]
    seen = set()
    for p in range(n):
        for t in range(0, rows, 2):
            at = (p * rows + t) * LANES
            part = jnp.dot(
                w, x_ref[:, at : at + 2 * LANES], preferred_element_type=jnp.float32
            )
            for k, i, j, l in tap_list():
                for h in range(2):
                    slot = (l, p + 2 - i, (t + h + 1 - j) % rows)
                    value = part[k * o : (k + 1) * o, h * LANES : (h + 1) * LANES]
                    if slot in seen:
                        acc[slot] += value
                    else:
                        acc[slot] = value
                        seen.add(slot)
    for q in range(n + 2):
        for y in range(rows):
            total = (
                pltpu.roll(acc[0, q, y], 1, 1)
                + acc[1, q, y]
                + pltpu.roll(acc[2, q, y], LANES - 1, 1)
            )
            if q == 0:
                low_ref[y] = total.astype(low_ref.dtype)
            elif q == n + 1:
                high_ref[y] = total.astype(high_ref.dtype)
            else:
                own_ref[(q - 1) * rows + y] = total
            if q == 1:
                first_ref[y] = total.astype(first_ref.dtype)
            if q == n:
                last_ref[y] = total.astype(last_ref.dtype)


def ordered(me_ref, o, in_refs, out_refs):
    for in_ref, out_ref in zip(in_refs, out_refs):
        for b in range(8):
            place = pl.ds(pl.multiple_of(owner(me_ref, b) * o, o), o)
            out_ref[b * o : (b + 1) * o] = in_ref[place]


def three_shifts(wide, dtype):
    return [
        pltpu.roll(wide, LANES - 1, 1).astype(dtype),
        wide.astype(dtype),
        pltpu.roll(wide, 1, 1).astype(dtype),
    ]


def own_gradient_body(
    rows,
    o,
    scale,
    me_ref,
    own_ref,
    below_ref,
    above_ref,
    bias_ref,
    go_ref,
    w_0_ref,
    w_1_ref,
    act_ref,
    total_ref,
    s_ref,
    partial_ref,
    w_0,
    w_1,
    wide_ref,
):
    f32, bf16 = jnp.float32, jnp.bfloat16
    ordered(me_ref, o, (w_0_ref, w_1_ref), (w_0, w_1))
    total = jnp.zeros((o, LANES), f32)
    for q in range(2):
        for y in range(rows):
            beside = below_ref if q == 0 else above_ref
            pre = own_ref[q * rows + y] + beside[y].astype(f32) + bias_ref[...]
            s = jax.nn.sigmoid(pre)
            slope = s * (1.0 + pre * (1.0 - s))
            wide = (go_ref[q * rows + y].astype(f32) * slope).astype(bf16).astype(f32)
            wide_ref[pl.ds(q * rows + y, o, stride=2 * rows), :] = pre * s
            total = total + wide
            shifts = three_shifts(wide, bf16)
            for k, i, j, l in tap_list():
                p = q - 1 + i
                if 0 <= p < 2:
                    at = (p * rows + (y + j - 1) % rows) * LANES
                    row = (k - 9 * p) * o
                    s_ref[row : row + o, at : at + LANES] = shifts[l]
    for t in range(0, 2 * rows, 2):
        at = slice(t * LANES, (t + 2) * LANES)
        w = w_0 if t < rows else w_1
        partial_ref[:, at] = jnp.dot(w[...], s_ref[:, at], preferred_element_type=f32)
    act_ref[...] = wide_ref[...].reshape(act_ref.shape).astype(bf16)
    total_ref[...] = jnp.broadcast_to(
        jnp.sum(total, axis=1, keepdims=True) * scale, total_ref.shape
    )


def rim_gradient_body(
    rows,
    o,
    me_ref,
    low_ref,
    high_ref,
    below_ref,
    above_ref,
    bias_ref,
    go_below_ref,
    go_above_ref,
    partial_ref,
    w_0_ref,
    w_1_ref,
    _,
    s_ref,
    other_ref,
    mine_ref,
    w_0,
    w_1,
):
    f32, bf16 = jnp.float32, jnp.bfloat16
    ordered(me_ref, o, (w_0_ref, w_1_ref), (w_0, w_1))
    sides = ((below_ref, low_ref, go_below_ref), (above_ref, high_ref, go_above_ref))
    for p, (theirs, ours, go) in enumerate(sides):
        for y in range(rows):
            pre = theirs[y].astype(f32) + ours[y].astype(f32) + bias_ref[...]
            s = jax.nn.sigmoid(pre)
            slope = s * (1.0 + pre * (1.0 - s))
            wide = (go[y].astype(f32) * slope).astype(bf16).astype(f32)
            shifts = three_shifts(wide, bf16)
            for j in range(3):
                for l in range(3):
                    at = (p * rows + (y + j - 1) % rows) * LANES
                    row = (3 * j + l) * o
                    s_ref[row : row + o, at : at + LANES] = shifts[l]
    for t in range(0, 2 * rows, 2):
        at = slice(t * LANES, (t + 2) * LANES)
        w = w_0 if t < rows else w_1
        part = jnp.dot(w[...], s_ref[:, at], preferred_element_type=f32)
        part = (part + partial_ref[:, at]).astype(bf16)
        for h in range(2):
            for b in range(8):
                cut = part[b * o : (b + 1) * o, h * LANES : (h + 1) * LANES]
                (mine_ref if b < 4 else other_ref)[b % 4, t + h] = cut


def filter_product(s_ref, x_ref, plane):
    half = x_ref.shape[1] // 2
    at = slice(plane * half, (plane + 1) * half)
    return lax.dot_general(
        s_ref[:, at], x_ref[:, at], (((1,), (1,)), ((), ())), preferred_element_type=jnp.float32
    )


def own_filter_body(s_ref, x_ref, out_ref, token_ref):
    token_ref[...] = jnp.zeros_like(token_ref)
    third = out_ref.shape[0] // 3
    low, high = (filter_product(s_ref, x_ref, p) for p in range(2))
    out_ref[:third] = low[:third]
    out_ref[third : 2 * third] = low[third:] + high[:third]
    out_ref[2 * third :] = high[third:]


def rim_filter_body(scale, taps, o, s_ref, x_ref, own_ref, total_ref, first_ref, second_ref):
    third = own_ref.shape[0] // 3
    cut = taps * o
    high = own_ref[:third] + filter_product(s_ref, x_ref, 1)
    low = own_ref[2 * third :] + filter_product(s_ref, x_ref, 0)
    dtype = first_ref.dtype
    first_ref[:third] = (high * scale).astype(dtype)
    first_ref[third:] = (own_ref[third:cut] * scale).astype(dtype)
    second_ref[: 2 * third - cut] = (own_ref[cut : 2 * third] * scale).astype(dtype)
    second_ref[2 * third - cut : 27 * o - cut] = (low * scale).astype(dtype)
    row = jnp.concatenate([total_ref[...]] * (second_ref.shape[1] // LANES), axis=1)
    second_ref[27 * o - cut :] = row.astype(dtype)


def pair_body(a_ref, b_ref, _, out_ref):
    f32 = jnp.float32
    out_ref[...] = (a_ref[...].astype(f32) + b_ref[...].astype(f32)).astype(out_ref.dtype)


def core_sum_body(mine_ref, other_ref, *outs):
    for r, out_ref in enumerate(outs):
        total = mine_ref[r].astype(jnp.float32) + other_ref[r].astype(jnp.float32)
        out_ref[...] = total.astype(out_ref.dtype)


def sum_body(a_ref, b_ref, c_ref, d_ref, out_ref):
    f32 = jnp.float32
    total = b_ref[...].astype(f32) + c_ref[...].astype(f32) + d_ref[...].astype(f32)
    out_ref[...] = a_ref[...] + total


def last_body(
    taps, a_ref, b_ref, c_ref, d_ref, g_ref, out_ref, bias_ref, grad_ref, wide_ref
):
    o = out_ref.shape[1]
    f32 = jnp.float32
    cells = g_ref.shape[0]
    for k in range(cells):
        wide_ref[pl.ds(k, o, stride=cells), :] = g_ref[k]
    grad_ref[...] = wide_ref[...].reshape(grad_ref.shape).astype(grad_ref.dtype)
    for k in range(27):
        left, right, at = (a_ref, b_ref, k) if k < taps else (c_ref, d_ref, k - taps)
        cut = slice(at * o, (at + 1) * o)
        out_ref[k] = left[cut].astype(f32) + right[cut].astype(f32)
    cut = slice((27 - taps) * o, (28 - taps) * o)
    column = (c_ref[cut].astype(f32) + d_ref[cut].astype(f32))[:, :o]
    same = lax.broadcasted_iota(jnp.int32, (o, o), 0) == lax.broadcasted_iota(jnp.int32, (o, o), 1)
    bias_ref[...] = jnp.sum(jnp.where(same, column, 0.0), axis=0, keepdims=True)


def in_hbm(value):
    return pltpu.with_memory_space_constraint(value, pltpu.HBM)


def rotate(value, axis, step):
    count = lax.axis_size(axis)
    return lax.ppermute(value, axis, [(i, (i + step) % count) for i in range(count)])


def swap(value, axis, bit):
    return lax.ppermute(value, axis, [(i, i ^ bit) for i in range(lax.axis_size(axis))])


def cross(value, phase):
    slabs, chans = lax.axis_size("slab"), lax.axis_size("chan")
    pairs = [
        (s * chans + c, (s ^ (1 + (c + phase) % 2)) * chans + c)
        for s in range(slabs)
        for c in range(chans)
    ]
    return lax.ppermute(value, ("slab", "chan"), pairs)


def on_device(x_in, weight, bias_vec, grad_out):
    o, _, c_all = weight.shape
    _, n, rows, depth = x_in.shape
    f32, bf16 = jnp.float32, jnp.bfloat16
    cells = n * rows
    flops = 2 * 27 * o * c_all * cells * depth
    scale = 1.0 / math.sqrt(lax.axis_size("slab") * cells * depth)
    me = lax.axis_index("chan").astype(jnp.int32).reshape(1)

    block_wide = [pltpu.VMEM((o * cells, depth), f32)]

    x_b = swap(x_in, "chan", 4)
    x_a = swap(x_in, "chan", 2)
    x_side = swap(x_in, "chan", 1)
    x_own, go, go_low, go_high, w_flat, *w_back, bias = call(
        functools.partial(prepare_body, n, rows),
        [
            shape_of((o, n, rows, depth), bf16),
            shape_of((cells, o, depth), bf16),
            shape_of((rows, o, depth), bf16),
            shape_of((rows, o, depth), bf16),
            shape_of((27 * o, c_all), bf16),
            *[shape_of((c_all, taps * o), bf16) for taps in (18, 18, 9, 9)],
            shape_of((o, LANES), f32),
        ],
        [in_hbm(a) for a in (x_in, grad_out, jnp.transpose(weight, (1, 0, 2)), bias_vec[None, :])],
        [HBM] * 4,
        [
            pltpu.VMEM((o, n, rows, depth), bf16),
            pltpu.VMEM((27, o, c_all), bf16),
            pltpu.VMEM((1, o), bf16),
            *block_wide,
            pltpu.SemaphoreType.DMA((4,)),
        ],
        name="prepare",
    )
    go_above = rotate(go_low, "slab", -1)
    go_below = rotate(go_high, "slab", 1)
    x_b, w_flat = lax.optimization_barrier((x_b, w_flat))
    x_ab = swap(x_b, "chan", 2)
    late_b, go_above, go_below = lax.optimization_barrier((x_b, go_above, go_below))
    x_a_side = swap(x_a, "chan", 1)
    x_b_side = swap(late_b, "chan", 1)
    early, late = (0, 1, 2, 3, 4, 5, 6), (7,)
    (x_all,) = call(
        functools.partial(assemble_body, early),
        [shape_of((c_all, cells * depth), bf16)],
        [me, x_own, x_a, x_b, x_ab, x_side, x_a_side, x_b_side],
        [SMEM] + [VMEM] * 7,
        block_wide,
        flops=ASSEMBLE_FLOPS,
        name="assemble",
    )
    x_ab_side = swap(x_ab, "chan", 1)
    own, low, high, first, last, x_all = call(
        functools.partial(forward_body, n, rows, o, late),
        [
            shape_of((cells, o, depth), f32),
            *[shape_of((rows, o, depth), bf16)] * 4,
            shape_of((c_all, cells * depth), bf16),
        ],
        [me, w_flat, x_ab_side, x_all],
        [SMEM] + [VMEM] * 3,
        [pltpu.VMEM((3, n + 2, rows, o, depth), f32), *block_wide],
        flops=FORWARD_FLOPS,
        name="forward",
        aliases={3: 5},
    )
    above = rotate(low, "slab", -1)
    below = rotate(high, "slab", 1)
    above_own = rotate(first, "slab", -1)
    below_own = rotate(last, "slab", 1)
    act, total, own_shifts, partial = call(
        functools.partial(own_gradient_body, rows, o, scale),
        [
            shape_of((o, n, rows, depth), bf16),
            shape_of((o, LANES), f32),
            shape_of((18 * o, cells * depth), bf16),
            shape_of((c_all, cells * depth), f32),
        ],
        [me, own, below, above, bias, go, *w_back[:2]],
        [SMEM] + [VMEM] * 7,
        [*[pltpu.VMEM((c_all, 18 * o), bf16)] * 2, *block_wide],
        flops=flops * 2 // 3,
        name="own_gradient",
    )
    filters, token = call(
        own_filter_body,
        [shape_of((27 * o, c_all), f32), shape_of((8, LANES), f32)],
        [own_shifts, x_all],
        flops=flops * 2 // 3,
        name="own_filter",
    )
    rim_shifts, other, mine = call(
        functools.partial(rim_gradient_body, rows, o),
        [
            shape_of((9 * o, cells * depth), bf16),
            shape_of((4, cells, o, depth), bf16),
            shape_of((4, cells, o, depth), bf16),
        ],
        [me, low, high, below_own, above_own, bias, go_below, go_above, partial, *w_back[2:], token],
        [SMEM] + [VMEM] * 10 + [ANY],
        [pltpu.VMEM((c_all, 9 * o), bf16)] * 2,
        flops=flops // 3,
        name="rim_gradient",
    )
    other = swap(other, "chan", 1)
    taps = 14
    first, second = call(
        functools.partial(rim_filter_body, scale, taps, o),
        [shape_of((taps * o, c_all), bf16), shape_of(((28 - taps) * o, c_all), bf16)],
        [rim_shifts, x_all, filters, total],
        flops=flops // 3,
        name="rim_filter",
    )
    first_far = cross(first, 0)
    second_far = cross(second, 0)
    g_own, g_a, g_b, g_ab = call(
        core_sum_body,
        [shape_of((cells, o, depth), f32)] + [shape_of((cells, o, depth), bf16)] * 3,
        [mine, other],
        name="core_sum",
    )
    g_ab = swap(g_ab, "chan", 6)
    g_b = swap(g_b, "chan", 4)
    g_a = swap(g_a, "chan", 2)
    first, second = (
        call(
            pair_body,
            [shape_of(a.shape, bf16)],
            [a, b, g_own],
            [VMEM] * 2 + [ANY],
            name="pair_sum",
        )[0]
        for a, b in ((first, first_far), (second, second_far))
    )
    first_far = cross(first, 1)
    second_far = cross(second, 1)
    (g_own,) = call(
        sum_body,
        [shape_of((cells, o, depth), f32)],
        [g_own, g_b, g_ab, g_a],
        flops=SUM_FLOPS,
        name="sum",
    )
    weight_grad, bias_grad, grad_in = call(
        functools.partial(last_body, taps),
        [
            shape_of((27, o, c_all), f32),
            shape_of((1, o), f32),
            shape_of((o, n, rows, depth), bf16),
        ],
        [first, first_far, second, second_far, g_own],
        scratch=block_wide,
        name="last",
    )
    return act, grad_in, jnp.transpose(weight_grad, (1, 0, 2)), bias_grad[0]


def solution(mesh):
    placed = (
        P("chan", "slab", None, None),
        P("chan", None, None),
        P("chan"),
        P("chan", "slab", None, None),
    )

    def body(x_in, weight, bias_vec, grad_out):
        tiled = (
            weight.shape[0] % 32 == 0
            and x_in.shape[3] == LANES
            and lax.axis_size("slab") == 4
            and lax.axis_size("chan") == 8
            and x_in.shape[1] == 2
        )
        return (on_device if tiled else plain)(x_in, weight, bias_vec, grad_out)

    return jax.shard_map(
        body,
        mesh=mesh,
        in_specs=placed,
        out_specs=(
            P("chan", "slab", None, None),
            P("chan", "slab", None, None),
            P("chan", None, None),
            P("chan"),
        ),
        check_vma=False,
    )
```

```python
import functools
import math

import jax
import jax.numpy as jnp
from jax import lax
from jax.experimental import pallas as pl
from jax.experimental.pallas import tpu as pltpu
from jax.sharding import PartitionSpec as P

LANES = 128
SUM_FLOPS = 24 * 10**8
ASSEMBLE_FLOPS = 40 * 10**8
VMEM = pl.BlockSpec(memory_space=pltpu.VMEM)
ANY = pl.BlockSpec(memory_space=pl.ANY)
HBM = pl.BlockSpec(memory_space=pltpu.HBM)
SMEM = pl.BlockSpec(memory_space=pltpu.SMEM)


def with_halo(block, sides, width):
    for axis, dim in sides:
        count = lax.axis_size(axis)
        forward = [(i, i + 1) for i in range(count - 1)]
        forward.append((count - 1, 0))
        backward = [(target, source) for source, target in forward]
        low = lax.ppermute(
            lax.slice_in_dim(block, block.shape[dim] - width, None, axis=dim), axis, forward
        )
        high = lax.ppermute(lax.slice_in_dim(block, 0, width, axis=dim), axis, backward)
        block = jnp.concatenate([low, block, high], axis=dim)
    return block


def tap_list():
    return [(9 * i + 3 * j + l, i, j, l) for i in range(3) for j in range(3) for l in range(3)]


def plain(x_in, weight, bias_vec, grad_out):
    out_local, n_taps, in_total = weight.shape
    n_planes, n_rows, n_depth = (x_in.shape[1], x_in.shape[2], x_in.shape[3])
    rimmed = with_halo(x_in, (("slab", 1),), 1)
    padded = lax.all_gather(rimmed, "chan", axis=0, tiled=True)
    own_planes = padded[:, 1 : n_planes + 1]
    pre_act = (
        jnp.zeros((out_local, n_planes, n_rows, n_depth), jnp.float32)
        + bias_vec.astype(jnp.float32)[:, None, None, None]
    )
    for i in range(3):
        w_plane = jnp.transpose(weight[:, 9 * i : 9 * i + 9], (1, 0, 2)).reshape(
            9 * out_local, in_total
        )
        plane_part = jnp.dot(
            w_plane,
            padded[:, i : i + n_planes].reshape(in_total, -1),
            preferred_element_type=jnp.float32,
        )
        plane_part = plane_part.reshape(9, out_local, n_planes, n_rows, n_depth)
        for j in range(3):
            for l in range(3):
                pre_act = pre_act + jnp.roll(plane_part[3 * j + l], (1 - j, 1 - l), axis=(2, 3))
    sigmoid_v = jax.nn.sigmoid(pre_act)
    activation = (pre_act * sigmoid_v).astype(jnp.bfloat16)
    slope = sigmoid_v * (1.0 + pre_act * (1.0 - sigmoid_v))
    grad_pre = (grad_out.astype(jnp.float32) * slope).astype(jnp.bfloat16)
    padded_grad = with_halo(grad_pre, (("slab", 1),), 1)
    shifted = jnp.stack(
        [
            jnp.roll(padded_grad[:, 2 - i : 2 - i + n_planes], (j - 1, l - 1), axis=(2, 3))
            for k, i, j, l in tap_list()
        ],
        0,
    )
    shifted = shifted.reshape(n_taps * out_local, -1)
    grad_scale = 1.0 / math.sqrt(lax.axis_size("slab") * n_planes * n_rows * n_depth)
    filter_local = lax.dot_general(
        shifted,
        own_planes.reshape(in_total, -1),
        (((1,), (1,)), ((), ())),
        preferred_element_type=jnp.float32,
    )
    filter_part = (
        jnp.transpose(filter_local.reshape(n_taps, out_local, in_total), (1, 0, 2)) * grad_scale
    )
    bias_part = grad_scale * jnp.sum(grad_pre.astype(jnp.float32), axis=(1, 2, 3))
    bias_row = jnp.concatenate(
        [bias_part[:, None, None], jnp.zeros((out_local, 1, in_total - 1), jnp.float32)], 2
    )
    summed_filters = lax.psum(jnp.concatenate([filter_part, bias_row], 1), "slab")
    weight_grad = summed_filters[:, :n_taps]
    bias_grad = summed_filters[:, n_taps, 0]
    flat_w = jnp.transpose(weight, (1, 0, 2)).reshape(n_taps * out_local, in_total)
    product = lax.dot_general(
        flat_w, shifted, (((0,), (0,)), ((), ())), preferred_element_type=jnp.float32
    )
    grad_in = lax.psum_scatter(
        product.reshape(
            in_total // lax.axis_size("chan") * lax.axis_size("chan"), n_planes, n_rows, n_depth
        ),
        "chan",
        scatter_dimension=0,
        tiled=True,
    )
    return (activation, grad_in.astype(jnp.bfloat16), weight_grad, bias_grad)


def call(body, out_shape, operands, specs=None, scratch=(), flops=0, name=None, aliases=None):
    read = sum(math.prod(a.shape) * a.dtype.itemsize for a in operands)
    written = sum(math.prod(a.shape) * a.dtype.itemsize for a in out_shape)
    return pl.pallas_call(
        body,
        out_shape=out_shape,
        in_specs=specs or [VMEM] * len(operands),
        out_specs=[VMEM] * len(out_shape),
        scratch_shapes=list(scratch),
        input_output_aliases=aliases or {},
        compiler_params=pltpu.CompilerParams(vmem_limit_bytes=24 * 2**20),
        cost_estimate=pl.CostEstimate(
            flops=flops, bytes_accessed=read + written, transcendentals=0
        ),
        name=name,
    )(*operands)


def shape_of(shape, dtype):
    return jax.ShapeDtypeStruct(shape, dtype)


def turned(value, wide_ref):
    o = value.shape[0]
    cells = wide_ref.shape[0] // o
    wide_ref[...] = value.astype(jnp.float32).reshape(wide_ref.shape)
    return [
        wide_ref[pl.ds(k, o, stride=cells), :].astype(value.dtype) for k in range(cells)
    ]


def prepare_body(
    n,
    rows,
    x_hbm,
    go_hbm,
    w_hbm,
    bias_hbm,
    x_ref,
    go_ref,
    go_low_ref,
    go_high_ref,
    flat_ref,
    own_0_ref,
    own_1_ref,
    rim_0_ref,
    rim_1_ref,
    bias_ref,
    go_in,
    w_in,
    bias_in,
    wide_ref,
    sems,
):
    copies = [
        pltpu.make_async_copy(source, target, sems.at[at])
        for at, (source, target) in enumerate(
            [(go_hbm, go_in), (w_hbm, w_in), (bias_hbm, bias_in), (x_hbm, x_ref)]
        )
    ]
    for copy in copies:
        copy.start()
    copies[0].wait()
    for k, value in enumerate(turned(go_in[...], wide_ref)):
        go_ref[k] = value
        if k < rows:
            go_low_ref[k] = value
        if k >= (n - 1) * rows:
            go_high_ref[k - (n - 1) * rows] = value
    copies[1].wait()
    copies[2].wait()
    copies[3].wait()
    flat = w_in[...].reshape(flat_ref.shape)
    flat_ref[...] = flat
    third = flat.shape[0] // 3
    own_0_ref[...] = jnp.transpose(flat[: 2 * third])
    own_1_ref[...] = jnp.transpose(flat[third:])
    rim_0_ref[...] = jnp.transpose(flat[2 * third :])
    rim_1_ref[...] = jnp.transpose(flat[:third])
    o = bias_ref.shape[0]
    row = jnp.broadcast_to(bias_in[...].astype(jnp.float32), (o, o))
    same = lax.broadcasted_iota(jnp.int32, (o, o), 0) == lax.broadcasted_iota(jnp.int32, (o, o), 1)
    column = jnp.sum(jnp.where(same, row, 0.0), axis=1, keepdims=True)
    bias_ref[...] = jnp.broadcast_to(column, bias_ref.shape)


def place_block(me_ref, b, block_ref, x_ref, wide_ref):
    o = block_ref.shape[0]
    place = pl.ds(pl.multiple_of(owner(me_ref, b) * o, o), o)
    for k, value in enumerate(turned(block_ref[...], wide_ref)):
        x_ref[place, k * LANES : (k + 1) * LANES] = value


def assemble_body(places, me_ref, *refs):
    blocks, (x_ref, wide_ref) = refs[: len(places)], refs[-2:]
    for b, block in zip(places, blocks):
        place_block(me_ref, b, block, x_ref, wide_ref)


def owner(me_ref, b):
    return jnp.bitwise_xor(me_ref[0], 2 * (b % 4) + b // 4)


def plane_sums(rows, o, w_ref, x_ref, acc, chosen):
    seen = set()
    for p in range(2):
        near = [i for i in range(3) if (p, i) in chosen]
        base = 9 * near[0]
        w = w_ref[base * o : 9 * (near[-1] + 1) * o]
        for t in range(0, rows, 2):
            at = (p * rows + t) * LANES
            part = jnp.dot(
                w, x_ref[:, at : at + 2 * LANES], preferred_element_type=jnp.float32
            )
            for k, i, j, l in tap_list():
                if i not in near:
                    continue
                for h in range(2):
                    slot = (l, chosen[p, i], (t + h + 1 - j) % rows)
                    value = part[(k - base) * o : (k - base + 1) * o, h * LANES : (h + 1) * LANES]
                    if slot in seen:
                        acc[slot] += value
                    else:
                        acc[slot] = value
                        seen.add(slot)
    return [
        [
            pltpu.roll(acc[0, q, y], 1, 1) + acc[1, q, y] + pltpu.roll(acc[2, q, y], LANES - 1, 1)
            for y in range(rows)
        ]
        for q in range(2)
    ]


def rim_forward_body(rows, o, place, me_ref, w_ref, block_ref, _, low_ref, high_ref, x_ref, acc, wide_ref):
    place_block(me_ref, place, block_ref, x_ref, wide_ref)
    sums = plane_sums(rows, o, w_ref, x_ref, acc, {(0, 2): 0, (1, 0): 1})
    for y in range(rows):
        low_ref[y] = sums[0][y].astype(low_ref.dtype)
        high_ref[y] = sums[1][y].astype(high_ref.dtype)


def own_forward_body(rows, o, w_ref, x_ref, own_ref, first_ref, last_ref, acc):
    sums = plane_sums(
        rows, o, w_ref, x_ref, acc, {(0, 0): 1, (0, 1): 0, (1, 1): 1, (1, 2): 0}
    )
    for y in range(rows):
        own_ref[y] = sums[0][y]
        own_ref[rows + y] = sums[1][y]
        first_ref[y] = sums[0][y].astype(first_ref.dtype)
        last_ref[y] = sums[1][y].astype(last_ref.dtype)


def ordered(me_ref, o, in_refs, out_refs):
    for in_ref, out_ref in zip(in_refs, out_refs):
        for b in range(8):
            place = pl.ds(pl.multiple_of(owner(me_ref, b) * o, o), o)
            out_ref[b * o : (b + 1) * o] = in_ref[place]


def three_shifts(wide, dtype):
    return [
        pltpu.roll(wide, LANES - 1, 1).astype(dtype),
        wide.astype(dtype),
        pltpu.roll(wide, 1, 1).astype(dtype),
    ]


def own_gradient_body(
    rows,
    o,
    scale,
    me_ref,
    own_ref,
    below_ref,
    above_ref,
    bias_ref,
    go_ref,
    w_0_ref,
    w_1_ref,
    act_ref,
    total_ref,
    s_ref,
    partial_ref,
    w_0,
    w_1,
    wide_ref,
):
    f32, bf16 = jnp.float32, jnp.bfloat16
    ordered(me_ref, o, (w_0_ref, w_1_ref), (w_0, w_1))
    total = jnp.zeros((o, LANES), f32)
    for q in range(2):
        for y in range(rows):
            beside = below_ref if q == 0 else above_ref
            pre = own_ref[q * rows + y] + beside[y].astype(f32) + bias_ref[...]
            s = jax.nn.sigmoid(pre)
            slope = s * (1.0 + pre * (1.0 - s))
            wide = (go_ref[q * rows + y].astype(f32) * slope).astype(bf16).astype(f32)
            wide_ref[pl.ds(q * rows + y, o, stride=2 * rows), :] = pre * s
            total = total + wide
            shifts = three_shifts(wide, bf16)
            for k, i, j, l in tap_list():
                p = q - 1 + i
                if 0 <= p < 2:
                    at = (p * rows + (y + j - 1) % rows) * LANES
                    row = (k - 9 * p) * o
                    s_ref[row : row + o, at : at + LANES] = shifts[l]
    for t in range(0, 2 * rows, 2):
        at = slice(t * LANES, (t + 2) * LANES)
        w = w_0 if t < rows else w_1
        partial_ref[:, at] = jnp.dot(w[...], s_ref[:, at], preferred_element_type=f32)
    act_ref[...] = wide_ref[...].reshape(act_ref.shape).astype(bf16)
    total_ref[...] = jnp.broadcast_to(
        jnp.sum(total, axis=1, keepdims=True) * scale, total_ref.shape
    )


def rim_gradient_body(
    rows,
    o,
    me_ref,
    low_ref,
    high_ref,
    below_ref,
    above_ref,
    bias_ref,
    go_below_ref,
    go_above_ref,
    partial_ref,
    w_0_ref,
    w_1_ref,
    _,
    s_ref,
    other_ref,
    mine_ref,
    w_0,
    w_1,
):
    f32, bf16 = jnp.float32, jnp.bfloat16
    ordered(me_ref, o, (w_0_ref, w_1_ref), (w_0, w_1))
    sides = ((below_ref, low_ref, go_below_ref), (above_ref, high_ref, go_above_ref))
    for p, (theirs, ours, go) in enumerate(sides):
        for y in range(rows):
            pre = theirs[y].astype(f32) + ours[y].astype(f32) + bias_ref[...]
            s = jax.nn.sigmoid(pre)
            slope = s * (1.0 + pre * (1.0 - s))
            wide = (go[y].astype(f32) * slope).astype(bf16).astype(f32)
            shifts = three_shifts(wide, bf16)
            for j in range(3):
                for l in range(3):
                    at = (p * rows + (y + j - 1) % rows) * LANES
                    row = (3 * j + l) * o
                    s_ref[row : row + o, at : at + LANES] = shifts[l]
    for t in range(0, 2 * rows, 2):
        at = slice(t * LANES, (t + 2) * LANES)
        w = w_0 if t < rows else w_1
        part = jnp.dot(w[...], s_ref[:, at], preferred_element_type=f32)
        part = (part + partial_ref[:, at]).astype(bf16)
        for h in range(2):
            for b in range(8):
                cut = part[b * o : (b + 1) * o, h * LANES : (h + 1) * LANES]
                (mine_ref if b < 4 else other_ref)[b % 4, t + h] = cut


def filter_product(s_ref, x_ref, plane):
    half = x_ref.shape[1] // 2
    at = slice(plane * half, (plane + 1) * half)
    return lax.dot_general(
        s_ref[:, at], x_ref[:, at], (((1,), (1,)), ((), ())), preferred_element_type=jnp.float32
    )


def own_filter_body(s_ref, x_ref, out_ref, token_ref):
    token_ref[...] = jnp.zeros_like(token_ref)
    third = out_ref.shape[0] // 3
    low, high = (filter_product(s_ref, x_ref, p) for p in range(2))
    out_ref[:third] = low[:third]
    out_ref[third : 2 * third] = low[third:] + high[:third]
    out_ref[2 * third :] = high[third:]


def rim_filter_body(scale, taps, o, s_ref, x_ref, own_ref, total_ref, first_ref, second_ref):
    third = own_ref.shape[0] // 3
    cut = taps * o
    high = own_ref[:third] + filter_product(s_ref, x_ref, 1)
    low = own_ref[2 * third :] + filter_product(s_ref, x_ref, 0)
    dtype = first_ref.dtype
    first_ref[:third] = (high * scale).astype(dtype)
    first_ref[third:] = (own_ref[third:cut] * scale).astype(dtype)
    second_ref[: 2 * third - cut] = (own_ref[cut : 2 * third] * scale).astype(dtype)
    second_ref[2 * third - cut : 27 * o - cut] = (low * scale).astype(dtype)
    row = jnp.concatenate([total_ref[...]] * (second_ref.shape[1] // LANES), axis=1)
    second_ref[27 * o - cut :] = row.astype(dtype)


def pair_body(a_ref, b_ref, _, out_ref):
    f32 = jnp.float32
    out_ref[...] = (a_ref[...].astype(f32) + b_ref[...].astype(f32)).astype(out_ref.dtype)


def core_sum_body(mine_ref, other_ref, *outs):
    for r, out_ref in enumerate(outs):
        total = mine_ref[r].astype(jnp.float32) + other_ref[r].astype(jnp.float32)
        out_ref[...] = total.astype(out_ref.dtype)


def sum_body(a_ref, b_ref, c_ref, d_ref, out_ref):
    f32 = jnp.float32
    total = b_ref[...].astype(f32) + c_ref[...].astype(f32) + d_ref[...].astype(f32)
    out_ref[...] = a_ref[...] + total


def last_body(
    taps, a_ref, b_ref, c_ref, d_ref, g_ref, out_ref, bias_ref, grad_ref, wide_ref
):
    o = out_ref.shape[1]
    f32 = jnp.float32
    cells = g_ref.shape[0]
    for k in range(cells):
        wide_ref[pl.ds(k, o, stride=cells), :] = g_ref[k]
    grad_ref[...] = wide_ref[...].reshape(grad_ref.shape).astype(grad_ref.dtype)
    for k in range(27):
        left, right, at = (a_ref, b_ref, k) if k < taps else (c_ref, d_ref, k - taps)
        cut = slice(at * o, (at + 1) * o)
        out_ref[k] = left[cut].astype(f32) + right[cut].astype(f32)
    cut = slice((27 - taps) * o, (28 - taps) * o)
    column = (c_ref[cut].astype(f32) + d_ref[cut].astype(f32))[:, :o]
    same = lax.broadcasted_iota(jnp.int32, (o, o), 0) == lax.broadcasted_iota(jnp.int32, (o, o), 1)
    bias_ref[...] = jnp.sum(jnp.where(same, column, 0.0), axis=0, keepdims=True)


def in_hbm(value):
    return pltpu.with_memory_space_constraint(value, pltpu.HBM)


def rotate(value, axis, step):
    count = lax.axis_size(axis)
    return lax.ppermute(value, axis, [(i, (i + step) % count) for i in range(count)])


def swap(value, axis, bit):
    return lax.ppermute(value, axis, [(i, i ^ bit) for i in range(lax.axis_size(axis))])


def cross(value, phase):
    slabs, chans = lax.axis_size("slab"), lax.axis_size("chan")
    pairs = [
        (s * chans + c, (s ^ (1 + (c + phase) % 2)) * chans + c)
        for s in range(slabs)
        for c in range(chans)
    ]
    return lax.ppermute(value, ("slab", "chan"), pairs)


def on_device(x_in, weight, bias_vec, grad_out):
    o, _, c_all = weight.shape
    _, n, rows, depth = x_in.shape
    f32, bf16 = jnp.float32, jnp.bfloat16
    cells = n * rows
    flops = 2 * 27 * o * c_all * cells * depth
    scale = 1.0 / math.sqrt(lax.axis_size("slab") * cells * depth)
    me = lax.axis_index("chan").astype(jnp.int32).reshape(1)

    block_wide = [pltpu.VMEM((o * cells, depth), f32)]

    x_b = swap(x_in, "chan", 4)
    x_a = swap(x_in, "chan", 2)
    x_side = swap(x_in, "chan", 1)
    x_own, go, go_low, go_high, w_flat, *w_back, bias = call(
        functools.partial(prepare_body, n, rows),
        [
            shape_of((o, n, rows, depth), bf16),
            shape_of((cells, o, depth), bf16),
            shape_of((rows, o, depth), bf16),
            shape_of((rows, o, depth), bf16),
            shape_of((27 * o, c_all), bf16),
            *[shape_of((c_all, taps * o), bf16) for taps in (18, 18, 9, 9)],
            shape_of((o, LANES), f32),
        ],
        [in_hbm(a) for a in (x_in, grad_out, jnp.transpose(weight, (1, 0, 2)), bias_vec[None, :])],
        [HBM] * 4,
        [
            pltpu.VMEM((o, n, rows, depth), bf16),
            pltpu.VMEM((27, o, c_all), bf16),
            pltpu.VMEM((1, o), bf16),
            *block_wide,
            pltpu.SemaphoreType.DMA((4,)),
        ],
        name="prepare",
    )
    go_above = rotate(go_low, "slab", -1)
    go_below = rotate(go_high, "slab", 1)
    x_b, w_flat = lax.optimization_barrier((x_b, w_flat))
    x_ab = swap(x_b, "chan", 2)
    late_b, go_above, go_below = lax.optimization_barrier((x_b, go_above, go_below))
    x_a_side = swap(x_a, "chan", 1)
    x_b_side = swap(late_b, "chan", 1)
    early = (0, 1, 2, 3, 4, 5, 6)
    (x_all,) = call(
        functools.partial(assemble_body, early),
        [shape_of((c_all, cells * depth), bf16)],
        [me, x_own, x_a, x_b, x_ab, x_side, x_a_side, x_b_side],
        [SMEM] + [VMEM] * 7,
        block_wide,
        flops=ASSEMBLE_FLOPS,
        name="assemble",
    )
    x_ab_side = swap(x_ab, "chan", 1)
    sums = [pltpu.VMEM((3, 2, rows, o, depth), f32)]
    low, high, x_all = call(
        functools.partial(rim_forward_body, rows, o, 7),
        [shape_of((rows, o, depth), bf16)] * 2 + [shape_of((c_all, cells * depth), bf16)],
        [me, w_flat, x_ab_side, x_all],
        [SMEM] + [VMEM] * 3,
        sums + block_wide,
        flops=flops // 3,
        name="rim_forward",
        aliases={3: 2},
    )
    own, first, last = call(
        functools.partial(own_forward_body, rows, o),
        [shape_of((cells, o, depth), f32)] + [shape_of((rows, o, depth), bf16)] * 2,
        [w_flat, x_all],
        scratch=sums,
        flops=flops * 2 // 3,
        name="own_forward",
    )
    above = rotate(low, "slab", -1)
    below = rotate(high, "slab", 1)
    above_own = rotate(first, "slab", -1)
    below_own = rotate(last, "slab", 1)
    act, total, own_shifts, partial = call(
        functools.partial(own_gradient_body, rows, o, scale),
        [
            shape_of((o, n, rows, depth), bf16),
            shape_of((o, LANES), f32),
            shape_of((18 * o, cells * depth), bf16),
            shape_of((c_all, cells * depth), f32),
        ],
        [me, own, below, above, bias, go, *w_back[:2]],
        [SMEM] + [VMEM] * 7,
        [*[pltpu.VMEM((c_all, 18 * o), bf16)] * 2, *block_wide],
        flops=flops * 2 // 3,
        name="own_gradient",
    )
    filters, token = call(
        own_filter_body,
        [shape_of((27 * o, c_all), f32), shape_of((8, LANES), f32)],
        [own_shifts, x_all],
        flops=flops * 2 // 3,
        name="own_filter",
    )
    rim_shifts, other, mine = call(
        functools.partial(rim_gradient_body, rows, o),
        [
            shape_of((9 * o, cells * depth), bf16),
            shape_of((4, cells, o, depth), bf16),
            shape_of((4, cells, o, depth), bf16),
        ],
        [me, low, high, below_own, above_own, bias, go_below, go_above, partial, *w_back[2:], token],
        [SMEM] + [VMEM] * 10 + [ANY],
        [pltpu.VMEM((c_all, 9 * o), bf16)] * 2,
        flops=flops // 3,
        name="rim_gradient",
    )
    other = swap(other, "chan", 1)
    taps = 14
    first, second = call(
        functools.partial(rim_filter_body, scale, taps, o),
        [shape_of((taps * o, c_all), bf16), shape_of(((28 - taps) * o, c_all), bf16)],
        [rim_shifts, x_all, filters, total],
        flops=flops // 3,
        name="rim_filter",
    )
    first_far = cross(first, 0)
    second_far = cross(second, 0)
    g_own, g_a, g_b, g_ab = call(
        core_sum_body,
        [shape_of((cells, o, depth), f32)] + [shape_of((cells, o, depth), bf16)] * 3,
        [mine, other],
        name="core_sum",
    )
    g_ab = swap(g_ab, "chan", 6)
    g_b = swap(g_b, "chan", 4)
    g_a = swap(g_a, "chan", 2)
    first, second = (
        call(
            pair_body,
            [shape_of(a.shape, bf16)],
            [a, b, g_own],
            [VMEM] * 2 + [ANY],
            name="pair_sum",
        )[0]
        for a, b in ((first, first_far), (second, second_far))
    )
    first_far = cross(first, 1)
    second_far = cross(second, 1)
    (g_own,) = call(
        sum_body,
        [shape_of((cells, o, depth), f32)],
        [g_own, g_b, g_ab, g_a],
        flops=SUM_FLOPS,
        name="sum",
    )
    weight_grad, bias_grad, grad_in = call(
        functools.partial(last_body, taps),
        [
            shape_of((27, o, c_all), f32),
            shape_of((1, o), f32),
            shape_of((o, n, rows, depth), bf16),
        ],
        [first, first_far, second, second_far, g_own],
        scratch=block_wide,
        name="last",
    )
    return act, grad_in, jnp.transpose(weight_grad, (1, 0, 2)), bias_grad[0]


def solution(mesh):
    placed = (
        P("chan", "slab", None, None),
        P("chan", None, None),
        P("chan"),
        P("chan", "slab", None, None),
    )

    def body(x_in, weight, bias_vec, grad_out):
        tiled = (
            weight.shape[0] % 32 == 0
            and x_in.shape[3] == LANES
            and lax.axis_size("slab") == 4
            and lax.axis_size("chan") == 8
            and x_in.shape[1] == 2
        )
        return (on_device if tiled else plain)(x_in, weight, bias_vec, grad_out)

    return jax.shard_map(
        body,
        mesh=mesh,
        in_specs=placed,
        out_specs=(
            P("chan", "slab", None, None),
            P("chan", "slab", None, None),
            P("chan", None, None),
            P("chan"),
        ),
        check_vma=False,
    )
```

```python
import functools
import math

import jax
import jax.numpy as jnp
from jax import lax
from jax.experimental import pallas as pl
from jax.experimental.pallas import tpu as pltpu
from jax.sharding import PartitionSpec as P

LANES = 128
FORWARD_FLOPS = 9 * 10**8
SUM_FLOPS = 24 * 10**8
ASSEMBLE_FLOPS = 40 * 10**8
VMEM = pl.BlockSpec(memory_space=pltpu.VMEM)
ANY = pl.BlockSpec(memory_space=pl.ANY)
HBM = pl.BlockSpec(memory_space=pltpu.HBM)
SMEM = pl.BlockSpec(memory_space=pltpu.SMEM)


def with_halo(block, sides, width):
    for axis, dim in sides:
        count = lax.axis_size(axis)
        forward = [(i, i + 1) for i in range(count - 1)]
        forward.append((count - 1, 0))
        backward = [(target, source) for source, target in forward]
        low = lax.ppermute(
            lax.slice_in_dim(block, block.shape[dim] - width, None, axis=dim), axis, forward
        )
        high = lax.ppermute(lax.slice_in_dim(block, 0, width, axis=dim), axis, backward)
        block = jnp.concatenate([low, block, high], axis=dim)
    return block


def tap_list():
    return [(9 * i + 3 * j + l, i, j, l) for i in range(3) for j in range(3) for l in range(3)]


def plain(x_in, weight, bias_vec, grad_out):
    out_local, n_taps, in_total = weight.shape
    n_planes, n_rows, n_depth = (x_in.shape[1], x_in.shape[2], x_in.shape[3])
    rimmed = with_halo(x_in, (("slab", 1),), 1)
    padded = lax.all_gather(rimmed, "chan", axis=0, tiled=True)
    own_planes = padded[:, 1 : n_planes + 1]
    pre_act = (
        jnp.zeros((out_local, n_planes, n_rows, n_depth), jnp.float32)
        + bias_vec.astype(jnp.float32)[:, None, None, None]
    )
    for i in range(3):
        w_plane = jnp.transpose(weight[:, 9 * i : 9 * i + 9], (1, 0, 2)).reshape(
            9 * out_local, in_total
        )
        plane_part = jnp.dot(
            w_plane,
            padded[:, i : i + n_planes].reshape(in_total, -1),
            preferred_element_type=jnp.float32,
        )
        plane_part = plane_part.reshape(9, out_local, n_planes, n_rows, n_depth)
        for j in range(3):
            for l in range(3):
                pre_act = pre_act + jnp.roll(plane_part[3 * j + l], (1 - j, 1 - l), axis=(2, 3))
    sigmoid_v = jax.nn.sigmoid(pre_act)
    activation = (pre_act * sigmoid_v).astype(jnp.bfloat16)
    slope = sigmoid_v * (1.0 + pre_act * (1.0 - sigmoid_v))
    grad_pre = (grad_out.astype(jnp.float32) * slope).astype(jnp.bfloat16)
    padded_grad = with_halo(grad_pre, (("slab", 1),), 1)
    shifted = jnp.stack(
        [
            jnp.roll(padded_grad[:, 2 - i : 2 - i + n_planes], (j - 1, l - 1), axis=(2, 3))
            for k, i, j, l in tap_list()
        ],
        0,
    )
    shifted = shifted.reshape(n_taps * out_local, -1)
    grad_scale = 1.0 / math.sqrt(lax.axis_size("slab") * n_planes * n_rows * n_depth)
    filter_local = lax.dot_general(
        shifted,
        own_planes.reshape(in_total, -1),
        (((1,), (1,)), ((), ())),
        preferred_element_type=jnp.float32,
    )
    filter_part = (
        jnp.transpose(filter_local.reshape(n_taps, out_local, in_total), (1, 0, 2)) * grad_scale
    )
    bias_part = grad_scale * jnp.sum(grad_pre.astype(jnp.float32), axis=(1, 2, 3))
    bias_row = jnp.concatenate(
        [bias_part[:, None, None], jnp.zeros((out_local, 1, in_total - 1), jnp.float32)], 2
    )
    summed_filters = lax.psum(jnp.concatenate([filter_part, bias_row], 1), "slab")
    weight_grad = summed_filters[:, :n_taps]
    bias_grad = summed_filters[:, n_taps, 0]
    flat_w = jnp.transpose(weight, (1, 0, 2)).reshape(n_taps * out_local, in_total)
    product = lax.dot_general(
        flat_w, shifted, (((0,), (0,)), ((), ())), preferred_element_type=jnp.float32
    )
    grad_in = lax.psum_scatter(
        product.reshape(
            in_total // lax.axis_size("chan") * lax.axis_size("chan"), n_planes, n_rows, n_depth
        ),
        "chan",
        scatter_dimension=0,
        tiled=True,
    )
    return (activation, grad_in.astype(jnp.bfloat16), weight_grad, bias_grad)


def call(body, out_shape, operands, specs=None, scratch=(), flops=0, name=None, aliases=None):
    read = sum(math.prod(a.shape) * a.dtype.itemsize for a in operands)
    written = sum(math.prod(a.shape) * a.dtype.itemsize for a in out_shape)
    return pl.pallas_call(
        body,
        out_shape=out_shape,
        in_specs=specs or [VMEM] * len(operands),
        out_specs=[VMEM] * len(out_shape),
        scratch_shapes=list(scratch),
        input_output_aliases=aliases or {},
        compiler_params=pltpu.CompilerParams(vmem_limit_bytes=24 * 2**20),
        cost_estimate=pl.CostEstimate(
            flops=flops, bytes_accessed=read + written, transcendentals=0
        ),
        name=name,
    )(*operands)


def shape_of(shape, dtype):
    return jax.ShapeDtypeStruct(shape, dtype)


def by_parity(slab_ref, a, b):
    even = lax.rem(slab_ref[0], 2) == 0
    f32 = jnp.float32
    wide = a.astype(f32), b.astype(f32)
    return (
        jnp.where(even, wide[0], wide[1]).astype(a.dtype),
        jnp.where(even, wide[1], wide[0]).astype(a.dtype),
    )


def turned(value, wide_ref):
    o = value.shape[0]
    cells = wide_ref.shape[0] // o
    wide_ref[...] = value.astype(jnp.float32).reshape(wide_ref.shape)
    return [
        wide_ref[pl.ds(k, o, stride=cells), :].astype(value.dtype) for k in range(cells)
    ]


def prepare_body(
    n,
    rows,
    slab_ref,
    x_hbm,
    go_hbm,
    w_hbm,
    bias_hbm,
    x_ref,
    go_ref,
    go_first_ref,
    go_second_ref,
    flat_ref,
    own_0_ref,
    own_1_ref,
    rim_0_ref,
    rim_1_ref,
    bias_ref,
    go_in,
    w_in,
    bias_in,
    wide_ref,
    sems,
):
    copies = [
        pltpu.make_async_copy(source, target, sems.at[at])
        for at, (source, target) in enumerate(
            [(go_hbm, go_in), (w_hbm, w_in), (bias_hbm, bias_in), (x_hbm, x_ref)]
        )
    ]
    for copy in copies:
        copy.start()
    copies[0].wait()
    values = turned(go_in[...], wide_ref)
    for k, value in enumerate(values):
        go_ref[k] = value
    for y in range(rows):
        low, high = values[y], values[(n - 1) * rows + y]
        go_first_ref[y], go_second_ref[y] = by_parity(slab_ref, high, low)
    copies[1].wait()
    copies[2].wait()
    copies[3].wait()
    flat = w_in[...].reshape(flat_ref.shape)
    flat_ref[...] = flat
    third = flat.shape[0] // 3
    own_0_ref[...] = jnp.transpose(flat[: 2 * third])
    own_1_ref[...] = jnp.transpose(flat[third:])
    rim_0_ref[...] = jnp.transpose(flat[2 * third :])
    rim_1_ref[...] = jnp.transpose(flat[:third])
    o = bias_ref.shape[0]
    row = jnp.broadcast_to(bias_in[...].astype(jnp.float32), (o, o))
    same = lax.broadcasted_iota(jnp.int32, (o, o), 0) == lax.broadcasted_iota(jnp.int32, (o, o), 1)
    column = jnp.sum(jnp.where(same, row, 0.0), axis=1, keepdims=True)
    bias_ref[...] = jnp.broadcast_to(column, bias_ref.shape)


def place_block(me_ref, b, block_ref, x_ref, wide_ref):
    o = block_ref.shape[0]
    place = pl.ds(pl.multiple_of(owner(me_ref, b) * o, o), o)
    for k, value in enumerate(turned(block_ref[...], wide_ref)):
        x_ref[place, k * LANES : (k + 1) * LANES] = value


def assemble_body(places, me_ref, *refs):
    blocks, (x_ref, wide_ref) = refs[: len(places)], refs[-2:]
    for b, block in zip(places, blocks):
        place_block(me_ref, b, block, x_ref, wide_ref)


def owner(me_ref, b):
    return jnp.bitwise_xor(me_ref[0], 2 * (b % 4) + b // 4)


def forward_body(n, rows, o, places, me_ref, slab_ref, w_ref, *refs):
    blocks = refs[: len(places)]
    own_ref, *sent, x_ref, acc, wide_ref = refs[len(places) + 1 :]
    for b, block in zip(places, blocks):
        place_block(me_ref, b, block, x_ref, wide_ref)
    w = w_ref[...]
    seen = set()
    for p in range(n):
        for t in range(0, rows, 2):
            at = (p * rows + t) * LANES
            part = jnp.dot(
                w, x_ref[:, at : at + 2 * LANES], preferred_element_type=jnp.float32
            )
            for k, i, j, l in tap_list():
                for h in range(2):
                    slot = (l, p + 2 - i, (t + h + 1 - j) % rows)
                    value = part[k * o : (k + 1) * o, h * LANES : (h + 1) * LANES]
                    if slot in seen:
                        acc[slot] += value
                    else:
                        acc[slot] = value
                        seen.add(slot)
    for y in range(rows):
        totals = [
            pltpu.roll(acc[0, q, y], 1, 1) + acc[1, q, y] + pltpu.roll(acc[2, q, y], LANES - 1, 1)
            for q in range(n + 2)
        ]
        for p in range(n):
            own_ref[p * rows + y] = totals[p + 1]
        for pair, low, high in ((sent[:2], 0, n + 1), (sent[2:], 1, n)):
            for ref, value in zip(pair, by_parity(slab_ref, totals[high], totals[low])):
                ref[y] = value.astype(ref.dtype)


def ordered(me_ref, o, in_refs, out_refs):
    for in_ref, out_ref in zip(in_refs, out_refs):
        for b in range(8):
            place = pl.ds(pl.multiple_of(owner(me_ref, b) * o, o), o)
            out_ref[b * o : (b + 1) * o] = in_ref[place]


def three_shifts(wide, dtype):
    return [
        pltpu.roll(wide, LANES - 1, 1).astype(dtype),
        wide.astype(dtype),
        pltpu.roll(wide, 1, 1).astype(dtype),
    ]


def own_gradient_body(
    rows,
    o,
    scale,
    me_ref,
    slab_ref,
    own_ref,
    first_ref,
    second_ref,
    bias_ref,
    go_ref,
    w_0_ref,
    w_1_ref,
    act_ref,
    total_ref,
    s_ref,
    partial_ref,
    w_0,
    w_1,
    wide_ref,
):
    f32, bf16 = jnp.float32, jnp.bfloat16
    ordered(me_ref, o, (w_0_ref, w_1_ref), (w_0, w_1))
    total = jnp.zeros((o, LANES), f32)
    for q in range(2):
        for y in range(rows):
            beside = by_parity(slab_ref, first_ref[y], second_ref[y])[1 - q]
            pre = own_ref[q * rows + y] + beside.astype(f32) + bias_ref[...]
            s = jax.nn.sigmoid(pre)
            slope = s * (1.0 + pre * (1.0 - s))
            wide = (go_ref[q * rows + y].astype(f32) * slope).astype(bf16).astype(f32)
            wide_ref[pl.ds(q * rows + y, o, stride=2 * rows), :] = pre * s
            total = total + wide
            shifts = three_shifts(wide, bf16)
            for k, i, j, l in tap_list():
                p = q - 1 + i
                if 0 <= p < 2:
                    at = (p * rows + (y + j - 1) % rows) * LANES
                    row = (k - 9 * p) * o
                    s_ref[row : row + o, at : at + LANES] = shifts[l]
    for t in range(0, 2 * rows, 2):
        at = slice(t * LANES, (t + 2) * LANES)
        w = w_0 if t < rows else w_1
        partial_ref[:, at] = jnp.dot(w[...], s_ref[:, at], preferred_element_type=f32)
    act_ref[...] = wide_ref[...].reshape(act_ref.shape).astype(bf16)
    total_ref[...] = jnp.broadcast_to(
        jnp.sum(total, axis=1, keepdims=True) * scale, total_ref.shape
    )


def rim_gradient_body(
    rows,
    o,
    me_ref,
    slab_ref,
    first_ref,
    second_ref,
    first_in_ref,
    second_in_ref,
    bias_ref,
    go_first_ref,
    go_second_ref,
    partial_ref,
    w_0_ref,
    w_1_ref,
    _,
    s_ref,
    other_ref,
    mine_ref,
    w_0,
    w_1,
):
    f32, bf16 = jnp.float32, jnp.bfloat16
    ordered(me_ref, o, (w_0_ref, w_1_ref), (w_0, w_1))
    pairs = (
        (first_in_ref, second_in_ref),
        (first_ref, second_ref),
        (go_first_ref, go_second_ref),
    )
    for p in range(2):
        for y in range(rows):
            theirs, ours, go = (
                by_parity(slab_ref, first[y], second[y])[1 - p].astype(f32)
                for first, second in pairs
            )
            pre = theirs + ours + bias_ref[...]
            s = jax.nn.sigmoid(pre)
            slope = s * (1.0 + pre * (1.0 - s))
            wide = (go * slope).astype(bf16).astype(f32)
            shifts = three_shifts(wide, bf16)
            for j in range(3):
                for l in range(3):
                    at = (p * rows + (y + j - 1) % rows) * LANES
                    row = (3 * j + l) * o
                    s_ref[row : row + o, at : at + LANES] = shifts[l]
    for t in range(0, 2 * rows, 2):
        at = slice(t * LANES, (t + 2) * LANES)
        w = w_0 if t < rows else w_1
        part = jnp.dot(w[...], s_ref[:, at], preferred_element_type=f32)
        part = (part + partial_ref[:, at]).astype(bf16)
        for h in range(2):
            for b in range(8):
                cut = part[b * o : (b + 1) * o, h * LANES : (h + 1) * LANES]
                (mine_ref if b < 4 else other_ref)[b % 4, t + h] = cut


def filter_product(s_ref, x_ref, plane):
    half = x_ref.shape[1] // 2
    at = slice(plane * half, (plane + 1) * half)
    return lax.dot_general(
        s_ref[:, at], x_ref[:, at], (((1,), (1,)), ((), ())), preferred_element_type=jnp.float32
    )


def own_filter_body(s_ref, x_ref, out_ref, token_ref):
    token_ref[...] = jnp.zeros_like(token_ref)
    third = out_ref.shape[0] // 3
    low, high = (filter_product(s_ref, x_ref, p) for p in range(2))
    out_ref[:third] = low[:third]
    out_ref[third : 2 * third] = low[third:] + high[:third]
    out_ref[2 * third :] = high[third:]


def rim_filter_body(scale, taps, o, s_ref, x_ref, own_ref, total_ref, first_ref, second_ref):
    third = own_ref.shape[0] // 3
    cut = taps * o
    high = own_ref[:third] + filter_product(s_ref, x_ref, 1)
    low = own_ref[2 * third :] + filter_product(s_ref, x_ref, 0)
    dtype = first_ref.dtype
    first_ref[:third] = (high * scale).astype(dtype)
    first_ref[third:] = (own_ref[third:cut] * scale).astype(dtype)
    second_ref[: 2 * third - cut] = (own_ref[cut : 2 * third] * scale).astype(dtype)
    second_ref[2 * third - cut : 27 * o - cut] = (low * scale).astype(dtype)
    row = jnp.concatenate([total_ref[...]] * (second_ref.shape[1] // LANES), axis=1)
    second_ref[27 * o - cut :] = row.astype(dtype)


def pair_body(a_ref, b_ref, _, out_ref):
    f32 = jnp.float32
    out_ref[...] = (a_ref[...].astype(f32) + b_ref[...].astype(f32)).astype(out_ref.dtype)


def core_sum_body(mine_ref, other_ref, *outs):
    for r, out_ref in enumerate(outs):
        total = mine_ref[r].astype(jnp.float32) + other_ref[r].astype(jnp.float32)
        out_ref[...] = total.astype(out_ref.dtype)


def sum_body(a_ref, b_ref, c_ref, d_ref, out_ref):
    f32 = jnp.float32
    total = b_ref[...].astype(f32) + c_ref[...].astype(f32) + d_ref[...].astype(f32)
    out_ref[...] = a_ref[...] + total


def last_body(
    taps, a_ref, b_ref, c_ref, d_ref, g_ref, out_ref, bias_ref, grad_ref, wide_ref
):
    o = out_ref.shape[1]
    f32 = jnp.float32
    cells = g_ref.shape[0]
    for k in range(cells):
        wide_ref[pl.ds(k, o, stride=cells), :] = g_ref[k]
    grad_ref[...] = wide_ref[...].reshape(grad_ref.shape).astype(grad_ref.dtype)
    for k in range(27):
        left, right, at = (a_ref, b_ref, k) if k < taps else (c_ref, d_ref, k - taps)
        cut = slice(at * o, (at + 1) * o)
        out_ref[k] = left[cut].astype(f32) + right[cut].astype(f32)
    cut = slice((27 - taps) * o, (28 - taps) * o)
    column = (c_ref[cut].astype(f32) + d_ref[cut].astype(f32))[:, :o]
    same = lax.broadcasted_iota(jnp.int32, (o, o), 0) == lax.broadcasted_iota(jnp.int32, (o, o), 1)
    bias_ref[...] = jnp.sum(jnp.where(same, column, 0.0), axis=0, keepdims=True)


def in_hbm(value):
    return pltpu.with_memory_space_constraint(value, pltpu.HBM)


def swap(value, axis, bit):
    return lax.ppermute(value, axis, [(i, i ^ bit) for i in range(lax.axis_size(axis))])


def cross(value, phase):
    slabs, chans = lax.axis_size("slab"), lax.axis_size("chan")
    pairs = [
        (s * chans + c, (s ^ (1 + (c + phase) % 2)) * chans + c)
        for s in range(slabs)
        for c in range(chans)
    ]
    return lax.ppermute(value, ("slab", "chan"), pairs)


def on_device(x_in, weight, bias_vec, grad_out):
    o, _, c_all = weight.shape
    _, n, rows, depth = x_in.shape
    f32, bf16 = jnp.float32, jnp.bfloat16
    cells = n * rows
    flops = 2 * 27 * o * c_all * cells * depth
    scale = 1.0 / math.sqrt(lax.axis_size("slab") * cells * depth)
    me = lax.axis_index("chan").astype(jnp.int32).reshape(1)
    slab = lax.axis_index("slab").astype(jnp.int32).reshape(1)

    block_wide = [pltpu.VMEM((o * cells, depth), f32)]

    x_b = swap(x_in, "chan", 4)
    x_a = swap(x_in, "chan", 2)
    x_side = swap(x_in, "chan", 1)
    x_own, go, go_first, go_second, w_flat, *w_back, bias = call(
        functools.partial(prepare_body, n, rows),
        [
            shape_of((o, n, rows, depth), bf16),
            shape_of((cells, o, depth), bf16),
            shape_of((rows, o, depth), bf16),
            shape_of((rows, o, depth), bf16),
            shape_of((27 * o, c_all), bf16),
            *[shape_of((c_all, taps * o), bf16) for taps in (18, 18, 9, 9)],
            shape_of((o, LANES), f32),
        ],
        [slab] + [in_hbm(a) for a in (x_in, grad_out, jnp.transpose(weight, (1, 0, 2)), bias_vec[None, :])],
        [SMEM] + [HBM] * 4,
        [
            pltpu.VMEM((o, n, rows, depth), bf16),
            pltpu.VMEM((27, o, c_all), bf16),
            pltpu.VMEM((1, o), bf16),
            *block_wide,
            pltpu.SemaphoreType.DMA((4,)),
        ],
        name="prepare",
    )
    go_first = swap(go_first, "slab", 1)
    go_second = swap(go_second, "slab", 3)
    x_b, w_flat = lax.optimization_barrier((x_b, w_flat))
    x_ab = swap(x_b, "chan", 2)
    late_b, go_first, go_second = lax.optimization_barrier((x_b, go_first, go_second))
    x_a_side = swap(x_a, "chan", 1)
    x_b_side = swap(late_b, "chan", 1)
    early, late = (0, 1, 2, 3, 4, 5, 6), (7,)
    (x_all,) = call(
        functools.partial(assemble_body, early),
        [shape_of((c_all, cells * depth), bf16)],
        [me, x_own, x_a, x_b, x_ab, x_side, x_a_side, x_b_side],
        [SMEM] + [VMEM] * 7,
        block_wide,
        flops=ASSEMBLE_FLOPS,
        name="assemble",
    )
    x_ab_side = swap(x_ab, "chan", 1)
    own, *sent, x_all = call(
        functools.partial(forward_body, n, rows, o, late),
        [
            shape_of((cells, o, depth), f32),
            *[shape_of((rows, o, depth), bf16)] * 4,
            shape_of((c_all, cells * depth), bf16),
        ],
        [me, slab, w_flat, x_ab_side, x_all],
        [SMEM] * 2 + [VMEM] * 3,
        [pltpu.VMEM((3, n + 2, rows, o, depth), f32), *block_wide],
        flops=FORWARD_FLOPS,
        name="forward",
        aliases={4: 5},
    )
    received = [swap(a, "slab", 1 + 2 * (at % 2)) for at, a in enumerate(sent)]
    act, total, own_shifts, partial = call(
        functools.partial(own_gradient_body, rows, o, scale),
        [
            shape_of((o, n, rows, depth), bf16),
            shape_of((o, LANES), f32),
            shape_of((18 * o, cells * depth), bf16),
            shape_of((c_all, cells * depth), f32),
        ],
        [me, slab, own, *received[:2], bias, go, *w_back[:2]],
        [SMEM] * 2 + [VMEM] * 7,
        [*[pltpu.VMEM((c_all, 18 * o), bf16)] * 2, *block_wide],
        flops=flops * 2 // 3,
        name="own_gradient",
    )
    filters, token = call(
        own_filter_body,
        [shape_of((27 * o, c_all), f32), shape_of((8, LANES), f32)],
        [own_shifts, x_all],
        flops=flops * 2 // 3,
        name="own_filter",
    )
    rim_shifts, other, mine = call(
        functools.partial(rim_gradient_body, rows, o),
        [
            shape_of((9 * o, cells * depth), bf16),
            shape_of((4, cells, o, depth), bf16),
            shape_of((4, cells, o, depth), bf16),
        ],
        [me, slab, *sent[:2], *received[2:], bias, go_first, go_second, partial, *w_back[2:], token],
        [SMEM] * 2 + [VMEM] * 10 + [ANY],
        [pltpu.VMEM((c_all, 9 * o), bf16)] * 2,
        flops=flops // 3,
        name="rim_gradient",
    )
    other = swap(other, "chan", 1)
    taps = 14
    first, second = call(
        functools.partial(rim_filter_body, scale, taps, o),
        [shape_of((taps * o, c_all), bf16), shape_of(((28 - taps) * o, c_all), bf16)],
        [rim_shifts, x_all, filters, total],
        flops=flops // 3,
        name="rim_filter",
    )
    first_far = cross(first, 0)
    second_far = cross(second, 0)
    g_own, g_a, g_b, g_ab = call(
        core_sum_body,
        [shape_of((cells, o, depth), f32)] + [shape_of((cells, o, depth), bf16)] * 3,
        [mine, other],
        name="core_sum",
    )
    g_ab = swap(g_ab, "chan", 6)
    g_b = swap(g_b, "chan", 4)
    g_a = swap(g_a, "chan", 2)
    first, second = (
        call(
            pair_body,
            [shape_of(a.shape, bf16)],
            [a, b, g_own],
            [VMEM] * 2 + [ANY],
            name="pair_sum",
        )[0]
        for a, b in ((first, first_far), (second, second_far))
    )
    first_far = cross(first, 1)
    second_far = cross(second, 1)
    (g_own,) = call(
        sum_body,
        [shape_of((cells, o, depth), f32)],
        [g_own, g_b, g_ab, g_a],
        flops=SUM_FLOPS,
        name="sum",
    )
    weight_grad, bias_grad, grad_in = call(
        functools.partial(last_body, taps),
        [
            shape_of((27, o, c_all), f32),
            shape_of((1, o), f32),
            shape_of((o, n, rows, depth), bf16),
        ],
        [first, first_far, second, second_far, g_own],
        scratch=block_wide,
        name="last",
    )
    return act, grad_in, jnp.transpose(weight_grad, (1, 0, 2)), bias_grad[0]


def solution(mesh):
    placed = (
        P("chan", "slab", None, None),
        P("chan", None, None),
        P("chan"),
        P("chan", "slab", None, None),
    )

    def body(x_in, weight, bias_vec, grad_out):
        tiled = (
            weight.shape[0] % 32 == 0
            and x_in.shape[3] == LANES
            and lax.axis_size("slab") == 4
            and lax.axis_size("chan") == 8
            and x_in.shape[1] == 2
        )
        return (on_device if tiled else plain)(x_in, weight, bias_vec, grad_out)

    return jax.shard_map(
        body,
        mesh=mesh,
        in_specs=placed,
        out_specs=(
            P("chan", "slab", None, None),
            P("chan", "slab", None, None),
            P("chan", None, None),
            P("chan"),
        ),
        check_vma=False,
    )
```

```python
import functools
import math

import jax
import jax.numpy as jnp
from jax import lax
from jax.experimental import pallas as pl
from jax.experimental.pallas import tpu as pltpu
from jax.sharding import PartitionSpec as P

LANES = 128
SUM_FLOPS = 24 * 10**8
ASSEMBLE_FLOPS = 40 * 10**8
VMEM = pl.BlockSpec(memory_space=pltpu.VMEM)
ANY = pl.BlockSpec(memory_space=pl.ANY)
HBM = pl.BlockSpec(memory_space=pltpu.HBM)
SMEM = pl.BlockSpec(memory_space=pltpu.SMEM)


def with_halo(block, sides, width):
    for axis, dim in sides:
        count = lax.axis_size(axis)
        forward = [(i, i + 1) for i in range(count - 1)]
        forward.append((count - 1, 0))
        backward = [(target, source) for source, target in forward]
        low = lax.ppermute(
            lax.slice_in_dim(block, block.shape[dim] - width, None, axis=dim), axis, forward
        )
        high = lax.ppermute(lax.slice_in_dim(block, 0, width, axis=dim), axis, backward)
        block = jnp.concatenate([low, block, high], axis=dim)
    return block


def tap_list():
    return [(9 * i + 3 * j + l, i, j, l) for i in range(3) for j in range(3) for l in range(3)]


def plain(x_in, weight, bias_vec, grad_out):
    out_local, n_taps, in_total = weight.shape
    n_planes, n_rows, n_depth = (x_in.shape[1], x_in.shape[2], x_in.shape[3])
    rimmed = with_halo(x_in, (("slab", 1),), 1)
    padded = lax.all_gather(rimmed, "chan", axis=0, tiled=True)
    own_planes = padded[:, 1 : n_planes + 1]
    pre_act = (
        jnp.zeros((out_local, n_planes, n_rows, n_depth), jnp.float32)
        + bias_vec.astype(jnp.float32)[:, None, None, None]
    )
    for i in range(3):
        w_plane = jnp.transpose(weight[:, 9 * i : 9 * i + 9], (1, 0, 2)).reshape(
            9 * out_local, in_total
        )
        plane_part = jnp.dot(
            w_plane,
            padded[:, i : i + n_planes].reshape(in_total, -1),
            preferred_element_type=jnp.float32,
        )
        plane_part = plane_part.reshape(9, out_local, n_planes, n_rows, n_depth)
        for j in range(3):
            for l in range(3):
                pre_act = pre_act + jnp.roll(plane_part[3 * j + l], (1 - j, 1 - l), axis=(2, 3))
    sigmoid_v = jax.nn.sigmoid(pre_act)
    activation = (pre_act * sigmoid_v).astype(jnp.bfloat16)
    slope = sigmoid_v * (1.0 + pre_act * (1.0 - sigmoid_v))
    grad_pre = (grad_out.astype(jnp.float32) * slope).astype(jnp.bfloat16)
    padded_grad = with_halo(grad_pre, (("slab", 1),), 1)
    shifted = jnp.stack(
        [
            jnp.roll(padded_grad[:, 2 - i : 2 - i + n_planes], (j - 1, l - 1), axis=(2, 3))
            for k, i, j, l in tap_list()
        ],
        0,
    )
    shifted = shifted.reshape(n_taps * out_local, -1)
    grad_scale = 1.0 / math.sqrt(lax.axis_size("slab") * n_planes * n_rows * n_depth)
    filter_local = lax.dot_general(
        shifted,
        own_planes.reshape(in_total, -1),
        (((1,), (1,)), ((), ())),
        preferred_element_type=jnp.float32,
    )
    filter_part = (
        jnp.transpose(filter_local.reshape(n_taps, out_local, in_total), (1, 0, 2)) * grad_scale
    )
    bias_part = grad_scale * jnp.sum(grad_pre.astype(jnp.float32), axis=(1, 2, 3))
    bias_row = jnp.concatenate(
        [bias_part[:, None, None], jnp.zeros((out_local, 1, in_total - 1), jnp.float32)], 2
    )
    summed_filters = lax.psum(jnp.concatenate([filter_part, bias_row], 1), "slab")
    weight_grad = summed_filters[:, :n_taps]
    bias_grad = summed_filters[:, n_taps, 0]
    flat_w = jnp.transpose(weight, (1, 0, 2)).reshape(n_taps * out_local, in_total)
    product = lax.dot_general(
        flat_w, shifted, (((0,), (0,)), ((), ())), preferred_element_type=jnp.float32
    )
    grad_in = lax.psum_scatter(
        product.reshape(
            in_total // lax.axis_size("chan") * lax.axis_size("chan"), n_planes, n_rows, n_depth
        ),
        "chan",
        scatter_dimension=0,
        tiled=True,
    )
    return (activation, grad_in.astype(jnp.bfloat16), weight_grad, bias_grad)


def call(body, out_shape, operands, specs=None, scratch=(), flops=0, name=None, aliases=None):
    read = sum(math.prod(a.shape) * a.dtype.itemsize for a in operands)
    written = sum(math.prod(a.shape) * a.dtype.itemsize for a in out_shape)
    return pl.pallas_call(
        body,
        out_shape=out_shape,
        in_specs=specs or [VMEM] * len(operands),
        out_specs=[VMEM] * len(out_shape),
        scratch_shapes=list(scratch),
        input_output_aliases=aliases or {},
        compiler_params=pltpu.CompilerParams(vmem_limit_bytes=24 * 2**20),
        cost_estimate=pl.CostEstimate(
            flops=flops, bytes_accessed=read + written, transcendentals=0
        ),
        name=name,
    )(*operands)


def shape_of(shape, dtype):
    return jax.ShapeDtypeStruct(shape, dtype)


def by_parity(slab_ref, a, b):
    even = lax.rem(slab_ref[0], 2) == 0
    f32 = jnp.float32
    wide = a.astype(f32), b.astype(f32)
    return (
        jnp.where(even, wide[0], wide[1]).astype(a.dtype),
        jnp.where(even, wide[1], wide[0]).astype(a.dtype),
    )


def turned(value, wide_ref):
    o = value.shape[0]
    cells = wide_ref.shape[0] // o
    wide_ref[...] = value.astype(jnp.float32).reshape(wide_ref.shape)
    return [
        wide_ref[pl.ds(k, o, stride=cells), :].astype(value.dtype) for k in range(cells)
    ]


def prepare_body(
    n,
    rows,
    slab_ref,
    x_hbm,
    go_hbm,
    w_hbm,
    bias_hbm,
    x_ref,
    go_ref,
    go_first_ref,
    go_second_ref,
    flat_ref,
    own_0_ref,
    own_1_ref,
    rim_0_ref,
    rim_1_ref,
    bias_ref,
    go_in,
    w_in,
    bias_in,
    wide_ref,
    sems,
):
    copies = [
        pltpu.make_async_copy(source, target, sems.at[at])
        for at, (source, target) in enumerate(
            [(go_hbm, go_in), (w_hbm, w_in), (bias_hbm, bias_in), (x_hbm, x_ref)]
        )
    ]
    for copy in copies:
        copy.start()
    copies[0].wait()
    values = turned(go_in[...], wide_ref)
    for k, value in enumerate(values):
        go_ref[k] = value
    for y in range(rows):
        low, high = values[y], values[(n - 1) * rows + y]
        go_first_ref[y], go_second_ref[y] = by_parity(slab_ref, high, low)
    copies[1].wait()
    copies[2].wait()
    copies[3].wait()
    flat = w_in[...].reshape(flat_ref.shape)
    flat_ref[...] = flat
    third = flat.shape[0] // 3
    own_0_ref[...] = jnp.transpose(flat[: 2 * third])
    own_1_ref[...] = jnp.transpose(flat[third:])
    rim_0_ref[...] = jnp.transpose(flat[2 * third :])
    rim_1_ref[...] = jnp.transpose(flat[:third])
    o = bias_ref.shape[0]
    row = jnp.broadcast_to(bias_in[...].astype(jnp.float32), (o, o))
    same = lax.broadcasted_iota(jnp.int32, (o, o), 0) == lax.broadcasted_iota(jnp.int32, (o, o), 1)
    column = jnp.sum(jnp.where(same, row, 0.0), axis=1, keepdims=True)
    bias_ref[...] = jnp.broadcast_to(column, bias_ref.shape)


def place_block(me_ref, b, block_ref, x_ref, wide_ref):
    o = block_ref.shape[0]
    place = pl.ds(pl.multiple_of(owner(me_ref, b) * o, o), o)
    for k, value in enumerate(turned(block_ref[...], wide_ref)):
        x_ref[place, k * LANES : (k + 1) * LANES] = value


def assemble_body(places, me_ref, *refs):
    blocks, (x_ref, wide_ref) = refs[: len(places)], refs[-2:]
    for b, block in zip(places, blocks):
        place_block(me_ref, b, block, x_ref, wide_ref)


def owner(me_ref, b):
    return jnp.bitwise_xor(me_ref[0], 2 * (b % 4) + b // 4)


def plane_sums(rows, o, w_ref, x_ref, acc, chosen):
    seen = set()
    for p in range(2):
        near = [i for i in range(3) if (p, i) in chosen]
        base = 9 * near[0]
        w = w_ref[base * o : 9 * (near[-1] + 1) * o]
        for t in range(0, rows, 2):
            at = (p * rows + t) * LANES
            part = jnp.dot(
                w, x_ref[:, at : at + 2 * LANES], preferred_element_type=jnp.float32
            )
            for k, i, j, l in tap_list():
                if i not in near:
                    continue
                for h in range(2):
                    slot = (l, chosen[p, i], (t + h + 1 - j) % rows)
                    value = part[(k - base) * o : (k - base + 1) * o, h * LANES : (h + 1) * LANES]
                    if slot in seen:
                        acc[slot] += value
                    else:
                        acc[slot] = value
                        seen.add(slot)
    return [
        [
            pltpu.roll(acc[0, q, y], 1, 1) + acc[1, q, y] + pltpu.roll(acc[2, q, y], LANES - 1, 1)
            for y in range(rows)
        ]
        for q in range(2)
    ]


def send_sums(slab_ref, sums, refs):
    for y, (low, high) in enumerate(zip(*sums)):
        for ref, value in zip(refs, by_parity(slab_ref, high, low)):
            ref[y] = value.astype(ref.dtype)


def rim_forward_body(
    rows, o, place, me_ref, slab_ref, w_ref, block_ref, _, first_ref, second_ref, x_ref, acc, wide_ref
):
    place_block(me_ref, place, block_ref, x_ref, wide_ref)
    sums = plane_sums(rows, o, w_ref, x_ref, acc, {(0, 2): 0, (1, 0): 1})
    send_sums(slab_ref, sums, (first_ref, second_ref))


def own_forward_body(rows, o, slab_ref, w_ref, x_ref, own_ref, first_ref, second_ref, acc):
    sums = plane_sums(
        rows, o, w_ref, x_ref, acc, {(0, 0): 1, (0, 1): 0, (1, 1): 1, (1, 2): 0}
    )
    for y in range(rows):
        own_ref[y] = sums[0][y]
        own_ref[rows + y] = sums[1][y]
    send_sums(slab_ref, sums, (first_ref, second_ref))


def ordered(me_ref, o, in_refs, out_refs):
    for in_ref, out_ref in zip(in_refs, out_refs):
        for b in range(8):
            place = pl.ds(pl.multiple_of(owner(me_ref, b) * o, o), o)
            out_ref[b * o : (b + 1) * o] = in_ref[place]


def three_shifts(wide, dtype):
    return [
        pltpu.roll(wide, LANES - 1, 1).astype(dtype),
        wide.astype(dtype),
        pltpu.roll(wide, 1, 1).astype(dtype),
    ]


def own_gradient_body(
    rows,
    o,
    scale,
    me_ref,
    slab_ref,
    own_ref,
    first_ref,
    second_ref,
    bias_ref,
    go_ref,
    w_0_ref,
    w_1_ref,
    act_ref,
    total_ref,
    s_ref,
    partial_ref,
    w_0,
    w_1,
    wide_ref,
):
    f32, bf16 = jnp.float32, jnp.bfloat16
    ordered(me_ref, o, (w_0_ref, w_1_ref), (w_0, w_1))
    total = jnp.zeros((o, LANES), f32)
    for q in range(2):
        for y in range(rows):
            beside = by_parity(slab_ref, first_ref[y], second_ref[y])[1 - q]
            pre = own_ref[q * rows + y] + beside.astype(f32) + bias_ref[...]
            s = jax.nn.sigmoid(pre)
            slope = s * (1.0 + pre * (1.0 - s))
            wide = (go_ref[q * rows + y].astype(f32) * slope).astype(bf16).astype(f32)
            wide_ref[pl.ds(q * rows + y, o, stride=2 * rows), :] = pre * s
            total = total + wide
            shifts = three_shifts(wide, bf16)
            for k, i, j, l in tap_list():
                p = q - 1 + i
                if 0 <= p < 2:
                    at = (p * rows + (y + j - 1) % rows) * LANES
                    row = (k - 9 * p) * o
                    s_ref[row : row + o, at : at + LANES] = shifts[l]
    for t in range(0, 2 * rows, 2):
        at = slice(t * LANES, (t + 2) * LANES)
        w = w_0 if t < rows else w_1
        partial_ref[:, at] = jnp.dot(w[...], s_ref[:, at], preferred_element_type=f32)
    act_ref[...] = wide_ref[...].reshape(act_ref.shape).astype(bf16)
    total_ref[...] = jnp.broadcast_to(
        jnp.sum(total, axis=1, keepdims=True) * scale, total_ref.shape
    )


def rim_gradient_body(
    rows,
    o,
    me_ref,
    slab_ref,
    first_ref,
    second_ref,
    first_in_ref,
    second_in_ref,
    bias_ref,
    go_first_ref,
    go_second_ref,
    partial_ref,
    w_0_ref,
    w_1_ref,
    _,
    s_ref,
    other_ref,
    mine_ref,
    w_0,
    w_1,
):
    f32, bf16 = jnp.float32, jnp.bfloat16
    ordered(me_ref, o, (w_0_ref, w_1_ref), (w_0, w_1))
    pairs = (
        (first_in_ref, second_in_ref),
        (first_ref, second_ref),
        (go_first_ref, go_second_ref),
    )
    for p in range(2):
        for y in range(rows):
            theirs, ours, go = (
                by_parity(slab_ref, first[y], second[y])[1 - p].astype(f32)
                for first, second in pairs
            )
            pre = theirs + ours + bias_ref[...]
            s = jax.nn.sigmoid(pre)
            slope = s * (1.0 + pre * (1.0 - s))
            wide = (go * slope).astype(bf16).astype(f32)
            shifts = three_shifts(wide, bf16)
            for j in range(3):
                for l in range(3):
                    at = (p * rows + (y + j - 1) % rows) * LANES
                    row = (3 * j + l) * o
                    s_ref[row : row + o, at : at + LANES] = shifts[l]
    for t in range(0, 2 * rows, 2):
        at = slice(t * LANES, (t + 2) * LANES)
        w = w_0 if t < rows else w_1
        part = jnp.dot(w[...], s_ref[:, at], preferred_element_type=f32)
        part = (part + partial_ref[:, at]).astype(bf16)
        for h in range(2):
            for b in range(8):
                cut = part[b * o : (b + 1) * o, h * LANES : (h + 1) * LANES]
                (mine_ref if b < 4 else other_ref)[b % 4, t + h] = cut


def filter_product(s_ref, x_ref, plane):
    half = x_ref.shape[1] // 2
    at = slice(plane * half, (plane + 1) * half)
    return lax.dot_general(
        s_ref[:, at], x_ref[:, at], (((1,), (1,)), ((), ())), preferred_element_type=jnp.float32
    )


def own_filter_body(s_ref, x_ref, out_ref, token_ref):
    token_ref[...] = jnp.zeros_like(token_ref)
    third = out_ref.shape[0] // 3
    low, high = (filter_product(s_ref, x_ref, p) for p in range(2))
    out_ref[:third] = low[:third]
    out_ref[third : 2 * third] = low[third:] + high[:third]
    out_ref[2 * third :] = high[third:]


def rim_filter_body(scale, taps, o, s_ref, x_ref, own_ref, total_ref, first_ref, second_ref):
    third = own_ref.shape[0] // 3
    cut = taps * o
    high = own_ref[:third] + filter_product(s_ref, x_ref, 1)
    low = own_ref[2 * third :] + filter_product(s_ref, x_ref, 0)
    dtype = first_ref.dtype
    first_ref[:third] = (high * scale).astype(dtype)
    first_ref[third:] = (own_ref[third:cut] * scale).astype(dtype)
    second_ref[: 2 * third - cut] = (own_ref[cut : 2 * third] * scale).astype(dtype)
    second_ref[2 * third - cut : 27 * o - cut] = (low * scale).astype(dtype)
    row = jnp.concatenate([total_ref[...]] * (second_ref.shape[1] // LANES), axis=1)
    second_ref[27 * o - cut :] = row.astype(dtype)


def pair_body(a_ref, b_ref, _, out_ref):
    f32 = jnp.float32
    out_ref[...] = (a_ref[...].astype(f32) + b_ref[...].astype(f32)).astype(out_ref.dtype)


def core_sum_body(mine_ref, other_ref, *outs):
    for r, out_ref in enumerate(outs):
        total = mine_ref[r].astype(jnp.float32) + other_ref[r].astype(jnp.float32)
        out_ref[...] = total.astype(out_ref.dtype)


def sum_body(a_ref, b_ref, c_ref, d_ref, out_ref):
    f32 = jnp.float32
    total = b_ref[...].astype(f32) + c_ref[...].astype(f32) + d_ref[...].astype(f32)
    out_ref[...] = a_ref[...] + total


def last_body(
    taps, a_ref, b_ref, c_ref, d_ref, g_ref, out_ref, bias_ref, grad_ref, wide_ref
):
    o = out_ref.shape[1]
    f32 = jnp.float32
    cells = g_ref.shape[0]
    for k in range(cells):
        wide_ref[pl.ds(k, o, stride=cells), :] = g_ref[k]
    grad_ref[...] = wide_ref[...].reshape(grad_ref.shape).astype(grad_ref.dtype)
    for k in range(27):
        left, right, at = (a_ref, b_ref, k) if k < taps else (c_ref, d_ref, k - taps)
        cut = slice(at * o, (at + 1) * o)
        out_ref[k] = left[cut].astype(f32) + right[cut].astype(f32)
    cut = slice((27 - taps) * o, (28 - taps) * o)
    column = (c_ref[cut].astype(f32) + d_ref[cut].astype(f32))[:, :o]
    same = lax.broadcasted_iota(jnp.int32, (o, o), 0) == lax.broadcasted_iota(jnp.int32, (o, o), 1)
    bias_ref[...] = jnp.sum(jnp.where(same, column, 0.0), axis=0, keepdims=True)


def in_hbm(value):
    return pltpu.with_memory_space_constraint(value, pltpu.HBM)


def swap(value, axis, bit):
    return lax.ppermute(value, axis, [(i, i ^ bit) for i in range(lax.axis_size(axis))])


def cross(value, phase):
    slabs, chans = lax.axis_size("slab"), lax.axis_size("chan")
    pairs = [
        (s * chans + c, (s ^ (1 + (c + phase) % 2)) * chans + c)
        for s in range(slabs)
        for c in range(chans)
    ]
    return lax.ppermute(value, ("slab", "chan"), pairs)


def on_device(x_in, weight, bias_vec, grad_out):
    o, _, c_all = weight.shape
    _, n, rows, depth = x_in.shape
    f32, bf16 = jnp.float32, jnp.bfloat16
    cells = n * rows
    flops = 2 * 27 * o * c_all * cells * depth
    scale = 1.0 / math.sqrt(lax.axis_size("slab") * cells * depth)
    me = lax.axis_index("chan").astype(jnp.int32).reshape(1)
    slab = lax.axis_index("slab").astype(jnp.int32).reshape(1)

    block_wide = [pltpu.VMEM((o * cells, depth), f32)]

    x_b = swap(x_in, "chan", 4)
    x_a = swap(x_in, "chan", 2)
    x_side = swap(x_in, "chan", 1)
    x_own, go, go_first, go_second, w_flat, *w_back, bias = call(
        functools.partial(prepare_body, n, rows),
        [
            shape_of((o, n, rows, depth), bf16),
            shape_of((cells, o, depth), bf16),
            shape_of((rows, o, depth), bf16),
            shape_of((rows, o, depth), bf16),
            shape_of((27 * o, c_all), bf16),
            *[shape_of((c_all, taps * o), bf16) for taps in (18, 18, 9, 9)],
            shape_of((o, LANES), f32),
        ],
        [slab] + [in_hbm(a) for a in (x_in, grad_out, jnp.transpose(weight, (1, 0, 2)), bias_vec[None, :])],
        [SMEM] + [HBM] * 4,
        [
            pltpu.VMEM((o, n, rows, depth), bf16),
            pltpu.VMEM((27, o, c_all), bf16),
            pltpu.VMEM((1, o), bf16),
            *block_wide,
            pltpu.SemaphoreType.DMA((4,)),
        ],
        name="prepare",
    )
    go_first = swap(go_first, "slab", 1)
    go_second = swap(go_second, "slab", 3)
    x_b, w_flat = lax.optimization_barrier((x_b, w_flat))
    x_ab = swap(x_b, "chan", 2)
    late_b, go_first, go_second = lax.optimization_barrier((x_b, go_first, go_second))
    x_a_side = swap(x_a, "chan", 1)
    x_b_side = swap(late_b, "chan", 1)
    early = (0, 1, 2, 3, 4, 5, 6)
    (x_all,) = call(
        functools.partial(assemble_body, early),
        [shape_of((c_all, cells * depth), bf16)],
        [me, x_own, x_a, x_b, x_ab, x_side, x_a_side, x_b_side],
        [SMEM] + [VMEM] * 7,
        block_wide,
        flops=ASSEMBLE_FLOPS,
        name="assemble",
    )
    x_ab_side = swap(x_ab, "chan", 1)
    sums = [pltpu.VMEM((3, 2, rows, o, depth), f32)]
    *sent, x_all = call(
        functools.partial(rim_forward_body, rows, o, 7),
        [shape_of((rows, o, depth), bf16)] * 2 + [shape_of((c_all, cells * depth), bf16)],
        [me, slab, w_flat, x_ab_side, x_all],
        [SMEM] * 2 + [VMEM] * 3,
        sums + block_wide,
        flops=flops // 3,
        name="rim_forward",
        aliases={4: 2},
    )
    own, *sent_own = call(
        functools.partial(own_forward_body, rows, o),
        [shape_of((cells, o, depth), f32)] + [shape_of((rows, o, depth), bf16)] * 2,
        [slab, w_flat, x_all],
        [SMEM] + [VMEM] * 2,
        sums,
        flops=flops * 2 // 3,
        name="own_forward",
    )
    sent += sent_own
    received = [swap(a, "slab", 1 + 2 * (at % 2)) for at, a in enumerate(sent)]
    act, total, own_shifts, partial = call(
        functools.partial(own_gradient_body, rows, o, scale),
        [
            shape_of((o, n, rows, depth), bf16),
            shape_of((o, LANES), f32),
            shape_of((18 * o, cells * depth), bf16),
            shape_of((c_all, cells * depth), f32),
        ],
        [me, slab, own, *received[:2], bias, go, *w_back[:2]],
        [SMEM] * 2 + [VMEM] * 7,
        [*[pltpu.VMEM((c_all, 18 * o), bf16)] * 2, *block_wide],
        flops=flops * 2 // 3,
        name="own_gradient",
    )
    filters, token = call(
        own_filter_body,
        [shape_of((27 * o, c_all), f32), shape_of((8, LANES), f32)],
        [own_shifts, x_all],
        flops=flops * 2 // 3,
        name="own_filter",
    )
    rim_shifts, other, mine = call(
        functools.partial(rim_gradient_body, rows, o),
        [
            shape_of((9 * o, cells * depth), bf16),
            shape_of((4, cells, o, depth), bf16),
            shape_of((4, cells, o, depth), bf16),
        ],
        [me, slab, *sent[:2], *received[2:], bias, go_first, go_second, partial, *w_back[2:], token],
        [SMEM] * 2 + [VMEM] * 10 + [ANY],
        [pltpu.VMEM((c_all, 9 * o), bf16)] * 2,
        flops=flops // 3,
        name="rim_gradient",
    )
    other = swap(other, "chan", 1)
    taps = 14
    first, second = call(
        functools.partial(rim_filter_body, scale, taps, o),
        [shape_of((taps * o, c_all), bf16), shape_of(((28 - taps) * o, c_all), bf16)],
        [rim_shifts, x_all, filters, total],
        flops=flops // 3,
        name="rim_filter",
    )
    first_far = cross(first, 0)
    second_far = cross(second, 0)
    g_own, g_a, g_b, g_ab = call(
        core_sum_body,
        [shape_of((cells, o, depth), f32)] + [shape_of((cells, o, depth), bf16)] * 3,
        [mine, other],
        name="core_sum",
    )
    g_ab = swap(g_ab, "chan", 6)
    g_b = swap(g_b, "chan", 4)
    g_a = swap(g_a, "chan", 2)
    first, second = (
        call(
            pair_body,
            [shape_of(a.shape, bf16)],
            [a, b, g_own],
            [VMEM] * 2 + [ANY],
            name="pair_sum",
        )[0]
        for a, b in ((first, first_far), (second, second_far))
    )
    first_far = cross(first, 1)
    second_far = cross(second, 1)
    (g_own,) = call(
        sum_body,
        [shape_of((cells, o, depth), f32)],
        [g_own, g_b, g_ab, g_a],
        flops=SUM_FLOPS,
        name="sum",
    )
    weight_grad, bias_grad, grad_in = call(
        functools.partial(last_body, taps),
        [
            shape_of((27, o, c_all), f32),
            shape_of((1, o), f32),
            shape_of((o, n, rows, depth), bf16),
        ],
        [first, first_far, second, second_far, g_own],
        scratch=block_wide,
        name="last",
    )
    return act, grad_in, jnp.transpose(weight_grad, (1, 0, 2)), bias_grad[0]


def solution(mesh):
    placed = (
        P("chan", "slab", None, None),
        P("chan", None, None),
        P("chan"),
        P("chan", "slab", None, None),
    )

    def body(x_in, weight, bias_vec, grad_out):
        tiled = (
            weight.shape[0] % 32 == 0
            and x_in.shape[3] == LANES
            and lax.axis_size("slab") == 4
            and lax.axis_size("chan") == 8
            and x_in.shape[1] == 2
        )
        return (on_device if tiled else plain)(x_in, weight, bias_vec, grad_out)

    return jax.shard_map(
        body,
        mesh=mesh,
        in_specs=placed,
        out_specs=(
            P("chan", "slab", None, None),
            P("chan", "slab", None, None),
            P("chan", None, None),
            P("chan"),
        ),
        check_vma=False,
    )
```

```python
import functools
import math

import jax
import jax.numpy as jnp
from jax import lax
from jax.experimental import pallas as pl
from jax.experimental.pallas import tpu as pltpu
from jax.sharding import PartitionSpec as P

LANES = 128
SUM_FLOPS = 24 * 10**8
ASSEMBLE_FLOPS = 40 * 10**8
VMEM = pl.BlockSpec(memory_space=pltpu.VMEM)
ANY = pl.BlockSpec(memory_space=pl.ANY)
HBM = pl.BlockSpec(memory_space=pltpu.HBM)
SMEM = pl.BlockSpec(memory_space=pltpu.SMEM)


def with_halo(block, sides, width):
    for axis, dim in sides:
        count = lax.axis_size(axis)
        forward = [(i, i + 1) for i in range(count - 1)]
        forward.append((count - 1, 0))
        backward = [(target, source) for source, target in forward]
        low = lax.ppermute(
            lax.slice_in_dim(block, block.shape[dim] - width, None, axis=dim), axis, forward
        )
        high = lax.ppermute(lax.slice_in_dim(block, 0, width, axis=dim), axis, backward)
        block = jnp.concatenate([low, block, high], axis=dim)
    return block


def tap_list():
    return [(9 * i + 3 * j + l, i, j, l) for i in range(3) for j in range(3) for l in range(3)]


def plain(x_in, weight, bias_vec, grad_out):
    out_local, n_taps, in_total = weight.shape
    n_planes, n_rows, n_depth = (x_in.shape[1], x_in.shape[2], x_in.shape[3])
    rimmed = with_halo(x_in, (("slab", 1),), 1)
    padded = lax.all_gather(rimmed, "chan", axis=0, tiled=True)
    own_planes = padded[:, 1 : n_planes + 1]
    pre_act = (
        jnp.zeros((out_local, n_planes, n_rows, n_depth), jnp.float32)
        + bias_vec.astype(jnp.float32)[:, None, None, None]
    )
    for i in range(3):
        w_plane = jnp.transpose(weight[:, 9 * i : 9 * i + 9], (1, 0, 2)).reshape(
            9 * out_local, in_total
        )
        plane_part = jnp.dot(
            w_plane,
            padded[:, i : i + n_planes].reshape(in_total, -1),
            preferred_element_type=jnp.float32,
        )
        plane_part = plane_part.reshape(9, out_local, n_planes, n_rows, n_depth)
        for j in range(3):
            for l in range(3):
                pre_act = pre_act + jnp.roll(plane_part[3 * j + l], (1 - j, 1 - l), axis=(2, 3))
    sigmoid_v = jax.nn.sigmoid(pre_act)
    activation = (pre_act * sigmoid_v).astype(jnp.bfloat16)
    slope = sigmoid_v * (1.0 + pre_act * (1.0 - sigmoid_v))
    grad_pre = (grad_out.astype(jnp.float32) * slope).astype(jnp.bfloat16)
    padded_grad = with_halo(grad_pre, (("slab", 1),), 1)
    shifted = jnp.stack(
        [
            jnp.roll(padded_grad[:, 2 - i : 2 - i + n_planes], (j - 1, l - 1), axis=(2, 3))
            for k, i, j, l in tap_list()
        ],
        0,
    )
    shifted = shifted.reshape(n_taps * out_local, -1)
    grad_scale = 1.0 / math.sqrt(lax.axis_size("slab") * n_planes * n_rows * n_depth)
    filter_local = lax.dot_general(
        shifted,
        own_planes.reshape(in_total, -1),
        (((1,), (1,)), ((), ())),
        preferred_element_type=jnp.float32,
    )
    filter_part = (
        jnp.transpose(filter_local.reshape(n_taps, out_local, in_total), (1, 0, 2)) * grad_scale
    )
    bias_part = grad_scale * jnp.sum(grad_pre.astype(jnp.float32), axis=(1, 2, 3))
    bias_row = jnp.concatenate(
        [bias_part[:, None, None], jnp.zeros((out_local, 1, in_total - 1), jnp.float32)], 2
    )
    summed_filters = lax.psum(jnp.concatenate([filter_part, bias_row], 1), "slab")
    weight_grad = summed_filters[:, :n_taps]
    bias_grad = summed_filters[:, n_taps, 0]
    flat_w = jnp.transpose(weight, (1, 0, 2)).reshape(n_taps * out_local, in_total)
    product = lax.dot_general(
        flat_w, shifted, (((0,), (0,)), ((), ())), preferred_element_type=jnp.float32
    )
    grad_in = lax.psum_scatter(
        product.reshape(
            in_total // lax.axis_size("chan") * lax.axis_size("chan"), n_planes, n_rows, n_depth
        ),
        "chan",
        scatter_dimension=0,
        tiled=True,
    )
    return (activation, grad_in.astype(jnp.bfloat16), weight_grad, bias_grad)


def call(body, out_shape, operands, specs=None, scratch=(), flops=0, name=None, aliases=None):
    read = sum(math.prod(a.shape) * a.dtype.itemsize for a in operands)
    written = sum(math.prod(a.shape) * a.dtype.itemsize for a in out_shape)
    return pl.pallas_call(
        body,
        out_shape=out_shape,
        in_specs=specs or [VMEM] * len(operands),
        out_specs=[VMEM] * len(out_shape),
        scratch_shapes=list(scratch),
        input_output_aliases=aliases or {},
        compiler_params=pltpu.CompilerParams(vmem_limit_bytes=24 * 2**20),
        cost_estimate=pl.CostEstimate(
            flops=flops, bytes_accessed=read + written, transcendentals=0
        ),
        name=name,
    )(*operands)


def shape_of(shape, dtype):
    return jax.ShapeDtypeStruct(shape, dtype)


def by_parity(slab_ref, a, b):
    even = lax.rem(slab_ref[0], 2) == 0
    f32 = jnp.float32
    wide = a.astype(f32), b.astype(f32)
    return (
        jnp.where(even, wide[0], wide[1]).astype(a.dtype),
        jnp.where(even, wide[1], wide[0]).astype(a.dtype),
    )


def turned(value, wide_ref):
    o = value.shape[0]
    cells = wide_ref.shape[0] // o
    wide_ref[...] = value.astype(jnp.float32).reshape(wide_ref.shape)
    return [
        wide_ref[pl.ds(k, o, stride=cells), :].astype(value.dtype) for k in range(cells)
    ]


def prepare_body(
    n,
    rows,
    slab_ref,
    x_hbm,
    go_hbm,
    w_hbm,
    bias_hbm,
    x_ref,
    go_ref,
    go_first_ref,
    go_second_ref,
    flat_ref,
    own_0_ref,
    own_1_ref,
    rim_0_ref,
    rim_1_ref,
    bias_ref,
    go_in,
    w_in,
    bias_in,
    wide_ref,
    sems,
):
    copies = [
        pltpu.make_async_copy(source, target, sems.at[at])
        for at, (source, target) in enumerate(
            [(go_hbm, go_in), (w_hbm, w_in), (bias_hbm, bias_in), (x_hbm, x_ref)]
        )
    ]
    for copy in copies:
        copy.start()
    copies[0].wait()
    values = turned(go_in[...], wide_ref)
    for k, value in enumerate(values):
        go_ref[k] = value
    for y in range(rows):
        low, high = values[y], values[(n - 1) * rows + y]
        go_first_ref[y], go_second_ref[y] = by_parity(slab_ref, high, low)
    copies[1].wait()
    copies[2].wait()
    copies[3].wait()
    flat = w_in[...].reshape(flat_ref.shape)
    flat_ref[...] = flat
    third = flat.shape[0] // 3
    own_0_ref[...] = jnp.transpose(flat[: 2 * third])
    own_1_ref[...] = jnp.transpose(flat[third:])
    rim_0_ref[...] = jnp.transpose(flat[2 * third :])
    rim_1_ref[...] = jnp.transpose(flat[:third])
    o = bias_ref.shape[0]
    row = jnp.broadcast_to(bias_in[...].astype(jnp.float32), (o, o))
    same = lax.broadcasted_iota(jnp.int32, (o, o), 0) == lax.broadcasted_iota(jnp.int32, (o, o), 1)
    column = jnp.sum(jnp.where(same, row, 0.0), axis=1, keepdims=True)
    bias_ref[...] = jnp.broadcast_to(column, bias_ref.shape)


def place_block(me_ref, b, block_ref, x_ref, wide_ref):
    o = block_ref.shape[0]
    place = pl.ds(pl.multiple_of(owner(me_ref, b) * o, o), o)
    for k, value in enumerate(turned(block_ref[...], wide_ref)):
        x_ref[place, k * LANES : (k + 1) * LANES] = value


def assemble_body(places, me_ref, *refs):
    blocks, (x_ref, wide_ref) = refs[: len(places)], refs[-2:]
    for b, block in zip(places, blocks):
        place_block(me_ref, b, block, x_ref, wide_ref)


def owner(me_ref, b):
    return jnp.bitwise_xor(me_ref[0], 2 * (b % 4) + b // 4)


def plane_sums(rows, o, w_ref, x_ref, acc, chosen):
    seen = set()
    for p in range(2):
        near = [i for i in range(3) if (p, i) in chosen]
        base = 9 * near[0]
        w = w_ref[base * o : 9 * (near[-1] + 1) * o]
        for t in range(0, rows, 2):
            at = (p * rows + t) * LANES
            part = jnp.dot(
                w, x_ref[:, at : at + 2 * LANES], preferred_element_type=jnp.float32
            )
            for k, i, j, l in tap_list():
                if i not in near:
                    continue
                for h in range(2):
                    slot = (l, chosen[p, i], (t + h + 1 - j) % rows)
                    value = part[(k - base) * o : (k - base + 1) * o, h * LANES : (h + 1) * LANES]
                    if slot in seen:
                        acc[slot] += value
                    else:
                        acc[slot] = value
                        seen.add(slot)
    return [
        [
            pltpu.roll(acc[0, q, y], 1, 1) + acc[1, q, y] + pltpu.roll(acc[2, q, y], LANES - 1, 1)
            for y in range(rows)
        ]
        for q in range(2)
    ]


def send_sums(slab_ref, sums, refs):
    for y, (low, high) in enumerate(zip(*sums)):
        for ref, value in zip(refs, by_parity(slab_ref, high, low)):
            ref[y] = value.astype(ref.dtype)


def rim_forward_body(
    rows, o, place, me_ref, slab_ref, w_ref, block_ref, _, first_ref, second_ref, x_ref, acc, wide_ref
):
    place_block(me_ref, place, block_ref, x_ref, wide_ref)
    sums = plane_sums(rows, o, w_ref, x_ref, acc, {(0, 2): 0, (1, 0): 1})
    send_sums(slab_ref, sums, (first_ref, second_ref))


def own_forward_body(rows, o, slab_ref, w_ref, x_ref, own_ref, first_ref, second_ref, acc):
    sums = plane_sums(
        rows, o, w_ref, x_ref, acc, {(0, 0): 1, (0, 1): 0, (1, 1): 1, (1, 2): 0}
    )
    for y in range(rows):
        own_ref[y] = sums[0][y]
        own_ref[rows + y] = sums[1][y]
    send_sums(slab_ref, sums, (first_ref, second_ref))


def ordered(me_ref, o, in_refs, out_refs):
    for in_ref, out_ref in zip(in_refs, out_refs):
        for b in range(8):
            place = pl.ds(pl.multiple_of(owner(me_ref, b) * o, o), o)
            out_ref[b * o : (b + 1) * o] = in_ref[place]


def three_shifts(wide, dtype):
    return [
        pltpu.roll(wide, LANES - 1, 1).astype(dtype),
        wide.astype(dtype),
        pltpu.roll(wide, 1, 1).astype(dtype),
    ]


def own_gradient_body(
    rows,
    o,
    scale,
    me_ref,
    slab_ref,
    own_ref,
    first_ref,
    second_ref,
    bias_ref,
    go_ref,
    w_0_ref,
    w_1_ref,
    act_ref,
    total_ref,
    s_ref,
    partial_ref,
    w_0,
    w_1,
    wide_ref,
):
    f32, bf16 = jnp.float32, jnp.bfloat16
    ordered(me_ref, o, (w_0_ref, w_1_ref), (w_0, w_1))
    total = jnp.zeros((o, LANES), f32)
    for q in range(2):
        for y in range(rows):
            beside = by_parity(slab_ref, first_ref[y], second_ref[y])[1 - q]
            pre = own_ref[q * rows + y] + beside.astype(f32) + bias_ref[...]
            s = jax.nn.sigmoid(pre)
            slope = s * (1.0 + pre * (1.0 - s))
            wide = (go_ref[q * rows + y].astype(f32) * slope).astype(bf16).astype(f32)
            wide_ref[pl.ds(q * rows + y, o, stride=2 * rows), :] = pre * s
            total = total + wide
            shifts = three_shifts(wide, bf16)
            for k, i, j, l in tap_list():
                p = q - 1 + i
                if 0 <= p < 2:
                    at = (p * rows + (y + j - 1) % rows) * LANES
                    row = (k - 9 * p) * o
                    s_ref[row : row + o, at : at + LANES] = shifts[l]
    for t in range(0, 2 * rows, 2):
        at = slice(t * LANES, (t + 2) * LANES)
        w = w_0 if t < rows else w_1
        partial_ref[:, at] = jnp.dot(w[...], s_ref[:, at], preferred_element_type=f32)
    act_ref[...] = wide_ref[...].reshape(act_ref.shape).astype(bf16)
    total_ref[...] = jnp.broadcast_to(
        jnp.sum(total, axis=1, keepdims=True) * scale, total_ref.shape
    )


def rim_gradient_body(
    rows,
    o,
    me_ref,
    slab_ref,
    first_ref,
    second_ref,
    first_in_ref,
    second_in_ref,
    bias_ref,
    go_first_ref,
    go_second_ref,
    partial_ref,
    w_0_ref,
    w_1_ref,
    s_ref,
    other_ref,
    mine_ref,
    w_0,
    w_1,
):
    f32, bf16 = jnp.float32, jnp.bfloat16
    ordered(me_ref, o, (w_0_ref, w_1_ref), (w_0, w_1))
    pairs = (
        (first_in_ref, second_in_ref),
        (first_ref, second_ref),
        (go_first_ref, go_second_ref),
    )
    for p in range(2):
        for y in range(rows):
            theirs, ours, go = (
                by_parity(slab_ref, first[y], second[y])[1 - p].astype(f32)
                for first, second in pairs
            )
            pre = theirs + ours + bias_ref[...]
            s = jax.nn.sigmoid(pre)
            slope = s * (1.0 + pre * (1.0 - s))
            wide = (go * slope).astype(bf16).astype(f32)
            shifts = three_shifts(wide, bf16)
            for j in range(3):
                for l in range(3):
                    at = (p * rows + (y + j - 1) % rows) * LANES
                    row = (3 * j + l) * o
                    s_ref[row : row + o, at : at + LANES] = shifts[l]
    for t in range(0, 2 * rows, 2):
        at = slice(t * LANES, (t + 2) * LANES)
        w = w_0 if t < rows else w_1
        part = jnp.dot(w[...], s_ref[:, at], preferred_element_type=f32)
        part = (part + partial_ref[:, at]).astype(bf16)
        for h in range(2):
            for b in range(8):
                cut = part[b * o : (b + 1) * o, h * LANES : (h + 1) * LANES]
                (mine_ref if b < 4 else other_ref)[b % 4, t + h] = cut


def filter_product(s_ref, x_ref, plane):
    half = x_ref.shape[1] // 2
    at = slice(plane * half, (plane + 1) * half)
    return lax.dot_general(
        s_ref[:, at], x_ref[:, at], (((1,), (1,)), ((), ())), preferred_element_type=jnp.float32
    )


def own_filter_body(s_ref, x_ref, out_ref):
    third = out_ref.shape[0] // 3
    low, high = (filter_product(s_ref, x_ref, p) for p in range(2))
    out_ref[:third] = low[:third]
    out_ref[third : 2 * third] = low[third:] + high[:third]
    out_ref[2 * third :] = high[third:]


def rim_filter_body(scale, taps, o, s_ref, x_ref, own_ref, total_ref, first_ref, second_ref):
    third = own_ref.shape[0] // 3
    cut = taps * o
    high = own_ref[:third] + filter_product(s_ref, x_ref, 1)
    low = own_ref[2 * third :] + filter_product(s_ref, x_ref, 0)
    dtype = first_ref.dtype
    first_ref[:third] = (high * scale).astype(dtype)
    first_ref[third:] = (own_ref[third:cut] * scale).astype(dtype)
    second_ref[: 2 * third - cut] = (own_ref[cut : 2 * third] * scale).astype(dtype)
    second_ref[2 * third - cut : 27 * o - cut] = (low * scale).astype(dtype)
    row = jnp.concatenate([total_ref[...]] * (second_ref.shape[1] // LANES), axis=1)
    second_ref[27 * o - cut :] = row.astype(dtype)


def pair_body(a_ref, b_ref, _, out_ref):
    f32 = jnp.float32
    out_ref[...] = (a_ref[...].astype(f32) + b_ref[...].astype(f32)).astype(out_ref.dtype)


def core_sum_body(mine_ref, other_ref, *outs):
    for r, out_ref in enumerate(outs):
        total = mine_ref[r].astype(jnp.float32) + other_ref[r].astype(jnp.float32)
        out_ref[...] = total.astype(out_ref.dtype)


def sum_body(a_ref, b_ref, c_ref, d_ref, out_ref):
    f32 = jnp.float32
    total = b_ref[...].astype(f32) + c_ref[...].astype(f32) + d_ref[...].astype(f32)
    out_ref[...] = a_ref[...] + total


def last_body(
    taps, a_ref, b_ref, c_ref, d_ref, g_ref, out_ref, bias_ref, grad_ref, wide_ref
):
    o = out_ref.shape[1]
    f32 = jnp.float32
    cells = g_ref.shape[0]
    for k in range(cells):
        wide_ref[pl.ds(k, o, stride=cells), :] = g_ref[k]
    grad_ref[...] = wide_ref[...].reshape(grad_ref.shape).astype(grad_ref.dtype)
    for k in range(27):
        left, right, at = (a_ref, b_ref, k) if k < taps else (c_ref, d_ref, k - taps)
        cut = slice(at * o, (at + 1) * o)
        out_ref[k] = left[cut].astype(f32) + right[cut].astype(f32)
    cut = slice((27 - taps) * o, (28 - taps) * o)
    column = (c_ref[cut].astype(f32) + d_ref[cut].astype(f32))[:, :o]
    same = lax.broadcasted_iota(jnp.int32, (o, o), 0) == lax.broadcasted_iota(jnp.int32, (o, o), 1)
    bias_ref[...] = jnp.sum(jnp.where(same, column, 0.0), axis=0, keepdims=True)


def in_hbm(value):
    return pltpu.with_memory_space_constraint(value, pltpu.HBM)


def swap(value, axis, bit):
    return lax.ppermute(value, axis, [(i, i ^ bit) for i in range(lax.axis_size(axis))])


def cross(value, phase):
    slabs, chans = lax.axis_size("slab"), lax.axis_size("chan")
    pairs = [
        (s * chans + c, (s ^ (1 + (c + phase) % 2)) * chans + c)
        for s in range(slabs)
        for c in range(chans)
    ]
    return lax.ppermute(value, ("slab", "chan"), pairs)


def on_device(x_in, weight, bias_vec, grad_out):
    o, _, c_all = weight.shape
    _, n, rows, depth = x_in.shape
    f32, bf16 = jnp.float32, jnp.bfloat16
    cells = n * rows
    flops = 2 * 27 * o * c_all * cells * depth
    scale = 1.0 / math.sqrt(lax.axis_size("slab") * cells * depth)
    me = lax.axis_index("chan").astype(jnp.int32).reshape(1)
    slab = lax.axis_index("slab").astype(jnp.int32).reshape(1)

    block_wide = [pltpu.VMEM((o * cells, depth), f32)]

    x_b = swap(x_in, "chan", 4)
    x_a = swap(x_in, "chan", 2)
    x_side = swap(x_in, "chan", 1)
    x_own, go, go_first, go_second, w_flat, *w_back, bias = call(
        functools.partial(prepare_body, n, rows),
        [
            shape_of((o, n, rows, depth), bf16),
            shape_of((cells, o, depth), bf16),
            shape_of((rows, o, depth), bf16),
            shape_of((rows, o, depth), bf16),
            shape_of((27 * o, c_all), bf16),
            *[shape_of((c_all, taps * o), bf16) for taps in (18, 18, 9, 9)],
            shape_of((o, LANES), f32),
        ],
        [slab] + [in_hbm(a) for a in (x_in, grad_out, jnp.transpose(weight, (1, 0, 2)), bias_vec[None, :])],
        [SMEM] + [HBM] * 4,
        [
            pltpu.VMEM((o, n, rows, depth), bf16),
            pltpu.VMEM((27, o, c_all), bf16),
            pltpu.VMEM((1, o), bf16),
            *block_wide,
            pltpu.SemaphoreType.DMA((4,)),
        ],
        name="prepare",
    )
    go_first = swap(go_first, "slab", 1)
    go_second = swap(go_second, "slab", 3)
    x_b, w_flat = lax.optimization_barrier((x_b, w_flat))
    x_ab = swap(x_b, "chan", 2)
    late_b, go_first, go_second = lax.optimization_barrier((x_b, go_first, go_second))
    x_a_side = swap(x_a, "chan", 1)
    x_b_side = swap(late_b, "chan", 1)
    early = (0, 1, 2, 3, 4, 5, 6)
    (x_all,) = call(
        functools.partial(assemble_body, early),
        [shape_of((c_all, cells * depth), bf16)],
        [me, x_own, x_a, x_b, x_ab, x_side, x_a_side, x_b_side],
        [SMEM] + [VMEM] * 7,
        block_wide,
        flops=ASSEMBLE_FLOPS,
        name="assemble",
    )
    x_ab_side = swap(x_ab, "chan", 1)
    sums = [pltpu.VMEM((3, 2, rows, o, depth), f32)]
    *sent, x_all = call(
        functools.partial(rim_forward_body, rows, o, 7),
        [shape_of((rows, o, depth), bf16)] * 2 + [shape_of((c_all, cells * depth), bf16)],
        [me, slab, w_flat, x_ab_side, x_all],
        [SMEM] * 2 + [VMEM] * 3,
        sums + block_wide,
        flops=flops // 3,
        name="rim_forward",
        aliases={4: 2},
    )
    own, *sent_own = call(
        functools.partial(own_forward_body, rows, o),
        [shape_of((cells, o, depth), f32)] + [shape_of((rows, o, depth), bf16)] * 2,
        [slab, w_flat, x_all],
        [SMEM] + [VMEM] * 2,
        sums,
        flops=flops * 2 // 3,
        name="own_forward",
    )
    sent += sent_own
    received = [swap(a, "slab", 1 + 2 * (at % 2)) for at, a in enumerate(sent)]
    act, total, own_shifts, partial = call(
        functools.partial(own_gradient_body, rows, o, scale),
        [
            shape_of((o, n, rows, depth), bf16),
            shape_of((o, LANES), f32),
            shape_of((18 * o, cells * depth), bf16),
            shape_of((c_all, cells * depth), f32),
        ],
        [me, slab, own, *received[:2], bias, go, *w_back[:2]],
        [SMEM] * 2 + [VMEM] * 7,
        [*[pltpu.VMEM((c_all, 18 * o), bf16)] * 2, *block_wide],
        flops=flops * 2 // 3,
        name="own_gradient",
    )
    (filters,) = call(
        own_filter_body,
        [shape_of((27 * o, c_all), f32)],
        [own_shifts, x_all],
        flops=flops * 2 // 3,
        name="own_filter",
    )
    rim_shifts, other, mine = call(
        functools.partial(rim_gradient_body, rows, o),
        [
            shape_of((9 * o, cells * depth), bf16),
            shape_of((4, cells, o, depth), bf16),
            shape_of((4, cells, o, depth), bf16),
        ],
        [me, slab, *sent[:2], *received[2:], bias, go_first, go_second, partial, *w_back[2:]],
        [SMEM] * 2 + [VMEM] * 10,
        [pltpu.VMEM((c_all, 9 * o), bf16)] * 2,
        flops=flops // 3,
        name="rim_gradient",
    )
    other = swap(other, "chan", 1)
    taps = 14
    first, second = call(
        functools.partial(rim_filter_body, scale, taps, o),
        [shape_of((taps * o, c_all), bf16), shape_of(((28 - taps) * o, c_all), bf16)],
        [rim_shifts, x_all, filters, total],
        flops=flops // 3,
        name="rim_filter",
    )
    first_far = cross(first, 0)
    second_far = cross(second, 0)
    g_own, g_a, g_b, g_ab = call(
        core_sum_body,
        [shape_of((cells, o, depth), f32)] + [shape_of((cells, o, depth), bf16)] * 3,
        [mine, other],
        name="core_sum",
    )
    g_ab = swap(g_ab, "chan", 6)
    g_b = swap(g_b, "chan", 4)
    g_a = swap(g_a, "chan", 2)
    first, second = (
        call(
            pair_body,
            [shape_of(a.shape, bf16)],
            [a, b, g_own],
            [VMEM] * 2 + [ANY],
            name="pair_sum",
        )[0]
        for a, b in ((first, first_far), (second, second_far))
    )
    first_far = cross(first, 1)
    second_far = cross(second, 1)
    (g_own,) = call(
        sum_body,
        [shape_of((cells, o, depth), f32)],
        [g_own, g_b, g_ab, g_a],
        flops=SUM_FLOPS,
        name="sum",
    )
    weight_grad, bias_grad, grad_in = call(
        functools.partial(last_body, taps),
        [
            shape_of((27, o, c_all), f32),
            shape_of((1, o), f32),
            shape_of((o, n, rows, depth), bf16),
        ],
        [first, first_far, second, second_far, g_own],
        scratch=block_wide,
        name="last",
    )
    return act, grad_in, jnp.transpose(weight_grad, (1, 0, 2)), bias_grad[0]


def solution(mesh):
    placed = (
        P("chan", "slab", None, None),
        P("chan", None, None),
        P("chan"),
        P("chan", "slab", None, None),
    )

    def body(x_in, weight, bias_vec, grad_out):
        tiled = (
            weight.shape[0] % 32 == 0
            and x_in.shape[3] == LANES
            and lax.axis_size("slab") == 4
            and lax.axis_size("chan") == 8
            and x_in.shape[1] == 2
        )
        return (on_device if tiled else plain)(x_in, weight, bias_vec, grad_out)

    return jax.shard_map(
        body,
        mesh=mesh,
        in_specs=placed,
        out_specs=(
            P("chan", "slab", None, None),
            P("chan", "slab", None, None),
            P("chan", None, None),
            P("chan"),
        ),
        check_vma=False,
    )
```
